32 devices in a mesh: seq: 2 (over y), ctx: 16 (over z, x, core).
Axes of the slice: x: 2, y: 2, z: 4, core: 2. Of those that a mesh axis runs over, the one named last changes fastest.
Arguments:
- tokens: bfloat16 [2, 4096, 1536], P('seq', 'ctx'), may hold values from -6 to 6
- cotangent: bfloat16 [2, 4096, 1536], P('seq', 'ctx'), may hold values from -6 to 6
- routes: int32 [2, 4096, 4], P('seq', 'ctx'), may hold values from 0 to 15, all different within a row
- fill_order: int32 [2, 4096], P('seq', 'ctx'), may hold values from 0 to 255, as said below
- pic_starts: int32 [2, 4], P('seq'), may hold values from 0 to 3840, as said below
- attn_gain: bfloat16 [1536], P(('seq', 'ctx')), may hold values from 0.5 to 1.5
- moe_gain: bfloat16 [1536], P(('seq', 'ctx')), may hold values from 0.5 to 1.5
- w_query: bfloat16 [1536, 1536], P(('seq', 'ctx')), may hold values from -0.15625 to 0.15625
- key_projection: bfloat16 [1536, 256], P(('seq', 'ctx')), may hold values from -0.15625 to 0.15625
- value_projection: bfloat16 [1536, 256], P(('seq', 'ctx')), may hold values from -0.15625 to 0.15625
- w_out: bfloat16 [1536, 1536], P(('seq', 'ctx')), may hold values from -1.75 to 1.75
- w_router: bfloat16 [1536, 16], P(('seq', 'ctx')), may hold values from -0.078125 to 0.078125
- expert_gate: bfloat16 [16, 1536, 768], P('ctx', 'seq'), may hold values from -0.15625 to 0.15625
- expert_up: bfloat16 [16, 1536, 768], P('ctx', 'seq'), may hold values from -0.15625 to 0.15625
- expert_down: bfloat16 [16, 768, 1536], P('ctx', 'seq'), may hold values from -0.4375 to 0.4375
Outputs:
- output: bfloat16 [2, 4096, 1536], P('seq', 'ctx')
- grad_input: float32 [2, 4096, 1536], P('seq', 'ctx')
- grad_attn_gain: float32 [1536], P(('seq', 'ctx'))
- grad_moe_gain: float32 [1536], P(('seq', 'ctx'))
- grad_query: float32 [1536, 1536], P(('seq', 'ctx'))
- grad_key: float32 [1536, 256], P(('seq', 'ctx'))
- grad_value: float32 [1536, 256], P(('seq', 'ctx'))
- grad_out: float32 [1536, 1536], P(('seq', 'ctx'))
- grad_router: float32 [1536, 16], P(('seq', 'ctx'))
- grad_expert_gate: float32 [16, 1536, 768], P('ctx', 'seq')
- grad_expert_up: float32 [16, 1536, 768], P('ctx', 'seq')
- grad_expert_down: float32 [16, 768, 1536], P('ctx', 'seq')
The draws below stay inside these ranges and needn't reach their ends.
Inputs may be any that keep to these rules, and one draw needn't show every extreme that they name: `fill_order`: within the 1 sequence times 256 positions of each device, every number from 0 to 255 appears once. `pic_starts`: the i-th span of a sequence starts within the i-th of 4 equal parts of it and ends inside that part.
All inputs are finite; a program needn't handle non-finite values.
Results may differ from the reference program's by a relative error of at most 0.024.
Values may be sent and summed in bfloat16 or wider, within the bound.
No kernel may reach another device: no remote copies, remote signals or barrier semaphores. Data moves between devices by JAX's collectives and lax.ppermute only.
A program may use at most 192 MiB of HBM per device.

```python
import math
import jax
import jax.numpy as jnp
from jax import lax

MODEL_WIDTH = 1536
QUERY_HEADS = 12
KEY_VALUE_HEADS = 2
HEAD_WIDTH = 128
FF = 768
TOP = 4
SEQUENCE_LENGTH = 4096
PIC = 256
NPIC = 4
SEQ_GRP = 1
EXPERTS = 16
SEQS = 2
STRETCH = 256
TOK_DEV = 256
CAP = 80
N_SEQ = 2
N_CTX = 16


def draw_fill_order(key, part):
    key = jax.random.fold_in(key, 11)
    query_groups = SEQS // SEQ_GRP
    pieces = SEQUENCE_LENGTH // STRETCH
    piece_keys = jax.random.split(key, query_groups * pieces)

    def shuffle(piece_key):
        return jax.random.permutation(piece_key, TOK_DEV)
    orders = jax.vmap(shuffle)(piece_keys)
    orders = orders.reshape(query_groups, pieces, SEQ_GRP, STRETCH).transpose(0, 2, 1, 3)
    return orders.reshape(SEQS, SEQUENCE_LENGTH).astype(jnp.int32)


def draw_pic_starts(key, part):
    key = jax.random.fold_in(key, 23)
    stride = SEQUENCE_LENGTH // NPIC
    offsets = jax.random.randint(key, (SEQS, NPIC), 0, stride - PIC + 1)
    return (jnp.arange(NPIC, dtype=jnp.int32)[None, :] * stride + offsets).astype(jnp.int32)


def block_scale(stream_key, shape, cuts, low, top_value):
    def one(dim, shards_of):
        heights = jax.random.uniform(jax.random.fold_in(jax.random.fold_in(stream_key, 6), dim), (shards_of,), jnp.float32, low / len(cuts), top_value / len(cuts))
        return jnp.repeat(jnp.exp(heights), shape[dim] // shards_of).reshape((-1,) + (1,) * (len(shape) - dim - 1))

    level = one(*cuts[0])
    for cut in cuts[1:]:
        level = level * one(*cut)
    return level


def distinct(key, rows, count, top, lift):
    order = jax.random.permutation(jax.random.fold_in(key, 1), count)
    favour = order
    for power in range(3):
        favour = favour * favour // count
    favour = favour * lift // count
    tickets = jax.random.randint(jax.random.fold_in(key, 2), (rows, count), 0, 4096) + favour
    fixed_rows = jax.random.permutation(jax.random.fold_in(key, 3), rows)[jnp.arange(count) % rows]
    tickets = jnp.where(jnp.arange(rows)[:, None] == fixed_rows[None, :], 1 << 14, tickets)
    score = tickets * count + jnp.arange(count)
    return lax.top_k(score.astype(jnp.int32), top)[1].astype(jnp.int32)


def bell_draw(own_key, dims, scale, most, cuts=(), kind=jnp.bfloat16):
    values = scale * jax.random.normal(own_key, dims, jnp.float32)
    if cuts:
        values = values * block_scale(own_key, dims, cuts, -0.22, 0.18)
    return jnp.clip(values, -most, most).astype(kind)


def setup_inputs(seed: int = 0) -> dict:
    splits = jax.random.split(jax.random.key(seed), 16)
    return {
        "tokens": bell_draw(splits[0], (SEQS, SEQUENCE_LENGTH, MODEL_WIDTH), 1.0, 6.0, ((0, 2), (1, 16))),
        "cotangent": bell_draw(splits[1], (SEQS, SEQUENCE_LENGTH, MODEL_WIDTH), 1.0, 6.0, ((0, 2), (1, 16))),
        "routes": distinct(splits[2], SEQS * SEQUENCE_LENGTH, EXPERTS, TOP, 2048).reshape((SEQS, SEQUENCE_LENGTH, TOP)),
        "fill_order": draw_fill_order(jax.random.fold_in(splits[15], 71), 0),
        "pic_starts": draw_pic_starts(jax.random.fold_in(splits[15], 71), 0),
        "attn_gain": jnp.clip(1.0 + 0.1 * jax.random.normal(splits[5], (MODEL_WIDTH,), jnp.float32), 0.5, 1.5).astype(jnp.bfloat16),
        "moe_gain": jnp.clip(1.0 + 0.1 * jax.random.normal(splits[6], (MODEL_WIDTH,), jnp.float32), 0.5, 1.5).astype(jnp.bfloat16),
        "w_query": bell_draw(splits[7], (MODEL_WIDTH, QUERY_HEADS * HEAD_WIDTH), MODEL_WIDTH ** -0.5, 0.15625, ((0, 32),)),
        "key_projection": bell_draw(splits[8], (MODEL_WIDTH, KEY_VALUE_HEADS * HEAD_WIDTH), MODEL_WIDTH ** -0.5, 0.15625, ((0, 32),)),
        "value_projection": bell_draw(splits[9], (MODEL_WIDTH, KEY_VALUE_HEADS * HEAD_WIDTH), MODEL_WIDTH ** -0.5, 0.15625, ((0, 32),)),
        "w_out": bell_draw(splits[10], (QUERY_HEADS * HEAD_WIDTH, MODEL_WIDTH), (MODEL_WIDTH // 128) ** -0.5, 1.75, ((0, 32),)),
        "w_router": bell_draw(splits[11], (MODEL_WIDTH, EXPERTS), (4 * MODEL_WIDTH) ** -0.5, 0.078125, ((0, 32),)),
        "expert_gate": bell_draw(splits[12], (EXPERTS, MODEL_WIDTH, FF), MODEL_WIDTH ** -0.5, 0.15625, ((0, 16), (1, 2))),
        "expert_up": bell_draw(splits[13], (EXPERTS, MODEL_WIDTH, FF), MODEL_WIDTH ** -0.5, 0.15625, ((0, 16), (1, 2))),
        "expert_down": bell_draw(splits[14], (EXPERTS, FF, MODEL_WIDTH), (FF // 4) ** -0.5, 0.4375, ((0, 16), (1, 2))),
    }


@jax.custom_vjp
def lower_bound(v):
    return lax.optimization_barrier(v.astype(jnp.bfloat16)).astype(jnp.float32)

@jax.custom_vjp
def lower_bound_reverse(v):
    return v

def low_keep(v):
    return (lower_bound(v), None)

def low_pass(kept, grad):
    return (grad,)

def back_keep(v):
    return (v, None)

def back_low(kept, grad):
    return (lower_bound(grad),)
lower_bound.defvjp(low_keep, low_pass)
lower_bound_reverse.defvjp(back_keep, back_low)
epsilon = 1e-06
rope_base = 10000.0
big_negative = -1e+30

def matrix_multiply(left, right):
    return jnp.dot(left, right, precision=lax.Precision.HIGHEST, preferred_element_type=jnp.float32)

def rms_norm(value_rows, gain):
    return value_rows * lax.rsqrt(lax.optimization_barrier(jnp.mean(value_rows * value_rows, -1, keepdims=True)) + epsilon) * gain

def rope_tables(positions):
    half = HEAD_WIDTH // 2
    inverse = rope_base ** (-(jnp.arange(half, dtype=jnp.float32) * 2.0 / HEAD_WIDTH))
    angles = positions.astype(jnp.float32)[:, None] * inverse[None, :]
    return (jnp.cos(angles), jnp.sin(angles))

def rotate_half(value_rows, cosine_table, sine_table):
    half = value_rows.shape[-1] // 2
    first = value_rows[..., :half]
    second = value_rows[..., half:]
    cosine_table = cosine_table[:, None, :]
    sine_table = sine_table[:, None, :]
    return jnp.concatenate([first * cosine_table - second * sine_table, second * cosine_table + first * sine_table], -1)

def span_ids(positions, starts):
    inside = (positions[None, :, None] >= starts[:, None, :]) & (positions[None, :, None] < starts[:, None, :] + PIC)
    labels = jnp.arange(1, NPIC + 1, dtype=jnp.int32)
    return (lax.optimization_barrier(jnp.sum(jnp.where(inside, labels, 0), -1)) - 1).astype(jnp.int32)

def place(picks, priority, experts, capacity):
    count = picks.shape[0]
    pairs = count * TOP
    flat = picks.reshape(pairs).astype(jnp.int32)
    ranks = (priority[:, None] * TOP + jnp.arange(TOP, dtype=jnp.int32)[None, :]).reshape(pairs).astype(jnp.int32)
    indices = jnp.arange(pairs, dtype=jnp.int32)
    pair_at = jnp.zeros((pairs,), jnp.int32).at[ranks].set(indices)
    ordered = flat[pair_at]
    hot = (ordered[:, None] == jnp.arange(experts, dtype=jnp.int32)[None, :]).astype(jnp.int32)
    pos_sorted = lax.optimization_barrier(jnp.sum((jnp.cumsum(hot, 0) - 1) * hot, 1)).astype(jnp.int32)
    position = jnp.zeros((pairs,), jnp.int32).at[pair_at].set(pos_sorted)
    kept = position < capacity
    pair_slot = jnp.where(kept, flat * capacity + position, experts * capacity).astype(jnp.int32)
    slot_pair = jnp.full((experts * capacity + 1,), pairs, jnp.int32).at[pair_slot].set(indices)[:experts * capacity]
    filled = slot_pair < pairs
    slot_token = (jnp.minimum(slot_pair, pairs - 1) // TOP).astype(jnp.int32)
    return (pair_slot, slot_pair, kept.reshape(count, TOP), filled, slot_token)

def attend_sequence(normalized_input, starts, w_query, key_projection, value_projection):
    positions = jnp.arange(SEQUENCE_LENGTH, dtype=jnp.int32)
    cosine_table, sine_table = rope_tables(positions)
    query_groups = QUERY_HEADS // KEY_VALUE_HEADS
    query_matrix = lower_bound_reverse(matrix_multiply(normalized_input, w_query)).reshape(SEQUENCE_LENGTH, QUERY_HEADS, HEAD_WIDTH)
    query_rotated = lower_bound(rotate_half(query_matrix, cosine_table, sine_table)).reshape(SEQUENCE_LENGTH, KEY_VALUE_HEADS, query_groups, HEAD_WIDTH)
    key_rows = lower_bound_reverse(matrix_multiply(normalized_input, key_projection)).reshape(SEQUENCE_LENGTH, KEY_VALUE_HEADS, HEAD_WIDTH)
    keys_r = lower_bound(rotate_half(key_rows, cosine_table, sine_table))
    value_rows = lower_bound(lower_bound_reverse(matrix_multiply(normalized_input, value_projection))).reshape(SEQUENCE_LENGTH, KEY_VALUE_HEADS, HEAD_WIDTH)
    labels = span_ids(positions, starts[None, :])[0]
    block = min(512, SEQUENCE_LENGTH)
    scale = 1.0 / math.sqrt(HEAD_WIDTH)

    def one_block(index):
        begin = (index * block).astype(jnp.int32)
        queries = lax.dynamic_slice_in_dim(query_rotated, begin, block, 0)
        query_pos = begin + jnp.arange(block, dtype=jnp.int32)
        query_lab = lax.dynamic_slice_in_dim(labels, begin, block, 0)
        scores = jnp.einsum('qhgd,khd->hgqk', queries, keys_r, precision=lax.Precision.HIGHEST) * scale
        scores = lower_bound_reverse(scores)
        allowed = (positions[None, :] <= query_pos[:, None]) | (query_lab[:, None] == labels[None, :]) & (query_lab[:, None] >= 0)
        scores = jnp.where(allowed[None, None], scores, big_negative)
        peak = lax.optimization_barrier(jnp.max(scores, -1, keepdims=True))
        expo = jnp.exp(scores - peak)
        probs = expo / lax.optimization_barrier(jnp.sum(expo, -1, keepdims=True))
        mixed = jnp.einsum('hgqk,khd->qhgd', lower_bound(probs), value_rows, precision=lax.Precision.HIGHEST)
        return mixed.reshape(block, QUERY_HEADS * HEAD_WIDTH)
    outputs = lax.map(jax.checkpoint(one_block), jnp.arange(SEQUENCE_LENGTH // block, dtype=jnp.int32))
    return lower_bound_reverse(lower_bound(outputs.reshape(SEQUENCE_LENGTH, QUERY_HEADS * HEAD_WIDTH)))

def to_blocks(value_rows):
    width = value_rows.shape[-1]
    return value_rows.reshape(SEQ_GRP, N_CTX, STRETCH, width).transpose(1, 0, 2, 3).reshape(N_CTX, TOK_DEV, width)

def from_blocks(value_rows):
    width = value_rows.shape[-1]
    return value_rows.reshape(N_CTX, SEQ_GRP, STRETCH, width).transpose(1, 0, 2, 3).reshape(SEQ_GRP, SEQUENCE_LENGTH, width)

def expert_rows(arguments):
    rows, gate_w, up_w, down_w = arguments
    flat = rows.reshape(-1, MODEL_WIDTH)
    gate_pre = lower_bound_reverse(matrix_multiply(flat, gate_w))
    up_pre = lower_bound_reverse(matrix_multiply(flat, up_w))
    hidden = lower_bound(jax.nn.gelu(gate_pre, approximate=True) * up_pre)
    result = lower_bound_reverse(lower_bound(matrix_multiply(hidden, down_w)))
    return result.reshape(rows.shape)

def layer_group(inputs, picks, priority, starts, gain_one, gain_two, w_query, key_projection, value_projection, w_out, w_router, gate_all, up_all, down_all):
    normalized_input = lower_bound(rms_norm(inputs, gain_one))

    def sequence(arguments):
        return attend_sequence(arguments[0], arguments[1], w_query, key_projection, value_projection)
    attended = lax.map(jax.checkpoint(sequence), (normalized_input, starts))
    branch = lower_bound_reverse(matrix_multiply(attended.reshape(-1, QUERY_HEADS * HEAD_WIDTH), w_out)).reshape(SEQ_GRP, SEQUENCE_LENGTH, MODEL_WIDTH)
    middle = inputs + branch
    enter = lower_bound(rms_norm(middle, gain_two))
    enter_b = to_blocks(enter)
    picks_b = to_blocks(picks)
    priority_b = to_blocks(priority[..., None])[..., 0]
    logits = lower_bound_reverse(jnp.einsum('ntd,de->nte', enter_b, w_router, precision=lax.Precision.HIGHEST))
    choose = (picks_b[..., None] == jnp.arange(EXPERTS, dtype=jnp.int32)).astype(jnp.float32)
    chosen = lax.optimization_barrier(jnp.sum(choose * logits[:, :, None, :], -1))
    gates = jax.nn.softmax(chosen, -1)
    pair_slot, slot_pair, kept, filled, slot_token = jax.vmap(lambda p, q: place(p, q, EXPERTS, CAP))(picks_b, priority_b)
    gathered = jnp.take_along_axis(enter_b, slot_token[..., None], axis=1)
    slot_in = lower_bound_reverse(jnp.where(filled[..., None], gathered, 0.0))
    by_expert = slot_in.reshape(N_CTX, EXPERTS, CAP, MODEL_WIDTH).transpose(1, 0, 2, 3)
    results = lax.map(jax.checkpoint(expert_rows), (by_expert, gate_all, up_all, down_all))
    results = results.transpose(1, 0, 2, 3).reshape(N_CTX, EXPERTS * CAP, MODEL_WIDTH)
    index = jnp.minimum(pair_slot, EXPERTS * CAP - 1)
    rows = jnp.take_along_axis(results, index[..., None], axis=1).reshape(N_CTX, TOK_DEV, TOP, MODEL_WIDTH)
    mixed = lax.optimization_barrier(jnp.sum((gates * kept.astype(jnp.float32))[..., None] * rows, 2))
    return middle + from_blocks(mixed)

def reference(tokens, cotangent, routes, fill_order, pic_starts, attn_gain, moe_gain, w_query, key_projection, value_projection, w_out, w_router, expert_gate, expert_up, expert_down):
    floats = tuple((item.astype(jnp.float32) for item in (tokens, attn_gain, moe_gain, w_query, key_projection, value_projection, w_out, w_router, expert_gate, expert_up, expert_down)))
    picks = routes.reshape(N_SEQ, SEQ_GRP, SEQUENCE_LENGTH, TOP)
    priority = fill_order.reshape(N_SEQ, SEQ_GRP, SEQUENCE_LENGTH)
    starts = pic_starts.reshape(N_SEQ, SEQ_GRP, NPIC)

    def forward(inputs, gain_one, gain_two, query_w, key_w, value_w, out_w, router_w, gate_all, up_all, down_all):

        def group(arguments):
            return layer_group(arguments[0], arguments[1], arguments[2], arguments[3], gain_one, gain_two, query_w, key_w, value_w, out_w, router_w, gate_all, up_all, down_all)
        grouped = inputs.reshape(N_SEQ, SEQ_GRP, SEQUENCE_LENGTH, MODEL_WIDTH)
        result = lax.map(jax.checkpoint(group), (grouped, picks, priority, starts))
        return result.reshape(SEQS, SEQUENCE_LENGTH, MODEL_WIDTH)
    result, pull = jax.vjp(forward, *floats)
    grads = pull(cotangent.astype(jnp.float32))
    return (result.astype(jnp.bfloat16), grads[0], grads[1], grads[2], grads[3], grads[4], grads[5], grads[6], grads[7], grads[8], grads[9], grads[10])
```

```python
import math

import jax
import jax.numpy as jnp
from jax import lax
from jax.sharding import PartitionSpec as P

QUERY_HEADS = 12
KEY_VALUE_HEADS = 2
HEAD_WIDTH = 128
TOP = 4
PIC = 256
NPIC = 4
LANES = 128

epsilon = 1e-06
rope_base = 10000.0
big_negative = -1e30
bf16 = jnp.bfloat16
f32 = jnp.float32


def matmul(left, right):
    return jnp.dot(left, right, preferred_element_type=f32)


def matmul_nt(left, right):
    return lax.dot_general(left, right, (((1,), (1,)), ((), ())), preferred_element_type=f32)


def matmul_tn(left, right):
    return lax.dot_general(left, right, (((0,), (0,)), ((), ())), preferred_element_type=f32)


def rms_scale(rows):
    return lax.rsqrt(jnp.mean(rows * rows, -1, keepdims=True) + epsilon)


def rms_norm(rows, gain):
    return rows * rms_scale(rows) * gain


def rope_tables(positions, head_size):
    half = head_size // 2
    inverse = rope_base ** (-(jnp.arange(half, dtype=f32) * 2.0 / head_size))
    angles = positions.astype(f32)[:, None] * inverse[None, :]
    return (jnp.cos(angles), jnp.sin(angles))


def rotate(rows, heads, cosine, sine):
    shaped = rows.reshape(rows.shape[0], heads, HEAD_WIDTH)
    half = HEAD_WIDTH // 2
    first, second = shaped[..., :half], shaped[..., half:]
    cosine, sine = cosine[:, None, :], sine[:, None, :]
    turned = jnp.concatenate(
        [first * cosine - second * sine, second * cosine + first * sine], -1
    )
    return turned.reshape(rows.shape)


def span_ids(positions, starts):
    inside = (positions[None, :, None] >= starts[:, None, :]) & (
        positions[None, :, None] < starts[:, None, :] + PIC
    )
    labels = jnp.arange(1, NPIC + 1, dtype=jnp.int32)
    return jnp.sum(jnp.where(inside, labels, 0), -1) - 1


def body(
    tokens,
    cotangent,
    routes,
    fill_order,
    pic_starts,
    attn_gain,
    moe_gain,
    w_query,
    key_projection,
    value_projection,
    w_out,
    w_router,
    expert_gate,
    expert_up,
    expert_down,
):
    sequences, stretch, width = tokens.shape
    count = sequences * stretch
    parts = lax.axis_size("ctx")
    experts = parts
    groups = QUERY_HEADS // KEY_VALUE_HEADS
    capacity = (5 * count * TOP + 4 * experts - 1) // (4 * experts)
    scale = 1.0 / math.sqrt(HEAD_WIDTH)
    query_width = QUERY_HEADS * HEAD_WIDTH
    key_width = KEY_VALUE_HEADS * HEAD_WIDTH
    own_rows = w_query.shape[0]
    hidden_width = expert_gate.shape[2]
    both = ("seq", "ctx")

    def padded(columns):
        block = jnp.concatenate(columns, 1)
        return jnp.pad(block, ((0, 0), (0, LANES - block.shape[1])))

    first_set = lax.all_gather(
        jnp.concatenate(
            [w_query, key_projection, value_projection, padded([attn_gain[:, None]])], 1
        ),
        both,
        axis=0,
        tiled=True,
    )
    second_set = lax.all_gather(
        jnp.concatenate([w_out, padded([w_router, moe_gain[:, None]])], 1),
        both,
        axis=0,
        tiled=True,
    )
    in_rows, down_rows = expert_gate.shape[1], expert_down.shape[1]
    expert_set = lax.all_gather(
        jnp.concatenate(
            [jnp.concatenate([expert_gate[0], expert_up[0]], 1), expert_down[0]], 0
        ),
        "seq",
        axis=0,
        tiled=False,
    )
    weight_qkv = first_set[:, : query_width + 2 * key_width]
    gain_one = first_set[:, query_width + 2 * key_width].astype(f32)
    full_out = second_set[:, :width]
    full_router = second_set[:, width : width + experts]
    gain_two = second_set[:, width + experts].astype(f32)
    gate_up = expert_set[:, :in_rows].reshape(-1, 2 * hidden_width)
    down = expert_set[:, in_rows:].reshape(-1, width)

    picks = routes.reshape(count, TOP)
    order = fill_order.reshape(count)
    routed = jnp.any(picks[:, :, None] == jnp.arange(experts, dtype=jnp.int32), 1)
    earlier = (order[None, :] < order[:, None]).astype(bf16)
    place = matmul(earlier, routed.astype(bf16)).astype(jnp.int32)
    place = jnp.where(routed, place, capacity)
    chosen_slot = (
        place.T[:, None, :] == jnp.arange(capacity, dtype=jnp.int32)[None, :, None]
    )
    slot_map = chosen_slot.astype(bf16).reshape(experts * capacity, count)
    kept = (place < capacity).astype(f32)

    def exchange(rows):
        return lax.all_to_all(rows, "ctx", split_axis=0, concat_axis=0, tiled=True)

    def exchange_rows(rows):
        return exchange(rows.reshape(experts, capacity, width)).reshape(-1, width)

    out_slope = cotangent.reshape(count, width)
    slope_rows = exchange_rows(matmul(slot_map, out_slope).astype(bf16))

    positions = lax.axis_index("ctx") * stretch + jnp.arange(stretch, dtype=jnp.int32)
    cosine, sine = rope_tables(positions, HEAD_WIDTH)
    inputs = tokens.astype(f32).reshape(count, width)
    normed = rms_norm(inputs, gain_one).astype(bf16)
    projected = matmul(normed, weight_qkv)
    query_rows = rotate(projected[:, :query_width], QUERY_HEADS, cosine, sine).astype(bf16)
    key_rows = rotate(
        projected[:, query_width : query_width + key_width], KEY_VALUE_HEADS, cosine, sine
    ).astype(bf16)
    value_rows = projected[:, query_width + key_width :].astype(bf16)
    key_values = lax.all_gather(
        jnp.concatenate([key_rows, value_rows], 1), "ctx", axis=0, tiled=True
    )

    labels = span_ids(positions, pic_starts)

    def allowed(start, span):
        key_pos = start + jnp.arange(span, dtype=jnp.int32)
        key_labels = span_ids(key_pos, pic_starts)
        causal = key_pos[None, :] <= positions[:, None]
        same = (labels[0][:, None] == key_labels[0][None, :]) & (labels[0][:, None] >= 0)
        return (causal | same)[None, None]

    query_lattice = query_rows.reshape(
        count, KEY_VALUE_HEADS, groups, HEAD_WIDTH
    ).transpose(1, 2, 0, 3)
    span = math.gcd(stretch * parts, 512)
    steps = stretch * parts // span

    def key_block(index):
        block = lax.dynamic_slice_in_dim(key_values, index * span, span, 0)
        keys = block[:, :key_width].reshape(span, KEY_VALUE_HEADS, HEAD_WIDTH)
        values = block[:, key_width:].reshape(span, KEY_VALUE_HEADS, HEAD_WIDTH)
        return keys, values, allowed(index * span, span)

    def attend(index, carry):
        running, total, accum = carry
        keys, values, mask = key_block(index)
        scores = scale * jnp.einsum(
            "hgcd,nhd->hgcn", query_lattice, keys, preferred_element_type=f32
        )
        scores = jnp.where(mask, scores, big_negative)
        newest = jnp.maximum(running, jnp.max(scores, -1))
        shrink = jnp.exp(running - newest)
        weights = jnp.where(mask, jnp.exp(scores - newest[..., None]), 0.0)
        total = total * shrink + jnp.sum(weights, -1)
        accum = accum * shrink[..., None] + jnp.einsum(
            "hgcn,nhd->hgcd", weights.astype(bf16), values, preferred_element_type=f32
        )
        return newest, total, accum

    shape = (KEY_VALUE_HEADS, groups, count)
    running, total, accum = lax.fori_loop(
        0,
        steps,
        attend,
        (
            jnp.full(shape, big_negative, f32),
            jnp.zeros(shape, f32),
            jnp.zeros(shape + (HEAD_WIDTH,), f32),
        ),
    )
    mixed_heads = accum / total[..., None]
    log_total = running + jnp.log(total)
    attended = mixed_heads.astype(bf16).transpose(2, 0, 1, 3).reshape(count, query_width)

    middle = inputs + matmul(attended, full_out)
    enter = rms_norm(middle, gain_two).astype(bf16)
    arrived = exchange_rows(matmul(slot_map, enter).astype(bf16))
    logits = matmul(enter, full_router)
    logits = jnp.where(routed, logits, big_negative)
    gates = jnp.where(routed, jnp.exp(logits - jnp.max(logits, -1, keepdims=True)), 0.0)
    gates = gates / jnp.sum(gates, -1, keepdims=True)
    slot_gates = jnp.sum(jnp.where(chosen_slot, gates.T[:, None, :], 0.0), -1)
    slot_gates = exchange(slot_gates).reshape(-1, 1)

    pre = matmul(arrived, gate_up)

    def activate(both_parts):
        return (
            jax.nn.gelu(both_parts[:, :hidden_width], approximate=True)
            * both_parts[:, hidden_width:]
        )

    hidden, pull_act = jax.vjp(activate, pre)
    hidden = hidden.astype(bf16)
    result = matmul(hidden, down).astype(bf16)
    slope_wide = slope_rows.astype(f32)
    slope_gates = jnp.sum(slope_wide * result.astype(f32), -1).reshape(experts, capacity)
    slope_slots = (slot_gates * slope_wide).astype(bf16)
    slope_hidden = matmul_nt(slope_slots, down)
    slope_pre = pull_act(slope_hidden)[0].astype(bf16)
    slope_arrived = matmul_nt(slope_pre, gate_up).astype(bf16)

    returned_slopes = exchange_rows(slope_arrived)
    returned_gates = exchange(slope_gates)
    returned = exchange_rows(result)

    grad_gate_up = matmul_tn(arrived, slope_pre).astype(bf16)
    grad_down = matmul_tn(hidden, slope_slots).astype(bf16)
    sectors = lax.axis_size("seq")
    grad_experts = lax.psum_scatter(
        jnp.concatenate(
            [
                grad_gate_up.reshape(sectors, in_rows, 2 * hidden_width),
                grad_down.reshape(sectors, down_rows, width),
            ],
            1,
        ),
        "seq",
        scatter_dimension=0,
        tiled=True,
    )[0].astype(f32)

    mix = jnp.where(chosen_slot, gates.T[:, None, :], 0.0).reshape(experts * capacity, count)
    mix_high = mix.astype(bf16)
    mix_low = (mix - mix_high.astype(f32)).astype(bf16)
    mixture = matmul_tn(mix_high, returned) + matmul_tn(mix_low, returned)
    output = (middle + mixture).astype(bf16).reshape(tokens.shape)

    slope_gate = jnp.sum(jnp.where(chosen_slot, returned_gates[:, :, None], 0.0), 1).T
    slope_logits = gates * (slope_gate - jnp.sum(gates * slope_gate, -1, keepdims=True))
    slope_logits = slope_logits.astype(bf16)
    grad_router = matmul_tn(enter, slope_logits)
    slope_enter = matmul_tn(slot_map, returned_slopes) + matmul_nt(slope_logits, full_router)

    pull_two = jax.vjp(rms_norm, middle, gain_two)[1]
    slope_middle, grad_gain_two = pull_two(slope_enter)
    slope_middle = out_slope.astype(f32) + slope_middle
    slope_branch = slope_middle.astype(bf16)
    grad_out = matmul_tn(attended, slope_branch)
    slope_attended = matmul_nt(slope_branch, full_out).astype(bf16)
    slope_lattice = slope_attended.reshape(
        count, KEY_VALUE_HEADS, groups, HEAD_WIDTH
    ).transpose(1, 2, 0, 3)
    delta = jnp.sum(slope_lattice.astype(f32) * mixed_heads, -1)

    grads_second = lax.psum_scatter(
        jnp.concatenate([grad_out, padded([grad_router, grad_gain_two[:, None]])], 1).astype(
            bf16
        ),
        both,
        scatter_dimension=0,
        tiled=True,
    ).astype(f32)

    def attend_back(index, carry):
        slope_q, slope_kv = carry
        keys, values, mask = key_block(index)
        scores = scale * jnp.einsum(
            "hgcd,nhd->hgcn", query_lattice, keys, preferred_element_type=f32
        )
        probs = jnp.where(mask, jnp.exp(scores - log_total[..., None]), 0.0)
        slope_probs = jnp.einsum(
            "hgcd,nhd->hgcn", slope_lattice, values, preferred_element_type=f32
        )
        slope_scores = (probs * (slope_probs - delta[..., None])).astype(bf16)
        slope_q = slope_q + scale * jnp.einsum(
            "hgcn,nhd->hgcd", slope_scores, keys, preferred_element_type=f32
        )
        slope_k = scale * jnp.einsum(
            "hgcn,hgcd->nhd", slope_scores, query_lattice, preferred_element_type=f32
        )
        slope_v = jnp.einsum(
            "hgcn,hgcd->nhd", probs.astype(bf16), slope_lattice, preferred_element_type=f32
        )
        both_kv = jnp.concatenate(
            [slope_k.reshape(span, key_width), slope_v.reshape(span, key_width)], 1
        ).astype(bf16)
        return slope_q, lax.dynamic_update_slice_in_dim(slope_kv, both_kv, index * span, 0)

    slope_q, slope_kv = lax.fori_loop(
        0,
        steps,
        attend_back,
        (
            jnp.zeros(shape + (HEAD_WIDTH,), f32),
            jnp.zeros((stretch * parts, 2 * key_width), bf16),
        ),
    )
    slope_kv = lax.psum_scatter(slope_kv, "ctx", scatter_dimension=0, tiled=True).astype(f32)
    slope_query = rotate(
        slope_q.transpose(2, 0, 1, 3).reshape(count, query_width), QUERY_HEADS, cosine, -sine
    )
    slope_key = rotate(slope_kv[:, :key_width], KEY_VALUE_HEADS, cosine, -sine)
    slope_projected = jnp.concatenate(
        [slope_query, slope_key, slope_kv[:, key_width:]], 1
    ).astype(bf16)
    grad_qkv = matmul_tn(normed, slope_projected)
    slope_normed = matmul_nt(slope_projected, weight_qkv)
    pull_one = jax.vjp(rms_norm, inputs, gain_one)[1]
    slope_inputs, grad_gain_one = pull_one(slope_normed)
    grad_input = (slope_middle + slope_inputs).reshape(tokens.shape)
    grads_first = lax.psum_scatter(
        jnp.concatenate([grad_qkv, padded([grad_gain_one[:, None]])], 1).astype(bf16),
        both,
        scatter_dimension=0,
        tiled=True,
    ).astype(f32)
    return (
        output,
        grad_input,
        grads_first[:, query_width + 2 * key_width],
        grads_second[:, width + experts],
        grads_first[:, :query_width],
        grads_first[:, query_width : query_width + key_width],
        grads_first[:, query_width + key_width : query_width + 2 * key_width],
        grads_second[:, :width],
        grads_second[:, width : width + experts],
        grad_experts[None, :in_rows, :hidden_width],
        grad_experts[None, :in_rows, hidden_width:],
        grad_experts[None, in_rows:],
    )


def solution(mesh):
    rows = P("seq", "ctx", None)
    shard = P(("seq", "ctx"), None)
    vector = P(("seq", "ctx"))
    expert = P("ctx", "seq", None)
    return jax.shard_map(
        body,
        mesh=mesh,
        in_specs=(rows, rows, rows, P("seq", "ctx"), P("seq", None), vector, vector)
        + (shard,) * 5
        + (expert,) * 3,
        out_specs=(rows, rows, vector, vector) + (shard,) * 5 + (expert,) * 3,
        check_vma=False,
    )
```

```python
import math

import jax
import jax.numpy as jnp
from jax import lax
from jax.experimental import pallas as pl
from jax.experimental.pallas import tpu as pltpu
from jax.sharding import PartitionSpec as P

QUERY_HEADS = 12
KEY_VALUE_HEADS = 2
HEAD_WIDTH = 128
TOP = 4
PIC = 256
NPIC = 4
LANES = 128
GROUPS = QUERY_HEADS // KEY_VALUE_HEADS
QUERY_WIDTH = QUERY_HEADS * HEAD_WIDTH
KEY_WIDTH = KEY_VALUE_HEADS * HEAD_WIDTH
SCALE = 1.0 / math.sqrt(HEAD_WIDTH)
EXP2_SCALE = SCALE * math.log2(math.e)
BLOCKS = 2
VMEM_BYTES = 48 << 20

epsilon = 1e-06
rope_base = 10000.0
big_negative = -1e30
bf16 = jnp.bfloat16
f32 = jnp.float32


def matmul(left, right):
    return jnp.dot(left, right, preferred_element_type=f32)


def matmul_nt(left, right):
    return lax.dot_general(left, right, (((1,), (1,)), ((), ())), preferred_element_type=f32)


def matmul_tn(left, right):
    return lax.dot_general(left, right, (((0,), (0,)), ((), ())), preferred_element_type=f32)


def rms_scale(rows):
    return lax.rsqrt(jnp.mean(rows * rows, -1, keepdims=True) + epsilon)


def rms_norm(rows, gain):
    return rows * rms_scale(rows) * gain


def rope_tables(positions, head_size):
    half = head_size // 2
    inverse = rope_base ** (-(jnp.arange(half, dtype=f32) * 2.0 / head_size))
    angles = positions.astype(f32)[:, None] * inverse[None, :]
    return (jnp.cos(angles), jnp.sin(angles))


def rotate(rows, heads, cosine, sine):
    shaped = rows.reshape(rows.shape[0], heads, HEAD_WIDTH)
    half = HEAD_WIDTH // 2
    first, second = shaped[..., :half], shaped[..., half:]
    cosine, sine = cosine[:, None, :], sine[:, None, :]
    turned = jnp.concatenate(
        [first * cosine - second * sine, second * cosine + first * sine], -1
    )
    return turned.reshape(rows.shape)


def bits(axis):
    size = lax.axis_size(axis)
    return [(axis, 1 << place) for place in reversed(range(size.bit_length() - 1))]


def swap(block, axis, bit):
    size = lax.axis_size(axis)
    return lax.ppermute(block, axis, [(index, index ^ bit) for index in range(size)])


def gather_blocks(block, stages, order):
    held = []
    for stage in stages:
        axis, bit = stage
        other = swap(block, axis, bit)
        upper = (lax.axis_index(axis) & bit) > 0
        place = sum(order.index(known) < order.index(stage) for known in held)
        block = jnp.stack(
            [jnp.where(upper, other, block), jnp.where(upper, block, other)], place
        )
        held.append(stage)
    return block


def scatter_sum(blocks, stages, order):
    left = list(order)
    for stage in stages:
        axis, bit = stage
        mine = ((lax.axis_index(axis) & bit) > 0).astype(jnp.int32)
        place = left.index(stage)
        sent = lax.dynamic_index_in_dim(blocks, 1 - mine, place, keepdims=False)
        kept = lax.dynamic_index_in_dim(blocks, mine, place, keepdims=False)
        blocks = kept.astype(f32) + swap(sent.astype(bf16), axis, bit).astype(f32)
        left.remove(stage)
        if left:
            blocks = blocks.astype(bf16)
    return blocks


def visible_keys(meta, step, stretch):
    span = BLOCKS * stretch
    keys = step * span + lax.broadcasted_iota(jnp.int32, (span, 1), 0)
    queries = meta[0] * stretch + lax.broadcasted_iota(jnp.int32, (1, stretch), 1)

    def label(positions):
        found = jnp.zeros(positions.shape, jnp.int32)
        for index in range(NPIC):
            start = meta[1 + index]
            inside = (positions >= start) & (positions < start + PIC)
            found = jnp.where(inside, index + 1, found)
        return found

    query_label = label(queries)
    return (keys <= queries) | ((label(keys) == query_label) & (query_label > 0))


def for_each_step(meta, stretch, steps, process, skip=None):
    span = BLOCKS * stretch
    low, high = meta[0] * stretch, (meta[0] + 1) * stretch

    def turn(step, carry):
        needed = step * span < high + PIC - 1
        edge = (step + 1) * span > low

        @pl.when(needed & edge)
        def _():
            process(step, True)

        @pl.when(needed & jnp.logical_not(edge))
        def _():
            process(step, False)

        if skip is not None:

            @pl.when(jnp.logical_not(needed))
            def _():
                skip(step)

        return carry

    lax.fori_loop(0, steps, turn, 0)


def head_columns(head, start=0):
    return slice(start + head * HEAD_WIDTH, start + (head + 1) * HEAD_WIDTH)


def attend_kernel(meta, query, key_value, out, log_total, peak, total, accum):
    stretch = query.shape[0]
    span = BLOCKS * stretch
    peak[...] = jnp.full(peak.shape, big_negative, f32)
    total[...] = jnp.zeros(total.shape, f32)
    accum[...] = jnp.zeros(accum.shape, f32)

    def process(step, edge):
        rows = pl.ds(pl.multiple_of(step * span, span), span)
        if edge:
            visible = visible_keys(meta, step, stretch)
        keys, values = [], []
        for group in range(KEY_VALUE_HEADS):
            keys.append(key_value[rows, head_columns(group)])
            turned = key_value[rows, head_columns(group, KEY_WIDTH)].T
            values.append(jnp.concatenate([turned, jnp.ones((16, span), bf16)], 0))

        def score(head):
            scores = matmul_nt(keys[head // GROUPS], query[:, head_columns(head)])
            if edge:
                scores = jnp.where(visible, scores, big_negative)
            old = peak[head : head + 1, :]
            return scores, old, jnp.maximum(old, jnp.max(scores, 0, keepdims=True))

        def weigh(head, scores, old, new):
            weights = jnp.exp2((scores - new) * EXP2_SCALE).astype(bf16)
            shrink = jnp.exp2((old - new) * EXP2_SCALE)
            sums = matmul(values[head // GROUPS], weights)
            row, columns = slice(head, head + 1), head_columns(head)
            peak[row, :] = new
            total[row, :] = total[row, :] * shrink + sums[HEAD_WIDTH : HEAD_WIDTH + 1]
            accum[columns, :] = accum[columns, :] * shrink + sums[:HEAD_WIDTH]

        waiting = []
        for head in range(QUERY_HEADS):
            waiting.append((head, *score(head)))
            if len(waiting) > 2:
                weigh(*waiting.pop(0))
        for item in waiting:
            weigh(*item)

    for_each_step(meta, stretch, key_value.shape[0] // span, process)
    for head in range(QUERY_HEADS):
        row, columns = slice(head, head + 1), head_columns(head)
        out[:, columns] = (accum[columns, :] / total[row, :]).T
        log_total[row, :] = peak[row, :] * EXP2_SCALE + jnp.log2(total[row, :])


def attend_back_kernel(
    meta, query, slope, log_total, delta, key_value, slope_query, slope_kv, accum
):
    stretch = query.shape[0]
    span = BLOCKS * stretch
    accum[...] = jnp.zeros(accum.shape, f32)

    def process(step, edge):
        rows = pl.ds(pl.multiple_of(step * span, span), span)
        if edge:
            visible = visible_keys(meta, step, stretch)
        for group in range(KEY_VALUE_HEADS):
            keys = key_value[rows, head_columns(group)]
            values = key_value[rows, head_columns(group, KEY_WIDTH)]
            keys_turned = keys.T
            slope_k = jnp.zeros((span, HEAD_WIDTH), f32)
            slope_v = jnp.zeros((span, HEAD_WIDTH), f32)
            for head in range(group * GROUPS, (group + 1) * GROUPS):
                row, columns = slice(head, head + 1), head_columns(head)
                own_query, own_slope = query[:, columns], slope[:, columns]
                scores = matmul_nt(keys, own_query)
                probs = jnp.exp2(scores * EXP2_SCALE - log_total[row, :])
                if edge:
                    probs = jnp.where(visible, probs, 0.0)
                slope_probs = matmul_nt(values, own_slope)
                slope_scores = (probs * (slope_probs - delta[row, :])).astype(bf16)
                slope_v = slope_v + matmul(probs.astype(bf16), own_slope)
                slope_k = slope_k + matmul(slope_scores, own_query)
                accum[columns, :] = accum[columns, :] + matmul(keys_turned, slope_scores)
            slope_kv[rows, head_columns(group)] = (slope_k * SCALE).astype(bf16)
            slope_kv[rows, head_columns(group, KEY_WIDTH)] = slope_v.astype(bf16)

    def skip(step):
        rows = pl.ds(pl.multiple_of(step * span, span), span)
        slope_kv[rows, :] = jnp.zeros((span, 2 * KEY_WIDTH), bf16)

    for_each_step(meta, stretch, key_value.shape[0] // span, process, skip)
    for head in range(QUERY_HEADS):
        columns = head_columns(head)
        slope_query[:, columns] = (accum[columns, :] * SCALE).T


def attention_call(kernel, outs, scratch, products, name, meta, *operands):
    vmem = pl.BlockSpec(memory_space=pltpu.VMEM)
    pairs = QUERY_HEADS * operands[0].shape[0] * operands[-1].shape[0]
    return pl.pallas_call(
        kernel,
        out_shape=outs,
        in_specs=[pl.BlockSpec(memory_space=pltpu.SMEM)] + [vmem] * len(operands),
        out_specs=(vmem,) * len(outs),
        scratch_shapes=[pltpu.VMEM(shape, f32) for shape in scratch],
        compiler_params=pltpu.CompilerParams(vmem_limit_bytes=VMEM_BYTES),
        cost_estimate=pl.CostEstimate(
            flops=products * 4 * HEAD_WIDTH * pairs,
            bytes_accessed=4 * QUERY_WIDTH * 1024,
            transcendentals=pairs,
        ),
        name=name,
    )(meta, *operands)


def attend(meta, query, key_value):
    stretch = query.shape[0]
    stats = (QUERY_HEADS, stretch)
    outs = (
        jax.ShapeDtypeStruct((stretch, QUERY_WIDTH), f32),
        jax.ShapeDtypeStruct(stats, f32),
    )
    scratch = [stats, stats, (QUERY_WIDTH, stretch)]
    return attention_call(attend_kernel, outs, scratch, 2, "attend", meta, query, key_value)


def attend_back(meta, query, slope, log_total, delta, key_value):
    stretch = query.shape[0]
    outs = (
        jax.ShapeDtypeStruct((stretch, QUERY_WIDTH), f32),
        jax.ShapeDtypeStruct(key_value.shape, bf16),
    )
    operands = (meta, query, slope, log_total, delta, key_value)
    scratch = [(QUERY_WIDTH, stretch)]
    return attention_call(attend_back_kernel, outs, scratch, 5, "attend_back", *operands)


def body(
    tokens,
    cotangent,
    routes,
    fill_order,
    pic_starts,
    attn_gain,
    moe_gain,
    w_query,
    key_projection,
    value_projection,
    w_out,
    w_router,
    expert_gate,
    expert_up,
    expert_down,
):
    sequences, stretch, width = tokens.shape
    count = sequences * stretch
    parts = lax.axis_size("ctx")
    experts = parts
    capacity = (5 * count * TOP + 4 * experts - 1) // (4 * experts)
    query_width, key_width = QUERY_WIDTH, KEY_WIDTH
    hidden_width = expert_gate.shape[2]
    both = ("seq", "ctx")
    seq_bits, ctx_bits = bits("seq"), bits("ctx")
    all_bits = seq_bits + ctx_bits
    outward = ctx_bits[:-2] + seq_bits + ctx_bits[-2:]
    inward = outward[::-1]

    def padded(columns):
        block = jnp.concatenate(columns, 1)
        return jnp.pad(block, ((0, 0), (0, LANES - block.shape[1])))

    first_set = lax.all_gather(
        jnp.concatenate(
            [w_query, key_projection, value_projection, padded([attn_gain[:, None]])], 1
        ),
        both,
        axis=0,
        tiled=True,
    )
    second_set = gather_blocks(
        jnp.concatenate([w_out, padded([w_router, moe_gain[:, None]])], 1), outward, all_bits
    ).reshape(width, -1)
    in_rows, down_rows = expert_gate.shape[1], expert_down.shape[1]
    expert_set = gather_blocks(
        jnp.concatenate(
            [jnp.concatenate([expert_gate[0], expert_up[0]], 1), expert_down[0]], 0
        ),
        seq_bits[::-1],
        seq_bits,
    ).reshape(-1, in_rows + down_rows, width)
    weight_qkv = first_set[:, : query_width + 2 * key_width]
    gain_one = first_set[:, query_width + 2 * key_width].astype(f32)
    full_out = second_set[:, :width]
    full_router = second_set[:, width : width + experts]
    gain_two = second_set[:, width + experts].astype(f32)
    gate_up = expert_set[:, :in_rows].reshape(-1, 2 * hidden_width)
    down = expert_set[:, in_rows:].reshape(-1, width)

    picks = routes.reshape(count, TOP)
    order = fill_order.reshape(count)
    routed = jnp.any(picks[:, :, None] == jnp.arange(experts, dtype=jnp.int32), 1)
    earlier = (order[None, :] < order[:, None]).astype(bf16)
    place = matmul(earlier, routed.astype(bf16)).astype(jnp.int32)
    place = jnp.where(routed, place, capacity)
    chosen_slot = (
        place.T[:, None, :] == jnp.arange(capacity, dtype=jnp.int32)[None, :, None]
    )
    slot_map = chosen_slot.astype(bf16).reshape(experts * capacity, count)
    kept = (place < capacity).astype(f32)

    def exchange(rows):
        return lax.all_to_all(rows, "ctx", split_axis=0, concat_axis=0, tiled=True)

    def exchange_rows(rows):
        return exchange(rows.reshape(experts, capacity, width)).reshape(-1, width)

    out_slope = cotangent.reshape(count, width)
    slope_rows = exchange_rows(matmul(slot_map, out_slope).astype(bf16))

    positions = lax.axis_index("ctx") * stretch + jnp.arange(stretch, dtype=jnp.int32)
    cosine, sine = rope_tables(positions, HEAD_WIDTH)
    inputs = tokens.astype(f32).reshape(count, width)
    normed = rms_norm(inputs, gain_one).astype(bf16)
    projected = matmul(normed, weight_qkv)
    query_rows = rotate(projected[:, :query_width], QUERY_HEADS, cosine, sine).astype(bf16)
    key_rows = rotate(
        projected[:, query_width : query_width + key_width], KEY_VALUE_HEADS, cosine, sine
    ).astype(bf16)
    value_rows = projected[:, query_width + key_width :].astype(bf16)
    key_values = lax.all_gather(
        jnp.concatenate([key_rows, value_rows], 1), "ctx", axis=0, tiled=True
    )

    meta = jnp.concatenate([lax.axis_index("ctx").astype(jnp.int32)[None], pic_starts[0]])
    mixed_heads, log_total = attend(meta, query_rows, key_values)
    mixed_heads, slope_rows = lax.optimization_barrier((mixed_heads, slope_rows))
    attended = mixed_heads.astype(bf16)

    middle = inputs + matmul(attended, full_out)
    enter = rms_norm(middle, gain_two).astype(bf16)
    arrived = exchange_rows(matmul(slot_map, enter).astype(bf16))
    logits = matmul(enter, full_router)
    logits = jnp.where(routed, logits, big_negative)
    gates = jnp.where(routed, jnp.exp(logits - jnp.max(logits, -1, keepdims=True)), 0.0)
    gates = gates / jnp.sum(gates, -1, keepdims=True)
    slot_gates = jnp.sum(jnp.where(chosen_slot, gates.T[:, None, :], 0.0), -1)
    slot_gates = exchange(slot_gates).reshape(-1, 1)

    pre = matmul(arrived, gate_up)

    def activate(both_parts):
        return (
            jax.nn.gelu(both_parts[:, :hidden_width], approximate=True)
            * both_parts[:, hidden_width:]
        )

    hidden, pull_act = jax.vjp(activate, pre)
    hidden = hidden.astype(bf16)
    result = matmul(hidden, down).astype(bf16)
    slope_wide = slope_rows.astype(f32)
    slope_gates = jnp.sum(slope_wide * result.astype(f32), -1).reshape(experts, capacity)
    slope_slots = (slot_gates * slope_wide).astype(bf16)
    slope_hidden = matmul_nt(slope_slots, down)
    slope_pre = pull_act(slope_hidden)[0].astype(bf16)
    slope_arrived = matmul_nt(slope_pre, gate_up).astype(bf16)

    returned_slopes = exchange_rows(slope_arrived)
    returned_gates = exchange(slope_gates)
    grad_gate_up = matmul_tn(arrived, slope_pre)
    grad_down = matmul_tn(hidden, slope_slots)
    sectors = lax.axis_size("seq")
    grad_experts = jnp.concatenate(
        [
            grad_gate_up.reshape(sectors, in_rows, 2 * hidden_width),
            grad_down.reshape(sectors, down_rows, width),
        ],
        1,
    ).astype(bf16)
    returned_slopes, grad_experts = lax.optimization_barrier((returned_slopes, grad_experts))
    returned = exchange_rows(lax.optimization_barrier((result, returned_slopes))[0])
    grad_experts = scatter_sum(
        grad_experts.reshape([2] * len(seq_bits) + [in_rows + down_rows, width]),
        seq_bits,
        seq_bits,
    )

    mix = jnp.where(chosen_slot, gates.T[:, None, :], 0.0).reshape(experts * capacity, count)
    mix_high = mix.astype(bf16)
    mix_low = (mix - mix_high.astype(f32)).astype(bf16)
    mixture = matmul_tn(mix_high, returned) + matmul_tn(mix_low, returned)
    output = (middle + mixture).astype(bf16).reshape(tokens.shape)

    slope_gate = jnp.sum(jnp.where(chosen_slot, returned_gates[:, :, None], 0.0), 1).T
    slope_logits = gates * (slope_gate - jnp.sum(gates * slope_gate, -1, keepdims=True))
    slope_logits = slope_logits.astype(bf16)
    grad_router = matmul_tn(enter, slope_logits)
    slope_enter = matmul_tn(slot_map, returned_slopes) + matmul_nt(slope_logits, full_router)

    pull_two = jax.vjp(rms_norm, middle, gain_two)[1]
    slope_middle, grad_gain_two = pull_two(slope_enter)
    slope_middle = out_slope.astype(f32) + slope_middle
    slope_branch = slope_middle.astype(bf16)
    grad_out = matmul_tn(attended, slope_branch)
    slope_attended = matmul_nt(slope_branch, full_out).astype(bf16)
    delta = slope_attended.astype(f32) * mixed_heads
    delta = jnp.sum(delta.reshape(count, QUERY_HEADS, HEAD_WIDTH), -1).T

    def scatter_rows(grads, stages, order):
        rows = grads.shape[0] >> len(order)
        return scatter_sum(grads.reshape([2] * len(order) + [rows, -1]), stages, order)

    grads_second = jnp.concatenate(
        [grad_out, padded([grad_router, grad_gain_two[:, None]])], 1
    ).astype(bf16)
    slope_attended, grads_second = lax.optimization_barrier((slope_attended, grads_second))
    grads_second = scatter_rows(grads_second, inward, all_bits)

    slope_q, slope_kv = attend_back(
        meta, query_rows, slope_attended, log_total, delta, key_values
    )
    slope_query = rotate(slope_q, QUERY_HEADS, cosine, -sine).astype(bf16)
    grads_query = scatter_rows(matmul_tn(normed, slope_query).astype(bf16), inward, all_bits)
    slope_kv = scatter_rows(slope_kv, ctx_bits[::-1], ctx_bits)
    slope_key = rotate(slope_kv[:, :key_width], KEY_VALUE_HEADS, cosine, -sine)
    slope_rest = jnp.concatenate([slope_key, slope_kv[:, key_width:]], 1).astype(bf16)
    grad_kv = matmul_tn(normed, slope_rest)
    slope_normed = matmul_nt(slope_query, weight_qkv[:, :query_width])
    slope_normed = slope_normed + matmul_nt(slope_rest, weight_qkv[:, query_width:])
    pull_one = jax.vjp(rms_norm, inputs, gain_one)[1]
    slope_inputs, grad_gain_one = pull_one(slope_normed)
    grad_input = (slope_middle + slope_inputs).reshape(tokens.shape)
    grads_rest = scatter_rows(
        jnp.concatenate([grad_kv, padded([grad_gain_one[:, None]])], 1).astype(bf16),
        inward,
        all_bits,
    )
    return (
        output,
        grad_input,
        grads_rest[:, 2 * key_width],
        grads_second[:, width + experts],
        grads_query,
        grads_rest[:, :key_width],
        grads_rest[:, key_width : 2 * key_width],
        grads_second[:, :width],
        grads_second[:, width : width + experts],
        grad_experts[None, :in_rows, :hidden_width],
        grad_experts[None, :in_rows, hidden_width:],
        grad_experts[None, in_rows:],
    )


def solution(mesh):
    rows = P("seq", "ctx", None)
    shard = P(("seq", "ctx"), None)
    vector = P(("seq", "ctx"))
    expert = P("ctx", "seq", None)
    return jax.shard_map(
        body,
        mesh=mesh,
        in_specs=(rows, rows, rows, P("seq", "ctx"), P("seq", None), vector, vector)
        + (shard,) * 5
        + (expert,) * 3,
        out_specs=(rows, rows, vector, vector) + (shard,) * 5 + (expert,) * 3,
        check_vma=False,
    )
```

```python
import math

import jax
import jax.numpy as jnp
from jax import lax
from jax.experimental import pallas as pl
from jax.experimental.pallas import tpu as pltpu
from jax.sharding import PartitionSpec as P

QUERY_HEADS = 12
KEY_VALUE_HEADS = 2
HEAD_WIDTH = 128
TOP = 4
PIC = 256
NPIC = 4
LANES = 128
GROUPS = QUERY_HEADS // KEY_VALUE_HEADS
QUERY_WIDTH = QUERY_HEADS * HEAD_WIDTH
KEY_WIDTH = KEY_VALUE_HEADS * HEAD_WIDTH
SCALE = 1.0 / math.sqrt(HEAD_WIDTH)
EXP2_SCALE = SCALE * math.log2(math.e)
BLOCKS = 2
VMEM_BYTES = 48 << 20

epsilon = 1e-06
rope_base = 10000.0
big_negative = -1e30
bf16 = jnp.bfloat16
f32 = jnp.float32


def matmul(left, right):
    return jnp.dot(left, right, preferred_element_type=f32)


def matmul_nt(left, right):
    return lax.dot_general(left, right, (((1,), (1,)), ((), ())), preferred_element_type=f32)


def matmul_tn(left, right):
    return lax.dot_general(left, right, (((0,), (0,)), ((), ())), preferred_element_type=f32)


def rms_scale(rows):
    return lax.rsqrt(jnp.mean(rows * rows, -1, keepdims=True) + epsilon)


def rms_norm(rows, gain):
    return rows * rms_scale(rows) * gain


def rope_tables(positions, head_size):
    half = head_size // 2
    inverse = rope_base ** (-(jnp.arange(half, dtype=f32) * 2.0 / head_size))
    angles = positions.astype(f32)[:, None] * inverse[None, :]
    return (jnp.cos(angles), jnp.sin(angles))


def rotate(rows, heads, cosine, sine):
    shaped = rows.reshape(rows.shape[0], heads, HEAD_WIDTH)
    half = HEAD_WIDTH // 2
    first, second = shaped[..., :half], shaped[..., half:]
    cosine, sine = cosine[:, None, :], sine[:, None, :]
    turned = jnp.concatenate(
        [first * cosine - second * sine, second * cosine + first * sine], -1
    )
    return turned.reshape(rows.shape)


def bits(axis):
    size = lax.axis_size(axis)
    return [(axis, 1 << place) for place in reversed(range(size.bit_length() - 1))]


def swap(block, axis, bit):
    size = lax.axis_size(axis)
    return lax.ppermute(block, axis, [(index, index ^ bit) for index in range(size)])


def gather_blocks(block, stages, order):
    held = []
    for stage in stages:
        axis, bit = stage
        other = swap(block, axis, bit)
        upper = (lax.axis_index(axis) & bit) > 0
        place = sum(order.index(known) < order.index(stage) for known in held)
        block = jnp.stack(
            [jnp.where(upper, other, block), jnp.where(upper, block, other)], place
        )
        held.append(stage)
    return block


class Sum:
    def __init__(self, grads, stages, order):
        rows = grads.shape[0] >> len(order)
        self.blocks = grads.reshape([2] * len(order) + [rows, -1])
        self.stages, self.left = list(stages), list(order)

    def step(self):
        axis, bit = stage = self.stages.pop(0)
        mine = ((lax.axis_index(axis) & bit) > 0).astype(jnp.int32)
        place = self.left.index(stage)
        sent = lax.dynamic_index_in_dim(self.blocks, 1 - mine, place, keepdims=False)
        kept = lax.dynamic_index_in_dim(self.blocks, mine, place, keepdims=False)
        total = kept.astype(f32) + swap(sent.astype(bf16), axis, bit).astype(f32)
        self.left.remove(stage)
        self.blocks = total.astype(bf16) if self.left else total


def together(sums, also=()):
    for item in sums:
        item.step()
    blocks, also = lax.optimization_barrier(([item.blocks for item in sums], also))
    for item, block in zip(sums, blocks):
        item.blocks = block
    return also


def exchange_small(rows, stages):
    shape = rows.shape
    rows = rows.reshape([2] * len(stages) + [-1])
    for place, (axis, bit) in enumerate(stages):
        upper = (lax.axis_index(axis) & bit) > 0
        mine = upper.astype(jnp.int32)
        kept = lax.dynamic_index_in_dim(rows, mine, place, keepdims=False)
        sent = lax.dynamic_index_in_dim(rows, 1 - mine, place, keepdims=False)
        other = swap(sent, axis, bit)
        rows = jnp.stack([jnp.where(upper, other, kept), jnp.where(upper, kept, other)], place)
    return rows.reshape(shape)


def visible_keys(meta, step, stretch):
    span = BLOCKS * stretch
    keys = step * span + lax.broadcasted_iota(jnp.int32, (span, 1), 0)
    queries = meta[0] * stretch + lax.broadcasted_iota(jnp.int32, (1, stretch), 1)

    def label(positions):
        found = jnp.zeros(positions.shape, jnp.int32)
        for index in range(NPIC):
            start = meta[1 + index]
            inside = (positions >= start) & (positions < start + PIC)
            found = jnp.where(inside, index + 1, found)
        return found

    query_label = label(queries)
    return (keys <= queries) | ((label(keys) == query_label) & (query_label > 0))


def for_each_step(meta, stretch, steps, process, skip=None):
    span = BLOCKS * stretch
    low, high = meta[0] * stretch, (meta[0] + 1) * stretch

    def turn(step, carry):
        needed = step * span < high + PIC - 1
        edge = (step + 1) * span > low

        @pl.when(needed & edge)
        def _():
            process(step, True)

        @pl.when(needed & jnp.logical_not(edge))
        def _():
            process(step, False)

        if skip is not None:

            @pl.when(jnp.logical_not(needed))
            def _():
                skip(step)

        return carry

    lax.fori_loop(0, steps, turn, 0)


def head_columns(head, start=0):
    return slice(start + head * HEAD_WIDTH, start + (head + 1) * HEAD_WIDTH)


def attend_kernel(meta, query, key_value, out, log_total, peak, total, accum):
    stretch = query.shape[0]
    span = BLOCKS * stretch
    peak[...] = jnp.full(peak.shape, big_negative, f32)
    total[...] = jnp.zeros(total.shape, f32)
    accum[...] = jnp.zeros(accum.shape, f32)

    def process(step, edge):
        rows = pl.ds(pl.multiple_of(step * span, span), span)
        if edge:
            visible = visible_keys(meta, step, stretch)
        keys, values = [], []
        for group in range(KEY_VALUE_HEADS):
            keys.append(key_value[rows, head_columns(group)])
            turned = key_value[rows, head_columns(group, KEY_WIDTH)].T
            values.append(jnp.concatenate([turned, jnp.ones((16, span), bf16)], 0))

        def score(head):
            scores = matmul_nt(keys[head // GROUPS], query[:, head_columns(head)])
            if edge:
                scores = jnp.where(visible, scores, big_negative)
            old = peak[head : head + 1, :]
            return scores, old, jnp.maximum(old, jnp.max(scores, 0, keepdims=True))

        def weigh(head, scores, old, new):
            weights = jnp.exp2((scores - new) * EXP2_SCALE).astype(bf16)
            shrink = jnp.exp2((old - new) * EXP2_SCALE)
            sums = matmul(values[head // GROUPS], weights)
            row, columns = slice(head, head + 1), head_columns(head)
            peak[row, :] = new
            total[row, :] = total[row, :] * shrink + sums[HEAD_WIDTH : HEAD_WIDTH + 1]
            accum[columns, :] = accum[columns, :] * shrink + sums[:HEAD_WIDTH]

        waiting = []
        for head in range(QUERY_HEADS):
            waiting.append((head, *score(head)))
            if len(waiting) > 2:
                weigh(*waiting.pop(0))
        for item in waiting:
            weigh(*item)

    for_each_step(meta, stretch, key_value.shape[0] // span, process)
    for head in range(QUERY_HEADS):
        row, columns = slice(head, head + 1), head_columns(head)
        out[:, columns] = (accum[columns, :] / total[row, :]).T
        log_total[row, :] = peak[row, :] * EXP2_SCALE + jnp.log2(total[row, :])


def attend_back_kernel(
    meta, query, slope, log_total, delta, key_value, slope_query, slope_kv, accum
):
    stretch = query.shape[0]
    span = BLOCKS * stretch
    accum[...] = jnp.zeros(accum.shape, f32)

    def process(step, edge):
        rows = pl.ds(pl.multiple_of(step * span, span), span)
        if edge:
            visible = visible_keys(meta, step, stretch)
        for group in range(KEY_VALUE_HEADS):
            keys = key_value[rows, head_columns(group)]
            values = key_value[rows, head_columns(group, KEY_WIDTH)]
            keys_turned = keys.T
            slope_k = jnp.zeros((span, HEAD_WIDTH), f32)
            slope_v = jnp.zeros((span, HEAD_WIDTH), f32)
            for head in range(group * GROUPS, (group + 1) * GROUPS):
                row, columns = slice(head, head + 1), head_columns(head)
                own_query, own_slope = query[:, columns], slope[:, columns]
                scores = matmul_nt(keys, own_query)
                probs = jnp.exp2(scores * EXP2_SCALE - log_total[row, :])
                if edge:
                    probs = jnp.where(visible, probs, 0.0)
                slope_probs = matmul_nt(values, own_slope)
                slope_scores = (probs * (slope_probs - delta[row, :])).astype(bf16)
                slope_v = slope_v + matmul(probs.astype(bf16), own_slope)
                slope_k = slope_k + matmul(slope_scores, own_query)
                accum[columns, :] = accum[columns, :] + matmul(keys_turned, slope_scores)
            slope_kv[rows, head_columns(group)] = (slope_k * SCALE).astype(bf16)
            slope_kv[rows, head_columns(group, KEY_WIDTH)] = slope_v.astype(bf16)

    def skip(step):
        rows = pl.ds(pl.multiple_of(step * span, span), span)
        slope_kv[rows, :] = jnp.zeros((span, 2 * KEY_WIDTH), bf16)

    for_each_step(meta, stretch, key_value.shape[0] // span, process, skip)
    for head in range(QUERY_HEADS):
        columns = head_columns(head)
        slope_query[:, columns] = (accum[columns, :] * SCALE).T


def attention_call(kernel, outs, scratch, products, name, meta, *operands):
    vmem = pl.BlockSpec(memory_space=pltpu.VMEM)
    pairs = QUERY_HEADS * operands[0].shape[0] * operands[-1].shape[0]
    return pl.pallas_call(
        kernel,
        out_shape=outs,
        in_specs=[pl.BlockSpec(memory_space=pltpu.SMEM)] + [vmem] * len(operands),
        out_specs=(vmem,) * len(outs),
        scratch_shapes=[pltpu.VMEM(shape, f32) for shape in scratch],
        compiler_params=pltpu.CompilerParams(vmem_limit_bytes=VMEM_BYTES),
        cost_estimate=pl.CostEstimate(
            flops=products * 4 * HEAD_WIDTH * pairs,
            bytes_accessed=4 * QUERY_WIDTH * 1024,
            transcendentals=pairs,
        ),
        name=name,
    )(meta, *operands)


def attend(meta, query, key_value):
    stretch = query.shape[0]
    stats = (QUERY_HEADS, stretch)
    outs = (
        jax.ShapeDtypeStruct((stretch, QUERY_WIDTH), f32),
        jax.ShapeDtypeStruct(stats, f32),
    )
    scratch = [stats, stats, (QUERY_WIDTH, stretch)]
    return attention_call(attend_kernel, outs, scratch, 2, "attend", meta, query, key_value)


def attend_back(meta, query, slope, log_total, delta, key_value):
    stretch = query.shape[0]
    outs = (
        jax.ShapeDtypeStruct((stretch, QUERY_WIDTH), f32),
        jax.ShapeDtypeStruct(key_value.shape, bf16),
    )
    operands = (meta, query, slope, log_total, delta, key_value)
    scratch = [(QUERY_WIDTH, stretch)]
    return attention_call(attend_back_kernel, outs, scratch, 5, "attend_back", *operands)


def body(
    tokens,
    cotangent,
    routes,
    fill_order,
    pic_starts,
    attn_gain,
    moe_gain,
    w_query,
    key_projection,
    value_projection,
    w_out,
    w_router,
    expert_gate,
    expert_up,
    expert_down,
):
    sequences, stretch, width = tokens.shape
    count = sequences * stretch
    parts = lax.axis_size("ctx")
    experts = parts
    capacity = (5 * count * TOP + 4 * experts - 1) // (4 * experts)
    query_width, key_width = QUERY_WIDTH, KEY_WIDTH
    hidden_width = expert_gate.shape[2]
    both = ("seq", "ctx")
    seq_bits, ctx_bits = bits("seq"), bits("ctx")
    all_bits = seq_bits + ctx_bits
    outward = ctx_bits[:-1] + seq_bits + ctx_bits[-1:]
    inward = outward[::-1]

    def padded(columns):
        block = jnp.concatenate(columns, 1)
        return jnp.pad(block, ((0, 0), (0, LANES - block.shape[1])))

    first_set = lax.all_gather(
        jnp.concatenate(
            [w_query, key_projection, value_projection, padded([attn_gain[:, None]])], 1
        ),
        both,
        axis=0,
        tiled=True,
    )
    second_set = gather_blocks(
        jnp.concatenate([w_out, padded([w_router, moe_gain[:, None]])], 1), outward, all_bits
    ).reshape(width, -1)
    gate_up = gather_blocks(
        jnp.concatenate([expert_gate[0], expert_up[0]], 1), seq_bits[::-1], seq_bits
    ).reshape(-1, 2 * hidden_width)
    down = gather_blocks(expert_down[0], seq_bits[::-1], seq_bits).reshape(-1, width)
    picks = routes.reshape(count, TOP)
    order = fill_order.reshape(count)
    routed = jnp.any(picks[:, :, None] == jnp.arange(experts, dtype=jnp.int32), 1)
    earlier = (order[None, :] < order[:, None]).astype(bf16)
    place = matmul(earlier, routed.astype(bf16)).astype(jnp.int32)
    place = jnp.where(routed, place, capacity)
    half = capacity // 2
    chosen_slot = [
        place.T[:, None, :]
        == (begin + jnp.arange(half, dtype=jnp.int32))[None, :, None]
        for begin in (0, half)
    ]
    slot_map = [chosen.astype(bf16).reshape(-1, count) for chosen in chosen_slot]

    def exchange_rows(rows):
        rows = rows.reshape(experts, half, width)
        rows = lax.all_to_all(rows, "ctx", split_axis=0, concat_axis=0, tiled=True)
        return rows.reshape(-1, width)

    out_slope = cotangent.reshape(count, width)
    slope_rows = [exchange_rows(matmul(part, out_slope).astype(bf16)) for part in slot_map]
    first_set, gate_up, slope_rows = lax.optimization_barrier((first_set, gate_up, slope_rows))

    weight_qkv = first_set[:, : query_width + 2 * key_width]
    gain_one = first_set[:, query_width + 2 * key_width].astype(f32)
    full_out = second_set[:, :width]
    full_router = second_set[:, width : width + experts]
    gain_two = second_set[:, width + experts].astype(f32)

    positions = lax.axis_index("ctx") * stretch + jnp.arange(stretch, dtype=jnp.int32)
    cosine, sine = rope_tables(positions, HEAD_WIDTH)
    inputs = tokens.astype(f32).reshape(count, width)
    normed = rms_norm(inputs, gain_one).astype(bf16)
    projected = matmul(normed, weight_qkv)
    query_rows = rotate(projected[:, :query_width], QUERY_HEADS, cosine, sine).astype(bf16)
    key_rows = rotate(
        projected[:, query_width : query_width + key_width], KEY_VALUE_HEADS, cosine, sine
    ).astype(bf16)
    value_rows = projected[:, query_width + key_width :].astype(bf16)
    key_values = lax.all_gather(
        jnp.concatenate([key_rows, value_rows], 1), "ctx", axis=0, tiled=True
    )

    meta = jnp.concatenate([lax.axis_index("ctx").astype(jnp.int32)[None], pic_starts[0]])
    mixed_heads, log_total = attend(meta, query_rows, key_values)
    mixed_heads, down = lax.optimization_barrier((mixed_heads, down))
    attended = mixed_heads.astype(bf16)

    middle = inputs + matmul(attended, full_out)
    enter = rms_norm(middle, gain_two).astype(bf16)
    arrived = [exchange_rows(matmul(part, enter).astype(bf16)) for part in slot_map]
    logits = matmul(enter, full_router)
    logits = jnp.where(routed, logits, big_negative)
    gates = jnp.where(routed, jnp.exp(logits - jnp.max(logits, -1, keepdims=True)), 0.0)
    gates = gates / jnp.sum(gates, -1, keepdims=True)
    slot_gates = exchange_small(
        jnp.concatenate(
            [jnp.sum(jnp.where(chosen, gates.T[:, None, :], 0.0), -1) for chosen in chosen_slot],
            1,
        ),
        ctx_bits,
    )

    def activate(both_parts):
        return (
            jax.nn.gelu(both_parts[:, :hidden_width], approximate=True)
            * both_parts[:, hidden_width:]
        )

    arrived[0], slot_gates = lax.optimization_barrier((arrived[0], slot_gates))
    result, slope_gates, returned_slopes, grad_gate_up, grad_down = [], [], [], 0.0, 0.0
    for index in range(2):
        pre = matmul(arrived[index], gate_up)
        hidden, pull_act = jax.vjp(activate, pre)
        hidden = hidden.astype(bf16)
        result.append(matmul(hidden, down).astype(bf16))
        slope_wide = slope_rows[index].astype(f32)
        slope_gates.append(
            jnp.sum(slope_wide * result[index].astype(f32), -1).reshape(experts, half)
        )
        own_gates = slot_gates[:, index * half : (index + 1) * half].reshape(-1, 1)
        slope_slots = (own_gates * slope_wide).astype(bf16)
        slope_pre = pull_act(matmul_nt(slope_slots, down))[0].astype(bf16)
        slope_arrived = matmul_nt(slope_pre, gate_up).astype(bf16)
        grad_gate_up = grad_gate_up + matmul_tn(arrived[index], slope_pre)
        grad_down = grad_down + matmul_tn(hidden, slope_slots)
        if index == 0:
            arrived[1], slope_arrived = lax.optimization_barrier((arrived[1], slope_arrived))
        else:
            slope_gates, slope_arrived = lax.optimization_barrier((slope_gates, slope_arrived))
        returned_slopes.append(exchange_rows(slope_arrived))
    returned_gates = exchange_small(jnp.concatenate(slope_gates, 1), ctx_bits)
    grad_gate_up, grad_down = grad_gate_up.astype(bf16), grad_down.astype(bf16)
    returned_slopes, grad_gate_up, grad_down, returned_gates = lax.optimization_barrier(
        (returned_slopes, grad_gate_up, grad_down, returned_gates)
    )
    returned = [exchange_rows(part) for part in result]
    gate_up_sum = Sum(grad_gate_up, seq_bits, seq_bits)
    down_sum = Sum(grad_down, seq_bits, seq_bits)
    while gate_up_sum.stages:
        gate_up_sum.step()

    slope_gate = 0.0
    for index, chosen in enumerate(chosen_slot):
        part = returned_gates[:, index * half : (index + 1) * half]
        slope_gate = slope_gate + jnp.sum(jnp.where(chosen, part[:, :, None], 0.0), 1).T
    slope_logits = gates * (slope_gate - jnp.sum(gates * slope_gate, -1, keepdims=True))
    slope_logits = slope_logits.astype(bf16)
    grad_router = matmul_tn(enter, slope_logits)
    slope_enter = matmul_nt(slope_logits, full_router)
    for part, rows in zip(slot_map, returned_slopes):
        slope_enter = slope_enter + matmul_tn(part, rows)

    pull_two = jax.vjp(rms_norm, middle, gain_two)[1]
    slope_middle, grad_gain_two = pull_two(slope_enter)
    slope_middle = out_slope.astype(f32) + slope_middle
    slope_branch = slope_middle.astype(bf16)
    grad_out = matmul_tn(attended, slope_branch)
    slope_attended = matmul_nt(slope_branch, full_out).astype(bf16)
    delta = slope_attended.astype(f32) * mixed_heads
    delta = jnp.sum(delta.reshape(count, QUERY_HEADS, HEAD_WIDTH), -1).T

    grad_out = grad_out.astype(bf16)
    slope_attended, grad_out, gate_up_sum.blocks = lax.optimization_barrier(
        (slope_attended, grad_out, gate_up_sum.blocks)
    )
    out_sum = Sum(grad_out, inward, all_bits)
    out_sum.step()
    out_sum.step()
    while down_sum.stages:
        down_sum.step()
    slope_q, slope_kv = attend_back(
        meta, query_rows, slope_attended, log_total, delta, key_values
    )
    slope_q, slope_kv, out_sum.blocks, down_sum.blocks, returned[0] = (
        lax.optimization_barrier(
            (slope_q, slope_kv, out_sum.blocks, down_sum.blocks, returned[0])
        )
    )
    slope_query = rotate(slope_q, QUERY_HEADS, cosine, -sine).astype(bf16)
    kv_sum = Sum(slope_kv, ctx_bits[::-1], ctx_bits)
    query_sum = Sum(matmul_tn(normed, slope_query).astype(bf16), inward, all_bits)
    together([kv_sum, query_sum])
    together([kv_sum, query_sum])
    returned[1] = together([kv_sum, query_sum], returned[1])
    while kv_sum.stages:
        together([kv_sum, out_sum])
    slope_kv = kv_sum.blocks
    output = middle
    for chosen, rows in zip(chosen_slot, returned):
        mix = jnp.where(chosen, gates.T[:, None, :], 0.0).reshape(-1, count)
        mix_high = mix.astype(bf16)
        mix_low = (mix - mix_high.astype(f32)).astype(bf16)
        output = output + matmul_tn(mix_high, rows) + matmul_tn(mix_low, rows)
    output = output.astype(bf16).reshape(tokens.shape)
    slope_key = rotate(slope_kv[:, :key_width], KEY_VALUE_HEADS, cosine, -sine)
    slope_rest = jnp.concatenate([slope_key, slope_kv[:, key_width:]], 1).astype(bf16)
    grad_kv = matmul_tn(normed, slope_rest)
    slope_normed = matmul_nt(slope_query, weight_qkv[:, :query_width])
    slope_normed = slope_normed + matmul_nt(slope_rest, weight_qkv[:, query_width:])
    pull_one = jax.vjp(rms_norm, inputs, gain_one)[1]
    slope_inputs, grad_gain_one = pull_one(slope_normed)
    grad_input = (slope_middle + slope_inputs).reshape(tokens.shape)
    rest = jnp.concatenate(
        [grad_kv, padded([grad_router, grad_gain_one[:, None], grad_gain_two[:, None]])], 1
    )
    rest_sum = Sum(rest.astype(bf16), inward, all_bits)
    while rest_sum.stages:
        together([item for item in (rest_sum, query_sum, out_sum) if item.stages])
    grads_rest, grads_query, grads_out = rest_sum.blocks, query_sum.blocks, out_sum.blocks
    return (
        output,
        grad_input,
        grads_rest[:, 2 * key_width + experts],
        grads_rest[:, 2 * key_width + experts + 1],
        grads_query,
        grads_rest[:, :key_width],
        grads_rest[:, key_width : 2 * key_width],
        grads_out,
        grads_rest[:, 2 * key_width : 2 * key_width + experts],
        gate_up_sum.blocks[None, :, :hidden_width],
        gate_up_sum.blocks[None, :, hidden_width:],
        down_sum.blocks[None],
    )


def solution(mesh):
    rows = P("seq", "ctx", None)
    shard = P(("seq", "ctx"), None)
    vector = P(("seq", "ctx"))
    expert = P("ctx", "seq", None)
    return jax.shard_map(
        body,
        mesh=mesh,
        in_specs=(rows, rows, rows, P("seq", "ctx"), P("seq", None), vector, vector)
        + (shard,) * 5
        + (expert,) * 3,
        out_specs=(rows, rows, vector, vector) + (shard,) * 5 + (expert,) * 3,
        check_vma=False,
    )
```

```python
import math

import jax
import jax.numpy as jnp
from jax import lax
from jax.experimental import pallas as pl
from jax.experimental.pallas import tpu as pltpu
from jax.sharding import PartitionSpec as P

QUERY_HEADS = 12
KEY_VALUE_HEADS = 2
HEAD_WIDTH = 128
TOP = 4
PIC = 256
NPIC = 4
LANES = 128
GROUPS = QUERY_HEADS // KEY_VALUE_HEADS
QUERY_WIDTH = QUERY_HEADS * HEAD_WIDTH
KEY_WIDTH = KEY_VALUE_HEADS * HEAD_WIDTH
SCALE = 1.0 / math.sqrt(HEAD_WIDTH)
EXP2_SCALE = SCALE * math.log2(math.e)
BLOCKS = 2
VMEM_BYTES = 48 << 20

epsilon = 1e-06
rope_base = 10000.0
big_negative = -1e30
bf16 = jnp.bfloat16
f32 = jnp.float32


def matmul(left, right):
    return jnp.dot(left, right, preferred_element_type=f32)


def matmul_nt(left, right):
    return lax.dot_general(left, right, (((1,), (1,)), ((), ())), preferred_element_type=f32)


def matmul_tn(left, right):
    return lax.dot_general(left, right, (((0,), (0,)), ((), ())), preferred_element_type=f32)


def rms_scale(rows):
    return lax.rsqrt(jnp.mean(rows * rows, -1, keepdims=True) + epsilon)


def rms_norm(rows, gain):
    return rows * rms_scale(rows) * gain


def rope_tables(positions, head_size):
    half = head_size // 2
    inverse = rope_base ** (-(jnp.arange(half, dtype=f32) * 2.0 / head_size))
    angles = positions.astype(f32)[:, None] * inverse[None, :]
    return (jnp.cos(angles), jnp.sin(angles))


def rotate(rows, heads, cosine, sine):
    shaped = rows.reshape(rows.shape[0], heads, HEAD_WIDTH)
    half = HEAD_WIDTH // 2
    first, second = shaped[..., :half], shaped[..., half:]
    cosine, sine = cosine[:, None, :], sine[:, None, :]
    turned = jnp.concatenate(
        [first * cosine - second * sine, second * cosine + first * sine], -1
    )
    return turned.reshape(rows.shape)


def bits(axis):
    size = lax.axis_size(axis)
    return [(axis, 1 << place) for place in reversed(range(size.bit_length() - 1))]


def swap(block, axis, bit):
    size = lax.axis_size(axis)
    return lax.ppermute(block, axis, [(index, index ^ bit) for index in range(size)])


def gather_blocks(block, stages, order):
    held = []
    for stage in stages:
        axis, bit = stage
        other = swap(block, axis, bit)
        upper = (lax.axis_index(axis) & bit) > 0
        place = sum(order.index(known) < order.index(stage) for known in held)
        block = jnp.stack(
            [jnp.where(upper, other, block), jnp.where(upper, block, other)], place
        )
        held.append(stage)
    return block


class Sum:
    def __init__(self, sent, kept, stages):
        self.sent, self.kept, self.stages = sent, kept, list(stages)

    def step(self):
        axis, bit = self.stages.pop(0)
        other = swap(self.sent, axis, bit)
        if not self.stages:
            self.total = self.kept.astype(f32) + other.astype(f32)
            return
        half = self.kept.shape[0] // 2
        self.sent = (self.kept[half:].astype(f32) + other[half:].astype(f32)).astype(bf16)
        self.kept = (self.kept[:half].astype(f32) + other[:half].astype(f32)).astype(bf16)


def together(sums, also=()):
    for item in sums:
        item.step()
    live = [item for item in sums if item.stages]
    sent, also = lax.optimization_barrier(([item.sent for item in live], also))
    for item, block in zip(live, sent):
        item.sent = block
    return also


def flips(stages, sizes):
    masks = []
    for block in range(1 << len(stages)):
        mask = 0
        for place, (axis, bit) in enumerate(stages):
            if (block >> (len(stages) - 1 - place)) & 1:
                mask |= bit * sizes[axis]
        masks.append(mask)
    return masks


def visible_keys(meta, step, stretch):
    span = BLOCKS * stretch
    keys = step * span + lax.broadcasted_iota(jnp.int32, (span, 1), 0)
    queries = meta[0] * stretch + lax.broadcasted_iota(jnp.int32, (1, stretch), 1)

    def label(positions):
        found = jnp.zeros(positions.shape, jnp.int32)
        for index in range(NPIC):
            start = meta[1 + index]
            inside = (positions >= start) & (positions < start + PIC)
            found = jnp.where(inside, index + 1, found)
        return found

    query_label = label(queries)
    return (keys <= queries) | ((label(keys) == query_label) & (query_label > 0))


def for_each_step(meta, stretch, steps, process, skip=None):
    span = BLOCKS * stretch
    low, high = meta[0] * stretch, (meta[0] + 1) * stretch

    def turn(step, carry):
        needed = step * span < high + PIC - 1
        edge = (step + 1) * span > low

        @pl.when(needed & edge)
        def _():
            process(step, True)

        @pl.when(needed & jnp.logical_not(edge))
        def _():
            process(step, False)

        if skip is not None:

            @pl.when(jnp.logical_not(needed))
            def _():
                skip(step)

        return carry

    lax.fori_loop(0, steps, turn, 0)


def head_columns(head, start=0):
    return slice(start + head * HEAD_WIDTH, start + (head + 1) * HEAD_WIDTH)


def attend_kernel(meta, query, key_value, out, log_total, peak, total, accum):
    stretch = query.shape[0]
    span = BLOCKS * stretch
    peak[...] = jnp.full(peak.shape, big_negative, f32)
    total[...] = jnp.zeros(total.shape, f32)
    accum[...] = jnp.zeros(accum.shape, f32)

    def process(step, edge):
        rows = pl.ds(pl.multiple_of(step * span, span), span)
        if edge:
            visible = visible_keys(meta, step, stretch)
        keys, values = [], []
        for group in range(KEY_VALUE_HEADS):
            keys.append(key_value[rows, head_columns(group)])
            turned = key_value[rows, head_columns(group, KEY_WIDTH)].T
            values.append(jnp.concatenate([turned, jnp.ones((16, span), bf16)], 0))

        def score(head):
            scores = matmul_nt(keys[head // GROUPS], query[:, head_columns(head)])
            if edge:
                scores = jnp.where(visible, scores, big_negative)
            old = peak[head : head + 1, :]
            return scores, old, jnp.maximum(old, jnp.max(scores, 0, keepdims=True))

        def weigh(head, scores, old, new):
            weights = jnp.exp2((scores - new) * EXP2_SCALE).astype(bf16)
            shrink = jnp.exp2((old - new) * EXP2_SCALE)
            sums = matmul(values[head // GROUPS], weights)
            row, columns = slice(head, head + 1), head_columns(head)
            peak[row, :] = new
            total[row, :] = total[row, :] * shrink + sums[HEAD_WIDTH : HEAD_WIDTH + 1]
            accum[columns, :] = accum[columns, :] * shrink + sums[:HEAD_WIDTH]

        waiting = []
        for head in range(QUERY_HEADS):
            waiting.append((head, *score(head)))
            if len(waiting) > 2:
                weigh(*waiting.pop(0))
        for item in waiting:
            weigh(*item)

    for_each_step(meta, stretch, key_value.shape[0] // span, process)
    for head in range(QUERY_HEADS):
        row, columns = slice(head, head + 1), head_columns(head)
        out[:, columns] = (accum[columns, :] / total[row, :]).T
        log_total[row, :] = peak[row, :] * EXP2_SCALE + jnp.log2(total[row, :])


def attend_back_kernel(
    meta, query, slope, log_total, delta, key_value, slope_query, slope_kv, accum
):
    stretch = query.shape[0]
    span = BLOCKS * stretch
    accum[...] = jnp.zeros(accum.shape, f32)
    count = (key_value.shape[0] // stretch).bit_length() - 1

    def relative_rows(step, part):
        flip = jnp.bitwise_xor(BLOCKS * step + part, meta[0])
        place = 0
        for bit in range(count):
            place = place + ((flip >> bit) & 1) * (1 << (count - 1 - bit))
        return pl.ds(pl.multiple_of(place * stretch, stretch), stretch)

    def process(step, edge):
        rows = pl.ds(pl.multiple_of(step * span, span), span)
        if edge:
            visible = visible_keys(meta, step, stretch)
        for group in range(KEY_VALUE_HEADS):
            keys = key_value[rows, head_columns(group)]
            values = key_value[rows, head_columns(group, KEY_WIDTH)]
            keys_turned = keys.T
            slope_k = jnp.zeros((span, HEAD_WIDTH), f32)
            slope_v = jnp.zeros((span, HEAD_WIDTH), f32)
            for head in range(group * GROUPS, (group + 1) * GROUPS):
                row, columns = slice(head, head + 1), head_columns(head)
                own_query, own_slope = query[:, columns], slope[:, columns]
                scores = matmul_nt(keys, own_query)
                probs = jnp.exp2(scores * EXP2_SCALE - log_total[row, :])
                if edge:
                    probs = jnp.where(visible, probs, 0.0)
                slope_probs = matmul_nt(values, own_slope)
                slope_scores = (probs * (slope_probs - delta[row, :])).astype(bf16)
                slope_v = slope_v + matmul(probs.astype(bf16), own_slope)
                slope_k = slope_k + matmul(slope_scores, own_query)
                accum[columns, :] = accum[columns, :] + matmul(keys_turned, slope_scores)
            for part in range(BLOCKS):
                own = slice(part * stretch, (part + 1) * stretch)
                place = relative_rows(step, part)
                slope_kv[place, head_columns(group)] = (slope_k[own] * SCALE).astype(bf16)
                slope_kv[place, head_columns(group, KEY_WIDTH)] = slope_v[own].astype(bf16)

    def skip(step):
        for part in range(BLOCKS):
            place = relative_rows(step, part)
            slope_kv[place, :] = jnp.zeros((stretch, 2 * KEY_WIDTH), bf16)

    for_each_step(meta, stretch, key_value.shape[0] // span, process, skip)
    for head in range(QUERY_HEADS):
        columns = head_columns(head)
        slope_query[:, columns] = (accum[columns, :] * SCALE).T


def expert_kernel(
    which,
    rows,
    slopes,
    chosen,
    gate_up,
    down,
    router,
    hidden_out,
    result_out,
    gates_out,
    slots_out,
    pre_out,
    slope_out,
):
    hidden_width = down.shape[0]
    incoming = rows[...]
    logits = jnp.where(chosen[...] > 0, matmul(incoming, router[...]), big_negative)
    shares = jnp.exp(logits - jnp.max(logits, -1, keepdims=True))
    shares = jnp.where(chosen[...] > 0, shares, 0.0)
    column = lax.broadcasted_iota(jnp.int32, shares.shape, 1)
    own = jnp.sum(jnp.where(column == which[0], shares, 0.0), -1, keepdims=True)
    gates = own / jnp.maximum(jnp.sum(shares, -1, keepdims=True), 1e-30)
    slots = (gates * slopes[...].astype(f32)).astype(bf16)
    slots_out[...] = slots
    pre = matmul(incoming, gate_up[...])
    gate, up = pre[:, :hidden_width], pre[:, hidden_width:]
    root, cubic = math.sqrt(2.0 / math.pi), 0.044715
    square = gate * gate
    bend = jnp.tanh(root * (gate + cubic * gate * square))
    gelu = 0.5 * gate * (1.0 + bend)
    rise = 0.5 * (1.0 + bend) + 0.5 * gate * (1.0 - bend * bend) * root * (
        1.0 + 3.0 * cubic * square
    )
    hidden = (gelu * up).astype(bf16)
    hidden_out[...] = hidden
    result = matmul(hidden, down[...]).astype(bf16)
    result_out[...] = result
    gates_out[...] = jnp.sum(slopes[...].astype(f32) * result.astype(f32), -1, keepdims=True)
    slope_hidden = matmul_nt(slots, down[...])
    slope_pre = jnp.concatenate([slope_hidden * up * rise, slope_hidden * gelu], 1).astype(bf16)
    pre_out[...] = slope_pre
    slope_out[...] = matmul_nt(slope_pre, gate_up[...]).astype(bf16)


def expert(which, rows, slopes, chosen, gate_up, down, router):
    count, width = rows.shape
    hidden_width = down.shape[0]
    block = count // 2

    def tile(columns):
        return pl.BlockSpec((block, columns), lambda step: (step, 0))

    def whole(array):
        return pl.BlockSpec(array.shape, lambda step: (0, 0))

    shapes = [(hidden_width, bf16), (width, bf16), (1, f32), (width, bf16)]
    shapes += [(2 * hidden_width, bf16), (width, bf16)]
    return pl.pallas_call(
        expert_kernel,
        grid=(2,),
        out_shape=[jax.ShapeDtypeStruct((count, columns), kind) for columns, kind in shapes],
        in_specs=[
            pl.BlockSpec(memory_space=pltpu.SMEM),
            tile(width),
            tile(width),
            tile(LANES),
            whole(gate_up),
            whole(down),
            whole(router),
        ],
        out_specs=[tile(columns) for columns, _ in shapes],
        compiler_params=pltpu.CompilerParams(vmem_limit_bytes=VMEM_BYTES),
        cost_estimate=pl.CostEstimate(
            flops=12 * count * width * hidden_width,
            bytes_accessed=20 * count * width,
            transcendentals=count * hidden_width,
        ),
        name="expert",
    )(which, rows, slopes, chosen, gate_up, down, router)


def attention_call(kernel, outs, scratch, products, name, meta, *operands):
    vmem = pl.BlockSpec(memory_space=pltpu.VMEM)
    pairs = QUERY_HEADS * operands[0].shape[0] * operands[-1].shape[0]
    return pl.pallas_call(
        kernel,
        out_shape=outs,
        in_specs=[pl.BlockSpec(memory_space=pltpu.SMEM)] + [vmem] * len(operands),
        out_specs=(vmem,) * len(outs),
        scratch_shapes=[pltpu.VMEM(shape, f32) for shape in scratch],
        compiler_params=pltpu.CompilerParams(vmem_limit_bytes=VMEM_BYTES),
        cost_estimate=pl.CostEstimate(
            flops=products * 4 * HEAD_WIDTH * pairs,
            bytes_accessed=4 * QUERY_WIDTH * 1024,
            transcendentals=pairs,
        ),
        name=name,
    )(meta, *operands)


def attend(meta, query, key_value):
    stretch = query.shape[0]
    stats = (QUERY_HEADS, stretch)
    outs = (
        jax.ShapeDtypeStruct((stretch, QUERY_WIDTH), f32),
        jax.ShapeDtypeStruct(stats, f32),
    )
    scratch = [stats, stats, (QUERY_WIDTH, stretch)]
    return attention_call(attend_kernel, outs, scratch, 2, "attend", meta, query, key_value)


def attend_back(meta, query, slope, log_total, delta, key_value):
    stretch = query.shape[0]
    outs = (
        jax.ShapeDtypeStruct((stretch, QUERY_WIDTH), f32),
        jax.ShapeDtypeStruct(key_value.shape, bf16),
    )
    operands = (meta, query, slope, log_total, delta, key_value)
    scratch = [(QUERY_WIDTH, stretch)]
    return attention_call(attend_back_kernel, outs, scratch, 5, "attend_back", *operands)


def body(
    tokens,
    cotangent,
    routes,
    fill_order,
    pic_starts,
    attn_gain,
    moe_gain,
    w_query,
    key_projection,
    value_projection,
    w_out,
    w_router,
    expert_gate,
    expert_up,
    expert_down,
):
    sequences, stretch, width = tokens.shape
    count = sequences * stretch
    parts = lax.axis_size("ctx")
    experts = parts
    capacity = (5 * count * TOP + 4 * experts - 1) // (4 * experts)
    query_width, key_width = QUERY_WIDTH, KEY_WIDTH
    hidden_width = expert_gate.shape[2]
    both = ("seq", "ctx")
    seq_bits, ctx_bits = bits("seq"), bits("ctx")
    all_bits = seq_bits + ctx_bits
    outward = ctx_bits[:-1] + seq_bits + ctx_bits[-1:]
    inward = ctx_bits[-1:] + seq_bits[::-1] + ctx_bits[-2::-1]
    sizes = {"seq": parts, "ctx": 1}
    me = lax.axis_index("seq") * parts + lax.axis_index("ctx")

    def padded(columns):
        block = jnp.concatenate(columns, 1)
        return jnp.pad(block, ((0, 0), (0, LANES - block.shape[1])))

    first_set = lax.all_gather(
        jnp.concatenate(
            [w_query, key_projection, value_projection, padded([attn_gain[:, None]])], 1
        ),
        both,
        axis=0,
        tiled=True,
    )
    second_set = gather_blocks(
        jnp.concatenate([w_out, padded([w_router, moe_gain[:, None]])], 1), outward, all_bits
    ).reshape(width, -1)

    own_rows = w_query.shape[0]
    owner = jnp.bitwise_xor(jnp.array(flips(inward, sizes), jnp.int32), me)
    feature = (owner[:, None] * own_rows + jnp.arange(own_rows, dtype=jnp.int32)).reshape(-1)
    turn = (jnp.arange(width, dtype=jnp.int32)[:, None] == feature[None, :]).astype(bf16)

    def relative(rows):
        return matmul(rows, turn).astype(bf16)

    def halves(left, right):
        middle = left.shape[1] // 2
        sent = matmul_tn(left[:, middle:], right).astype(bf16)
        return sent, matmul_tn(left[:, :middle], right).astype(bf16)

    picks = routes.reshape(count, TOP)
    order = fill_order.reshape(count)
    routed = jnp.any(picks[:, :, None] == jnp.arange(experts, dtype=jnp.int32), 1)
    earlier = (order[None, :] < order[:, None]).astype(bf16)
    place = matmul(earlier, routed.astype(bf16)).astype(jnp.int32)
    place = jnp.where(routed, place, capacity)
    half = capacity // 2
    chosen_slot = [
        place.T[:, None, :]
        == (begin + jnp.arange(half, dtype=jnp.int32))[None, :, None]
        for begin in (0, half)
    ]
    slot_map = [chosen.astype(bf16).reshape(-1, count) for chosen in chosen_slot]

    def exchange_rows(rows):
        rows = rows.reshape(experts, half, width)
        rows = lax.all_to_all(rows, "ctx", split_axis=0, concat_axis=0, tiled=True)
        return rows.reshape(-1, width)

    out_slope = cotangent.reshape(count, width)
    slot_routes = jnp.concatenate(
        [matmul(part, routed.astype(bf16)).reshape(experts, half, experts) for part in slot_map], 1
    ).astype(bf16)
    slot_routes = lax.all_to_all(slot_routes, "ctx", split_axis=0, concat_axis=0, tiled=True)
    slot_routes = jnp.pad(slot_routes, ((0, 0), (0, 0), (0, LANES - experts)))
    slot_routes = [
        slot_routes[:, begin : begin + half].reshape(-1, LANES) for begin in (0, half)
    ]
    slope_rows = [exchange_rows(matmul(part, out_slope).astype(bf16)) for part in slot_map]
    gate_up = jnp.concatenate([expert_gate[0], expert_up[0]], 1)
    first_set, slot_routes, slope_rows[0], gate_up = lax.optimization_barrier(
        (first_set, slot_routes, slope_rows[0], gate_up)
    )
    gate_up = gather_blocks(gate_up, seq_bits[::-1], seq_bits).reshape(-1, 2 * hidden_width)

    weight_qkv = first_set[:, : query_width + 2 * key_width]
    gain_one = first_set[:, query_width + 2 * key_width].astype(f32)
    full_out = second_set[:, :width]
    full_router = second_set[:, width : width + experts]
    gain_two = second_set[:, width + experts].astype(f32)

    positions = lax.axis_index("ctx") * stretch + jnp.arange(stretch, dtype=jnp.int32)
    cosine, sine = rope_tables(positions, HEAD_WIDTH)
    inputs = tokens.astype(f32).reshape(count, width)
    normed = rms_norm(inputs, gain_one).astype(bf16)
    projected = matmul(normed, weight_qkv)
    query_rows = rotate(projected[:, :query_width], QUERY_HEADS, cosine, sine).astype(bf16)
    key_rows = rotate(
        projected[:, query_width : query_width + key_width], KEY_VALUE_HEADS, cosine, sine
    ).astype(bf16)
    value_rows = projected[:, query_width + key_width :].astype(bf16)
    key_values = lax.all_gather(
        jnp.concatenate([key_rows, value_rows], 1), "ctx", axis=0, tiled=True
    )

    key_values, gate_up, down = lax.optimization_barrier((key_values, gate_up, expert_down[0]))
    down = gather_blocks(down, seq_bits[::-1], seq_bits).reshape(-1, width)
    meta = jnp.concatenate([lax.axis_index("ctx").astype(jnp.int32)[None], pic_starts[0]])
    mixed_heads, log_total = attend(meta, query_rows, key_values)
    mixed_heads, slope_rows[1] = lax.optimization_barrier((mixed_heads, slope_rows[1]))
    attended = mixed_heads.astype(bf16)

    middle = inputs + matmul(attended, full_out)
    enter = rms_norm(middle, gain_two).astype(bf16)
    arrived = [exchange_rows(matmul(part, enter).astype(bf16)) for part in slot_map]

    def gates_of(rows, chosen):
        logits = jnp.where(chosen, matmul(rows, full_router), big_negative)
        shares = jnp.exp(logits - jnp.max(logits, -1, keepdims=True))
        shares = jnp.where(chosen, shares, 0.0)
        return shares / jnp.maximum(jnp.sum(shares, -1, keepdims=True), 1e-30)

    gates = gates_of(enter, routed)

    normed_turned, attended_turned, enter_turned = map(relative, (normed, attended, enter))
    arrived[0], normed_turned, attended_turned, enter_turned = lax.optimization_barrier(
        (arrived[0], normed_turned, attended_turned, enter_turned)
    )
    which = lax.axis_index("ctx").astype(jnp.int32)[None]
    router = second_set[:, width:]
    hidden, result, slope_gates, slope_slots, slope_pre, slope_arrived = ([] for _ in range(6))
    for index in range(2):
        made = list(expert(
            which, arrived[index], slope_rows[index], slot_routes[index], gate_up, down, router)
        )
        if index == 0:
            arrived[1], made[-1] = lax.optimization_barrier((arrived[1], made[-1]))
        for kept, item in zip(
            (hidden, result, slope_gates, slope_slots, slope_pre, slope_arrived), made
        ):
            kept.append(item)
    returned_slopes = [exchange_rows(slope_arrived[0])]
    slope_gates = jnp.concatenate([item.reshape(experts, half) for item in slope_gates], 1)
    slope_gates, returned_slopes[0] = lax.optimization_barrier((slope_gates, returned_slopes[0]))
    returned_gates = lax.all_to_all(slope_gates, "ctx", split_axis=0, concat_axis=0, tiled=True)
    slope_arrived[1], returned_gates = lax.optimization_barrier((slope_arrived[1], returned_gates))
    returned_slopes.append(exchange_rows(slope_arrived[1]))
    grad_gate_up = sum(matmul_tn(arrived[i], slope_pre[i]) for i in range(2)).astype(bf16)
    grad_down = sum(matmul_tn(hidden[i], slope_slots[i]) for i in range(2)).astype(bf16)
    returned_slopes[1], grad_down = lax.optimization_barrier((returned_slopes[1], grad_down))
    returned = [exchange_rows(part) for part in result]

    def sector_sum(grads):
        blocks = grads.reshape([2] * len(seq_bits) + [-1, grads.shape[1]])
        for axis, bit in seq_bits:
            mine = ((lax.axis_index(axis) & bit) > 0).astype(jnp.int32)
            sent = lax.dynamic_index_in_dim(blocks, 1 - mine, 0, keepdims=False)
            kept = lax.dynamic_index_in_dim(blocks, mine, 0, keepdims=False)
            blocks = kept.astype(f32) + swap(sent.astype(bf16), axis, bit).astype(f32)
        return blocks

    grad_gate_up, grad_down = sector_sum(grad_gate_up), sector_sum(grad_down)

    slope_gate = 0.0
    for index, chosen in enumerate(chosen_slot):
        part = returned_gates[:, index * half : (index + 1) * half]
        slope_gate = slope_gate + jnp.sum(jnp.where(chosen, part[:, :, None], 0.0), 1).T
    slope_logits = gates * (slope_gate - jnp.sum(gates * slope_gate, -1, keepdims=True))
    slope_logits = slope_logits.astype(bf16)
    grad_router = matmul_tn(enter_turned, slope_logits)
    slope_enter = matmul_nt(slope_logits, full_router)
    for part, rows in zip(slot_map, returned_slopes):
        slope_enter = slope_enter + matmul_tn(part, rows)

    pull_two = jax.vjp(rms_norm, middle, gain_two)[1]
    slope_middle, grad_gain_two = pull_two(slope_enter)
    slope_middle = out_slope.astype(f32) + slope_middle
    slope_branch = slope_middle.astype(bf16)
    slope_attended = matmul_nt(slope_branch, full_out).astype(bf16)
    delta = slope_attended.astype(f32) * mixed_heads
    delta = jnp.sum(delta.reshape(count, QUERY_HEADS, HEAD_WIDTH), -1).T

    out_sum = Sum(*halves(attended_turned, slope_branch), inward)
    slope_attended, out_sum.sent, grad_gate_up = lax.optimization_barrier(
        (slope_attended, out_sum.sent, grad_gate_up)
    )
    out_sum.step()
    out_sum.step()
    slope_q, slope_kv = attend_back(
        meta, query_rows, slope_attended, log_total, delta, key_values
    )
    slope_q, slope_kv, out_sum.sent, returned[0] = lax.optimization_barrier(
        (slope_q, slope_kv, out_sum.sent, returned[0])
    )
    middle_row = slope_kv.shape[0] // 2
    kv_sum = Sum(slope_kv[middle_row:], slope_kv[:middle_row], ctx_bits[::-1])
    slope_query = rotate(slope_q, QUERY_HEADS, cosine, -sine).astype(bf16)
    query_sum = Sum(*halves(normed_turned, slope_query), inward)
    kv_sum.sent, query_sum.sent = lax.optimization_barrier((kv_sum.sent, query_sum.sent))
    together([kv_sum, query_sum])
    together([kv_sum, query_sum])
    together([kv_sum, query_sum])
    while kv_sum.stages:
        returned[1], grad_down = together([kv_sum, out_sum], (returned[1], grad_down))
    slope_kv = kv_sum.total
    output = middle
    for chosen, rows in zip(chosen_slot, returned):
        mix = jnp.where(chosen, gates.T[:, None, :], 0.0).reshape(-1, count)
        mix_high = mix.astype(bf16)
        mix_low = (mix - mix_high.astype(f32)).astype(bf16)
        output = output + matmul_tn(mix_high, rows) + matmul_tn(mix_low, rows)
    output = output.astype(bf16).reshape(tokens.shape)
    slope_key = rotate(slope_kv[:, :key_width], KEY_VALUE_HEADS, cosine, -sine)
    slope_rest = jnp.concatenate([slope_key, slope_kv[:, key_width:]], 1).astype(bf16)
    rest_sum = Sum(*halves(normed_turned, slope_rest), inward)
    slope_normed = matmul_nt(slope_query, weight_qkv[:, :query_width])
    slope_normed = slope_normed + matmul_nt(slope_rest, weight_qkv[:, query_width:])
    pull_one = jax.vjp(rms_norm, inputs, gain_one)[1]
    slope_inputs, grad_gain_one = pull_one(slope_normed)
    grad_input = (slope_middle + slope_inputs).reshape(tokens.shape)
    gains = relative(jnp.stack([grad_gain_one, grad_gain_two]).astype(bf16)).T
    small = padded([grad_router.astype(bf16), gains])
    small_sum = Sum(small[width // 2 :], small[: width // 2], inward)
    together([item for item in (rest_sum, query_sum) if item.stages])
    while rest_sum.stages:
        together([item for item in (rest_sum, small_sum, query_sum, out_sum) if item.stages])
    for item in (small_sum, query_sum, out_sum):
        while item.stages:
            item.step()
    return (
        output,
        grad_input,
        small_sum.total[:, experts],
        small_sum.total[:, experts + 1],
        query_sum.total,
        rest_sum.total[:, :key_width],
        rest_sum.total[:, key_width:],
        out_sum.total,
        small_sum.total[:, :experts],
        grad_gate_up[None, :, :hidden_width],
        grad_gate_up[None, :, hidden_width:],
        grad_down[None],
    )


def solution(mesh):
    rows = P("seq", "ctx", None)
    shard = P(("seq", "ctx"), None)
    vector = P(("seq", "ctx"))
    expert = P("ctx", "seq", None)
    return jax.shard_map(
        body,
        mesh=mesh,
        in_specs=(rows, rows, rows, P("seq", "ctx"), P("seq", None), vector, vector)
        + (shard,) * 5
        + (expert,) * 3,
        out_specs=(rows, rows, vector, vector) + (shard,) * 5 + (expert,) * 3,
        check_vma=False,
    )
```

```python
import functools
import math

import jax
import jax.numpy as jnp
from jax import lax
from jax.experimental import pallas as pl
from jax.experimental.pallas import tpu as pltpu
from jax.sharding import PartitionSpec as P

QUERY_HEADS = 12
KEY_VALUE_HEADS = 2
HEAD_WIDTH = 128
TOP = 4
PIC = 256
NPIC = 4
LANES = 128
GROUPS = QUERY_HEADS // KEY_VALUE_HEADS
QUERY_WIDTH = QUERY_HEADS * HEAD_WIDTH
KEY_WIDTH = KEY_VALUE_HEADS * HEAD_WIDTH
SCALE = 1.0 / math.sqrt(HEAD_WIDTH)
EXP2_SCALE = SCALE * math.log2(math.e)
BLOCKS = 2
VMEM_BYTES = 48 << 20

epsilon = 1e-06
rope_base = 10000.0
big_negative = -1e30
bf16 = jnp.bfloat16
f32 = jnp.float32


def matmul(left, right):
    return jnp.dot(left, right, preferred_element_type=f32)


def matmul_nt(left, right):
    return lax.dot_general(left, right, (((1,), (1,)), ((), ())), preferred_element_type=f32)


def matmul_tn(left, right):
    return lax.dot_general(left, right, (((0,), (0,)), ((), ())), preferred_element_type=f32)


def rms_scale(rows):
    return lax.rsqrt(jnp.mean(rows * rows, -1, keepdims=True) + epsilon)


def rms_norm(rows, gain):
    return rows * rms_scale(rows) * gain


def rope_tables(positions, head_size):
    half = head_size // 2
    inverse = rope_base ** (-(jnp.arange(half, dtype=f32) * 2.0 / head_size))
    angles = positions.astype(f32)[:, None] * inverse[None, :]
    return (jnp.cos(angles), jnp.sin(angles))


def rotate(rows, heads, cosine, sine):
    shaped = rows.reshape(rows.shape[0], heads, HEAD_WIDTH)
    half = HEAD_WIDTH // 2
    first, second = shaped[..., :half], shaped[..., half:]
    cosine, sine = cosine[:, None, :], sine[:, None, :]
    turned = jnp.concatenate(
        [first * cosine - second * sine, second * cosine + first * sine], -1
    )
    return turned.reshape(rows.shape)


def bits(axis):
    size = lax.axis_size(axis)
    return [(axis, 1 << place) for place in reversed(range(size.bit_length() - 1))]


def swap(block, axis, bit):
    size = lax.axis_size(axis)
    return lax.ppermute(block, axis, [(index, index ^ bit) for index in range(size)])


def gather_blocks(block, stages, order, arrived=None):
    held = []
    for stage in stages:
        axis, bit = stage
        other = swap(block, axis, bit)
        if arrived is not None and stage == stages[-1]:
            other = arrived(other)
        upper = (lax.axis_index(axis) & bit) > 0
        place = sum(order.index(known) < order.index(stage) for known in held)
        block = jnp.stack(
            [jnp.where(upper, other, block), jnp.where(upper, block, other)], place
        )
        held.append(stage)
    return block


class Sum:
    def __init__(self, sent, kept, stages):
        self.sent, self.kept, self.stages = sent, kept, list(stages)

    def step(self):
        axis, bit = self.stages.pop(0)
        other = swap(self.sent, axis, bit)
        if not self.stages:
            self.total = self.kept.astype(f32) + other.astype(f32)
            return
        half = self.kept.shape[0] // 2
        self.sent = (self.kept[half:].astype(f32) + other[half:].astype(f32)).astype(bf16)
        self.kept = (self.kept[:half].astype(f32) + other[:half].astype(f32)).astype(bf16)


def together(sums, also=()):
    for item in sums:
        item.step()
    live = [item for item in sums if item.stages]
    sent, also = lax.optimization_barrier(([item.sent for item in live], also))
    for item, block in zip(live, sent):
        item.sent = block
    return also


def flips(stages, sizes):
    masks = []
    for block in range(1 << len(stages)):
        mask = 0
        for place, (axis, bit) in enumerate(stages):
            if (block >> (len(stages) - 1 - place)) & 1:
                mask |= bit * sizes[axis]
        masks.append(mask)
    return masks


def visible_keys(meta, step, stretch):
    span = BLOCKS * stretch
    keys = step * span + lax.broadcasted_iota(jnp.int32, (span, 1), 0)
    queries = meta[0] * stretch + lax.broadcasted_iota(jnp.int32, (1, stretch), 1)

    def label(positions):
        found = jnp.zeros(positions.shape, jnp.int32)
        for index in range(NPIC):
            start = meta[1 + index]
            inside = (positions >= start) & (positions < start + PIC)
            found = jnp.where(inside, index + 1, found)
        return found

    query_label = label(queries)
    return (keys <= queries) | ((label(keys) == query_label) & (query_label > 0))


def for_each_step(meta, stretch, steps, process, skip=None):
    span = BLOCKS * stretch
    low, high = meta[0] * stretch, (meta[0] + 1) * stretch

    def turn(step, carry):
        needed = step * span < high + PIC - 1
        edge = (step + 1) * span > low

        @pl.when(needed & edge)
        def _():
            process(step, True)

        @pl.when(needed & jnp.logical_not(edge))
        def _():
            process(step, False)

        if skip is not None:

            @pl.when(jnp.logical_not(needed))
            def _():
                skip(step)

        return carry

    lax.fori_loop(0, steps, turn, 0)


def head_columns(head, start=0):
    return slice(start + head * HEAD_WIDTH, start + (head + 1) * HEAD_WIDTH)


def attend_kernel(meta, query, key_value, out, log_total, peak, total, accum):
    stretch = query.shape[0]
    span = BLOCKS * stretch
    peak[...] = jnp.full(peak.shape, big_negative, f32)
    total[...] = jnp.zeros(total.shape, f32)
    accum[...] = jnp.zeros(accum.shape, f32)

    def process(step, edge):
        rows = pl.ds(pl.multiple_of(step * span, span), span)
        if edge:
            visible = visible_keys(meta, step, stretch)
        keys, values = [], []
        for group in range(KEY_VALUE_HEADS):
            keys.append(key_value[rows, head_columns(group)])
            turned = key_value[rows, head_columns(group, KEY_WIDTH)].T
            values.append(jnp.concatenate([turned, jnp.ones((16, span), bf16)], 0))

        def score(head):
            scores = matmul_nt(keys[head // GROUPS], query[:, head_columns(head)])
            if edge:
                scores = jnp.where(visible, scores, big_negative)
            old = peak[head : head + 1, :]
            return scores, old, jnp.maximum(old, jnp.max(scores, 0, keepdims=True))

        def weigh(head, scores, old, new):
            weights = jnp.exp2((scores - new) * EXP2_SCALE).astype(bf16)
            shrink = jnp.exp2((old - new) * EXP2_SCALE)
            sums = matmul(values[head // GROUPS], weights)
            row, columns = slice(head, head + 1), head_columns(head)
            peak[row, :] = new
            total[row, :] = total[row, :] * shrink + sums[HEAD_WIDTH : HEAD_WIDTH + 1]
            accum[columns, :] = accum[columns, :] * shrink + sums[:HEAD_WIDTH]

        waiting = []
        for head in range(QUERY_HEADS):
            waiting.append((head, *score(head)))
            if len(waiting) > 2:
                weigh(*waiting.pop(0))
        for item in waiting:
            weigh(*item)

    for_each_step(meta, stretch, key_value.shape[0] // span, process)
    for head in range(QUERY_HEADS):
        row, columns = slice(head, head + 1), head_columns(head)
        out[:, columns] = (accum[columns, :] / total[row, :]).T
        log_total[row, :] = peak[row, :] * EXP2_SCALE + jnp.log2(total[row, :])


def attend_back_kernel(
    orders, meta, query, slope, log_total, mixed, key_value, slope_query, *outs_scratch
):
    outs, accum, delta = outs_scratch[:4], outs_scratch[4], outs_scratch[5]
    stretch = query.shape[0]
    span = BLOCKS * stretch
    accum[...] = jnp.zeros(accum.shape, f32)
    for head in range(QUERY_HEADS):
        columns = head_columns(head)
        product = slope[:, columns].astype(f32) * mixed[:, columns]
        delta[head : head + 1, :] = jnp.sum(product.T, 0, keepdims=True)

    def store(step, part, which, columns, block):
        flip = jnp.bitwise_xor(BLOCKS * step + part, meta[0])
        first, *others = orders[which]
        place = 0
        for index, bit in enumerate(others):
            place = place + ((flip // bit) & 1) * (1 << (len(others) - 1 - index))
        place = pl.ds(pl.multiple_of(place * stretch, stretch), stretch)
        goes = ((flip // first) & 1) == 1

        @pl.when(goes)
        def _():
            outs[2 * which][place, columns] = block

        @pl.when(jnp.logical_not(goes))
        def _():
            outs[2 * which + 1][place, columns] = block

    def process(step, edge):
        rows = pl.ds(pl.multiple_of(step * span, span), span)
        if edge:
            visible = visible_keys(meta, step, stretch)
        for group in range(KEY_VALUE_HEADS):
            keys = key_value[rows, head_columns(group)]
            values = key_value[rows, head_columns(group, KEY_WIDTH)]
            keys_turned = keys.T
            slope_k = jnp.zeros((span, HEAD_WIDTH), f32)
            slope_v = jnp.zeros((span, HEAD_WIDTH), f32)
            for head in range(group * GROUPS, (group + 1) * GROUPS):
                row, columns = slice(head, head + 1), head_columns(head)
                own_query, own_slope = query[:, columns], slope[:, columns]
                scores = matmul_nt(keys, own_query)
                probs = jnp.exp2(scores * EXP2_SCALE - log_total[row, :])
                if edge:
                    probs = jnp.where(visible, probs, 0.0)
                slope_probs = matmul_nt(values, own_slope)
                slope_scores = (probs * (slope_probs - delta[row, :])).astype(bf16)
                slope_v = slope_v + matmul(probs.astype(bf16), own_slope)
                slope_k = slope_k + matmul(slope_scores, own_query)
                accum[columns, :] = accum[columns, :] + matmul(keys_turned, slope_scores)
            for which, block in enumerate(((slope_k * SCALE).astype(bf16), slope_v.astype(bf16))):
                for part in range(BLOCKS):
                    own = block[part * stretch : (part + 1) * stretch]
                    store(step, part, which, head_columns(group), own)

    def skip(step):
        for which in range(2):
            for part in range(BLOCKS):
                store(step, part, which, slice(None), jnp.zeros((stretch, KEY_WIDTH), bf16))

    for_each_step(meta, stretch, key_value.shape[0] // span, process, skip)
    for head in range(QUERY_HEADS):
        columns = head_columns(head)
        slope_query[:, columns] = (accum[columns, :] * SCALE).T


def expert_kernel(
    which,
    rows,
    slopes,
    chosen,
    gate_up,
    down,
    router,
    hidden_out,
    result_out,
    gates_out,
    slots_out,
    pre_out,
    slope_out,
):
    hidden_width = down.shape[0]
    incoming = rows[...]
    logits = jnp.where(chosen[...] > 0, matmul(incoming, router[...]), big_negative)
    shares = jnp.exp(logits - jnp.max(logits, -1, keepdims=True))
    shares = jnp.where(chosen[...] > 0, shares, 0.0)
    column = lax.broadcasted_iota(jnp.int32, shares.shape, 1)
    own = jnp.sum(jnp.where(column == which[0], shares, 0.0), -1, keepdims=True)
    gates = own / jnp.maximum(jnp.sum(shares, -1, keepdims=True), 1e-30)
    slots = (gates * slopes[...].astype(f32)).astype(bf16)
    slots_out[...] = slots
    pre = matmul(incoming, gate_up[...])
    gate, up = pre[:, :hidden_width], pre[:, hidden_width:]
    root, cubic = math.sqrt(2.0 / math.pi), 0.044715
    square = gate * gate
    bend = jnp.tanh(root * (gate + cubic * gate * square))
    gelu = 0.5 * gate * (1.0 + bend)
    rise = 0.5 * (1.0 + bend) + 0.5 * gate * (1.0 - bend * bend) * root * (
        1.0 + 3.0 * cubic * square
    )
    hidden = (gelu * up).astype(bf16)
    hidden_out[...] = hidden
    result = matmul(hidden, down[...]).astype(bf16)
    result_out[...] = result
    gates_out[...] = jnp.sum(slopes[...].astype(f32) * result.astype(f32), -1, keepdims=True)
    slope_hidden = matmul_nt(slots, down[...])
    slope_pre = jnp.concatenate([slope_hidden * up * rise, slope_hidden * gelu], 1).astype(bf16)
    pre_out[...] = slope_pre
    slope_out[...] = matmul_nt(slope_pre, gate_up[...]).astype(bf16)


def expert(which, rows, slopes, chosen, gate_up, down, router):
    count, width = rows.shape
    hidden_width = down.shape[0]
    block = count // 2

    def tile(columns):
        return pl.BlockSpec((block, columns), lambda step: (step, 0))

    def whole(array):
        return pl.BlockSpec(array.shape, lambda step: (0, 0))

    shapes = [(hidden_width, bf16), (width, bf16), (1, f32), (width, bf16)]
    shapes += [(2 * hidden_width, bf16), (width, bf16)]
    return pl.pallas_call(
        expert_kernel,
        grid=(2,),
        out_shape=[jax.ShapeDtypeStruct((count, columns), kind) for columns, kind in shapes],
        in_specs=[
            pl.BlockSpec(memory_space=pltpu.SMEM),
            tile(width),
            tile(width),
            tile(LANES),
            whole(gate_up),
            whole(down),
            whole(router),
        ],
        out_specs=[tile(columns) for columns, _ in shapes],
        compiler_params=pltpu.CompilerParams(vmem_limit_bytes=VMEM_BYTES),
        cost_estimate=pl.CostEstimate(
            flops=12 * count * width * hidden_width,
            bytes_accessed=20 * count * width,
            transcendentals=count * hidden_width,
        ),
        name="expert",
    )(which, rows, slopes, chosen, gate_up, down, router)


def attention_call(kernel, outs, scratch, products, name, meta, *operands):
    vmem = pl.BlockSpec(memory_space=pltpu.VMEM)
    pairs = QUERY_HEADS * operands[0].shape[0] * operands[-1].shape[0]
    return pl.pallas_call(
        kernel,
        out_shape=outs,
        in_specs=[pl.BlockSpec(memory_space=pltpu.SMEM)] + [vmem] * len(operands),
        out_specs=(vmem,) * len(outs),
        scratch_shapes=[pltpu.VMEM(shape, f32) for shape in scratch],
        compiler_params=pltpu.CompilerParams(vmem_limit_bytes=VMEM_BYTES),
        cost_estimate=pl.CostEstimate(
            flops=products * pairs, bytes_accessed=QUERY_WIDTH * 1024, transcendentals=0
        ),
        name=name,
    )(meta, *operands)


def attend(meta, query, key_value):
    stretch = query.shape[0]
    stats = (QUERY_HEADS, stretch)
    outs = (
        jax.ShapeDtypeStruct((stretch, QUERY_WIDTH), f32),
        jax.ShapeDtypeStruct(stats, f32),
    )
    scratch = [stats, stats, (QUERY_WIDTH, stretch)]
    return attention_call(attend_kernel, outs, scratch, 2, "attend", meta, query, key_value)


def attend_back(orders, meta, query, slope, log_total, mixed, key_value):
    stretch, rows = query.shape[0], key_value.shape[0]
    outs = (jax.ShapeDtypeStruct((stretch, QUERY_WIDTH), f32),)
    outs += (jax.ShapeDtypeStruct((rows // 2, KEY_WIDTH), bf16),) * 4
    operands = (meta, query, slope, log_total, mixed, key_value)
    scratch = [(QUERY_WIDTH, stretch), (QUERY_HEADS, stretch)]
    kernel = functools.partial(attend_back_kernel, orders)
    return attention_call(kernel, outs, scratch, 5, "attend_back", *operands)


def body(
    tokens,
    cotangent,
    routes,
    fill_order,
    pic_starts,
    attn_gain,
    moe_gain,
    w_query,
    key_projection,
    value_projection,
    w_out,
    w_router,
    expert_gate,
    expert_up,
    expert_down,
):
    sequences, stretch, width = tokens.shape
    count = sequences * stretch
    parts = lax.axis_size("ctx")
    experts = parts
    capacity = (5 * count * TOP + 4 * experts - 1) // (4 * experts)
    query_width, key_width = QUERY_WIDTH, KEY_WIDTH
    hidden_width = expert_gate.shape[2]
    both = ("seq", "ctx")
    seq_bits, ctx_bits = bits("seq"), bits("ctx")
    all_bits = seq_bits + ctx_bits
    outward = ctx_bits[:-1] + seq_bits + ctx_bits[-1:]
    inward = ctx_bits[-1:] + seq_bits[::-1] + ctx_bits[-2::-1]
    sizes = {"seq": parts, "ctx": 1}
    me = lax.axis_index("seq") * parts + lax.axis_index("ctx")

    def padded(columns):
        block = jnp.concatenate(columns, 1)
        return jnp.pad(block, ((0, 0), (0, LANES - block.shape[1])))

    first_set = lax.all_gather(
        jnp.concatenate(
            [w_query, key_projection, value_projection, padded([attn_gain[:, None]])], 1
        ),
        both,
        axis=0,
        tiled=True,
    )
    second_set = gather_blocks(
        jnp.concatenate([w_out, padded([w_router, moe_gain[:, None]])], 1), outward, all_bits
    ).reshape(width, -1)

    own_rows = w_query.shape[0]
    owner = jnp.bitwise_xor(jnp.array(flips(inward, sizes), jnp.int32), me)
    feature = (owner[:, None] * own_rows + jnp.arange(own_rows, dtype=jnp.int32)).reshape(-1)
    turn = (jnp.arange(width, dtype=jnp.int32)[:, None] == feature[None, :]).astype(bf16)

    def relative(rows):
        return matmul(rows, turn).astype(bf16)

    def halves(left, right):
        middle = left.shape[1] // 2
        sent = matmul_tn(left[:, middle:], right).astype(bf16)
        return sent, matmul_tn(left[:, :middle], right).astype(bf16)

    picks = routes.reshape(count, TOP)
    order = fill_order.reshape(count)
    routed = jnp.any(picks[:, :, None] == jnp.arange(experts, dtype=jnp.int32), 1)
    earlier = (order[None, :] < order[:, None]).astype(bf16)
    place = matmul(earlier, routed.astype(bf16)).astype(jnp.int32)
    place = jnp.where(routed, place, capacity)
    half = capacity // 2
    chosen_slot = [
        place.T[:, None, :]
        == (begin + jnp.arange(half, dtype=jnp.int32))[None, :, None]
        for begin in (0, half)
    ]
    slot_map = [chosen.astype(bf16).reshape(-1, count) for chosen in chosen_slot]

    def exchange_rows(rows):
        rows = rows.reshape(experts, half, width)
        rows = lax.all_to_all(rows, "ctx", split_axis=0, concat_axis=0, tiled=True)
        return rows.reshape(-1, width)

    out_slope = cotangent.reshape(count, width)
    slot_routes = jnp.concatenate(
        [matmul(part, routed.astype(bf16)).reshape(experts, half, experts) for part in slot_map], 1
    ).astype(bf16)
    slot_routes = lax.all_to_all(slot_routes, "ctx", split_axis=0, concat_axis=0, tiled=True)
    slot_routes = jnp.pad(slot_routes, ((0, 0), (0, 0), (0, LANES - experts)))
    slot_routes = [
        slot_routes[:, begin : begin + half].reshape(-1, LANES) for begin in (0, half)
    ]
    slope_rows = [exchange_rows(matmul(part, out_slope).astype(bf16)) for part in slot_map]
    gate_up = jnp.concatenate([expert_gate[0], expert_up[0]], 1)
    first_set, slot_routes, slope_rows[0], gate_up = lax.optimization_barrier(
        (first_set, slot_routes, slope_rows[0], gate_up)
    )
    weight_qkv = first_set[:, : query_width + 2 * key_width]
    gain_one = first_set[:, query_width + 2 * key_width].astype(f32)
    full_out = second_set[:, :width]
    full_router = second_set[:, width : width + experts]
    gain_two = second_set[:, width + experts].astype(f32)

    positions = lax.axis_index("ctx") * stretch + jnp.arange(stretch, dtype=jnp.int32)
    cosine, sine = rope_tables(positions, HEAD_WIDTH)
    inputs = tokens.astype(f32).reshape(count, width)
    normed = rms_norm(inputs, gain_one).astype(bf16)
    projected = matmul(normed, weight_qkv)
    query_rows = rotate(projected[:, :query_width], QUERY_HEADS, cosine, sine).astype(bf16)
    key_rows = rotate(
        projected[:, query_width : query_width + key_width], KEY_VALUE_HEADS, cosine, sine
    ).astype(bf16)
    value_rows = projected[:, query_width + key_width :].astype(bf16)
    key_values = lax.all_gather(
        jnp.concatenate([key_rows, value_rows], 1), "ctx", axis=0, tiled=True
    )

    meta = jnp.concatenate([lax.axis_index("ctx").astype(jnp.int32)[None], pic_starts[0]])
    mixed_heads, log_total = attend(meta, query_rows, key_values)

    def with_attention(other):
        nonlocal mixed_heads
        mixed_heads, other, slope_rows[1] = lax.optimization_barrier(
            (mixed_heads, other, slope_rows[1])
        )
        return other

    gate_up = gather_blocks(gate_up, seq_bits[::-1], seq_bits, with_attention)
    gate_up = gate_up.reshape(-1, 2 * hidden_width)
    down = gather_blocks(
        lax.optimization_barrier((expert_down[0], key_values))[0], seq_bits[::-1], seq_bits
    ).reshape(-1, width)
    attended = mixed_heads.astype(bf16)

    middle = inputs + matmul(attended, full_out)
    enter = rms_norm(middle, gain_two).astype(bf16)
    arrived = [exchange_rows(matmul(part, enter).astype(bf16)) for part in slot_map]

    def gates_of(rows, chosen):
        logits = jnp.where(chosen, matmul(rows, full_router), big_negative)
        shares = jnp.exp(logits - jnp.max(logits, -1, keepdims=True))
        shares = jnp.where(chosen, shares, 0.0)
        return shares / jnp.maximum(jnp.sum(shares, -1, keepdims=True), 1e-30)

    gates = gates_of(enter, routed)

    normed_turned, attended_turned, enter_turned = map(relative, (normed, attended, enter))
    arrived[0], normed_turned, attended_turned, enter_turned = lax.optimization_barrier(
        (arrived[0], normed_turned, attended_turned, enter_turned)
    )
    which = lax.axis_index("ctx").astype(jnp.int32)[None]
    router = second_set[:, width:]
    hidden, result, slope_gates, slope_slots, slope_pre, slope_arrived = ([] for _ in range(6))
    for index in range(2):
        made = list(expert(
            which, arrived[index], slope_rows[index], slot_routes[index], gate_up, down, router)
        )
        if index == 0:
            arrived[1], made[-1] = lax.optimization_barrier((arrived[1], made[-1]))
        for kept, item in zip(
            (hidden, result, slope_gates, slope_slots, slope_pre, slope_arrived), made
        ):
            kept.append(item)
    returned_slopes = [exchange_rows(slope_arrived[0])]
    slope_gates = jnp.concatenate([item.reshape(experts, half) for item in slope_gates], 1)
    slope_gates, returned_slopes[0] = lax.optimization_barrier((slope_gates, returned_slopes[0]))
    returned_gates = lax.all_to_all(slope_gates, "ctx", split_axis=0, concat_axis=0, tiled=True)
    slope_arrived[1], returned_gates = lax.optimization_barrier((slope_arrived[1], returned_gates))
    returned_slopes.append(exchange_rows(slope_arrived[1]))
    grad_gate_up = sum(matmul_tn(arrived[i], slope_pre[i]) for i in range(2)).astype(bf16)
    grad_down = sum(matmul_tn(hidden[i], slope_slots[i]) for i in range(2)).astype(bf16)
    def sector_halves(grads):
        return grads.reshape([2] * len(seq_bits) + [-1, grads.shape[1]])

    def sector_sum(blocks, arrived):
        for axis, bit in seq_bits:
            mine = ((lax.axis_index(axis) & bit) > 0).astype(jnp.int32)
            sent = lax.dynamic_index_in_dim(blocks, 1 - mine, 0, keepdims=False)
            kept = lax.dynamic_index_in_dim(blocks, mine, 0, keepdims=False)
            other = swap(sent.astype(bf16), axis, bit)
            if (axis, bit) == seq_bits[-1]:
                other = arrived(other)
            blocks = kept.astype(f32) + other.astype(f32)
        return blocks

    def with_slopes(other):
        nonlocal grad_down
        returned_slopes[1], other, grad_down = lax.optimization_barrier(
            (returned_slopes[1], other, grad_down)
        )
        return other

    grad_gate_up = sector_sum(sector_halves(grad_gate_up), with_slopes)
    returned = jnp.concatenate([part.reshape(experts, half, width) for part in result], 1)
    returned = lax.all_to_all(returned, "ctx", split_axis=0, concat_axis=0, tiled=True)

    slope_gate = 0.0
    for index, chosen in enumerate(chosen_slot):
        part = returned_gates[:, index * half : (index + 1) * half]
        slope_gate = slope_gate + jnp.sum(jnp.where(chosen, part[:, :, None], 0.0), 1).T
    slope_logits = gates * (slope_gate - jnp.sum(gates * slope_gate, -1, keepdims=True))
    slope_logits = slope_logits.astype(bf16)
    grad_router = matmul_tn(enter_turned, slope_logits)
    slope_enter = matmul_nt(slope_logits, full_router)
    for part, rows in zip(slot_map, returned_slopes):
        slope_enter = slope_enter + matmul_tn(part, rows)

    pull_two = jax.vjp(rms_norm, middle, gain_two)[1]
    slope_middle, grad_gain_two = pull_two(slope_enter)
    slope_middle = out_slope.astype(f32) + slope_middle
    slope_branch = slope_middle.astype(bf16)
    slope_attended = matmul_nt(slope_branch, full_out).astype(bf16)

    out_sum = Sum(*halves(attended_turned, slope_branch), inward)
    out_sum.step()
    out_sum.step()
    orders = (ctx_bits[::-1], ctx_bits[-1:] + ctx_bits[:-1])
    backs = attend_back(
        [[bit for _, bit in order] for order in orders],
        meta,
        query_rows,
        slope_attended,
        log_total,
        mixed_heads,
        key_values,
    )

    def after_back(other):
        nonlocal backs
        backs, other, out_sum.sent = lax.optimization_barrier((backs, other, out_sum.sent))
        return other

    grad_down = sector_sum(sector_halves(grad_down), after_back)
    slope_q, *slope_kv = backs
    key_sum = Sum(*slope_kv[:2], orders[0])
    value_sum = Sum(*slope_kv[2:], orders[1])
    slope_query = rotate(slope_q, QUERY_HEADS, cosine, -sine).astype(bf16)
    query_sum = Sum(*halves(normed_turned, slope_query), inward)
    kv_sums = [key_sum, value_sum]
    together(kv_sums + [query_sum])
    returned = together(kv_sums + [query_sum], returned)
    together(kv_sums + [query_sum])
    while key_sum.stages:
        together(kv_sums + [item for item in (query_sum, out_sum) if item.stages])
    output = middle
    for chosen, rows in ((jnp.concatenate(chosen_slot, 1), returned.reshape(-1, width)),):
        mix = jnp.where(chosen, gates.T[:, None, :], 0.0).reshape(-1, count)
        mix_high = mix.astype(bf16)
        mix_low = (mix - mix_high.astype(f32)).astype(bf16)
        output = output + matmul_tn(mix_high, rows) + matmul_tn(mix_low, rows)
    output = output.astype(bf16).reshape(tokens.shape)
    slope_key = rotate(key_sum.total, KEY_VALUE_HEADS, cosine, -sine)
    slope_rest = jnp.concatenate([slope_key, value_sum.total], 1).astype(bf16)
    slope_normed = matmul_nt(slope_query, weight_qkv[:, :query_width])
    slope_normed = slope_normed + matmul_nt(slope_rest, weight_qkv[:, query_width:])
    pull_one = jax.vjp(rms_norm, inputs, gain_one)[1]
    slope_inputs, grad_gain_one = pull_one(slope_normed)
    grad_input = (slope_middle + slope_inputs).reshape(tokens.shape)
    gains = relative(jnp.stack([grad_gain_one, grad_gain_two]).astype(bf16)).T
    small = padded([grad_router.astype(bf16), gains])
    rest_sum = Sum(
        *(
            jnp.concatenate([grads, part], 1)
            for grads, part in zip(
                halves(normed_turned, slope_rest), (small[width // 2 :], small[: width // 2])
            )
        ),
        inward,
    )
    while rest_sum.stages:
        together([item for item in (rest_sum, query_sum, out_sum) if item.stages])
    for item in (query_sum, out_sum):
        while item.stages:
            item.step()
    grads_rest = rest_sum.total
    return (
        output,
        grad_input,
        grads_rest[:, 2 * key_width + experts],
        grads_rest[:, 2 * key_width + experts + 1],
        query_sum.total,
        grads_rest[:, :key_width],
        grads_rest[:, key_width : 2 * key_width],
        out_sum.total,
        grads_rest[:, 2 * key_width : 2 * key_width + experts],
        grad_gate_up[None, :, :hidden_width],
        grad_gate_up[None, :, hidden_width:],
        grad_down[None],
    )


def solution(mesh):
    rows = P("seq", "ctx", None)
    shard = P(("seq", "ctx"), None)
    vector = P(("seq", "ctx"))
    expert = P("ctx", "seq", None)
    return jax.shard_map(
        body,
        mesh=mesh,
        in_specs=(rows, rows, rows, P("seq", "ctx"), P("seq", None), vector, vector)
        + (shard,) * 5
        + (expert,) * 3,
        out_specs=(rows, rows, vector, vector) + (shard,) * 5 + (expert,) * 3,
        check_vma=False,
    )
```

```python
import functools
import math

import jax
import jax.numpy as jnp
from jax import lax
from jax.experimental import pallas as pl
from jax.experimental.pallas import tpu as pltpu
from jax.sharding import PartitionSpec as P

QUERY_HEADS = 12
KEY_VALUE_HEADS = 2
HEAD_WIDTH = 128
TOP = 4
PIC = 256
NPIC = 4
LANES = 128
GROUPS = QUERY_HEADS // KEY_VALUE_HEADS
QUERY_WIDTH = QUERY_HEADS * HEAD_WIDTH
KEY_WIDTH = KEY_VALUE_HEADS * HEAD_WIDTH
SCALE = 1.0 / math.sqrt(HEAD_WIDTH)
EXP2_SCALE = SCALE * math.log2(math.e)
BLOCKS = 2
VMEM_BYTES = 48 << 20

epsilon = 1e-06
rope_base = 10000.0
big_negative = -1e30
bf16 = jnp.bfloat16
f32 = jnp.float32


def matmul(left, right):
    return jnp.dot(left, right, preferred_element_type=f32)


def matmul_nt(left, right):
    return lax.dot_general(left, right, (((1,), (1,)), ((), ())), preferred_element_type=f32)


def matmul_tn(left, right):
    return lax.dot_general(left, right, (((0,), (0,)), ((), ())), preferred_element_type=f32)


def rms_scale(rows):
    return lax.rsqrt(jnp.mean(rows * rows, -1, keepdims=True) + epsilon)


def rms_norm(rows, gain):
    return rows * rms_scale(rows) * gain


def rope_tables(positions, head_size):
    half = head_size // 2
    inverse = rope_base ** (-(jnp.arange(half, dtype=f32) * 2.0 / head_size))
    angles = positions.astype(f32)[:, None] * inverse[None, :]
    return (jnp.cos(angles), jnp.sin(angles))


def rotate(rows, heads, cosine, sine):
    shaped = rows.reshape(rows.shape[0], heads, HEAD_WIDTH)
    half = HEAD_WIDTH // 2
    first, second = shaped[..., :half], shaped[..., half:]
    cosine, sine = cosine[:, None, :], sine[:, None, :]
    turned = jnp.concatenate(
        [first * cosine - second * sine, second * cosine + first * sine], -1
    )
    return turned.reshape(rows.shape)


def bits(axis):
    size = lax.axis_size(axis)
    return [(axis, 1 << place) for place in reversed(range(size.bit_length() - 1))]


def swap(block, axis, bit):
    size = lax.axis_size(axis)
    return lax.ppermute(block, axis, [(index, index ^ bit) for index in range(size)])


def gather_blocks(block, stages, order, arrived=None):
    held = []
    for stage in stages:
        axis, bit = stage
        other = swap(block, axis, bit)
        if arrived is not None and stage == stages[-1]:
            other = arrived(other)
        upper = (lax.axis_index(axis) & bit) > 0
        place = sum(order.index(known) < order.index(stage) for known in held)
        block = jnp.stack(
            [jnp.where(upper, other, block), jnp.where(upper, block, other)], place
        )
        held.append(stage)
    return block


class Sum:
    def __init__(self, sent, kept, stages):
        self.sent, self.kept, self.stages = sent, kept, list(stages)

    def step(self):
        axis, bit = self.stages.pop(0)
        other = swap(self.sent, axis, bit)
        if not self.stages:
            self.total = self.kept.astype(f32) + other.astype(f32)
            return
        half = self.kept.shape[0] // 2
        self.sent = (self.kept[half:].astype(f32) + other[half:].astype(f32)).astype(bf16)
        self.kept = (self.kept[:half].astype(f32) + other[:half].astype(f32)).astype(bf16)


def together(sums, also=()):
    for item in sums:
        item.step()
    live = [item for item in sums if item.stages]
    sent, also = lax.optimization_barrier(([item.sent for item in live], also))
    for item, block in zip(live, sent):
        item.sent = block
    return also


def flips(stages, sizes):
    masks = []
    for block in range(1 << len(stages)):
        mask = 0
        for place, (axis, bit) in enumerate(stages):
            if (block >> (len(stages) - 1 - place)) & 1:
                mask |= bit * sizes[axis]
        masks.append(mask)
    return masks


def visible_keys(meta, step, stretch):
    span = BLOCKS * stretch
    keys = step * span + lax.broadcasted_iota(jnp.int32, (span, 1), 0)
    queries = meta[0] * stretch + lax.broadcasted_iota(jnp.int32, (1, stretch), 1)

    def label(positions):
        found = jnp.zeros(positions.shape, jnp.int32)
        for index in range(NPIC):
            start = meta[1 + index]
            inside = (positions >= start) & (positions < start + PIC)
            found = jnp.where(inside, index + 1, found)
        return found

    query_label = label(queries)
    return (keys <= queries) | ((label(keys) == query_label) & (query_label > 0))


def for_each_step(meta, stretch, steps, process, skip=None):
    span = BLOCKS * stretch
    low, high = meta[0] * stretch, (meta[0] + 1) * stretch

    def turn(step, carry):
        needed = step * span < high + PIC - 1
        edge = (step + 1) * span > low

        @pl.when(needed & edge)
        def _():
            process(step, True)

        @pl.when(needed & jnp.logical_not(edge))
        def _():
            process(step, False)

        if skip is not None:

            @pl.when(jnp.logical_not(needed))
            def _():
                skip(step)

        return carry

    lax.fori_loop(0, steps, turn, 0)


def head_columns(head, start=0):
    return slice(start + head * HEAD_WIDTH, start + (head + 1) * HEAD_WIDTH)


def attend_kernel(meta, query, key_value, out, log_total, peak, total, accum):
    stretch = query.shape[0]
    span = BLOCKS * stretch
    peak[...] = jnp.full(peak.shape, big_negative, f32)
    total[...] = jnp.zeros(total.shape, f32)
    accum[...] = jnp.zeros(accum.shape, f32)

    def process(step, edge):
        rows = pl.ds(pl.multiple_of(step * span, span), span)
        if edge:
            visible = visible_keys(meta, step, stretch)
        keys, values = [], []
        for group in range(KEY_VALUE_HEADS):
            keys.append(key_value[rows, head_columns(group)])
            turned = key_value[rows, head_columns(group, KEY_WIDTH)].T
            values.append(jnp.concatenate([turned, jnp.ones((16, span), bf16)], 0))

        def score(head):
            scores = matmul_nt(keys[head // GROUPS], query[:, head_columns(head)])
            if edge:
                scores = jnp.where(visible, scores, big_negative)
            old = peak[head : head + 1, :]
            return scores, old, jnp.maximum(old, jnp.max(scores, 0, keepdims=True))

        def weigh(head, scores, old, new):
            weights = jnp.exp2((scores - new) * EXP2_SCALE).astype(bf16)
            shrink = jnp.exp2((old - new) * EXP2_SCALE)
            sums = matmul(values[head // GROUPS], weights)
            row, columns = slice(head, head + 1), head_columns(head)
            peak[row, :] = new
            total[row, :] = total[row, :] * shrink + sums[HEAD_WIDTH : HEAD_WIDTH + 1]
            accum[columns, :] = accum[columns, :] * shrink + sums[:HEAD_WIDTH]

        waiting = []
        for head in range(QUERY_HEADS):
            waiting.append((head, *score(head)))
            if len(waiting) > 2:
                weigh(*waiting.pop(0))
        for item in waiting:
            weigh(*item)

    for_each_step(meta, stretch, key_value.shape[0] // span, process)
    for head in range(QUERY_HEADS):
        row, columns = slice(head, head + 1), head_columns(head)
        out[:, columns] = (accum[columns, :] / total[row, :]).T
        log_total[row, :] = peak[row, :] * EXP2_SCALE + jnp.log2(total[row, :])


def attend_back_kernel(
    orders, meta, query, slope, log_total, mixed, key_value, slope_query, *outs_scratch
):
    outs, accum, delta = outs_scratch[:2], outs_scratch[2], outs_scratch[3]
    stretch = query.shape[0]
    span = BLOCKS * stretch
    accum[...] = jnp.zeros(accum.shape, f32)
    for head in range(QUERY_HEADS):
        columns = head_columns(head)
        product = slope[:, columns].astype(f32) * mixed[:, columns]
        delta[head : head + 1, :] = jnp.sum(product.T, 0, keepdims=True)

    def store(step, part, which, columns, block):
        flip = jnp.bitwise_xor(BLOCKS * step + part, meta[0])
        first, *others = orders[which]
        place = 0
        for index, bit in enumerate(others):
            place = place + ((flip // bit) & 1) * (1 << (len(others) - 1 - index))
        place = pl.ds(pl.multiple_of(place * stretch, stretch), stretch)
        outs[which][(flip // first) & 1, place, columns] = block

    def process(step, edge):
        rows = pl.ds(pl.multiple_of(step * span, span), span)
        if edge:
            visible = visible_keys(meta, step, stretch)
        for group in range(KEY_VALUE_HEADS):
            keys = key_value[rows, head_columns(group)]
            values = key_value[rows, head_columns(group, KEY_WIDTH)]
            keys_turned = keys.T
            slope_k = jnp.zeros((span, HEAD_WIDTH), f32)
            slope_v = jnp.zeros((span, HEAD_WIDTH), f32)
            for head in range(group * GROUPS, (group + 1) * GROUPS):
                row, columns = slice(head, head + 1), head_columns(head)
                own_query, own_slope = query[:, columns], slope[:, columns]
                scores = matmul_nt(keys, own_query)
                probs = jnp.exp2(scores * EXP2_SCALE - log_total[row, :])
                if edge:
                    probs = jnp.where(visible, probs, 0.0)
                slope_probs = matmul_nt(values, own_slope)
                slope_scores = (probs * (slope_probs - delta[row, :])).astype(bf16)
                slope_v = slope_v + matmul(probs.astype(bf16), own_slope)
                slope_k = slope_k + matmul(slope_scores, own_query)
                accum[columns, :] = accum[columns, :] + matmul(keys_turned, slope_scores)
            for which, block in enumerate(((slope_k * SCALE).astype(bf16), slope_v.astype(bf16))):
                for part in range(BLOCKS):
                    own = block[part * stretch : (part + 1) * stretch]
                    store(step, part, which, head_columns(group), own)

    def skip(step):
        for which in range(2):
            for part in range(BLOCKS):
                store(step, part, which, slice(None), jnp.zeros((stretch, KEY_WIDTH), bf16))

    for_each_step(meta, stretch, key_value.shape[0] // span, process, skip)
    for head in range(QUERY_HEADS):
        columns = head_columns(head)
        slope_query[:, columns] = (accum[columns, :] * SCALE).T


def expert_kernel(
    which,
    rows,
    slopes,
    chosen,
    gate_up,
    down,
    router,
    hidden_out,
    result_out,
    gates_out,
    slots_out,
    pre_out,
    slope_out,
):
    hidden_width = down.shape[0]
    incoming = rows[...]
    logits = jnp.where(chosen[...] > 0, matmul(incoming, router[...]), big_negative)
    shares = jnp.exp(logits - jnp.max(logits, -1, keepdims=True))
    shares = jnp.where(chosen[...] > 0, shares, 0.0)
    column = lax.broadcasted_iota(jnp.int32, shares.shape, 1)
    own = jnp.sum(jnp.where(column == which[0], shares, 0.0), -1, keepdims=True)
    gates = own / jnp.maximum(jnp.sum(shares, -1, keepdims=True), 1e-30)
    slots = (gates * slopes[...].astype(f32)).astype(bf16)
    slots_out[...] = slots
    pre = matmul(incoming, gate_up[...])
    gate, up = pre[:, :hidden_width], pre[:, hidden_width:]
    root, cubic = math.sqrt(2.0 / math.pi), 0.044715
    square = gate * gate
    bend = jnp.tanh(root * (gate + cubic * gate * square))
    gelu = 0.5 * gate * (1.0 + bend)
    rise = 0.5 * (1.0 + bend) + 0.5 * gate * (1.0 - bend * bend) * root * (
        1.0 + 3.0 * cubic * square
    )
    hidden = (gelu * up).astype(bf16)
    hidden_out[...] = hidden
    result = matmul(hidden, down[...]).astype(bf16)
    result_out[...] = result
    gates_out[...] = jnp.sum(slopes[...].astype(f32) * result.astype(f32), -1, keepdims=True)
    slope_hidden = matmul_nt(slots, down[...])
    slope_pre = jnp.concatenate([slope_hidden * up * rise, slope_hidden * gelu], 1).astype(bf16)
    pre_out[...] = slope_pre
    slope_out[...] = matmul_nt(slope_pre, gate_up[...]).astype(bf16)


def expert(which, rows, slopes, chosen, gate_up, down, router):
    count, width = rows.shape
    hidden_width = down.shape[0]
    block = count // 2

    def tile(columns):
        return pl.BlockSpec((block, columns), lambda step: (step, 0))

    def whole(array):
        return pl.BlockSpec(array.shape, lambda step: (0, 0))

    shapes = [(hidden_width, bf16), (width, bf16), (1, f32), (width, bf16)]
    shapes += [(2 * hidden_width, bf16), (width, bf16)]
    return pl.pallas_call(
        expert_kernel,
        grid=(2,),
        out_shape=[jax.ShapeDtypeStruct((count, columns), kind) for columns, kind in shapes],
        in_specs=[
            pl.BlockSpec(memory_space=pltpu.SMEM),
            tile(width),
            tile(width),
            tile(LANES),
            whole(gate_up),
            whole(down),
            whole(router),
        ],
        out_specs=[tile(columns) for columns, _ in shapes],
        compiler_params=pltpu.CompilerParams(vmem_limit_bytes=VMEM_BYTES),
        cost_estimate=pl.CostEstimate(
            flops=12 * count * width * hidden_width,
            bytes_accessed=20 * count * width,
            transcendentals=count * hidden_width,
        ),
        name="expert",
    )(which, rows, slopes, chosen, gate_up, down, router)


def attention_call(kernel, outs, scratch, products, name, meta, *operands):
    vmem = pl.BlockSpec(memory_space=pltpu.VMEM)
    pairs = QUERY_HEADS * operands[0].shape[0] * operands[-1].shape[0]
    return pl.pallas_call(
        kernel,
        out_shape=outs,
        in_specs=[pl.BlockSpec(memory_space=pltpu.SMEM)] + [vmem] * len(operands),
        out_specs=(vmem,) * len(outs),
        scratch_shapes=[pltpu.VMEM(shape, f32) for shape in scratch],
        compiler_params=pltpu.CompilerParams(vmem_limit_bytes=VMEM_BYTES),
        cost_estimate=pl.CostEstimate(
            flops=products * pairs, bytes_accessed=QUERY_WIDTH * 1024, transcendentals=0
        ),
        name=name,
    )(meta, *operands)


def attend(meta, query, key_value):
    stretch = query.shape[0]
    stats = (QUERY_HEADS, stretch)
    outs = (
        jax.ShapeDtypeStruct((stretch, QUERY_WIDTH), f32),
        jax.ShapeDtypeStruct(stats, f32),
    )
    scratch = [stats, stats, (QUERY_WIDTH, stretch)]
    return attention_call(attend_kernel, outs, scratch, 2, "attend", meta, query, key_value)


def attend_back(orders, meta, query, slope, log_total, mixed, key_value):
    stretch, rows = query.shape[0], key_value.shape[0]
    outs = (jax.ShapeDtypeStruct((stretch, QUERY_WIDTH), f32),)
    outs += (jax.ShapeDtypeStruct((2, rows // 2, KEY_WIDTH), bf16),) * 2
    operands = (meta, query, slope, log_total, mixed, key_value)
    scratch = [(QUERY_WIDTH, stretch), (QUERY_HEADS, stretch)]
    kernel = functools.partial(attend_back_kernel, orders)
    return attention_call(kernel, outs, scratch, 5, "attend_back", *operands)


def body(
    tokens,
    cotangent,
    routes,
    fill_order,
    pic_starts,
    attn_gain,
    moe_gain,
    w_query,
    key_projection,
    value_projection,
    w_out,
    w_router,
    expert_gate,
    expert_up,
    expert_down,
):
    sequences, stretch, width = tokens.shape
    count = sequences * stretch
    parts = lax.axis_size("ctx")
    experts = parts
    capacity = (5 * count * TOP + 4 * experts - 1) // (4 * experts)
    query_width, key_width = QUERY_WIDTH, KEY_WIDTH
    hidden_width = expert_gate.shape[2]
    both = ("seq", "ctx")
    seq_bits, ctx_bits = bits("seq"), bits("ctx")
    all_bits = seq_bits + ctx_bits
    outward = ctx_bits[:-1] + seq_bits + ctx_bits[-1:]
    inward = ctx_bits[-1:] + seq_bits[::-1] + ctx_bits[-2::-1]
    sizes = {"seq": parts, "ctx": 1}
    me = lax.axis_index("seq") * parts + lax.axis_index("ctx")

    def padded(columns):
        block = jnp.concatenate(columns, 1)
        return jnp.pad(block, ((0, 0), (0, LANES - block.shape[1])))

    first_set = lax.all_gather(
        jnp.concatenate(
            [w_query, key_projection, value_projection, padded([attn_gain[:, None]])], 1
        ),
        both,
        axis=0,
        tiled=True,
    )
    second_set = gather_blocks(
        jnp.concatenate([w_out, padded([w_router, moe_gain[:, None]])], 1), outward, all_bits
    ).reshape(width, -1)

    own_rows = w_query.shape[0]
    owner = jnp.bitwise_xor(jnp.array(flips(inward, sizes), jnp.int32), me)
    feature = (owner[:, None] * own_rows + jnp.arange(own_rows, dtype=jnp.int32)).reshape(-1)
    turn = (jnp.arange(width, dtype=jnp.int32)[:, None] == feature[None, :]).astype(bf16)

    def relative(rows):
        return matmul(rows, turn).astype(bf16)

    def halves(left, right):
        middle = left.shape[1] // 2
        sent = matmul_tn(left[:, middle:], right).astype(bf16)
        return sent, matmul_tn(left[:, :middle], right).astype(bf16)

    picks = routes.reshape(count, TOP)
    order = fill_order.reshape(count)
    routed = jnp.any(picks[:, :, None] == jnp.arange(experts, dtype=jnp.int32), 1)
    earlier = (order[None, :] < order[:, None]).astype(bf16)
    place = matmul(earlier, routed.astype(bf16)).astype(jnp.int32)
    place = jnp.where(routed, place, capacity)
    half = capacity // 2
    chosen_slot = [
        place.T[:, None, :]
        == (begin + jnp.arange(half, dtype=jnp.int32))[None, :, None]
        for begin in (0, half)
    ]
    slot_map = [chosen.astype(bf16).reshape(-1, count) for chosen in chosen_slot]

    def exchange_rows(rows):
        rows = rows.reshape(experts, half, width)
        rows = lax.all_to_all(rows, "ctx", split_axis=0, concat_axis=0, tiled=True)
        return rows.reshape(-1, width)

    out_slope = cotangent.reshape(count, width)
    slot_routes = jnp.concatenate(
        [matmul(part, routed.astype(bf16)).reshape(experts, half, experts) for part in slot_map], 1
    ).astype(bf16)
    slot_routes = lax.all_to_all(slot_routes, "ctx", split_axis=0, concat_axis=0, tiled=True)
    slot_routes = jnp.pad(slot_routes, ((0, 0), (0, 0), (0, LANES - experts)))
    slot_routes = [
        slot_routes[:, begin : begin + half].reshape(-1, LANES) for begin in (0, half)
    ]
    slope_rows = [matmul(part, out_slope).astype(bf16) for part in slot_map]
    slope_rows = jnp.concatenate([part.reshape(experts, half, width) for part in slope_rows], 1)
    slope_rows = lax.all_to_all(slope_rows, "ctx", split_axis=0, concat_axis=0, tiled=True)
    gate_up = jnp.concatenate([expert_gate[0], expert_up[0]], 1)
    first_set, slot_routes, slope_rows, gate_up = lax.optimization_barrier(
        (first_set, slot_routes, slope_rows, gate_up)
    )
    slope_rows = [
        slope_rows[:, begin : begin + half].reshape(-1, width) for begin in (0, half)
    ]
    weight_qkv = first_set[:, : query_width + 2 * key_width]
    gain_one = first_set[:, query_width + 2 * key_width].astype(f32)
    full_out = second_set[:, :width]
    full_router = second_set[:, width : width + experts]
    gain_two = second_set[:, width + experts].astype(f32)

    positions = lax.axis_index("ctx") * stretch + jnp.arange(stretch, dtype=jnp.int32)
    cosine, sine = rope_tables(positions, HEAD_WIDTH)
    inputs = tokens.astype(f32).reshape(count, width)
    normed = rms_norm(inputs, gain_one).astype(bf16)
    projected = matmul(normed, weight_qkv)
    query_rows = rotate(projected[:, :query_width], QUERY_HEADS, cosine, sine).astype(bf16)
    key_rows = rotate(
        projected[:, query_width : query_width + key_width], KEY_VALUE_HEADS, cosine, sine
    ).astype(bf16)
    value_rows = projected[:, query_width + key_width :].astype(bf16)
    key_values = lax.all_gather(
        jnp.concatenate([key_rows, value_rows], 1), "ctx", axis=0, tiled=True
    )

    meta = jnp.concatenate([lax.axis_index("ctx").astype(jnp.int32)[None], pic_starts[0]])
    mixed_heads, log_total = attend(meta, query_rows, key_values)

    def with_attention(other):
        nonlocal mixed_heads
        mixed_heads, other = lax.optimization_barrier((mixed_heads, other))
        return other

    gate_up = gather_blocks(gate_up, seq_bits[::-1], seq_bits, with_attention)
    gate_up = gate_up.reshape(-1, 2 * hidden_width)
    down = gather_blocks(
        lax.optimization_barrier((expert_down[0], key_values))[0], seq_bits[::-1], seq_bits
    ).reshape(-1, width)
    attended = mixed_heads.astype(bf16)

    middle = inputs + matmul(attended, full_out)
    enter = rms_norm(middle, gain_two).astype(bf16)
    arrived = [exchange_rows(matmul(part, enter).astype(bf16)) for part in slot_map]

    def gates_of(rows, chosen):
        logits = jnp.where(chosen, matmul(rows, full_router), big_negative)
        shares = jnp.exp(logits - jnp.max(logits, -1, keepdims=True))
        shares = jnp.where(chosen, shares, 0.0)
        return shares / jnp.maximum(jnp.sum(shares, -1, keepdims=True), 1e-30)

    gates = gates_of(enter, routed)

    normed_turned, attended_turned, enter_turned = map(relative, (normed, attended, enter))
    arrived[0], normed_turned, attended_turned, enter_turned = lax.optimization_barrier(
        (arrived[0], normed_turned, attended_turned, enter_turned)
    )
    which = lax.axis_index("ctx").astype(jnp.int32)[None]
    router = second_set[:, width:]
    hidden, result, slope_gates, slope_slots, slope_pre, slope_arrived = ([] for _ in range(6))
    for index in range(2):
        made = list(expert(
            which, arrived[index], slope_rows[index], slot_routes[index], gate_up, down, router)
        )
        if index == 0:
            arrived[1], made[-1] = lax.optimization_barrier((arrived[1], made[-1]))
        for kept, item in zip(
            (hidden, result, slope_gates, slope_slots, slope_pre, slope_arrived), made
        ):
            kept.append(item)
    returned_slopes = [exchange_rows(slope_arrived[0])]
    slope_gates = jnp.concatenate([item.reshape(experts, half) for item in slope_gates], 1)
    slope_gates, returned_slopes[0] = lax.optimization_barrier((slope_gates, returned_slopes[0]))
    returned_gates = lax.all_to_all(slope_gates, "ctx", split_axis=0, concat_axis=0, tiled=True)
    slope_arrived[1], returned_gates, slope_pre, slope_slots = lax.optimization_barrier(
        (slope_arrived[1], returned_gates, slope_pre, slope_slots)
    )
    returned_slopes.append(exchange_rows(slope_arrived[1]))
    grad_gate, grad_up = (
        sum(matmul_tn(arrived[i], slope_pre[i][:, columns]) for i in range(2)).astype(bf16)
        for columns in (slice(0, hidden_width), slice(hidden_width, None))
    )
    grad_down = sum(matmul_tn(hidden[i], slope_slots[i]) for i in range(2)).astype(bf16)
    def sector_halves(grads):
        return grads.reshape([2] * len(seq_bits) + [-1, grads.shape[1]])

    def sector_sum(blocks, arrived):
        for axis, bit in seq_bits:
            mine = ((lax.axis_index(axis) & bit) > 0).astype(jnp.int32)
            sent = lax.dynamic_index_in_dim(blocks, 1 - mine, 0, keepdims=False)
            kept = lax.dynamic_index_in_dim(blocks, mine, 0, keepdims=False)
            other = swap(sent.astype(bf16), axis, bit)
            if (axis, bit) == seq_bits[-1]:
                other = arrived(other)
            blocks = kept.astype(f32) + other.astype(f32)
        return blocks

    def with_slopes(other):
        nonlocal grad_gate, grad_up
        returned_slopes[1], other, grad_gate, grad_up = lax.optimization_barrier(
            (returned_slopes[1], other, grad_gate, grad_up)
        )
        return other

    grad_down = sector_sum(sector_halves(grad_down), with_slopes)
    returned = jnp.concatenate([part.reshape(experts, half, width) for part in result], 1)
    returned = lax.all_to_all(returned, "ctx", split_axis=0, concat_axis=0, tiled=True)

    slope_gate = 0.0
    for index, chosen in enumerate(chosen_slot):
        part = returned_gates[:, index * half : (index + 1) * half]
        slope_gate = slope_gate + jnp.sum(jnp.where(chosen, part[:, :, None], 0.0), 1).T
    slope_logits = gates * (slope_gate - jnp.sum(gates * slope_gate, -1, keepdims=True))
    slope_logits = slope_logits.astype(bf16)
    grad_router = matmul_tn(enter_turned, slope_logits)
    slope_enter = matmul_nt(slope_logits, full_router)
    for part, rows in zip(slot_map, returned_slopes):
        slope_enter = slope_enter + matmul_tn(part, rows)

    pull_two = jax.vjp(rms_norm, middle, gain_two)[1]
    slope_middle, grad_gain_two = pull_two(slope_enter)
    slope_middle = out_slope.astype(f32) + slope_middle
    slope_branch = slope_middle.astype(bf16)
    slope_attended = matmul_nt(slope_branch, full_out).astype(bf16)

    out_sum = Sum(*halves(attended_turned, slope_branch), inward)
    orders = (ctx_bits[::-1], ctx_bits[-1:] + ctx_bits[:-1])
    backs = attend_back(
        [[bit for _, bit in order] for order in orders],
        meta,
        query_rows,
        slope_attended,
        log_total,
        mixed_heads,
        key_values,
    )
    slope_q, slope_k, slope_v = backs


    def after_back(other):
        nonlocal slope_q, slope_k, slope_v
        slope_q, slope_k, slope_v, other = lax.optimization_barrier(
            (slope_q, slope_k, slope_v, other)
        )
        return other

    grad_gate = sector_sum(sector_halves(grad_gate), after_back)
    key_sum = Sum(slope_k[1], slope_k[0], orders[0])
    value_sum = Sum(slope_v[1], slope_v[0], orders[1])
    kv_sums = [key_sum, value_sum]
    together(kv_sums)
    slope_query = rotate(slope_q, QUERY_HEADS, cosine, -sine).astype(bf16)
    query_sum = Sum(*halves(normed_turned, slope_query), inward)
    query_sum.step()
    out_sum.step()
    while len(key_sum.stages) > 1:
        together(kv_sums)
    query_sum.step()
    for item in kv_sums:
        item.step()
    totals = [item.total for item in kv_sums]

    def with_totals(other):
        nonlocal totals, returned
        totals, query_sum.sent, out_sum.sent, returned, other = lax.optimization_barrier(
            (totals, query_sum.sent, out_sum.sent, returned, other)
        )
        return other

    grad_up = sector_sum(sector_halves(grad_up), with_totals)
    key_sum.total, value_sum.total = totals
    output = middle
    for chosen, rows in ((jnp.concatenate(chosen_slot, 1), returned.reshape(-1, width)),):
        mix = jnp.where(chosen, gates.T[:, None, :], 0.0).reshape(-1, count)
        mix_high = mix.astype(bf16)
        mix_low = (mix - mix_high.astype(f32)).astype(bf16)
        output = output + matmul_tn(mix_high, rows) + matmul_tn(mix_low, rows)
    output = output.astype(bf16).reshape(tokens.shape)
    slope_key = rotate(key_sum.total, KEY_VALUE_HEADS, cosine, -sine)
    slope_rest = jnp.concatenate([slope_key, value_sum.total], 1).astype(bf16)
    slope_normed = matmul_nt(slope_query, weight_qkv[:, :query_width])
    slope_normed = slope_normed + matmul_nt(slope_rest, weight_qkv[:, query_width:])
    pull_one = jax.vjp(rms_norm, inputs, gain_one)[1]
    slope_inputs, grad_gain_one = pull_one(slope_normed)
    grad_input = (slope_middle + slope_inputs).reshape(tokens.shape)
    gains = relative(jnp.stack([grad_gain_one, grad_gain_two]).astype(bf16)).T
    small = padded([grad_router.astype(bf16), gains])
    rest_sum = Sum(
        *(
            jnp.concatenate([grads, part], 1)
            for grads, part in zip(
                halves(normed_turned, slope_rest), (small[width // 2 :], small[: width // 2])
            )
        ),
        inward,
    )
    while rest_sum.stages:
        together([item for item in (rest_sum, query_sum, out_sum) if item.stages])
    for item in (query_sum, out_sum):
        while item.stages:
            item.step()
    grads_rest = rest_sum.total
    return (
        output,
        grad_input,
        grads_rest[:, 2 * key_width + experts],
        grads_rest[:, 2 * key_width + experts + 1],
        query_sum.total,
        grads_rest[:, :key_width],
        grads_rest[:, key_width : 2 * key_width],
        out_sum.total,
        grads_rest[:, 2 * key_width : 2 * key_width + experts],
        grad_gate[None],
        grad_up[None],
        grad_down[None],
    )


def solution(mesh):
    rows = P("seq", "ctx", None)
    shard = P(("seq", "ctx"), None)
    vector = P(("seq", "ctx"))
    expert = P("ctx", "seq", None)
    return jax.shard_map(
        body,
        mesh=mesh,
        in_specs=(rows, rows, rows, P("seq", "ctx"), P("seq", None), vector, vector)
        + (shard,) * 5
        + (expert,) * 3,
        out_specs=(rows, rows, vector, vector) + (shard,) * 5 + (expert,) * 3,
        check_vma=False,
    )
```

```python
import functools
import math

import jax
import jax.numpy as jnp
from jax import lax
from jax.experimental import pallas as pl
from jax.experimental.pallas import tpu as pltpu
from jax.sharding import PartitionSpec as P

QUERY_HEADS = 12
KEY_VALUE_HEADS = 2
HEAD_WIDTH = 128
TOP = 4
PIC = 256
NPIC = 4
LANES = 128
GROUPS = QUERY_HEADS // KEY_VALUE_HEADS
QUERY_WIDTH = QUERY_HEADS * HEAD_WIDTH
KEY_WIDTH = KEY_VALUE_HEADS * HEAD_WIDTH
SCALE = 1.0 / math.sqrt(HEAD_WIDTH)
EXP2_SCALE = SCALE * math.log2(math.e)
BLOCKS = 2
VMEM_BYTES = 48 << 20

epsilon = 1e-06
rope_base = 10000.0
big_negative = -1e30
bf16 = jnp.bfloat16
f32 = jnp.float32


def matmul(left, right):
    return jnp.dot(left, right, preferred_element_type=f32)


def matmul_nt(left, right):
    return lax.dot_general(left, right, (((1,), (1,)), ((), ())), preferred_element_type=f32)


def matmul_tn(left, right):
    return lax.dot_general(left, right, (((0,), (0,)), ((), ())), preferred_element_type=f32)


def rms_scale(rows):
    return lax.rsqrt(jnp.mean(rows * rows, -1, keepdims=True) + epsilon)


def rms_norm(rows, gain):
    return rows * rms_scale(rows) * gain


def rope_tables(positions, head_size):
    half = head_size // 2
    inverse = rope_base ** (-(jnp.arange(half, dtype=f32) * 2.0 / head_size))
    angles = positions.astype(f32)[:, None] * inverse[None, :]
    return (jnp.cos(angles), jnp.sin(angles))


def rotate(rows, heads, cosine, sine):
    shaped = rows.reshape(rows.shape[0], heads, HEAD_WIDTH)
    half = HEAD_WIDTH // 2
    first, second = shaped[..., :half], shaped[..., half:]
    cosine, sine = cosine[:, None, :], sine[:, None, :]
    turned = jnp.concatenate(
        [first * cosine - second * sine, second * cosine + first * sine], -1
    )
    return turned.reshape(rows.shape)


def bits(axis):
    size = lax.axis_size(axis)
    return [(axis, 1 << place) for place in reversed(range(size.bit_length() - 1))]


def swap(block, axis, bit):
    size = lax.axis_size(axis)
    return lax.ppermute(block, axis, [(index, index ^ bit) for index in range(size)])


def gather_blocks(block, stages, order, arrived=None):
    held = []
    for stage in stages:
        axis, bit = stage
        other = swap(block, axis, bit)
        if arrived is not None and stage == stages[-1]:
            other = arrived(other)
        upper = (lax.axis_index(axis) & bit) > 0
        place = sum(order.index(known) < order.index(stage) for known in held)
        block = jnp.stack(
            [jnp.where(upper, other, block), jnp.where(upper, block, other)], place
        )
        held.append(stage)
    return block


class Sum:
    def __init__(self, sent, kept, stages):
        self.sent, self.kept, self.stages = sent, kept, list(stages)

    def step(self):
        axis, bit = self.stages.pop(0)
        other = swap(self.sent, axis, bit)
        if not self.stages:
            self.total = self.kept.astype(f32) + other.astype(f32)
            return
        half = self.kept.shape[0] // 2
        self.sent = (self.kept[half:].astype(f32) + other[half:].astype(f32)).astype(bf16)
        self.kept = (self.kept[:half].astype(f32) + other[:half].astype(f32)).astype(bf16)


def together(sums, also=()):
    for item in sums:
        item.step()
    live = [item for item in sums if item.stages]
    sent, also = lax.optimization_barrier(([item.sent for item in live], also))
    for item, block in zip(live, sent):
        item.sent = block
    return also


def flips(stages, sizes):
    masks = []
    for block in range(1 << len(stages)):
        mask = 0
        for place, (axis, bit) in enumerate(stages):
            if (block >> (len(stages) - 1 - place)) & 1:
                mask |= bit * sizes[axis]
        masks.append(mask)
    return masks


def visible_keys(meta, step, stretch):
    span = BLOCKS * stretch
    keys = step * span + lax.broadcasted_iota(jnp.int32, (span, 1), 0)
    queries = meta[0] * stretch + lax.broadcasted_iota(jnp.int32, (1, stretch), 1)

    def label(positions):
        found = jnp.zeros(positions.shape, jnp.int32)
        for index in range(NPIC):
            start = meta[1 + index]
            inside = (positions >= start) & (positions < start + PIC)
            found = jnp.where(inside, index + 1, found)
        return found

    query_label = label(queries)
    return (keys <= queries) | ((label(keys) == query_label) & (query_label > 0))


def for_each_step(meta, stretch, steps, process, skip=None):
    span = BLOCKS * stretch
    low, high = meta[0] * stretch, (meta[0] + 1) * stretch

    def turn(step, carry):
        needed = step * span < high + PIC - 1
        edge = (step + 1) * span > low

        @pl.when(needed & edge)
        def _():
            process(step, True)

        @pl.when(needed & jnp.logical_not(edge))
        def _():
            process(step, False)

        if skip is not None:

            @pl.when(jnp.logical_not(needed))
            def _():
                skip(step)

        return carry

    lax.fori_loop(0, steps, turn, 0)


def head_columns(head, start=0):
    return slice(start + head * HEAD_WIDTH, start + (head + 1) * HEAD_WIDTH)


def attend_kernel(meta, query, key_value, out, log_total, peak, total, accum):
    stretch = query.shape[0]
    span = BLOCKS * stretch
    peak[...] = jnp.full(peak.shape, big_negative, f32)
    total[...] = jnp.zeros(total.shape, f32)
    accum[...] = jnp.zeros(accum.shape, f32)

    def process(step, edge):
        rows = pl.ds(pl.multiple_of(step * span, span), span)
        if edge:
            visible = visible_keys(meta, step, stretch)
        keys, values = [], []
        for group in range(KEY_VALUE_HEADS):
            keys.append(key_value[rows, head_columns(group)])
            turned = key_value[rows, head_columns(group, KEY_WIDTH)].T
            values.append(jnp.concatenate([turned, jnp.ones((16, span), bf16)], 0))

        def score(head):
            scores = matmul_nt(keys[head // GROUPS], query[:, head_columns(head)])
            if edge:
                scores = jnp.where(visible, scores, big_negative)
            old = peak[head : head + 1, :]
            return scores, old, jnp.maximum(old, jnp.max(scores, 0, keepdims=True))

        def weigh(head, scores, old, new):
            weights = jnp.exp2((scores - new) * EXP2_SCALE).astype(bf16)
            shrink = jnp.exp2((old - new) * EXP2_SCALE)
            sums = matmul(values[head // GROUPS], weights)
            row, columns = slice(head, head + 1), head_columns(head)
            peak[row, :] = new
            total[row, :] = total[row, :] * shrink + sums[HEAD_WIDTH : HEAD_WIDTH + 1]
            accum[columns, :] = accum[columns, :] * shrink + sums[:HEAD_WIDTH]

        waiting = []
        for head in range(QUERY_HEADS):
            waiting.append((head, *score(head)))
            if len(waiting) > 2:
                weigh(*waiting.pop(0))
        for item in waiting:
            weigh(*item)

    for_each_step(meta, stretch, key_value.shape[0] // span, process)
    for head in range(QUERY_HEADS):
        row, columns = slice(head, head + 1), head_columns(head)
        out[:, columns] = (accum[columns, :] / total[row, :]).T
        log_total[row, :] = peak[row, :] * EXP2_SCALE + jnp.log2(total[row, :])


def attend_back_kernel(
    orders, meta, query, slope, log_total, mixed, key_value, slope_query, *outs_scratch
):
    outs, accum, delta = outs_scratch[:2], outs_scratch[2], outs_scratch[3]
    stretch = query.shape[0]
    span = BLOCKS * stretch
    accum[...] = jnp.zeros(accum.shape, f32)
    for head in range(QUERY_HEADS):
        columns = head_columns(head)
        product = slope[:, columns].astype(f32) * mixed[:, columns]
        delta[head : head + 1, :] = jnp.sum(product.T, 0, keepdims=True)

    def store(step, part, which, columns, block):
        flip = jnp.bitwise_xor(BLOCKS * step + part, meta[0])
        first, *others = orders[which]
        place = 0
        for index, bit in enumerate(others):
            place = place + ((flip // bit) & 1) * (1 << (len(others) - 1 - index))
        place = pl.ds(pl.multiple_of(place * stretch, stretch), stretch)
        outs[which][(flip // first) & 1, place, columns] = block

    def process(step, edge):
        rows = pl.ds(pl.multiple_of(step * span, span), span)
        if edge:
            visible = visible_keys(meta, step, stretch)
        for group in range(KEY_VALUE_HEADS):
            keys = key_value[rows, head_columns(group)]
            values = key_value[rows, head_columns(group, KEY_WIDTH)]
            keys_turned = keys.T
            slope_k = jnp.zeros((span, HEAD_WIDTH), f32)
            slope_v = jnp.zeros((span, HEAD_WIDTH), f32)
            for head in range(group * GROUPS, (group + 1) * GROUPS):
                row, columns = slice(head, head + 1), head_columns(head)
                own_query, own_slope = query[:, columns], slope[:, columns]
                scores = matmul_nt(keys, own_query)
                probs = jnp.exp2(scores * EXP2_SCALE - log_total[row, :])
                if edge:
                    probs = jnp.where(visible, probs, 0.0)
                slope_probs = matmul_nt(values, own_slope)
                slope_scores = (probs * (slope_probs - delta[row, :])).astype(bf16)
                slope_v = slope_v + matmul(probs.astype(bf16), own_slope)
                slope_k = slope_k + matmul(slope_scores, own_query)
                accum[columns, :] = accum[columns, :] + matmul(keys_turned, slope_scores)
            for which, block in enumerate(((slope_k * SCALE).astype(bf16), slope_v.astype(bf16))):
                for part in range(BLOCKS):
                    own = block[part * stretch : (part + 1) * stretch]
                    store(step, part, which, head_columns(group), own)

    def skip(step):
        for which in range(2):
            for part in range(BLOCKS):
                store(step, part, which, slice(None), jnp.zeros((stretch, KEY_WIDTH), bf16))

    for_each_step(meta, stretch, key_value.shape[0] // span, process, skip)
    for head in range(QUERY_HEADS):
        columns = head_columns(head)
        slope_query[:, columns] = (accum[columns, :] * SCALE).T


def expert_kernel(
    which,
    rows,
    slopes,
    chosen,
    gate_up,
    down,
    router,
    hidden_out,
    result_out,
    gates_out,
    slots_out,
    pre_out,
    slope_out,
):
    hidden_width = down.shape[0]
    incoming = rows[...]
    logits = jnp.where(chosen[...] > 0, matmul(incoming, router[...]), big_negative)
    shares = jnp.exp(logits - jnp.max(logits, -1, keepdims=True))
    shares = jnp.where(chosen[...] > 0, shares, 0.0)
    column = lax.broadcasted_iota(jnp.int32, shares.shape, 1)
    own = jnp.sum(jnp.where(column == which[0], shares, 0.0), -1, keepdims=True)
    gates = own / jnp.maximum(jnp.sum(shares, -1, keepdims=True), 1e-30)
    slots = (gates * slopes[...].astype(f32)).astype(bf16)
    slots_out[...] = slots
    pre = matmul(incoming, gate_up[...])
    gate, up = pre[:, :hidden_width], pre[:, hidden_width:]
    root, cubic = math.sqrt(2.0 / math.pi), 0.044715
    square = gate * gate
    bend = jnp.tanh(root * (gate + cubic * gate * square))
    gelu = 0.5 * gate * (1.0 + bend)
    rise = 0.5 * (1.0 + bend) + 0.5 * gate * (1.0 - bend * bend) * root * (
        1.0 + 3.0 * cubic * square
    )
    hidden = (gelu * up).astype(bf16)
    hidden_out[...] = hidden
    result = matmul(hidden, down[...]).astype(bf16)
    result_out[...] = result
    gates_out[...] = jnp.sum(slopes[...].astype(f32) * result.astype(f32), -1, keepdims=True)
    slope_hidden = matmul_nt(slots, down[...])
    slope_pre = jnp.concatenate([slope_hidden * up * rise, slope_hidden * gelu], 1).astype(bf16)
    pre_out[...] = slope_pre
    slope_out[...] = matmul_nt(slope_pre, gate_up[...]).astype(bf16)


def expert(which, rows, slopes, chosen, gate_up, down, router):
    count, width = rows.shape
    hidden_width = down.shape[0]
    block = count // 2

    def tile(columns):
        return pl.BlockSpec((block, columns), lambda step: (step, 0))

    def whole(array):
        return pl.BlockSpec(array.shape, lambda step: (0, 0))

    shapes = [(hidden_width, bf16), (width, bf16), (1, f32), (width, bf16)]
    shapes += [(2 * hidden_width, bf16), (width, bf16)]
    return pl.pallas_call(
        expert_kernel,
        grid=(2,),
        out_shape=[jax.ShapeDtypeStruct((count, columns), kind) for columns, kind in shapes],
        in_specs=[
            pl.BlockSpec(memory_space=pltpu.SMEM),
            tile(width),
            tile(width),
            tile(LANES),
            whole(gate_up),
            whole(down),
            whole(router),
        ],
        out_specs=[tile(columns) for columns, _ in shapes],
        compiler_params=pltpu.CompilerParams(vmem_limit_bytes=VMEM_BYTES),
        cost_estimate=pl.CostEstimate(
            flops=12 * count * width * hidden_width,
            bytes_accessed=20 * count * width,
            transcendentals=count * hidden_width,
        ),
        name="expert",
    )(which, rows, slopes, chosen, gate_up, down, router)


def attention_call(kernel, outs, scratch, products, name, meta, *operands):
    vmem = pl.BlockSpec(memory_space=pltpu.VMEM)
    pairs = QUERY_HEADS * operands[0].shape[0] * operands[-1].shape[0]
    return pl.pallas_call(
        kernel,
        out_shape=outs,
        in_specs=[pl.BlockSpec(memory_space=pltpu.SMEM)] + [vmem] * len(operands),
        out_specs=(vmem,) * len(outs),
        scratch_shapes=[pltpu.VMEM(shape, f32) for shape in scratch],
        compiler_params=pltpu.CompilerParams(vmem_limit_bytes=VMEM_BYTES),
        cost_estimate=pl.CostEstimate(
            flops=products * pairs, bytes_accessed=QUERY_WIDTH * 1024, transcendentals=0
        ),
        name=name,
    )(meta, *operands)


def attend(meta, query, key_value):
    stretch = query.shape[0]
    stats = (QUERY_HEADS, stretch)
    outs = (
        jax.ShapeDtypeStruct((stretch, QUERY_WIDTH), f32),
        jax.ShapeDtypeStruct(stats, f32),
    )
    scratch = [stats, stats, (QUERY_WIDTH, stretch)]
    return attention_call(attend_kernel, outs, scratch, 2, "attend", meta, query, key_value)


def attend_back(orders, meta, query, slope, log_total, mixed, key_value):
    stretch, rows = query.shape[0], key_value.shape[0]
    outs = (jax.ShapeDtypeStruct((stretch, QUERY_WIDTH), f32),)
    outs += (jax.ShapeDtypeStruct((2, rows // 2, KEY_WIDTH), bf16),) * 2
    operands = (meta, query, slope, log_total, mixed, key_value)
    scratch = [(QUERY_WIDTH, stretch), (QUERY_HEADS, stretch)]
    kernel = functools.partial(attend_back_kernel, orders)
    return attention_call(kernel, outs, scratch, 5, "attend_back", *operands)


def body(
    tokens,
    cotangent,
    routes,
    fill_order,
    pic_starts,
    attn_gain,
    moe_gain,
    w_query,
    key_projection,
    value_projection,
    w_out,
    w_router,
    expert_gate,
    expert_up,
    expert_down,
):
    sequences, stretch, width = tokens.shape
    count = sequences * stretch
    parts = lax.axis_size("ctx")
    experts = parts
    capacity = (5 * count * TOP + 4 * experts - 1) // (4 * experts)
    query_width, key_width = QUERY_WIDTH, KEY_WIDTH
    hidden_width = expert_gate.shape[2]
    seq_bits, ctx_bits = bits("seq"), bits("ctx")
    all_bits = seq_bits + ctx_bits
    inward = ctx_bits[-1:] + seq_bits[::-1] + ctx_bits[-2::-1]
    sizes = {"seq": parts, "ctx": 1}
    me = lax.axis_index("seq") * parts + lax.axis_index("ctx")

    def padded(columns):
        block = jnp.concatenate(columns, 1)
        return jnp.pad(block, ((0, 0), (0, LANES - block.shape[1])))

    own_rows = w_query.shape[0]
    owner = jnp.bitwise_xor(jnp.array(flips(inward, sizes), jnp.int32), me)
    feature = (owner[:, None] * own_rows + jnp.arange(own_rows, dtype=jnp.int32)).reshape(-1)
    turn = (jnp.arange(width, dtype=jnp.int32)[:, None] == feature[None, :]).astype(bf16)

    def relative(rows):
        return matmul(rows, turn).astype(bf16)

    def halves(left, right):
        middle = left.shape[1] // 2
        sent = matmul_tn(left[:, middle:], right).astype(bf16)
        return sent, matmul_tn(left[:, :middle], right).astype(bf16)

    picks = routes.reshape(count, TOP)
    order = fill_order.reshape(count)
    routed = jnp.any(picks[:, :, None] == jnp.arange(experts, dtype=jnp.int32), 1)
    earlier = (order[None, :] < order[:, None]).astype(bf16)
    place = matmul(earlier, routed.astype(bf16)).astype(jnp.int32)
    place = jnp.where(routed, place, capacity)
    half = capacity // 2
    chosen_slot = [
        place.T[:, None, :]
        == (begin + jnp.arange(half, dtype=jnp.int32))[None, :, None]
        for begin in (0, half)
    ]
    slot_map = [chosen.astype(bf16).reshape(-1, count) for chosen in chosen_slot]

    def exchange_rows(rows):
        rows = rows.reshape(experts, half, width)
        rows = lax.all_to_all(rows, "ctx", split_axis=0, concat_axis=0, tiled=True)
        return rows.reshape(-1, width)

    out_slope = cotangent.reshape(count, width)
    slot_routes = jnp.concatenate(
        [matmul(part, routed.astype(bf16)).reshape(experts, half, experts) for part in slot_map], 1
    ).astype(bf16)
    slot_routes = lax.all_to_all(slot_routes, "ctx", split_axis=0, concat_axis=0, tiled=True)
    slot_routes = jnp.pad(slot_routes, ((0, 0), (0, 0), (0, LANES - experts)))
    slot_routes = [
        slot_routes[:, begin : begin + half].reshape(-1, LANES) for begin in (0, half)
    ]
    slope_rows = [matmul(part, out_slope).astype(bf16) for part in slot_map]
    slope_rows = jnp.concatenate([part.reshape(experts, half, width) for part in slope_rows], 1)

    block = jnp.concatenate(
        [
            w_query,
            key_projection,
            value_projection,
            padded([attn_gain[:, None]]),
            w_out,
            padded([w_router, moe_gain[:, None]]),
        ],
        1,
    )
    first_width = query_width + 2 * key_width + LANES
    expert_parts = [expert_gate[0], expert_up[0]]
    turns = inward[::-1]
    for index, stage in enumerate(turns):
        other = swap(block if index < 2 else mine, *stage)
        if index in (1, 2) and len(seq_bits) == 1:
            part = index - 1
            other, expert_parts[part] = lax.optimization_barrier(
                (other, (expert_parts[part], swap(expert_parts[part], *seq_bits[0])))
            )
        if index < 2:
            block = jnp.concatenate([block, other], 0)
        if index == 1:
            block, slope_rows = lax.optimization_barrier((block, slope_rows))
            slope_rows = lax.all_to_all(slope_rows, "ctx", split_axis=0, concat_axis=0, tiled=True)
            mine, second_set = block[:, :first_width], block[:, first_width:]
        if index > 2:
            arrived = swap(second_set, *turns[index - 1])
            if index < len(turns) - 1:
                other, arrived = lax.optimization_barrier((other, arrived))
            second_set = jnp.concatenate([second_set, arrived], 0)
        if 2 <= index < len(turns) - 1:
            mine = jnp.concatenate([mine, other], 0)
    mine, other, slope_rows, slot_routes = lax.optimization_barrier(
        (mine, other, slope_rows, slot_routes)
    )
    slope_rows = [
        slope_rows[:, begin : begin + half].reshape(-1, width) for begin in (0, half)
    ]
    qkv_width = query_width + 2 * key_width
    weight_low, weight_high = mine[:, :qkv_width], other[:, :qkv_width]
    gain_one = jnp.concatenate([mine[:, qkv_width], other[:, qkv_width]]).astype(f32)

    def whole_expert(part):
        if isinstance(part, tuple):
            own, other = part
            upper = lax.axis_index("seq") > 0
            pair = [jnp.where(upper, other, own), jnp.where(upper, own, other)]
            return jnp.concatenate(pair, 0)
        return gather_blocks(part, seq_bits[::-1], seq_bits).reshape(-1, part.shape[1])

    gate_up = jnp.concatenate([whole_expert(part) for part in expert_parts], 1)
    second_set = jnp.concatenate([second_set, swap(second_set, *turns[-1])], 0)
    second_set = matmul(turn, second_set).astype(bf16)
    full_out = second_set[:, :width]
    full_router = second_set[:, width : width + experts]
    gain_two = second_set[:, width + experts].astype(f32)

    positions = lax.axis_index("ctx") * stretch + jnp.arange(stretch, dtype=jnp.int32)
    cosine, sine = rope_tables(positions, HEAD_WIDTH)
    inputs = tokens.reshape(count, width)
    inputs_turned = relative(inputs).astype(f32)
    inputs = inputs.astype(f32)
    normed_turned = (inputs_turned * rms_scale(inputs) * gain_one).astype(bf16)
    projected = matmul(normed_turned[:, : width // 2], weight_low)
    projected = projected + matmul(normed_turned[:, width // 2 :], weight_high)
    query_rows = rotate(projected[:, :query_width], QUERY_HEADS, cosine, sine).astype(bf16)
    key_rows = rotate(
        projected[:, query_width : query_width + key_width], KEY_VALUE_HEADS, cosine, sine
    ).astype(bf16)
    value_rows = projected[:, query_width + key_width :].astype(bf16)
    key_values = lax.all_gather(
        jnp.concatenate([key_rows, value_rows], 1), "ctx", axis=0, tiled=True
    )

    meta = jnp.concatenate([lax.axis_index("ctx").astype(jnp.int32)[None], pic_starts[0]])
    mixed_heads, log_total = attend(meta, query_rows, key_values)

    def with_attention(other):
        nonlocal mixed_heads
        mixed_heads, other = lax.optimization_barrier((mixed_heads, other))
        return other

    down = gather_blocks(
        lax.optimization_barrier((expert_down[0], gain_one))[0],
        seq_bits[::-1],
        seq_bits,
        with_attention,
    ).reshape(-1, width)
    attended = mixed_heads.astype(bf16)

    middle = inputs + matmul(attended, full_out)
    enter = rms_norm(middle, gain_two).astype(bf16)
    arrived = [exchange_rows(matmul(part, enter).astype(bf16)) for part in slot_map]

    def gates_of(rows, chosen):
        logits = jnp.where(chosen, matmul(rows, full_router), big_negative)
        shares = jnp.exp(logits - jnp.max(logits, -1, keepdims=True))
        shares = jnp.where(chosen, shares, 0.0)
        return shares / jnp.maximum(jnp.sum(shares, -1, keepdims=True), 1e-30)

    gates = gates_of(enter, routed)

    attended_turned, enter_turned = map(relative, (attended, enter))
    arrived[0], attended_turned, enter_turned = lax.optimization_barrier(
        (arrived[0], attended_turned, enter_turned)
    )
    which = lax.axis_index("ctx").astype(jnp.int32)[None]
    router = second_set[:, width:]
    hidden, result, slope_gates, slope_slots, slope_pre, slope_arrived = ([] for _ in range(6))
    for index in range(2):
        made = list(expert(
            which, arrived[index], slope_rows[index], slot_routes[index], gate_up, down, router)
        )
        if index == 0:
            arrived[1], made[-1] = lax.optimization_barrier((arrived[1], made[-1]))
        for kept, item in zip(
            (hidden, result, slope_gates, slope_slots, slope_pre, slope_arrived), made
        ):
            kept.append(item)
    returned_slopes = [exchange_rows(slope_arrived[0])]
    slope_gates = jnp.concatenate([item.reshape(experts, half) for item in slope_gates], 1)
    slope_gates, returned_slopes[0] = lax.optimization_barrier((slope_gates, returned_slopes[0]))
    returned_gates = lax.all_to_all(slope_gates, "ctx", split_axis=0, concat_axis=0, tiled=True)
    slope_arrived[1], returned_gates, slope_pre, slope_slots = lax.optimization_barrier(
        (slope_arrived[1], returned_gates, slope_pre, slope_slots)
    )
    returned_slopes.append(exchange_rows(slope_arrived[1]))
    grad_gate, grad_up = (
        sum(matmul_tn(arrived[i], slope_pre[i][:, columns]) for i in range(2)).astype(bf16)
        for columns in (slice(0, hidden_width), slice(hidden_width, None))
    )
    grad_down = sum(matmul_tn(hidden[i], slope_slots[i]) for i in range(2)).astype(bf16)
    def sector_halves(grads):
        return grads.reshape([2] * len(seq_bits) + [-1, grads.shape[1]])

    def sector_sum(blocks, arrived):
        for axis, bit in seq_bits:
            mine = ((lax.axis_index(axis) & bit) > 0).astype(jnp.int32)
            sent = lax.dynamic_index_in_dim(blocks, 1 - mine, 0, keepdims=False)
            kept = lax.dynamic_index_in_dim(blocks, mine, 0, keepdims=False)
            other = swap(sent.astype(bf16), axis, bit)
            if (axis, bit) == seq_bits[-1]:
                other = arrived(other)
            blocks = kept.astype(f32) + other.astype(f32)
        return blocks

    def with_slopes(other):
        nonlocal grad_gate, grad_up
        returned_slopes[1], other, grad_gate, grad_up = lax.optimization_barrier(
            (returned_slopes[1], other, grad_gate, grad_up)
        )
        return other

    grad_down = sector_sum(sector_halves(grad_down), with_slopes)
    returned = jnp.concatenate([part.reshape(experts, half, width) for part in result], 1)
    returned = lax.all_to_all(returned, "ctx", split_axis=0, concat_axis=0, tiled=True)

    slope_gate = 0.0
    for index, chosen in enumerate(chosen_slot):
        part = returned_gates[:, index * half : (index + 1) * half]
        slope_gate = slope_gate + jnp.sum(jnp.where(chosen, part[:, :, None], 0.0), 1).T
    slope_logits = gates * (slope_gate - jnp.sum(gates * slope_gate, -1, keepdims=True))
    slope_logits = slope_logits.astype(bf16)
    grad_router = matmul_tn(enter_turned, slope_logits)
    slope_enter = matmul_nt(slope_logits, full_router)
    for part, rows in zip(slot_map, returned_slopes):
        slope_enter = slope_enter + matmul_tn(part, rows)

    pull_two = jax.vjp(rms_norm, middle, gain_two)[1]
    slope_middle, grad_gain_two = pull_two(slope_enter)
    slope_middle = out_slope.astype(f32) + slope_middle
    slope_branch = slope_middle.astype(bf16)
    slope_attended = matmul_nt(slope_branch, full_out).astype(bf16)

    out_sum = Sum(*halves(attended_turned, slope_branch), inward)
    orders = (ctx_bits[::-1], ctx_bits[-1:] + ctx_bits[:-1])
    backs = attend_back(
        [[bit for _, bit in order] for order in orders],
        meta,
        query_rows,
        slope_attended,
        log_total,
        mixed_heads,
        key_values,
    )
    slope_q, slope_k, slope_v = backs


    def after_back(other):
        nonlocal slope_q, slope_k, slope_v
        slope_q, slope_k, slope_v, other = lax.optimization_barrier(
            (slope_q, slope_k, slope_v, other)
        )
        return other

    grad_gate = sector_sum(sector_halves(grad_gate), after_back)
    key_sum = Sum(slope_k[1], slope_k[0], orders[0])
    value_sum = Sum(slope_v[1], slope_v[0], orders[1])
    kv_sums = [key_sum, value_sum]
    slope_query = rotate(slope_q, QUERY_HEADS, cosine, -sine).astype(bf16)
    query_sum = Sum(*halves(normed_turned, slope_query), inward)
    out_sum.step()
    while len(key_sum.stages) > 1:
        together(kv_sums + [query_sum])
    query_sum.step()
    for item in kv_sums:
        item.step()
    totals = [item.total for item in kv_sums]

    def with_totals(other):
        nonlocal totals, returned
        totals, query_sum.sent, out_sum.sent, returned, other = lax.optimization_barrier(
            (totals, query_sum.sent, out_sum.sent, returned, other)
        )
        return other

    grad_up = sector_sum(sector_halves(grad_up), with_totals)
    key_sum.total, value_sum.total = totals
    output = middle
    for chosen, rows in ((jnp.concatenate(chosen_slot, 1), returned.reshape(-1, width)),):
        mix = jnp.where(chosen, gates.T[:, None, :], 0.0).reshape(-1, count)
        mix_high = mix.astype(bf16)
        mix_low = (mix - mix_high.astype(f32)).astype(bf16)
        output = output + matmul_tn(mix_high, rows) + matmul_tn(mix_low, rows)
    output = output.astype(bf16).reshape(tokens.shape)
    slope_key = rotate(key_sum.total, KEY_VALUE_HEADS, cosine, -sine)
    slope_rest = jnp.concatenate([slope_key, value_sum.total], 1).astype(bf16)
    slope_normed = jnp.concatenate(
        [
            matmul_nt(slope_query, part[:, :query_width])
            + matmul_nt(slope_rest, part[:, query_width:])
            for part in (weight_low, weight_high)
        ],
        1,
    )
    pull_one = jax.vjp(rms_norm, inputs_turned, gain_one)[1]
    slope_inputs, grad_gain_one = pull_one(slope_normed)
    slope_high = slope_inputs.astype(bf16)
    slope_low = (slope_inputs - slope_high.astype(f32)).astype(bf16)
    grad_input = slope_middle + matmul_nt(slope_high, turn) + matmul_nt(slope_low, turn)
    grad_input = grad_input.reshape(tokens.shape)
    gains = jnp.stack(
        [grad_gain_one.astype(bf16), relative(grad_gain_two.astype(bf16)[None])[0]], 1
    )
    small = padded([grad_router.astype(bf16), gains])
    rest_sum = Sum(
        *(
            jnp.concatenate([grads, part], 1)
            for grads, part in zip(
                halves(normed_turned, slope_rest), (small[width // 2 :], small[: width // 2])
            )
        ),
        inward,
    )
    while rest_sum.stages:
        together([item for item in (rest_sum, query_sum, out_sum) if item.stages])
    for item in (query_sum, out_sum):
        while item.stages:
            item.step()
    grads_rest = rest_sum.total
    return (
        output,
        grad_input,
        grads_rest[:, 2 * key_width + experts],
        grads_rest[:, 2 * key_width + experts + 1],
        query_sum.total,
        grads_rest[:, :key_width],
        grads_rest[:, key_width : 2 * key_width],
        out_sum.total,
        grads_rest[:, 2 * key_width : 2 * key_width + experts],
        grad_gate[None],
        grad_up[None],
        grad_down[None],
    )


def solution(mesh):
    rows = P("seq", "ctx", None)
    shard = P(("seq", "ctx"), None)
    vector = P(("seq", "ctx"))
    expert = P("ctx", "seq", None)
    return jax.shard_map(
        body,
        mesh=mesh,
        in_specs=(rows, rows, rows, P("seq", "ctx"), P("seq", None), vector, vector)
        + (shard,) * 5
        + (expert,) * 3,
        out_specs=(rows, rows, vector, vector) + (shard,) * 5 + (expert,) * 3,
        check_vma=False,
    )
```

```python
import functools
import math

import jax
import jax.numpy as jnp
from jax import lax
from jax.experimental import pallas as pl
from jax.experimental.pallas import tpu as pltpu
from jax.sharding import PartitionSpec as P

QUERY_HEADS = 12
KEY_VALUE_HEADS = 2
HEAD_WIDTH = 128
TOP = 4
PIC = 256
NPIC = 4
LANES = 128
GROUPS = QUERY_HEADS // KEY_VALUE_HEADS
QUERY_WIDTH = QUERY_HEADS * HEAD_WIDTH
KEY_WIDTH = KEY_VALUE_HEADS * HEAD_WIDTH
SCALE = 1.0 / math.sqrt(HEAD_WIDTH)
EXP2_SCALE = SCALE * math.log2(math.e)
BLOCKS = 2
VMEM_BYTES = 48 << 20

epsilon = 1e-06
rope_base = 10000.0
big_negative = -1e30
bf16 = jnp.bfloat16
f32 = jnp.float32


def matmul(left, right):
    return jnp.dot(left, right, preferred_element_type=f32)


def matmul_nt(left, right):
    return lax.dot_general(left, right, (((1,), (1,)), ((), ())), preferred_element_type=f32)


def matmul_tn(left, right):
    return lax.dot_general(left, right, (((0,), (0,)), ((), ())), preferred_element_type=f32)


def rms_scale(rows):
    return lax.rsqrt(jnp.mean(rows * rows, -1, keepdims=True) + epsilon)


def rms_norm(rows, gain):
    return rows * rms_scale(rows) * gain


def rope_tables(positions, head_size):
    half = head_size // 2
    inverse = rope_base ** (-(jnp.arange(half, dtype=f32) * 2.0 / head_size))
    angles = positions.astype(f32)[:, None] * inverse[None, :]
    return (jnp.cos(angles), jnp.sin(angles))


def rotate(rows, heads, cosine, sine):
    shaped = rows.reshape(rows.shape[0], heads, HEAD_WIDTH)
    half = HEAD_WIDTH // 2
    first, second = shaped[..., :half], shaped[..., half:]
    cosine, sine = cosine[:, None, :], sine[:, None, :]
    turned = jnp.concatenate(
        [first * cosine - second * sine, second * cosine + first * sine], -1
    )
    return turned.reshape(rows.shape)


def bits(axis):
    size = lax.axis_size(axis)
    return [(axis, 1 << place) for place in reversed(range(size.bit_length() - 1))]


def swap(block, axis, bit):
    size = lax.axis_size(axis)
    return lax.ppermute(block, axis, [(index, index ^ bit) for index in range(size)])


def gather_blocks(block, stages, order, arrived=None):
    held = []
    for stage in stages:
        axis, bit = stage
        other = swap(block, axis, bit)
        if arrived is not None and stage == stages[-1]:
            other = arrived(other)
        upper = (lax.axis_index(axis) & bit) > 0
        place = sum(order.index(known) < order.index(stage) for known in held)
        block = jnp.stack(
            [jnp.where(upper, other, block), jnp.where(upper, block, other)], place
        )
        held.append(stage)
    return block


class Sum:
    def __init__(self, sent, kept, stages):
        self.sent, self.kept, self.stages = sent, kept, list(stages)

    def step(self):
        axis, bit = self.stages.pop(0)
        other = swap(self.sent, axis, bit)
        if not self.stages:
            self.total = self.kept.astype(f32) + other.astype(f32)
            return
        half = self.kept.shape[0] // 2
        self.sent = (self.kept[half:].astype(f32) + other[half:].astype(f32)).astype(bf16)
        self.kept = (self.kept[:half].astype(f32) + other[:half].astype(f32)).astype(bf16)


def together(sums, also=()):
    for item in sums:
        item.step()
    live = [item for item in sums if item.stages]
    sent, also = lax.optimization_barrier(([item.sent for item in live], also))
    for item, block in zip(live, sent):
        item.sent = block
    return also


def flips(stages, sizes):
    masks = []
    for block in range(1 << len(stages)):
        mask = 0
        for place, (axis, bit) in enumerate(stages):
            if (block >> (len(stages) - 1 - place)) & 1:
                mask |= bit * sizes[axis]
        masks.append(mask)
    return masks


def visible_keys(meta, step, stretch):
    span = BLOCKS * stretch
    keys = step * span + lax.broadcasted_iota(jnp.int32, (span, 1), 0)
    queries = meta[0] * stretch + lax.broadcasted_iota(jnp.int32, (1, stretch), 1)

    def label(positions):
        found = jnp.zeros(positions.shape, jnp.int32)
        for index in range(NPIC):
            start = meta[1 + index]
            inside = (positions >= start) & (positions < start + PIC)
            found = jnp.where(inside, index + 1, found)
        return found

    query_label = label(queries)
    return (keys <= queries) | ((label(keys) == query_label) & (query_label > 0))


def for_each_step(meta, stretch, steps, process, skip=None):
    span = BLOCKS * stretch
    low, high = meta[0] * stretch, (meta[0] + 1) * stretch

    def turn(step, carry):
        needed = step * span < high + PIC - 1
        edge = (step + 1) * span > low

        @pl.when(needed & edge)
        def _():
            process(step, True)

        @pl.when(needed & jnp.logical_not(edge))
        def _():
            process(step, False)

        if skip is not None:

            @pl.when(jnp.logical_not(needed))
            def _():
                skip(step)

        return carry

    lax.fori_loop(0, steps, turn, 0)


def head_columns(head, start=0):
    return slice(start + head * HEAD_WIDTH, start + (head + 1) * HEAD_WIDTH)


def attend_kernel(meta, query, key_value, out, log_total, peak, total, accum):
    stretch = query.shape[0]
    span = BLOCKS * stretch
    peak[...] = jnp.full(peak.shape, big_negative, f32)
    total[...] = jnp.zeros(total.shape, f32)
    accum[...] = jnp.zeros(accum.shape, f32)

    def process(step, edge):
        rows = pl.ds(pl.multiple_of(step * span, span), span)
        if edge:
            visible = visible_keys(meta, step, stretch)
        keys, values = [], []
        for group in range(KEY_VALUE_HEADS):
            keys.append(key_value[rows, head_columns(group)])
            turned = key_value[rows, head_columns(group, KEY_WIDTH)].T
            values.append(jnp.concatenate([turned, jnp.ones((16, span), bf16)], 0))

        def score(head):
            scores = matmul_nt(keys[head // GROUPS], query[:, head_columns(head)])
            if edge:
                scores = jnp.where(visible, scores, big_negative)
            old = peak[head : head + 1, :]
            return scores, old, jnp.maximum(old, jnp.max(scores, 0, keepdims=True))

        def weigh(head, scores, old, new):
            weights = jnp.exp2((scores - new) * EXP2_SCALE).astype(bf16)
            shrink = jnp.exp2((old - new) * EXP2_SCALE)
            sums = matmul(values[head // GROUPS], weights)
            row, columns = slice(head, head + 1), head_columns(head)
            peak[row, :] = new
            total[row, :] = total[row, :] * shrink + sums[HEAD_WIDTH : HEAD_WIDTH + 1]
            accum[columns, :] = accum[columns, :] * shrink + sums[:HEAD_WIDTH]

        waiting = []
        for head in range(QUERY_HEADS):
            waiting.append((head, *score(head)))
            if len(waiting) > 2:
                weigh(*waiting.pop(0))
        for item in waiting:
            weigh(*item)

    for_each_step(meta, stretch, key_value.shape[0] // span, process)
    for head in range(QUERY_HEADS):
        row, columns = slice(head, head + 1), head_columns(head)
        out[:, columns] = (accum[columns, :] / total[row, :]).T
        log_total[row, :] = peak[row, :] * EXP2_SCALE + jnp.log2(total[row, :])


def attend_back_kernel(
    order, meta, query, slope, log_total, mixed, key_value, slope_query, *outs_scratch
):
    out, accum, delta = outs_scratch
    stretch = query.shape[0]
    span = BLOCKS * stretch
    accum[...] = jnp.zeros(accum.shape, f32)
    for head in range(QUERY_HEADS):
        columns = head_columns(head)
        product = slope[:, columns].astype(f32) * mixed[:, columns]
        delta[head : head + 1, :] = jnp.sum(product.T, 0, keepdims=True)

    def store(step, part, columns, block):
        flip = jnp.bitwise_xor(BLOCKS * step + part, meta[0])
        first, *others = order
        place = 0
        for index, bit in enumerate(others):
            place = place + ((flip // bit) & 1) * (1 << (len(others) - 1 - index))
        place = pl.ds(pl.multiple_of(place * stretch, stretch), stretch)
        out[(flip // first) & 1, place, columns] = block

    def process(step, edge):
        rows = pl.ds(pl.multiple_of(step * span, span), span)
        if edge:
            visible = visible_keys(meta, step, stretch)
        for group in range(KEY_VALUE_HEADS):
            keys = key_value[rows, head_columns(group)]
            values = key_value[rows, head_columns(group, KEY_WIDTH)]
            keys_turned = keys.T
            slope_k = jnp.zeros((span, HEAD_WIDTH), f32)
            slope_v = jnp.zeros((span, HEAD_WIDTH), f32)
            for head in range(group * GROUPS, (group + 1) * GROUPS):
                row, columns = slice(head, head + 1), head_columns(head)
                own_query, own_slope = query[:, columns], slope[:, columns]
                scores = matmul_nt(keys, own_query)
                probs = jnp.exp2(scores * EXP2_SCALE - log_total[row, :])
                if edge:
                    probs = jnp.where(visible, probs, 0.0)
                slope_probs = matmul_nt(values, own_slope)
                slope_scores = (probs * (slope_probs - delta[row, :])).astype(bf16)
                slope_v = slope_v + matmul(probs.astype(bf16), own_slope)
                slope_k = slope_k + matmul(slope_scores, own_query)
                accum[columns, :] = accum[columns, :] + matmul(keys_turned, slope_scores)
            for which, block in enumerate(((slope_k * SCALE).astype(bf16), slope_v.astype(bf16))):
                for part in range(BLOCKS):
                    own = block[part * stretch : (part + 1) * stretch]
                    store(step, part, head_columns(group, which * KEY_WIDTH), own)

    def skip(step):
        for part in range(BLOCKS):
            store(step, part, slice(None), jnp.zeros((stretch, 2 * KEY_WIDTH), bf16))

    for_each_step(meta, stretch, key_value.shape[0] // span, process, skip)
    for head in range(QUERY_HEADS):
        columns = head_columns(head)
        slope_query[:, columns] = (accum[columns, :] * SCALE).T


def expert_kernel(
    which,
    rows,
    slopes,
    chosen,
    gate_up,
    down,
    router,
    hidden_out,
    result_out,
    gates_out,
    slots_out,
    pre_out,
    slope_out,
):
    hidden_width = down.shape[0]
    incoming = rows[...]
    logits = jnp.where(chosen[...] > 0, matmul(incoming, router[...]), big_negative)
    shares = jnp.exp(logits - jnp.max(logits, -1, keepdims=True))
    shares = jnp.where(chosen[...] > 0, shares, 0.0)
    column = lax.broadcasted_iota(jnp.int32, shares.shape, 1)
    own = jnp.sum(jnp.where(column == which[0], shares, 0.0), -1, keepdims=True)
    gates = own / jnp.maximum(jnp.sum(shares, -1, keepdims=True), 1e-30)
    slots = (gates * slopes[...].astype(f32)).astype(bf16)
    slots_out[...] = slots
    pre = matmul(incoming, gate_up[...])
    gate, up = pre[:, :hidden_width], pre[:, hidden_width:]
    root, cubic = math.sqrt(2.0 / math.pi), 0.044715
    square = gate * gate
    bend = jnp.tanh(root * (gate + cubic * gate * square))
    gelu = 0.5 * gate * (1.0 + bend)
    rise = 0.5 * (1.0 + bend) + 0.5 * gate * (1.0 - bend * bend) * root * (
        1.0 + 3.0 * cubic * square
    )
    hidden = (gelu * up).astype(bf16)
    hidden_out[...] = hidden
    result = matmul(hidden, down[...]).astype(bf16)
    result_out[...] = result
    gates_out[...] = jnp.sum(slopes[...].astype(f32) * result.astype(f32), -1, keepdims=True)
    slope_hidden = matmul_nt(slots, down[...])
    slope_pre = jnp.concatenate([slope_hidden * up * rise, slope_hidden * gelu], 1).astype(bf16)
    pre_out[...] = slope_pre
    slope_out[...] = matmul_nt(slope_pre, gate_up[...]).astype(bf16)


def expert(which, rows, slopes, chosen, gate_up, down, router):
    count, width = rows.shape
    hidden_width = down.shape[0]
    block = count // 2

    def tile(columns):
        return pl.BlockSpec((block, columns), lambda step: (step, 0))

    def whole(array):
        return pl.BlockSpec(array.shape, lambda step: (0, 0))

    shapes = [(hidden_width, bf16), (width, bf16), (1, f32), (width, bf16)]
    shapes += [(2 * hidden_width, bf16), (width, bf16)]
    return pl.pallas_call(
        expert_kernel,
        grid=(2,),
        out_shape=[jax.ShapeDtypeStruct((count, columns), kind) for columns, kind in shapes],
        in_specs=[
            pl.BlockSpec(memory_space=pltpu.SMEM),
            tile(width),
            tile(width),
            tile(LANES),
            whole(gate_up),
            whole(down),
            whole(router),
        ],
        out_specs=[tile(columns) for columns, _ in shapes],
        compiler_params=pltpu.CompilerParams(vmem_limit_bytes=VMEM_BYTES),
        cost_estimate=pl.CostEstimate(
            flops=12 * count * width * hidden_width,
            bytes_accessed=20 * count * width,
            transcendentals=count * hidden_width,
        ),
        name="expert",
    )(which, rows, slopes, chosen, gate_up, down, router)


def attention_call(kernel, outs, scratch, products, name, meta, *operands):
    vmem = pl.BlockSpec(memory_space=pltpu.VMEM)
    pairs = QUERY_HEADS * operands[0].shape[0] * operands[-1].shape[0]
    return pl.pallas_call(
        kernel,
        out_shape=outs,
        in_specs=[pl.BlockSpec(memory_space=pltpu.SMEM)] + [vmem] * len(operands),
        out_specs=(vmem,) * len(outs),
        scratch_shapes=[pltpu.VMEM(shape, f32) for shape in scratch],
        compiler_params=pltpu.CompilerParams(vmem_limit_bytes=VMEM_BYTES),
        cost_estimate=pl.CostEstimate(
            flops=products * pairs, bytes_accessed=QUERY_WIDTH * 1024, transcendentals=0
        ),
        name=name,
    )(meta, *operands)


def attend(meta, query, key_value):
    stretch = query.shape[0]
    stats = (QUERY_HEADS, stretch)
    outs = (
        jax.ShapeDtypeStruct((stretch, QUERY_WIDTH), f32),
        jax.ShapeDtypeStruct(stats, f32),
    )
    scratch = [stats, stats, (QUERY_WIDTH, stretch)]
    return attention_call(attend_kernel, outs, scratch, 2, "attend", meta, query, key_value)


def attend_back(order, meta, query, slope, log_total, mixed, key_value):
    stretch, rows = query.shape[0], key_value.shape[0]
    outs = (jax.ShapeDtypeStruct((stretch, QUERY_WIDTH), f32),)
    outs += (jax.ShapeDtypeStruct((2, rows // 2, 2 * KEY_WIDTH), bf16),)
    operands = (meta, query, slope, log_total, mixed, key_value)
    scratch = [(QUERY_WIDTH, stretch), (QUERY_HEADS, stretch)]
    kernel = functools.partial(attend_back_kernel, order)
    return attention_call(kernel, outs, scratch, 5, "attend_back", *operands)


def body(
    tokens,
    cotangent,
    routes,
    fill_order,
    pic_starts,
    attn_gain,
    moe_gain,
    w_query,
    key_projection,
    value_projection,
    w_out,
    w_router,
    expert_gate,
    expert_up,
    expert_down,
):
    sequences, stretch, width = tokens.shape
    count = sequences * stretch
    parts = lax.axis_size("ctx")
    experts = parts
    capacity = (5 * count * TOP + 4 * experts - 1) // (4 * experts)
    query_width, key_width = QUERY_WIDTH, KEY_WIDTH
    hidden_width = expert_gate.shape[2]
    seq_bits, ctx_bits = bits("seq"), bits("ctx")
    all_bits = seq_bits + ctx_bits
    inward = ctx_bits[-1:] + seq_bits[::-1] + ctx_bits[-2::-1]
    sizes = {"seq": parts, "ctx": 1}
    me = lax.axis_index("seq") * parts + lax.axis_index("ctx")

    def padded(columns):
        block = jnp.concatenate(columns, 1)
        return jnp.pad(block, ((0, 0), (0, LANES - block.shape[1])))

    own_rows = w_query.shape[0]

    def feature(stages):
        owner = jnp.bitwise_xor(jnp.array(flips(stages, sizes), jnp.int32), me)
        return (owner[:, None] * own_rows + jnp.arange(own_rows, dtype=jnp.int32)).reshape(-1)

    def same(left, right):
        return (left[:, None] == right[None, :]).astype(bf16)

    turns = ctx_bits[:-2] + seq_bits + ctx_bits[-2:]
    natural = jnp.arange(width, dtype=jnp.int32)
    gathered, summed = feature(turns[::-1]), feature(inward)
    turn, turn_in, across = same(natural, summed), same(natural, gathered), same(gathered, summed)

    def relative(rows):
        return matmul(rows, turn).astype(bf16)

    def halves(left, right):
        middle = left.shape[1] // 2
        sent = matmul_tn(left[:, middle:], right).astype(bf16)
        return sent, matmul_tn(left[:, :middle], right).astype(bf16)

    picks = routes.reshape(count, TOP)
    order = fill_order.reshape(count)
    routed = jnp.any(picks[:, :, None] == jnp.arange(experts, dtype=jnp.int32), 1)
    earlier = (order[None, :] < order[:, None]).astype(bf16)
    place = matmul(earlier, routed.astype(bf16)).astype(jnp.int32)
    place = jnp.where(routed, place, capacity)
    half = capacity // 2
    chosen_slot = [
        place.T[:, None, :]
        == (begin + jnp.arange(half, dtype=jnp.int32))[None, :, None]
        for begin in (0, half)
    ]
    slot_map = [chosen.astype(bf16).reshape(-1, count) for chosen in chosen_slot]

    def exchange_rows(rows):
        rows = rows.reshape(experts, half, width)
        rows = lax.all_to_all(rows, "ctx", split_axis=0, concat_axis=0, tiled=True)
        return rows.reshape(-1, width)

    out_slope = cotangent.reshape(count, width)
    slot_routes = jnp.concatenate(
        [matmul(part, routed.astype(bf16)).reshape(experts, half, experts) for part in slot_map], 1
    ).astype(bf16)
    slot_routes = lax.all_to_all(slot_routes, "ctx", split_axis=0, concat_axis=0, tiled=True)
    slot_routes = jnp.pad(slot_routes, ((0, 0), (0, 0), (0, LANES - experts)))
    slot_routes = [
        slot_routes[:, begin : begin + half].reshape(-1, LANES) for begin in (0, half)
    ]
    slope_rows = [matmul(part, out_slope).astype(bf16) for part in slot_map]
    slope_rows = jnp.concatenate([part.reshape(experts, half, width) for part in slope_rows], 1)

    block = jnp.concatenate(
        [
            w_query,
            key_projection,
            value_projection,
            padded([attn_gain[:, None]]),
            w_out,
            padded([w_router, moe_gain[:, None]]),
        ],
        1,
    )
    first_width = query_width + 2 * key_width + LANES
    expert_parts = [expert_gate[0], expert_up[0]]
    for index, stage in enumerate(turns):
        other = swap(block if index < 2 else mine, *stage)
        if index in (1, 3) and len(seq_bits) == 1:
            part = index // 2
            other, expert_parts[part] = lax.optimization_barrier(
                (other, (expert_parts[part], swap(expert_parts[part], *seq_bits[0])))
            )
        if index < 2:
            block = jnp.concatenate([block, other], 0)
        if index == 1:
            block, slope_rows = lax.optimization_barrier((block, slope_rows))
            slope_rows = lax.all_to_all(slope_rows, "ctx", split_axis=0, concat_axis=0, tiled=True)
            mine, second_set = block[:, :first_width], block[:, first_width:]
        if index > 2:
            arrived = swap(second_set, *turns[index - 1])
            if index < len(turns) - 1:
                other, arrived = lax.optimization_barrier((other, arrived))
            second_set = jnp.concatenate([second_set, arrived], 0)
        if 2 <= index < len(turns) - 1:
            mine = jnp.concatenate([mine, other], 0)
    inputs = tokens.reshape(count, width)
    inputs_turned = matmul(inputs, turn_in)
    inputs = inputs.astype(f32)
    inputs_scaled = inputs_turned * rms_scale(inputs)
    mine, other, slope_rows, slot_routes, inputs_scaled = lax.optimization_barrier(
        (mine, other, slope_rows, slot_routes, inputs_scaled)
    )
    slope_rows = [
        slope_rows[:, begin : begin + half].reshape(-1, width) for begin in (0, half)
    ]
    qkv_width = query_width + 2 * key_width
    weight_low, weight_high = mine[:, :qkv_width], other[:, :qkv_width]
    gain_one = jnp.concatenate([mine[:, qkv_width], other[:, qkv_width]]).astype(f32)

    def whole_expert(part):
        if isinstance(part, tuple):
            own, other = part
            upper = lax.axis_index("seq") > 0
            pair = [jnp.where(upper, other, own), jnp.where(upper, own, other)]
            return jnp.concatenate(pair, 0)
        return gather_blocks(part, seq_bits[::-1], seq_bits).reshape(-1, part.shape[1])

    gate_up = jnp.concatenate([whole_expert(part) for part in expert_parts], 1)
    second_set = jnp.concatenate([second_set, swap(second_set, *turns[-1])], 0)
    second_set = matmul(turn_in, second_set).astype(bf16)
    full_out = second_set[:, :width]
    full_router = second_set[:, width : width + experts]
    gain_two = second_set[:, width + experts].astype(f32)

    positions = lax.axis_index("ctx") * stretch + jnp.arange(stretch, dtype=jnp.int32)
    cosine, sine = rope_tables(positions, HEAD_WIDTH)
    normed = (inputs_scaled * gain_one).astype(bf16)

    def project(columns):
        low = matmul(normed[:, : width // 2], weight_low[:, columns])
        return low + matmul(normed[:, width // 2 :], weight_high[:, columns])

    projected = project(slice(query_width, None))
    key_rows = rotate(projected[:, :key_width], KEY_VALUE_HEADS, cosine, sine)
    key_values = lax.all_gather(
        jnp.concatenate([key_rows, projected[:, key_width:]], 1).astype(bf16),
        "ctx",
        axis=0,
        tiled=True,
    )
    projected = project(slice(0, query_width))
    query_rows = rotate(projected, QUERY_HEADS, cosine, sine).astype(bf16)
    meta = jnp.concatenate([lax.axis_index("ctx").astype(jnp.int32)[None], pic_starts[0]])
    mixed_heads, log_total = attend(meta, query_rows, key_values)

    def with_attention(other):
        nonlocal mixed_heads
        mixed_heads, other = lax.optimization_barrier((mixed_heads, other))
        return other

    down = gather_blocks(
        lax.optimization_barrier((expert_down[0], gain_one))[0],
        seq_bits[::-1],
        seq_bits,
        with_attention,
    ).reshape(-1, width)
    attended = mixed_heads.astype(bf16)

    middle = inputs + matmul(attended, full_out)
    enter = rms_norm(middle, gain_two).astype(bf16)
    arrived = [exchange_rows(matmul(part, enter).astype(bf16)) for part in slot_map]

    def gates_of(rows, chosen):
        logits = jnp.where(chosen, matmul(rows, full_router), big_negative)
        shares = jnp.exp(logits - jnp.max(logits, -1, keepdims=True))
        shares = jnp.where(chosen, shares, 0.0)
        return shares / jnp.maximum(jnp.sum(shares, -1, keepdims=True), 1e-30)

    gates = gates_of(enter, routed)

    attended_turned, enter_turned = map(relative, (attended, enter))
    normed_turned = matmul(normed, across).astype(bf16)
    arrived[0], attended_turned, enter_turned, normed_turned = lax.optimization_barrier(
        (arrived[0], attended_turned, enter_turned, normed_turned)
    )
    which = lax.axis_index("ctx").astype(jnp.int32)[None]
    router = second_set[:, width:]
    hidden, result, slope_gates, slope_slots, slope_pre, slope_arrived = ([] for _ in range(6))
    for index in range(2):
        made = list(expert(
            which, arrived[index], slope_rows[index], slot_routes[index], gate_up, down, router)
        )
        if index == 0:
            arrived[1], made[-1] = lax.optimization_barrier((arrived[1], made[-1]))
        for kept, item in zip(
            (hidden, result, slope_gates, slope_slots, slope_pre, slope_arrived), made
        ):
            kept.append(item)
    returned_slopes = [exchange_rows(slope_arrived[0])]
    slope_gates = jnp.concatenate([item.reshape(experts, half) for item in slope_gates], 1)
    slope_gates, returned_slopes[0] = lax.optimization_barrier((slope_gates, returned_slopes[0]))
    returned_gates = lax.all_to_all(slope_gates, "ctx", split_axis=0, concat_axis=0, tiled=True)
    slope_arrived[1], returned_gates, slope_pre, slope_slots = lax.optimization_barrier(
        (slope_arrived[1], returned_gates, slope_pre, slope_slots)
    )
    returned_slopes.append(exchange_rows(slope_arrived[1]))
    grad_gate, grad_up = (
        sum(matmul_tn(arrived[i], slope_pre[i][:, columns]) for i in range(2)).astype(bf16)
        for columns in (slice(0, hidden_width), slice(hidden_width, None))
    )
    grad_down = sum(matmul_tn(hidden[i], slope_slots[i]) for i in range(2)).astype(bf16)
    def sector_halves(grads):
        return grads.reshape([2] * len(seq_bits) + [-1, grads.shape[1]])

    def sector_sum(blocks, arrived):
        for axis, bit in seq_bits:
            mine = ((lax.axis_index(axis) & bit) > 0).astype(jnp.int32)
            sent = lax.dynamic_index_in_dim(blocks, 1 - mine, 0, keepdims=False)
            kept = lax.dynamic_index_in_dim(blocks, mine, 0, keepdims=False)
            other = swap(sent.astype(bf16), axis, bit)
            if (axis, bit) == seq_bits[-1]:
                other = arrived(other)
            blocks = kept.astype(f32) + other.astype(f32)
        return blocks

    def with_slopes(other):
        nonlocal grad_gate, grad_up
        returned_slopes[1], other, grad_gate, grad_up = lax.optimization_barrier(
            (returned_slopes[1], other, grad_gate, grad_up)
        )
        return other

    grad_down = sector_sum(sector_halves(grad_down), with_slopes)
    returned = jnp.concatenate([part.reshape(experts, half, width) for part in result], 1)
    returned = lax.all_to_all(returned, "ctx", split_axis=0, concat_axis=0, tiled=True)

    slope_gate = 0.0
    for index, chosen in enumerate(chosen_slot):
        part = returned_gates[:, index * half : (index + 1) * half]
        slope_gate = slope_gate + jnp.sum(jnp.where(chosen, part[:, :, None], 0.0), 1).T
    slope_logits = gates * (slope_gate - jnp.sum(gates * slope_gate, -1, keepdims=True))
    slope_logits = slope_logits.astype(bf16)
    grad_router = matmul_tn(enter_turned, slope_logits)
    slope_enter = matmul_nt(slope_logits, full_router)
    for part, rows in zip(slot_map, returned_slopes):
        slope_enter = slope_enter + matmul_tn(part, rows)

    pull_two = jax.vjp(rms_norm, middle, gain_two)[1]
    slope_middle, grad_gain_two = pull_two(slope_enter)
    slope_middle = out_slope.astype(f32) + slope_middle
    slope_branch = slope_middle.astype(bf16)
    slope_attended = matmul_nt(slope_branch, full_out).astype(bf16)

    out_sum = Sum(*halves(attended_turned, slope_branch), inward)
    kv_order = ctx_bits[::-1]
    slope_q, slope_kv = attend_back(
        [bit for _, bit in kv_order],
        meta,
        query_rows,
        slope_attended,
        log_total,
        mixed_heads,
        key_values,
    )

    def after_back(other):
        nonlocal slope_q, slope_kv
        slope_q, slope_kv, other = lax.optimization_barrier((slope_q, slope_kv, other))
        return other

    grad_gate = sector_sum(sector_halves(grad_gate), after_back)
    grad_up = sector_sum(sector_halves(grad_up), after_back)
    kv_sum = Sum(slope_kv[1], slope_kv[0], kv_order)
    together([kv_sum])
    slope_query = rotate(slope_q, QUERY_HEADS, cosine, -sine).astype(bf16)
    query_sum = Sum(*halves(normed_turned, slope_query), inward)
    out_sum.step()
    together([kv_sum, query_sum])
    slope_normed = [
        matmul_nt(slope_query, part[:, :query_width]) for part in (weight_low, weight_high)
    ]
    together([kv_sum, query_sum, out_sum])
    while len(kv_sum.stages) > 1:
        together([kv_sum, query_sum])
    kv_sum.step()
    query_sum.step()
    kv_sum.total, query_sum.sent, slope_normed = lax.optimization_barrier(
        (kv_sum.total, query_sum.sent, slope_normed)
    )
    slope_key = rotate(kv_sum.total[:, :key_width], KEY_VALUE_HEADS, cosine, -sine)
    slope_rest = jnp.concatenate([slope_key, kv_sum.total[:, key_width:]], 1).astype(bf16)
    slope_normed = jnp.concatenate(
        [
            early + matmul_nt(slope_rest, part[:, query_width:])
            for early, part in zip(slope_normed, (weight_low, weight_high))
        ],
        1,
    )
    pull_one = jax.vjp(rms_norm, inputs_turned, gain_one)[1]
    slope_inputs, grad_gain_one = pull_one(slope_normed)
    gains = jnp.stack(
        [
            matmul(grad_gain_one.astype(bf16)[None], across)[0].astype(bf16),
            relative(grad_gain_two.astype(bf16)[None])[0],
        ],
        1,
    )
    small = padded([grad_router.astype(bf16), gains])
    rest_sum = Sum(
        *(
            jnp.concatenate([grads, part], 1)
            for grads, part in zip(
                halves(normed_turned, slope_rest), (small[width // 2 :], small[: width // 2])
            )
        ),
        inward,
    )
    together([item for item in (rest_sum, query_sum) if item.stages])
    returned, slope_inputs = together(
        [item for item in (rest_sum, query_sum, out_sum) if item.stages],
        (returned, slope_inputs),
    )
    while rest_sum.stages:
        together([item for item in (rest_sum, query_sum, out_sum) if item.stages])
    for item in (query_sum, out_sum):
        while item.stages:
            item.step()
    grads_rest = rest_sum.total
    slope_high = slope_inputs.astype(bf16)
    slope_low = (slope_inputs - slope_high.astype(f32)).astype(bf16)
    grad_input = slope_middle + matmul_nt(slope_high, turn_in) + matmul_nt(slope_low, turn_in)
    grad_input = grad_input.reshape(tokens.shape)
    output = middle
    for chosen, rows in ((jnp.concatenate(chosen_slot, 1), returned.reshape(-1, width)),):
        mix = jnp.where(chosen, gates.T[:, None, :], 0.0).reshape(-1, count)
        mix_high = mix.astype(bf16)
        mix_low = (mix - mix_high.astype(f32)).astype(bf16)
        output = output + matmul_tn(mix_high, rows) + matmul_tn(mix_low, rows)
    output = output.astype(bf16).reshape(tokens.shape)
    return (
        output,
        grad_input,
        grads_rest[:, 2 * key_width + experts],
        grads_rest[:, 2 * key_width + experts + 1],
        query_sum.total,
        grads_rest[:, :key_width],
        grads_rest[:, key_width : 2 * key_width],
        out_sum.total,
        grads_rest[:, 2 * key_width : 2 * key_width + experts],
        grad_gate[None],
        grad_up[None],
        grad_down[None],
    )


def solution(mesh):
    rows = P("seq", "ctx", None)
    shard = P(("seq", "ctx"), None)
    vector = P(("seq", "ctx"))
    expert = P("ctx", "seq", None)
    return jax.shard_map(
        body,
        mesh=mesh,
        in_specs=(rows, rows, rows, P("seq", "ctx"), P("seq", None), vector, vector)
        + (shard,) * 5
        + (expert,) * 3,
        out_specs=(rows, rows, vector, vector) + (shard,) * 5 + (expert,) * 3,
        check_vma=False,
    )
```

```python
import functools
import math

import jax
import jax.numpy as jnp
from jax import lax
from jax.experimental import pallas as pl
from jax.experimental.pallas import tpu as pltpu
from jax.sharding import PartitionSpec as P

QUERY_HEADS = 12
KEY_VALUE_HEADS = 2
HEAD_WIDTH = 128
TOP = 4
PIC = 256
NPIC = 4
LANES = 128
GROUPS = QUERY_HEADS // KEY_VALUE_HEADS
QUERY_WIDTH = QUERY_HEADS * HEAD_WIDTH
KEY_WIDTH = KEY_VALUE_HEADS * HEAD_WIDTH
SCALE = 1.0 / math.sqrt(HEAD_WIDTH)
EXP2_SCALE = SCALE * math.log2(math.e)
BLOCKS = 2
SKEW = 1
VMEM_BYTES = 48 << 20

epsilon = 1e-06
rope_base = 10000.0
big_negative = -1e30
bf16 = jnp.bfloat16
f32 = jnp.float32


def matmul(left, right):
    return jnp.dot(left, right, preferred_element_type=f32)


def matmul_nt(left, right):
    return lax.dot_general(left, right, (((1,), (1,)), ((), ())), preferred_element_type=f32)


def matmul_tn(left, right):
    return lax.dot_general(left, right, (((0,), (0,)), ((), ())), preferred_element_type=f32)


def rms_scale(rows):
    return lax.rsqrt(jnp.mean(rows * rows, -1, keepdims=True) + epsilon)


def rms_norm(rows, gain):
    return rows * rms_scale(rows) * gain


def rope_tables(positions, head_size):
    half = head_size // 2
    inverse = rope_base ** (-(jnp.arange(half, dtype=f32) * 2.0 / head_size))
    angles = positions.astype(f32)[:, None] * inverse[None, :]
    return (jnp.cos(angles), jnp.sin(angles))


def rotate(rows, heads, cosine, sine):
    shaped = rows.reshape(rows.shape[0], heads, HEAD_WIDTH)
    half = HEAD_WIDTH // 2
    first, second = shaped[..., :half], shaped[..., half:]
    cosine, sine = cosine[:, None, :], sine[:, None, :]
    turned = jnp.concatenate(
        [first * cosine - second * sine, second * cosine + first * sine], -1
    )
    return turned.reshape(rows.shape)


def bits(axis):
    size = lax.axis_size(axis)
    return [(axis, 1 << place) for place in reversed(range(size.bit_length() - 1))]


def swap(block, axis, bit):
    size = lax.axis_size(axis)
    return lax.ppermute(block, axis, [(index, index ^ bit) for index in range(size)])


def gather_blocks(block, stages, order, arrived=None):
    held = []
    for stage in stages:
        axis, bit = stage
        other = swap(block, axis, bit)
        if arrived is not None and stage == stages[-1]:
            other = arrived(other)
        upper = (lax.axis_index(axis) & bit) > 0
        place = sum(order.index(known) < order.index(stage) for known in held)
        block = jnp.stack(
            [jnp.where(upper, other, block), jnp.where(upper, block, other)], place
        )
        held.append(stage)
    return block


class Sum:
    def __init__(self, sent, kept, stages):
        self.sent, self.kept, self.stages = sent, kept, list(stages)

    def step(self):
        axis, bit = self.stages.pop(0)
        other = swap(self.sent, axis, bit)
        if not self.stages:
            self.total = self.kept.astype(f32) + other.astype(f32)
            return
        half = self.kept.shape[0] // 2
        self.sent = (self.kept[half:].astype(f32) + other[half:].astype(f32)).astype(bf16)
        self.kept = (self.kept[:half].astype(f32) + other[:half].astype(f32)).astype(bf16)


def together(sums, also=()):
    for item in sums:
        item.step()
    live = [item for item in sums if item.stages]
    sent, also = lax.optimization_barrier(([item.sent for item in live], also))
    for item, block in zip(live, sent):
        item.sent = block
    return also


def flips(stages, sizes):
    masks = []
    for block in range(1 << len(stages)):
        mask = 0
        for place, (axis, bit) in enumerate(stages):
            if (block >> (len(stages) - 1 - place)) & 1:
                mask |= bit * sizes[axis]
        masks.append(mask)
    return masks


def visible_keys(meta, step, stretch):
    span = BLOCKS * stretch
    keys = step * span + lax.broadcasted_iota(jnp.int32, (span, 1), 0)
    queries = meta[0] * stretch + lax.broadcasted_iota(jnp.int32, (1, stretch), 1)

    def label(positions):
        found = jnp.zeros(positions.shape, jnp.int32)
        for index in range(NPIC):
            start = meta[1 + index]
            inside = (positions >= start) & (positions < start + PIC)
            found = jnp.where(inside, index + 1, found)
        return found

    query_label = label(queries)
    return (keys <= queries) | ((label(keys) == query_label) & (query_label > 0))


def for_each_step(meta, stretch, steps, process, skip=None):
    span = BLOCKS * stretch
    low, high = meta[0] * stretch, (meta[0] + 1) * stretch

    def turn(step, carry):
        needed = step * span < high + PIC - 1
        edge = (step + 1) * span > low

        @pl.when(needed & edge)
        def _():
            process(step, True)

        @pl.when(needed & jnp.logical_not(edge))
        def _():
            process(step, False)

        if skip is not None:

            @pl.when(jnp.logical_not(needed))
            def _():
                skip(step)

        return carry

    lax.fori_loop(0, steps, turn, 0)


def head_columns(head, start=0):
    return slice(start + head * HEAD_WIDTH, start + (head + 1) * HEAD_WIDTH)


def attend_kernel(meta, query, key_value, out, log_total, peak, total, accum):
    stretch = query.shape[0]
    span = BLOCKS * stretch
    peak[...] = jnp.full(peak.shape, big_negative, f32)
    total[...] = jnp.zeros(total.shape, f32)
    accum[...] = jnp.zeros(accum.shape, f32)

    def process(step, edge):
        rows = pl.ds(pl.multiple_of(step * span, span), span)
        if edge:
            visible = visible_keys(meta, step, stretch)
        keys, values = [], []
        for group in range(KEY_VALUE_HEADS):
            keys.append(key_value[rows, head_columns(group)])
            turned = key_value[rows, head_columns(group, KEY_WIDTH)].T
            values.append(jnp.concatenate([turned, jnp.ones((16, span), bf16)], 0))

        def score(head):
            scores = matmul_nt(keys[head // GROUPS], query[:, head_columns(head)])
            if edge:
                scores = jnp.where(visible, scores, big_negative)
            old = peak[head : head + 1, :]
            return scores, old, jnp.maximum(old, jnp.max(scores, 0, keepdims=True))

        def weigh(head, scores, old, new):
            weights = jnp.exp2((scores - new) * EXP2_SCALE).astype(bf16)
            shrink = jnp.exp2((old - new) * EXP2_SCALE)
            sums = matmul(values[head // GROUPS], weights)
            row, columns = slice(head, head + 1), head_columns(head)
            peak[row, :] = new
            total[row, :] = total[row, :] * shrink + sums[HEAD_WIDTH : HEAD_WIDTH + 1]
            accum[columns, :] = accum[columns, :] * shrink + sums[:HEAD_WIDTH]

        waiting = []
        for head in range(QUERY_HEADS):
            waiting.append((head, *score(head)))
            if len(waiting) > 2:
                weigh(*waiting.pop(0))
        for item in waiting:
            weigh(*item)

    for_each_step(meta, stretch, key_value.shape[0] // span, process)
    for head in range(QUERY_HEADS):
        row, columns = slice(head, head + 1), head_columns(head)
        out[:, columns] = (accum[columns, :] / total[row, :]).T
        log_total[row, :] = peak[row, :] * EXP2_SCALE + jnp.log2(total[row, :])


def attend_back_kernel(
    order,
    group,
    meta,
    query,
    slope,
    log_total,
    mixed,
    key_value,
    slope_query,
    out,
    accum,
    delta,
):
    stretch = query.shape[0]
    span = BLOCKS * stretch
    accum[...] = jnp.zeros(accum.shape, f32)
    for index in range(GROUPS):
        columns = head_columns(group * GROUPS + index)
        product = slope[:, columns].astype(f32) * mixed[:, columns]
        delta[index : index + 1, :] = jnp.sum(product.T, 0, keepdims=True)

    def store(step, part, columns, block):
        flip = jnp.bitwise_xor(BLOCKS * step + part, meta[0])
        first, *others = order
        place = 0
        for index, bit in enumerate(others):
            place = place + ((flip // bit) & 1) * (1 << (len(others) - 1 - index))
        place = pl.ds(pl.multiple_of(place * stretch, stretch), stretch)
        out[(flip // first) & 1, place, columns] = block

    def process(step, edge):
        rows = pl.ds(pl.multiple_of(step * span, span), span)
        if edge:
            visible = visible_keys(meta, step, stretch)
        keys = key_value[rows, head_columns(group)]
        values = key_value[rows, head_columns(group, KEY_WIDTH)]
        keys_turned = keys.T

        def slopes_of(index):
            columns = head_columns(group * GROUPS + index)
            row = slice(group * GROUPS + index, group * GROUPS + index + 1)
            scores = matmul_nt(keys, query[:, columns])
            probs = jnp.exp2(scores * EXP2_SCALE - log_total[row, :])
            if edge:
                probs = jnp.where(visible, probs, 0.0)
            slope_probs = matmul_nt(values, slope[:, columns])
            slope_scores = (probs * (slope_probs - delta[index : index + 1, :])).astype(bf16)
            return index, probs.astype(bf16), slope_scores

        slope_k = jnp.zeros((span, HEAD_WIDTH), f32)
        slope_v = jnp.zeros((span, HEAD_WIDTH), f32)
        waiting = []
        for index in range(GROUPS + SKEW):
            if index < GROUPS:
                waiting.append(slopes_of(index))
            if index >= SKEW:
                own, probs, slope_scores = waiting.pop(0)
                columns, place = head_columns(group * GROUPS + own), head_columns(own)
                slope_v = slope_v + matmul(probs, slope[:, columns])
                slope_k = slope_k + matmul(slope_scores, query[:, columns])
                accum[place, :] = accum[place, :] + matmul(keys_turned, slope_scores)
        slope_k, slope_v = (slope_k * SCALE).astype(bf16), slope_v.astype(bf16)
        for which, block in enumerate((slope_k, slope_v)):
            for part in range(BLOCKS):
                own = block[part * stretch : (part + 1) * stretch]
                store(step, part, head_columns(which), own)

    def skip(step):
        for part in range(BLOCKS):
            store(step, part, slice(None), jnp.zeros((stretch, 2 * HEAD_WIDTH), bf16))

    for_each_step(meta, stretch, key_value.shape[0] // span, process, skip)
    for index in range(GROUPS):
        columns = head_columns(index)
        slope_query[:, columns] = (accum[columns, :] * SCALE).T


def expert_kernel(
    which,
    rows,
    slopes,
    chosen,
    gate_up,
    down,
    router,
    hidden_out,
    result_out,
    gates_out,
    slots_out,
    pre_out,
    slope_out,
):
    hidden_width = down.shape[0]
    incoming = rows[...]
    logits = jnp.where(chosen[...] > 0, matmul(incoming, router[...]), big_negative)
    shares = jnp.exp(logits - jnp.max(logits, -1, keepdims=True))
    shares = jnp.where(chosen[...] > 0, shares, 0.0)
    column = lax.broadcasted_iota(jnp.int32, shares.shape, 1)
    own = jnp.sum(jnp.where(column == which[0], shares, 0.0), -1, keepdims=True)
    gates = own / jnp.maximum(jnp.sum(shares, -1, keepdims=True), 1e-30)
    slots = (gates * slopes[...].astype(f32)).astype(bf16)
    slots_out[...] = slots
    pre = matmul(incoming, gate_up[...])
    gate, up = pre[:, :hidden_width], pre[:, hidden_width:]
    root, cubic = math.sqrt(2.0 / math.pi), 0.044715
    square = gate * gate
    bend = jnp.tanh(root * (gate + cubic * gate * square))
    gelu = 0.5 * gate * (1.0 + bend)
    rise = 0.5 * (1.0 + bend) + 0.5 * gate * (1.0 - bend * bend) * root * (
        1.0 + 3.0 * cubic * square
    )
    hidden = (gelu * up).astype(bf16)
    hidden_out[...] = hidden
    result = matmul(hidden, down[...]).astype(bf16)
    result_out[...] = result
    gates_out[...] = jnp.sum(slopes[...].astype(f32) * result.astype(f32), -1, keepdims=True)
    slope_hidden = matmul_nt(slots, down[...])
    slope_pre = jnp.concatenate([slope_hidden * up * rise, slope_hidden * gelu], 1).astype(bf16)
    pre_out[...] = slope_pre
    slope_out[...] = matmul_nt(slope_pre, gate_up[...]).astype(bf16)


def expert(which, rows, slopes, chosen, gate_up, down, router):
    count, width = rows.shape
    hidden_width = down.shape[0]
    block = count // 2

    def tile(columns):
        return pl.BlockSpec((block, columns), lambda step: (step, 0))

    def whole(array):
        return pl.BlockSpec(array.shape, lambda step: (0, 0))

    shapes = [(hidden_width, bf16), (width, bf16), (1, f32), (width, bf16)]
    shapes += [(2 * hidden_width, bf16), (width, bf16)]
    return pl.pallas_call(
        expert_kernel,
        grid=(2,),
        out_shape=[jax.ShapeDtypeStruct((count, columns), kind) for columns, kind in shapes],
        in_specs=[
            pl.BlockSpec(memory_space=pltpu.SMEM),
            tile(width),
            tile(width),
            tile(LANES),
            whole(gate_up),
            whole(down),
            whole(router),
        ],
        out_specs=[tile(columns) for columns, _ in shapes],
        compiler_params=pltpu.CompilerParams(vmem_limit_bytes=VMEM_BYTES),
        cost_estimate=pl.CostEstimate(
            flops=12 * count * width * hidden_width,
            bytes_accessed=20 * count * width,
            transcendentals=count * hidden_width,
        ),
        name="expert",
    )(which, rows, slopes, chosen, gate_up, down, router)


def attention_call(kernel, outs, scratch, products, name, meta, *operands):
    vmem = pl.BlockSpec(memory_space=pltpu.VMEM)
    pairs = QUERY_HEADS * operands[0].shape[0] * operands[-1].shape[0]
    return pl.pallas_call(
        kernel,
        out_shape=outs,
        in_specs=[pl.BlockSpec(memory_space=pltpu.SMEM)] + [vmem] * len(operands),
        out_specs=(vmem,) * len(outs),
        scratch_shapes=[pltpu.VMEM(*shape) for shape in scratch],
        compiler_params=pltpu.CompilerParams(vmem_limit_bytes=VMEM_BYTES),
        cost_estimate=pl.CostEstimate(
            flops=products * pairs, bytes_accessed=QUERY_WIDTH * 1024, transcendentals=0
        ),
        name=name,
    )(meta, *operands)


def attend(meta, query, key_value):
    stretch = query.shape[0]
    stats = (QUERY_HEADS, stretch)
    outs = (
        jax.ShapeDtypeStruct((stretch, QUERY_WIDTH), f32),
        jax.ShapeDtypeStruct(stats, f32),
    )
    scratch = [(stats, f32), (stats, f32), ((QUERY_WIDTH, stretch), f32)]
    return attention_call(attend_kernel, outs, scratch, 2, "attend", meta, query, key_value)


def attend_back(order, group, meta, query, slope, log_total, mixed, key_value):
    stretch, rows = query.shape[0], key_value.shape[0]
    group_width = GROUPS * HEAD_WIDTH
    outs = (
        jax.ShapeDtypeStruct((stretch, group_width), f32),
        jax.ShapeDtypeStruct((2, rows // 2, 2 * HEAD_WIDTH), bf16),
    )
    operands = (meta, query, slope, log_total, mixed, key_value)
    scratch = [((group_width, stretch), f32), ((GROUPS, stretch), f32)]
    kernel = functools.partial(attend_back_kernel, order, group)
    return attention_call(kernel, outs, scratch, 2, "attend_back", *operands)


def body(
    tokens,
    cotangent,
    routes,
    fill_order,
    pic_starts,
    attn_gain,
    moe_gain,
    w_query,
    key_projection,
    value_projection,
    w_out,
    w_router,
    expert_gate,
    expert_up,
    expert_down,
):
    sequences, stretch, width = tokens.shape
    count = sequences * stretch
    parts = lax.axis_size("ctx")
    experts = parts
    capacity = (5 * count * TOP + 4 * experts - 1) // (4 * experts)
    query_width, key_width = QUERY_WIDTH, KEY_WIDTH
    hidden_width = expert_gate.shape[2]
    seq_bits, ctx_bits = bits("seq"), bits("ctx")
    all_bits = seq_bits + ctx_bits
    inward = ctx_bits[-1:] + seq_bits[::-1] + ctx_bits[-2::-1]
    sizes = {"seq": parts, "ctx": 1}
    me = lax.axis_index("seq") * parts + lax.axis_index("ctx")

    def padded(columns):
        block = jnp.concatenate(columns, 1)
        return jnp.pad(block, ((0, 0), (0, LANES - block.shape[1])))

    own_rows = w_query.shape[0]

    def feature(stages):
        owner = jnp.bitwise_xor(jnp.array(flips(stages, sizes), jnp.int32), me)
        return (owner[:, None] * own_rows + jnp.arange(own_rows, dtype=jnp.int32)).reshape(-1)

    def same(left, right):
        return (left[:, None] == right[None, :]).astype(bf16)

    turns = ctx_bits[:-2] + seq_bits + ctx_bits[-2:]
    natural = jnp.arange(width, dtype=jnp.int32)
    gathered, summed = feature(turns[::-1]), feature(inward)
    turn, turn_in, across = same(natural, summed), same(natural, gathered), same(gathered, summed)

    def relative(rows):
        return matmul(rows, turn).astype(bf16)

    def halves(left, right):
        middle = left.shape[1] // 2
        sent = matmul_tn(left[:, middle:], right).astype(bf16)
        return sent, matmul_tn(left[:, :middle], right).astype(bf16)

    picks = routes.reshape(count, TOP)
    order = fill_order.reshape(count)
    routed = jnp.any(picks[:, :, None] == jnp.arange(experts, dtype=jnp.int32), 1)
    earlier = (order[None, :] < order[:, None]).astype(bf16)
    place = matmul(earlier, routed.astype(bf16)).astype(jnp.int32)
    place = jnp.where(routed, place, capacity)
    half = capacity // 2
    chosen_slot = [
        place.T[:, None, :]
        == (begin + jnp.arange(half, dtype=jnp.int32))[None, :, None]
        for begin in (0, half)
    ]
    slot_map = [chosen.astype(bf16).reshape(-1, count) for chosen in chosen_slot]

    def exchange_rows(rows):
        rows = rows.reshape(experts, half, width)
        rows = lax.all_to_all(rows, "ctx", split_axis=0, concat_axis=0, tiled=True)
        return rows.reshape(-1, width)

    out_slope = cotangent.reshape(count, width)
    slot_routes = jnp.concatenate(
        [matmul(part, routed.astype(bf16)).reshape(experts, half, experts) for part in slot_map], 1
    ).astype(bf16)
    slot_routes = lax.all_to_all(slot_routes, "ctx", split_axis=0, concat_axis=0, tiled=True)
    slot_routes = jnp.pad(slot_routes, ((0, 0), (0, 0), (0, LANES - experts)))
    slot_routes = [
        slot_routes[:, begin : begin + half].reshape(-1, LANES) for begin in (0, half)
    ]
    slope_rows = [matmul(part, out_slope).astype(bf16) for part in slot_map]
    slope_rows = jnp.concatenate([part.reshape(experts, half, width) for part in slope_rows], 1)

    mine = jnp.concatenate(
        [w_query, key_projection, value_projection, padded([attn_gain[:, None]])], 1
    )
    second_set = jnp.concatenate([w_out, padded([w_router, moe_gain[:, None]])], 1)
    gate_up = jnp.concatenate([expert_gate[0], expert_up[0]], 1)
    for index, stage in enumerate(turns):
        other = swap(mine, *stage)
        if index == len(turns) - 3:
            other, gate_up = lax.optimization_barrier((other, gate_up))
        if index == len(turns) - 2:
            other, second_set = lax.optimization_barrier((other, second_set))
            if len(seq_bits) == 1:
                other, gate_up = lax.optimization_barrier(
                    (other, (gate_up, swap(gate_up, *seq_bits[0])))
                )
        if index < len(turns) - 1:
            mine = jnp.concatenate([mine, other], 0)
        if index == 1:
            mine, slope_rows = lax.optimization_barrier((mine, slope_rows))
            slope_rows = lax.all_to_all(slope_rows, "ctx", split_axis=0, concat_axis=0, tiled=True)
    inputs = tokens.reshape(count, width)
    inputs_turned = matmul(inputs, turn_in)
    inputs = inputs.astype(f32)
    inputs_scaled = inputs_turned * rms_scale(inputs)
    mine, other, slope_rows, slot_routes, inputs_scaled = lax.optimization_barrier(
        (mine, other, slope_rows, slot_routes, inputs_scaled)
    )
    slope_rows = [
        slope_rows[:, begin : begin + half].reshape(-1, width) for begin in (0, half)
    ]
    qkv_width = query_width + 2 * key_width
    weight_low, weight_high = mine[:, :qkv_width], other[:, :qkv_width]
    gain_one = jnp.concatenate([mine[:, qkv_width], other[:, qkv_width]]).astype(f32)

    def whole_expert(part):
        if isinstance(part, tuple):
            own, other = part
            upper = lax.axis_index("seq") > 0
            pair = [jnp.where(upper, other, own), jnp.where(upper, own, other)]
            return jnp.concatenate(pair, 0)
        return gather_blocks(part, seq_bits[::-1], seq_bits).reshape(-1, part.shape[1])

    gate_up = whole_expert(gate_up)
    for stage in inward[:0:-1]:
        second_set = jnp.concatenate([second_set, swap(second_set, *stage)], 0)
    second_high = swap(second_set, *inward[0])

    positions = lax.axis_index("ctx") * stretch + jnp.arange(stretch, dtype=jnp.int32)
    cosine, sine = rope_tables(positions, HEAD_WIDTH)
    normed = (inputs_scaled * gain_one).astype(bf16)

    def project(columns):
        low = matmul(normed[:, : width // 2], weight_low[:, columns])
        return low + matmul(normed[:, width // 2 :], weight_high[:, columns])

    projected = project(slice(query_width, None))
    key_rows = rotate(projected[:, :key_width], KEY_VALUE_HEADS, cosine, sine)
    key_values = lax.all_gather(
        jnp.concatenate([key_rows, projected[:, key_width:]], 1).astype(bf16),
        "ctx",
        axis=0,
        tiled=True,
    )
    projected = project(slice(0, query_width))
    query_rows = rotate(projected, QUERY_HEADS, cosine, sine).astype(bf16)
    meta = jnp.concatenate([lax.axis_index("ctx").astype(jnp.int32)[None], pic_starts[0]])
    mixed_heads, log_total = attend(meta, query_rows, key_values)

    def with_attention(other):
        nonlocal mixed_heads
        mixed_heads, other = lax.optimization_barrier((mixed_heads, other))
        return other

    down = gather_blocks(
        lax.optimization_barrier((expert_down[0], gain_one))[0],
        seq_bits[::-1],
        seq_bits,
        with_attention,
    ).reshape(-1, width)
    second_high = with_attention(second_high)
    out_parts = (second_set[:, :width], second_high[:, :width])
    router = jnp.concatenate([second_set[:, width:], second_high[:, width:]], 0)
    router = matmul(turn, router).astype(bf16)
    full_router, gain_two = router[:, :experts], router[:, experts].astype(f32)
    attended_turned = relative(mixed_heads.astype(bf16))
    middle_feature = width // 2

    middle = matmul(attended_turned[:, :middle_feature], out_parts[0])
    middle = inputs + middle + matmul(attended_turned[:, middle_feature:], out_parts[1])
    enter = rms_norm(middle, gain_two).astype(bf16)
    arrived = [exchange_rows(matmul(part, enter).astype(bf16)) for part in slot_map]

    def gates_of(rows, chosen):
        logits = jnp.where(chosen, matmul(rows, full_router), big_negative)
        shares = jnp.exp(logits - jnp.max(logits, -1, keepdims=True))
        shares = jnp.where(chosen, shares, 0.0)
        return shares / jnp.maximum(jnp.sum(shares, -1, keepdims=True), 1e-30)

    gates = gates_of(enter, routed)

    enter_turned = relative(enter)
    normed_turned = matmul(normed, across).astype(bf16)
    arrived[0], enter_turned, normed_turned = lax.optimization_barrier(
        (arrived[0], enter_turned, normed_turned)
    )
    which = lax.axis_index("ctx").astype(jnp.int32)[None]
    hidden, result, slope_gates, slope_slots, slope_pre, slope_arrived = ([] for _ in range(6))
    for index in range(2):
        made = list(expert(
            which, arrived[index], slope_rows[index], slot_routes[index], gate_up, down, router)
        )
        if index == 0:
            arrived[1], made[-1] = lax.optimization_barrier((arrived[1], made[-1]))
        for kept, item in zip(
            (hidden, result, slope_gates, slope_slots, slope_pre, slope_arrived), made
        ):
            kept.append(item)
    returned_slopes = [exchange_rows(slope_arrived[0])]
    slope_gates = jnp.concatenate([item.reshape(experts, half) for item in slope_gates], 1)
    slope_gates, returned_slopes[0] = lax.optimization_barrier((slope_gates, returned_slopes[0]))
    returned_gates = lax.all_to_all(slope_gates, "ctx", split_axis=0, concat_axis=0, tiled=True)
    slope_arrived[1], returned_gates, slope_pre, slope_slots = lax.optimization_barrier(
        (slope_arrived[1], returned_gates, slope_pre, slope_slots)
    )
    returned_slopes.append(exchange_rows(slope_arrived[1]))
    grad_gate, grad_up = (
        sum(matmul_tn(arrived[i], slope_pre[i][:, columns]) for i in range(2)).astype(bf16)
        for columns in (slice(0, hidden_width), slice(hidden_width, None))
    )
    grad_down = sum(matmul_tn(hidden[i], slope_slots[i]) for i in range(2)).astype(bf16)
    def sector_halves(grads):
        return grads.reshape([2] * len(seq_bits) + [-1, grads.shape[1]])

    def sector_sum(blocks, arrived):
        for axis, bit in seq_bits:
            mine = ((lax.axis_index(axis) & bit) > 0).astype(jnp.int32)
            sent = lax.dynamic_index_in_dim(blocks, 1 - mine, 0, keepdims=False)
            kept = lax.dynamic_index_in_dim(blocks, mine, 0, keepdims=False)
            other = swap(sent.astype(bf16), axis, bit)
            if (axis, bit) == seq_bits[-1]:
                other = arrived(other)
            blocks = kept.astype(f32) + other.astype(f32)
        return blocks

    def with_slopes(other):
        nonlocal grad_gate, grad_up
        returned_slopes[1], other, grad_gate, grad_up = lax.optimization_barrier(
            (returned_slopes[1], other, grad_gate, grad_up)
        )
        return other

    grad_down = sector_sum(sector_halves(grad_down), with_slopes)
    returned = jnp.concatenate([part.reshape(experts, half, width) for part in result], 1)
    returned = lax.all_to_all(returned, "ctx", split_axis=0, concat_axis=0, tiled=True)

    slope_gate = 0.0
    for index, chosen in enumerate(chosen_slot):
        part = returned_gates[:, index * half : (index + 1) * half]
        slope_gate = slope_gate + jnp.sum(jnp.where(chosen, part[:, :, None], 0.0), 1).T
    slope_logits = gates * (slope_gate - jnp.sum(gates * slope_gate, -1, keepdims=True))
    slope_logits = slope_logits.astype(bf16)
    grad_router = matmul_tn(enter_turned, slope_logits)
    slope_enter = matmul_nt(slope_logits, full_router)
    for part, rows in zip(slot_map, returned_slopes):
        slope_enter = slope_enter + matmul_tn(part, rows)

    pull_two = jax.vjp(rms_norm, middle, gain_two)[1]
    slope_middle, grad_gain_two = pull_two(slope_enter)
    slope_middle = out_slope.astype(f32) + slope_middle
    slope_branch = slope_middle.astype(bf16)
    slope_attended = jnp.concatenate(
        [matmul_nt(slope_branch, part).astype(bf16) for part in out_parts], 1
    )
    slope_attended = matmul_nt(slope_attended, turn).astype(bf16)

    out_sum = Sum(*halves(attended_turned, slope_branch), inward)
    kv_order = ctx_bits[::-1]

    def back(group, meta):
        order = [bit for _, bit in kv_order]
        return attend_back(
            order, group, meta, query_rows, slope_attended, log_total, mixed_heads, key_values
        )

    first_q, first_kv = back(0, meta)

    def after_first(other):
        nonlocal first_q, first_kv, meta
        first_q, first_kv, meta, other = lax.optimization_barrier(
            (first_q, first_kv, meta, other)
        )
        return other

    grad_gate = sector_sum(sector_halves(grad_gate), after_first)
    first_sum = Sum(first_kv[1], first_kv[0], kv_order)
    first_sum.step()
    second_q, second_kv = back(1, meta)

    def after_second(other):
        nonlocal second_q, second_kv
        second_q, second_kv, first_sum.sent, other = lax.optimization_barrier(
            (second_q, second_kv, first_sum.sent, other)
        )
        return other

    grad_up = sector_sum(sector_halves(grad_up), after_second)
    second_sum = Sum(second_kv[1], second_kv[0], kv_order)
    slope_query = jnp.concatenate([first_q, second_q], 1)
    slope_query = rotate(slope_query, QUERY_HEADS, cosine, -sine).astype(bf16)
    query_sum = Sum(*halves(normed_turned, slope_query), inward)
    out_sum.step()
    together([first_sum, second_sum, query_sum])
    query_sum.step()
    while len(first_sum.stages) > 1:
        together([first_sum, second_sum])
    slope_normed = [
        matmul_nt(slope_query, part[:, :query_width]) for part in (weight_low, weight_high)
    ]
    first_sum.step()
    second_sum.step()
    first_sum.total, second_sum.sent, query_sum.sent, out_sum.sent = lax.optimization_barrier(
        (first_sum.total, second_sum.sent, query_sum.sent, out_sum.sent)
    )
    out_sum.step()
    second_sum.step()
    totals = [item.total for item in (first_sum, second_sum)]
    totals[1], slope_normed = lax.optimization_barrier((totals[1], slope_normed))
    slope_key = jnp.concatenate([total[:, :HEAD_WIDTH] for total in totals], 1)
    slope_key = rotate(slope_key, KEY_VALUE_HEADS, cosine, -sine)
    slope_rest = [slope_key] + [total[:, HEAD_WIDTH:] for total in totals]
    slope_rest = jnp.concatenate(slope_rest, 1).astype(bf16)
    slope_normed = jnp.concatenate(
        [
            early + matmul_nt(slope_rest, part[:, query_width:])
            for early, part in zip(slope_normed, (weight_low, weight_high))
        ],
        1,
    )
    pull_one = jax.vjp(rms_norm, inputs_turned, gain_one)[1]
    slope_inputs, grad_gain_one = pull_one(slope_normed)
    gains = jnp.stack(
        [
            matmul(grad_gain_one.astype(bf16)[None], across)[0].astype(bf16),
            relative(grad_gain_two.astype(bf16)[None])[0],
        ],
        1,
    )
    small = padded([grad_router.astype(bf16), gains])
    rest_sum = Sum(
        *(
            jnp.concatenate([grads, part], 1)
            for grads, part in zip(
                halves(normed_turned, slope_rest), (small[width // 2 :], small[: width // 2])
            )
        ),
        inward,
    )
    together([item for item in (rest_sum, query_sum) if item.stages])
    returned, slope_inputs = together(
        [item for item in (rest_sum, query_sum, out_sum) if item.stages],
        (returned, slope_inputs),
    )
    while rest_sum.stages:
        together([item for item in (rest_sum, query_sum, out_sum) if item.stages])
    for item in (query_sum, out_sum):
        while item.stages:
            item.step()
    grads_rest = rest_sum.total
    slope_high = slope_inputs.astype(bf16)
    slope_low = (slope_inputs - slope_high.astype(f32)).astype(bf16)
    grad_input = slope_middle + matmul_nt(slope_high, turn_in) + matmul_nt(slope_low, turn_in)
    grad_input = grad_input.reshape(tokens.shape)
    output = middle
    for chosen, rows in ((jnp.concatenate(chosen_slot, 1), returned.reshape(-1, width)),):
        mix = jnp.where(chosen, gates.T[:, None, :], 0.0).reshape(-1, count)
        mix_high = mix.astype(bf16)
        mix_low = (mix - mix_high.astype(f32)).astype(bf16)
        output = output + matmul_tn(mix_high, rows) + matmul_tn(mix_low, rows)
    output = output.astype(bf16).reshape(tokens.shape)
    return (
        output,
        grad_input,
        grads_rest[:, 2 * key_width + experts],
        grads_rest[:, 2 * key_width + experts + 1],
        query_sum.total,
        grads_rest[:, :key_width],
        grads_rest[:, key_width : 2 * key_width],
        out_sum.total,
        grads_rest[:, 2 * key_width : 2 * key_width + experts],
        grad_gate[None],
        grad_up[None],
        grad_down[None],
    )


def solution(mesh):
    rows = P("seq", "ctx", None)
    shard = P(("seq", "ctx"), None)
    vector = P(("seq", "ctx"))
    expert = P("ctx", "seq", None)
    return jax.shard_map(
        body,
        mesh=mesh,
        in_specs=(rows, rows, rows, P("seq", "ctx"), P("seq", None), vector, vector)
        + (shard,) * 5
        + (expert,) * 3,
        out_specs=(rows, rows, vector, vector) + (shard,) * 5 + (expert,) * 3,
        check_vma=False,
    )
```

```python
import functools
import math

import jax
import jax.numpy as jnp
from jax import lax
from jax.experimental import pallas as pl
from jax.experimental.pallas import tpu as pltpu
from jax.sharding import PartitionSpec as P

QUERY_HEADS = 12
KEY_VALUE_HEADS = 2
HEAD_WIDTH = 128
TOP = 4
PIC = 256
NPIC = 4
LANES = 128
GROUPS = QUERY_HEADS // KEY_VALUE_HEADS
QUERY_WIDTH = QUERY_HEADS * HEAD_WIDTH
KEY_WIDTH = KEY_VALUE_HEADS * HEAD_WIDTH
SCALE = 1.0 / math.sqrt(HEAD_WIDTH)
EXP2_SCALE = SCALE * math.log2(math.e)
BLOCKS = 2
SKEW = 1
VMEM_BYTES = 48 << 20

epsilon = 1e-06
rope_base = 10000.0
big_negative = -1e30
bf16 = jnp.bfloat16
f32 = jnp.float32


def matmul(left, right):
    return jnp.dot(left, right, preferred_element_type=f32)


def matmul_nt(left, right):
    return lax.dot_general(left, right, (((1,), (1,)), ((), ())), preferred_element_type=f32)


def matmul_tn(left, right):
    return lax.dot_general(left, right, (((0,), (0,)), ((), ())), preferred_element_type=f32)


def rms_scale(rows):
    return lax.rsqrt(jnp.mean(rows * rows, -1, keepdims=True) + epsilon)


def rms_norm(rows, gain):
    return rows * rms_scale(rows) * gain


def rope_tables(positions, head_size):
    half = head_size // 2
    inverse = rope_base ** (-(jnp.arange(half, dtype=f32) * 2.0 / head_size))
    angles = positions.astype(f32)[:, None] * inverse[None, :]
    return (jnp.cos(angles), jnp.sin(angles))


def rotate(rows, heads, cosine, sine):
    shaped = rows.reshape(rows.shape[0], heads, HEAD_WIDTH)
    half = HEAD_WIDTH // 2
    first, second = shaped[..., :half], shaped[..., half:]
    cosine, sine = cosine[:, None, :], sine[:, None, :]
    turned = jnp.concatenate(
        [first * cosine - second * sine, second * cosine + first * sine], -1
    )
    return turned.reshape(rows.shape)


def bits(axis):
    size = lax.axis_size(axis)
    return [(axis, 1 << place) for place in reversed(range(size.bit_length() - 1))]


def swap(block, axis, bit):
    size = lax.axis_size(axis)
    return lax.ppermute(block, axis, [(index, index ^ bit) for index in range(size)])


def gather_blocks(block, stages, order, arrived=None):
    held = []
    for stage in stages:
        axis, bit = stage
        other = swap(block, axis, bit)
        if arrived is not None and stage == stages[-1]:
            other = arrived(other)
        upper = (lax.axis_index(axis) & bit) > 0
        place = sum(order.index(known) < order.index(stage) for known in held)
        block = jnp.stack(
            [jnp.where(upper, other, block), jnp.where(upper, block, other)], place
        )
        held.append(stage)
    return block


class Sum:
    def __init__(self, sent, kept, stages):
        self.sent, self.kept, self.stages = sent, kept, list(stages)

    def step(self):
        axis, bit = self.stages.pop(0)
        other = swap(self.sent, axis, bit)
        if not self.stages:
            self.total = self.kept.astype(f32) + other.astype(f32)
            return
        half = self.kept.shape[0] // 2
        self.sent = (self.kept[half:].astype(f32) + other[half:].astype(f32)).astype(bf16)
        self.kept = (self.kept[:half].astype(f32) + other[:half].astype(f32)).astype(bf16)


def together(sums, also=()):
    for item in sums:
        item.step()
    live = [item for item in sums if item.stages]
    sent, also = lax.optimization_barrier(([item.sent for item in live], also))
    for item, block in zip(live, sent):
        item.sent = block
    return also


def flips(stages, sizes):
    masks = []
    for block in range(1 << len(stages)):
        mask = 0
        for place, (axis, bit) in enumerate(stages):
            if (block >> (len(stages) - 1 - place)) & 1:
                mask |= bit * sizes[axis]
        masks.append(mask)
    return masks


def visible_keys(meta, step, stretch):
    span = BLOCKS * stretch
    keys = step * span + lax.broadcasted_iota(jnp.int32, (span, 1), 0)
    queries = meta[0] * stretch + lax.broadcasted_iota(jnp.int32, (1, stretch), 1)

    def label(positions):
        found = jnp.zeros(positions.shape, jnp.int32)
        for index in range(NPIC):
            start = meta[1 + index]
            inside = (positions >= start) & (positions < start + PIC)
            found = jnp.where(inside, index + 1, found)
        return found

    query_label = label(queries)
    return (keys <= queries) | ((label(keys) == query_label) & (query_label > 0))


def for_each_step(meta, stretch, steps, process, skip=None):
    span = BLOCKS * stretch
    low, high = meta[0] * stretch, (meta[0] + 1) * stretch

    def turn(step, carry):
        needed = step * span < high + PIC - 1
        edge = (step + 1) * span > low

        @pl.when(needed & edge)
        def _():
            process(step, True)

        @pl.when(needed & jnp.logical_not(edge))
        def _():
            process(step, False)

        if skip is not None:

            @pl.when(jnp.logical_not(needed))
            def _():
                skip(step)

        return carry

    lax.fori_loop(0, steps, turn, 0)


def head_columns(head, start=0):
    return slice(start + head * HEAD_WIDTH, start + (head + 1) * HEAD_WIDTH)


def attend_kernel(meta, query, key_value, out, log_total, peak, total, accum):
    stretch = query.shape[0]
    span = BLOCKS * stretch
    peak[...] = jnp.full(peak.shape, big_negative, f32)
    total[...] = jnp.zeros(total.shape, f32)
    accum[...] = jnp.zeros(accum.shape, f32)

    def process(step, edge):
        rows = pl.ds(pl.multiple_of(step * span, span), span)
        if edge:
            visible = visible_keys(meta, step, stretch)
        keys, values = [], []
        for group in range(KEY_VALUE_HEADS):
            keys.append(key_value[rows, head_columns(group)])
            turned = key_value[rows, head_columns(group, KEY_WIDTH)].T
            values.append(jnp.concatenate([turned, jnp.ones((16, span), bf16)], 0))

        def score(head):
            scores = matmul_nt(keys[head // GROUPS], query[:, head_columns(head)])
            if edge:
                scores = jnp.where(visible, scores, big_negative)
            old = peak[head : head + 1, :]
            return scores, old, jnp.maximum(old, jnp.max(scores, 0, keepdims=True))

        def weigh(head, scores, old, new):
            weights = jnp.exp2((scores - new) * EXP2_SCALE).astype(bf16)
            shrink = jnp.exp2((old - new) * EXP2_SCALE)
            sums = matmul(values[head // GROUPS], weights)
            row, columns = slice(head, head + 1), head_columns(head)
            peak[row, :] = new
            total[row, :] = total[row, :] * shrink + sums[HEAD_WIDTH : HEAD_WIDTH + 1]
            accum[columns, :] = accum[columns, :] * shrink + sums[:HEAD_WIDTH]

        waiting = []
        for head in range(QUERY_HEADS):
            waiting.append((head, *score(head)))
            if len(waiting) > 2:
                weigh(*waiting.pop(0))
        for item in waiting:
            weigh(*item)

    for_each_step(meta, stretch, key_value.shape[0] // span, process)
    for head in range(QUERY_HEADS):
        row, columns = slice(head, head + 1), head_columns(head)
        out[:, columns] = (accum[columns, :] / total[row, :]).T
        log_total[row, :] = peak[row, :] * EXP2_SCALE + jnp.log2(total[row, :])


def attend_back_kernel(
    order,
    group,
    meta,
    query,
    slope,
    log_total,
    mixed,
    key_value,
    slope_query,
    out,
    accum,
    delta,
):
    stretch = query.shape[0]
    span = BLOCKS * stretch
    accum[...] = jnp.zeros(accum.shape, f32)
    for index in range(GROUPS):
        columns = head_columns(group * GROUPS + index)
        product = slope[:, columns].astype(f32) * mixed[:, columns]
        delta[index : index + 1, :] = jnp.sum(product.T, 0, keepdims=True)

    def store(step, part, columns, block):
        flip = jnp.bitwise_xor(BLOCKS * step + part, meta[0])
        first, *others = order
        place = 0
        for index, bit in enumerate(others):
            place = place + ((flip // bit) & 1) * (1 << (len(others) - 1 - index))
        place = pl.ds(pl.multiple_of(place * stretch, stretch), stretch)
        out[(flip // first) & 1, place, columns] = block

    def process(step, edge):
        rows = pl.ds(pl.multiple_of(step * span, span), span)
        if edge:
            visible = visible_keys(meta, step, stretch)
        keys = key_value[rows, head_columns(group)]
        values = key_value[rows, head_columns(group, KEY_WIDTH)]
        keys_turned = keys.T

        def slopes_of(index):
            columns = head_columns(group * GROUPS + index)
            row = slice(group * GROUPS + index, group * GROUPS + index + 1)
            scores = matmul_nt(keys, query[:, columns])
            probs = jnp.exp2(scores * EXP2_SCALE - log_total[row, :])
            if edge:
                probs = jnp.where(visible, probs, 0.0)
            slope_probs = matmul_nt(values, slope[:, columns])
            slope_scores = (probs * (slope_probs - delta[index : index + 1, :])).astype(bf16)
            return index, probs.astype(bf16), slope_scores

        slope_k = jnp.zeros((span, HEAD_WIDTH), f32)
        slope_v = jnp.zeros((span, HEAD_WIDTH), f32)
        waiting = []
        for index in range(GROUPS + SKEW):
            if index < GROUPS:
                waiting.append(slopes_of(index))
            if index >= SKEW:
                own, probs, slope_scores = waiting.pop(0)
                columns, place = head_columns(group * GROUPS + own), head_columns(own)
                slope_v = slope_v + matmul(probs, slope[:, columns])
                slope_k = slope_k + matmul(slope_scores, query[:, columns])
                accum[place, :] = accum[place, :] + matmul(keys_turned, slope_scores)
        slope_k, slope_v = (slope_k * SCALE).astype(bf16), slope_v.astype(bf16)
        for which, block in enumerate((slope_k, slope_v)):
            for part in range(BLOCKS):
                own = block[part * stretch : (part + 1) * stretch]
                store(step, part, head_columns(which), own)

    def skip(step):
        for part in range(BLOCKS):
            store(step, part, slice(None), jnp.zeros((stretch, 2 * HEAD_WIDTH), bf16))

    for_each_step(meta, stretch, key_value.shape[0] // span, process, skip)
    for index in range(GROUPS):
        columns = head_columns(index)
        slope_query[:, columns] = (accum[columns, :] * SCALE).T


def expert_kernel(
    which,
    rows,
    slopes,
    chosen,
    gate_up,
    down,
    router,
    hidden_out,
    result_out,
    gates_out,
    slots_out,
    pre_out,
    slope_out,
):
    hidden_width = down.shape[0]
    incoming = rows[...]
    logits = jnp.where(chosen[...] > 0, matmul(incoming, router[...]), big_negative)
    shares = jnp.exp(logits - jnp.max(logits, -1, keepdims=True))
    shares = jnp.where(chosen[...] > 0, shares, 0.0)
    column = lax.broadcasted_iota(jnp.int32, shares.shape, 1)
    own = jnp.sum(jnp.where(column == which[0], shares, 0.0), -1, keepdims=True)
    gates = own / jnp.maximum(jnp.sum(shares, -1, keepdims=True), 1e-30)
    slots = (gates * slopes[...].astype(f32)).astype(bf16)
    slots_out[...] = slots
    pre = matmul(incoming, gate_up[...])
    gate, up = pre[:, :hidden_width], pre[:, hidden_width:]
    root, cubic = math.sqrt(2.0 / math.pi), 0.044715
    square = gate * gate
    bend = jnp.tanh(root * (gate + cubic * gate * square))
    gelu = 0.5 * gate * (1.0 + bend)
    rise = 0.5 * (1.0 + bend) + 0.5 * gate * (1.0 - bend * bend) * root * (
        1.0 + 3.0 * cubic * square
    )
    hidden = (gelu * up).astype(bf16)
    hidden_out[...] = hidden
    result = matmul(hidden, down[...]).astype(bf16)
    result_out[...] = result
    gates_out[...] = jnp.sum(slopes[...].astype(f32) * result.astype(f32), -1, keepdims=True)
    slope_hidden = matmul_nt(slots, down[...])
    slope_pre = jnp.concatenate([slope_hidden * up * rise, slope_hidden * gelu], 1).astype(bf16)
    pre_out[...] = slope_pre
    slope_out[...] = matmul_nt(slope_pre, gate_up[...]).astype(bf16)


def expert(which, rows, slopes, chosen, gate_up, down, router):
    count, width = rows.shape
    hidden_width = down.shape[0]
    block = count // 2

    def tile(columns):
        return pl.BlockSpec((block, columns), lambda step: (step, 0))

    def whole(array):
        return pl.BlockSpec(array.shape, lambda step: (0, 0))

    shapes = [(hidden_width, bf16), (width, bf16), (1, f32), (width, bf16)]
    shapes += [(2 * hidden_width, bf16), (width, bf16)]
    return pl.pallas_call(
        expert_kernel,
        grid=(2,),
        out_shape=[jax.ShapeDtypeStruct((count, columns), kind) for columns, kind in shapes],
        in_specs=[
            pl.BlockSpec(memory_space=pltpu.SMEM),
            tile(width),
            tile(width),
            tile(LANES),
            whole(gate_up),
            whole(down),
            whole(router),
        ],
        out_specs=[tile(columns) for columns, _ in shapes],
        compiler_params=pltpu.CompilerParams(vmem_limit_bytes=VMEM_BYTES),
        cost_estimate=pl.CostEstimate(
            flops=12 * count * width * hidden_width,
            bytes_accessed=20 * count * width,
            transcendentals=count * hidden_width,
        ),
        name="expert",
    )(which, rows, slopes, chosen, gate_up, down, router)


def attention_call(kernel, outs, scratch, products, name, meta, *operands):
    vmem = pl.BlockSpec(memory_space=pltpu.VMEM)
    pairs = QUERY_HEADS * operands[0].shape[0] * operands[-1].shape[0]
    return pl.pallas_call(
        kernel,
        out_shape=outs,
        in_specs=[pl.BlockSpec(memory_space=pltpu.SMEM)] + [vmem] * len(operands),
        out_specs=(vmem,) * len(outs),
        scratch_shapes=[pltpu.VMEM(*shape) for shape in scratch],
        compiler_params=pltpu.CompilerParams(vmem_limit_bytes=VMEM_BYTES),
        cost_estimate=pl.CostEstimate(
            flops=products * pairs, bytes_accessed=QUERY_WIDTH * 1024, transcendentals=0
        ),
        name=name,
    )(meta, *operands)


def attend(meta, query, key_value):
    stretch = query.shape[0]
    stats = (QUERY_HEADS, stretch)
    outs = (
        jax.ShapeDtypeStruct((stretch, QUERY_WIDTH), f32),
        jax.ShapeDtypeStruct(stats, f32),
    )
    scratch = [(stats, f32), (stats, f32), ((QUERY_WIDTH, stretch), f32)]
    return attention_call(attend_kernel, outs, scratch, 2, "attend", meta, query, key_value)


def attend_back(order, group, meta, query, slope, log_total, mixed, key_value):
    stretch, rows = query.shape[0], key_value.shape[0]
    group_width = GROUPS * HEAD_WIDTH
    outs = (
        jax.ShapeDtypeStruct((stretch, group_width), f32),
        jax.ShapeDtypeStruct((2, rows // 2, 2 * HEAD_WIDTH), bf16),
    )
    operands = (meta, query, slope, log_total, mixed, key_value)
    scratch = [((group_width, stretch), f32), ((GROUPS, stretch), f32)]
    kernel = functools.partial(attend_back_kernel, order, group)
    return attention_call(kernel, outs, scratch, 2, "attend_back", *operands)


def body(
    tokens,
    cotangent,
    routes,
    fill_order,
    pic_starts,
    attn_gain,
    moe_gain,
    w_query,
    key_projection,
    value_projection,
    w_out,
    w_router,
    expert_gate,
    expert_up,
    expert_down,
):
    sequences, stretch, width = tokens.shape
    count = sequences * stretch
    parts = lax.axis_size("ctx")
    experts = parts
    capacity = (5 * count * TOP + 4 * experts - 1) // (4 * experts)
    query_width, key_width = QUERY_WIDTH, KEY_WIDTH
    hidden_width = expert_gate.shape[2]
    seq_bits, ctx_bits = bits("seq"), bits("ctx")
    all_bits = seq_bits + ctx_bits
    inward = ctx_bits[-1:] + seq_bits[::-1] + ctx_bits[-2::-1]
    sizes = {"seq": parts, "ctx": 1}
    me = lax.axis_index("seq") * parts + lax.axis_index("ctx")

    def padded(columns):
        block = jnp.concatenate(columns, 1)
        return jnp.pad(block, ((0, 0), (0, LANES - block.shape[1])))

    own_rows = w_query.shape[0]

    def feature(stages):
        owner = jnp.bitwise_xor(jnp.array(flips(stages, sizes), jnp.int32), me)
        return (owner[:, None] * own_rows + jnp.arange(own_rows, dtype=jnp.int32)).reshape(-1)

    def same(left, right):
        return (left[:, None] == right[None, :]).astype(bf16)

    turns = ctx_bits[:-2] + seq_bits + ctx_bits[-2:]
    natural = jnp.arange(width, dtype=jnp.int32)
    gathered, summed = feature(turns[::-1]), feature(inward)
    turn, turn_in, across = same(natural, summed), same(natural, gathered), same(gathered, summed)

    def relative(rows):
        return matmul(rows, turn).astype(bf16)

    def halves(left, right):
        middle = left.shape[1] // 2
        sent = matmul_tn(left[:, middle:], right).astype(bf16)
        return sent, matmul_tn(left[:, :middle], right).astype(bf16)

    picks = routes.reshape(count, TOP)
    order = fill_order.reshape(count)
    routed = jnp.any(picks[:, :, None] == jnp.arange(experts, dtype=jnp.int32), 1)
    earlier = (order[None, :] < order[:, None]).astype(bf16)
    place = matmul(earlier, routed.astype(bf16)).astype(jnp.int32)
    place = jnp.where(routed, place, capacity)
    half = capacity // 2
    chosen_slot = [
        place.T[:, None, :]
        == (begin + jnp.arange(half, dtype=jnp.int32))[None, :, None]
        for begin in (0, half)
    ]
    slot_map = [chosen.astype(bf16).reshape(-1, count) for chosen in chosen_slot]

    def exchange_rows(rows):
        rows = rows.reshape(experts, half, width)
        rows = lax.all_to_all(rows, "ctx", split_axis=0, concat_axis=0, tiled=True)
        return rows.reshape(-1, width)

    out_slope = cotangent.reshape(count, width)
    slot_routes = jnp.concatenate(
        [matmul(part, routed.astype(bf16)).reshape(experts, half, experts) for part in slot_map], 1
    ).astype(bf16)
    slot_routes = lax.all_to_all(slot_routes, "ctx", split_axis=0, concat_axis=0, tiled=True)
    slot_routes = jnp.pad(slot_routes, ((0, 0), (0, 0), (0, LANES - experts)))
    slot_routes = [
        slot_routes[:, begin : begin + half].reshape(-1, LANES) for begin in (0, half)
    ]
    slope_rows = [matmul(part, out_slope).astype(bf16) for part in slot_map]
    slope_rows = jnp.concatenate([part.reshape(experts, half, width) for part in slope_rows], 1)

    block = jnp.concatenate(
        [
            w_query,
            key_projection,
            value_projection,
            padded([attn_gain[:, None]]),
            w_out,
            padded([w_router, moe_gain[:, None]]),
        ],
        1,
    )
    first_width = query_width + 2 * key_width + LANES
    expert_parts = [expert_gate[0], expert_up[0]]
    for index, stage in enumerate(turns):
        other = swap(block if index < 2 else mine, *stage)
        if index in (1, 3) and len(seq_bits) == 1:
            part = index // 2
            other, expert_parts[part] = lax.optimization_barrier(
                (other, (expert_parts[part], swap(expert_parts[part], *seq_bits[0])))
            )
        if index < 2:
            block = jnp.concatenate([block, other], 0)
        if index == 1:
            block, slope_rows = lax.optimization_barrier((block, slope_rows))
            slope_rows = lax.all_to_all(slope_rows, "ctx", split_axis=0, concat_axis=0, tiled=True)
            mine, second_set = block[:, :first_width], block[:, first_width:]
        if index > 2:
            arrived = swap(second_set, *turns[index - 1])
            if index < len(turns) - 1:
                other, arrived = lax.optimization_barrier((other, arrived))
            second_set = jnp.concatenate([second_set, arrived], 0)
        if 2 <= index < len(turns) - 1:
            mine = jnp.concatenate([mine, other], 0)
    inputs = tokens.reshape(count, width)
    inputs_turned = matmul(inputs, turn_in)
    inputs = inputs.astype(f32)
    inputs_scaled = inputs_turned * rms_scale(inputs)
    mine, other, slope_rows, slot_routes, inputs_scaled = lax.optimization_barrier(
        (mine, other, slope_rows, slot_routes, inputs_scaled)
    )
    slope_rows = [
        slope_rows[:, begin : begin + half].reshape(-1, width) for begin in (0, half)
    ]
    qkv_width = query_width + 2 * key_width
    weight_low, weight_high = mine[:, :qkv_width], other[:, :qkv_width]
    gain_one = jnp.concatenate([mine[:, qkv_width], other[:, qkv_width]]).astype(f32)

    def whole_expert(part):
        if isinstance(part, tuple):
            own, other = part
            upper = lax.axis_index("seq") > 0
            pair = [jnp.where(upper, other, own), jnp.where(upper, own, other)]
            return jnp.concatenate(pair, 0)
        return gather_blocks(part, seq_bits[::-1], seq_bits).reshape(-1, part.shape[1])

    gate_up = jnp.concatenate([whole_expert(part) for part in expert_parts], 1)
    second_set = jnp.concatenate([second_set, swap(second_set, *turns[-1])], 0)
    second_set = matmul(turn_in, second_set).astype(bf16)
    full_out = second_set[:, :width]
    full_router = second_set[:, width : width + experts]
    gain_two = second_set[:, width + experts].astype(f32)

    positions = lax.axis_index("ctx") * stretch + jnp.arange(stretch, dtype=jnp.int32)
    cosine, sine = rope_tables(positions, HEAD_WIDTH)
    normed = (inputs_scaled * gain_one).astype(bf16)

    def project(columns):
        low = matmul(normed[:, : width // 2], weight_low[:, columns])
        return low + matmul(normed[:, width // 2 :], weight_high[:, columns])

    projected = project(slice(query_width, None))
    key_rows = rotate(projected[:, :key_width], KEY_VALUE_HEADS, cosine, sine)
    key_values = lax.all_gather(
        jnp.concatenate([key_rows, projected[:, key_width:]], 1).astype(bf16),
        "ctx",
        axis=0,
        tiled=True,
    )
    projected = project(slice(0, query_width))
    query_rows = rotate(projected, QUERY_HEADS, cosine, sine).astype(bf16)
    meta = jnp.concatenate([lax.axis_index("ctx").astype(jnp.int32)[None], pic_starts[0]])
    mixed_heads, log_total = attend(meta, query_rows, key_values)

    def with_attention(other):
        nonlocal mixed_heads
        mixed_heads, other = lax.optimization_barrier((mixed_heads, other))
        return other

    down = gather_blocks(
        lax.optimization_barrier((expert_down[0], gain_one))[0],
        seq_bits[::-1],
        seq_bits,
        with_attention,
    ).reshape(-1, width)
    attended = mixed_heads.astype(bf16)

    middle = inputs + matmul(attended, full_out)
    enter = rms_norm(middle, gain_two).astype(bf16)
    arrived = [exchange_rows(matmul(part, enter).astype(bf16)) for part in slot_map]

    def gates_of(rows, chosen):
        logits = jnp.where(chosen, matmul(rows, full_router), big_negative)
        shares = jnp.exp(logits - jnp.max(logits, -1, keepdims=True))
        shares = jnp.where(chosen, shares, 0.0)
        return shares / jnp.maximum(jnp.sum(shares, -1, keepdims=True), 1e-30)

    gates = gates_of(enter, routed)

    attended_turned, enter_turned = map(relative, (attended, enter))
    normed_turned = matmul(normed, across).astype(bf16)
    arrived[0], attended_turned, enter_turned, normed_turned = lax.optimization_barrier(
        (arrived[0], attended_turned, enter_turned, normed_turned)
    )
    which = lax.axis_index("ctx").astype(jnp.int32)[None]
    router = second_set[:, width:]
    hidden, result, slope_gates, slope_slots, slope_pre, slope_arrived = ([] for _ in range(6))
    for index in range(2):
        made = list(expert(
            which, arrived[index], slope_rows[index], slot_routes[index], gate_up, down, router)
        )
        if index == 0:
            arrived[1], made[-1] = lax.optimization_barrier((arrived[1], made[-1]))
        for kept, item in zip(
            (hidden, result, slope_gates, slope_slots, slope_pre, slope_arrived), made
        ):
            kept.append(item)
    returned_slopes = [exchange_rows(slope_arrived[0])]
    slope_gates = jnp.concatenate([item.reshape(experts, half) for item in slope_gates], 1)
    slope_gates, returned_slopes[0] = lax.optimization_barrier((slope_gates, returned_slopes[0]))
    returned_gates = lax.all_to_all(slope_gates, "ctx", split_axis=0, concat_axis=0, tiled=True)
    slope_arrived[1], returned_gates, slope_pre, slope_slots = lax.optimization_barrier(
        (slope_arrived[1], returned_gates, slope_pre, slope_slots)
    )
    returned_slopes.append(exchange_rows(slope_arrived[1]))
    grad_gate, grad_up = (
        sum(matmul_tn(arrived[i], slope_pre[i][:, columns]) for i in range(2)).astype(bf16)
        for columns in (slice(0, hidden_width), slice(hidden_width, None))
    )
    grad_down = sum(matmul_tn(hidden[i], slope_slots[i]) for i in range(2)).astype(bf16)
    def sector_halves(grads):
        return grads.reshape([2] * len(seq_bits) + [-1, grads.shape[1]])

    def sector_sum(blocks, arrived):
        for axis, bit in seq_bits:
            mine = ((lax.axis_index(axis) & bit) > 0).astype(jnp.int32)
            sent = lax.dynamic_index_in_dim(blocks, 1 - mine, 0, keepdims=False)
            kept = lax.dynamic_index_in_dim(blocks, mine, 0, keepdims=False)
            other = swap(sent.astype(bf16), axis, bit)
            if (axis, bit) == seq_bits[-1]:
                other = arrived(other)
            blocks = kept.astype(f32) + other.astype(f32)
        return blocks

    def with_slopes(other):
        nonlocal grad_gate, grad_up
        returned_slopes[1], other, grad_gate, grad_up = lax.optimization_barrier(
            (returned_slopes[1], other, grad_gate, grad_up)
        )
        return other

    grad_down = sector_sum(sector_halves(grad_down), with_slopes)
    returned = jnp.concatenate([part.reshape(experts, half, width) for part in result], 1)
    returned = lax.all_to_all(returned, "ctx", split_axis=0, concat_axis=0, tiled=True)

    slope_gate = 0.0
    for index, chosen in enumerate(chosen_slot):
        part = returned_gates[:, index * half : (index + 1) * half]
        slope_gate = slope_gate + jnp.sum(jnp.where(chosen, part[:, :, None], 0.0), 1).T
    slope_logits = gates * (slope_gate - jnp.sum(gates * slope_gate, -1, keepdims=True))
    slope_logits = slope_logits.astype(bf16)
    grad_router = matmul_tn(enter_turned, slope_logits)
    slope_enter = matmul_nt(slope_logits, full_router)
    for part, rows in zip(slot_map, returned_slopes):
        slope_enter = slope_enter + matmul_tn(part, rows)

    pull_two = jax.vjp(rms_norm, middle, gain_two)[1]
    slope_middle, grad_gain_two = pull_two(slope_enter)
    slope_middle = out_slope.astype(f32) + slope_middle
    slope_branch = slope_middle.astype(bf16)
    slope_attended = matmul_nt(slope_branch, full_out).astype(bf16)

    out_sum = Sum(*halves(attended_turned, slope_branch), inward)
    kv_order = ctx_bits[::-1]

    def back(group, meta):
        order = [bit for _, bit in kv_order]
        return attend_back(
            order, group, meta, query_rows, slope_attended, log_total, mixed_heads, key_values
        )

    first_q, first_kv = back(0, meta)

    def after_first(other):
        nonlocal first_q, first_kv, meta, grad_up
        first_q, first_kv, meta, grad_up, other = lax.optimization_barrier(
            (first_q, first_kv, meta, grad_up, other)
        )
        return other

    grad_gate = sector_sum(sector_halves(grad_gate), after_first)
    first_sum = Sum(first_kv[1], first_kv[0], kv_order)
    first_sum.step()
    second_q, second_kv = back(1, meta)

    def after_second(other):
        nonlocal second_q, second_kv
        second_q, second_kv, first_sum.sent, other = lax.optimization_barrier(
            (second_q, second_kv, first_sum.sent, other)
        )
        return other

    grad_up = sector_sum(sector_halves(grad_up), after_second)
    second_sum = Sum(second_kv[1], second_kv[0], kv_order)
    slope_query = jnp.concatenate([first_q, second_q], 1)
    slope_query = rotate(slope_query, QUERY_HEADS, cosine, -sine).astype(bf16)
    query_sum = Sum(*halves(normed_turned, slope_query), inward)
    out_sum.step()
    together([first_sum, second_sum, query_sum])
    query_sum.step()
    while len(first_sum.stages) > 1:
        together([first_sum, second_sum])
    slope_normed = [
        matmul_nt(slope_query, part[:, :query_width]) for part in (weight_low, weight_high)
    ]
    first_sum.step()
    second_sum.step()
    first_sum.total, second_sum.sent, query_sum.sent, out_sum.sent, returned = (
        lax.optimization_barrier(
            (first_sum.total, second_sum.sent, query_sum.sent, out_sum.sent, returned)
        )
    )
    output = middle
    for chosen, rows in ((jnp.concatenate(chosen_slot, 1), returned.reshape(-1, width)),):
        mix = jnp.where(chosen, gates.T[:, None, :], 0.0).reshape(-1, count)
        mix_high = mix.astype(bf16)
        mix_low = (mix - mix_high.astype(f32)).astype(bf16)
        output = output + matmul_tn(mix_high, rows) + matmul_tn(mix_low, rows)
    output = output.astype(bf16).reshape(tokens.shape)
    out_sum.step()
    second_sum.step()
    totals = [item.total for item in (first_sum, second_sum)]
    totals[1], slope_normed, output = lax.optimization_barrier(
        (totals[1], slope_normed, output)
    )
    slope_key = jnp.concatenate([total[:, :HEAD_WIDTH] for total in totals], 1)
    slope_key = rotate(slope_key, KEY_VALUE_HEADS, cosine, -sine)
    slope_rest = [slope_key] + [total[:, HEAD_WIDTH:] for total in totals]
    slope_rest = jnp.concatenate(slope_rest, 1).astype(bf16)
    slope_normed = jnp.concatenate(
        [
            early + matmul_nt(slope_rest, part[:, query_width:])
            for early, part in zip(slope_normed, (weight_low, weight_high))
        ],
        1,
    )
    pull_one = jax.vjp(rms_norm, inputs_turned, gain_one)[1]
    slope_inputs, grad_gain_one = pull_one(slope_normed)
    gains = jnp.stack(
        [
            matmul(grad_gain_one.astype(bf16)[None], across)[0].astype(bf16),
            relative(grad_gain_two.astype(bf16)[None])[0],
        ],
        1,
    )
    small = padded([grad_router.astype(bf16), gains])
    rest_sum = Sum(
        *(
            jnp.concatenate([grads, part], 1)
            for grads, part in zip(
                halves(normed_turned, slope_rest), (small[width // 2 :], small[: width // 2])
            )
        ),
        inward,
    )
    together([item for item in (rest_sum, query_sum) if item.stages])
    slope_inputs = together(
        [item for item in (rest_sum, query_sum, out_sum) if item.stages], slope_inputs
    )
    while rest_sum.stages:
        together([item for item in (rest_sum, query_sum, out_sum) if item.stages])
    for item in (query_sum, out_sum):
        while item.stages:
            item.step()
    grads_rest = rest_sum.total
    slope_high = slope_inputs.astype(bf16)
    slope_low = (slope_inputs - slope_high.astype(f32)).astype(bf16)
    grad_input = slope_middle + matmul_nt(slope_high, turn_in) + matmul_nt(slope_low, turn_in)
    grad_input = grad_input.reshape(tokens.shape)
    return (
        output,
        grad_input,
        grads_rest[:, 2 * key_width + experts],
        grads_rest[:, 2 * key_width + experts + 1],
        query_sum.total,
        grads_rest[:, :key_width],
        grads_rest[:, key_width : 2 * key_width],
        out_sum.total,
        grads_rest[:, 2 * key_width : 2 * key_width + experts],
        grad_gate[None],
        grad_up[None],
        grad_down[None],
    )


def solution(mesh):
    rows = P("seq", "ctx", None)
    shard = P(("seq", "ctx"), None)
    vector = P(("seq", "ctx"))
    expert = P("ctx", "seq", None)
    return jax.shard_map(
        body,
        mesh=mesh,
        in_specs=(rows, rows, rows, P("seq", "ctx"), P("seq", None), vector, vector)
        + (shard,) * 5
        + (expert,) * 3,
        out_specs=(rows, rows, vector, vector) + (shard,) * 5 + (expert,) * 3,
        check_vma=False,
    )
```

```python
import functools
import math

import jax
import jax.numpy as jnp
from jax import lax
from jax.experimental import pallas as pl
from jax.experimental.pallas import tpu as pltpu
from jax.sharding import PartitionSpec as P

QUERY_HEADS = 12
KEY_VALUE_HEADS = 2
HEAD_WIDTH = 128
TOP = 4
PIC = 256
NPIC = 4
LANES = 128
GROUPS = QUERY_HEADS // KEY_VALUE_HEADS
QUERY_WIDTH = QUERY_HEADS * HEAD_WIDTH
KEY_WIDTH = KEY_VALUE_HEADS * HEAD_WIDTH
SCALE = 1.0 / math.sqrt(HEAD_WIDTH)
EXP2_SCALE = SCALE * math.log2(math.e)
BLOCKS = 2
SKEW = 1
VMEM_BYTES = 48 << 20

epsilon = 1e-06
rope_base = 10000.0
big_negative = -1e30
bf16 = jnp.bfloat16
f32 = jnp.float32


def matmul(left, right):
    return jnp.dot(left, right, preferred_element_type=f32)


def matmul_nt(left, right):
    return lax.dot_general(left, right, (((1,), (1,)), ((), ())), preferred_element_type=f32)


def matmul_tn(left, right):
    return lax.dot_general(left, right, (((0,), (0,)), ((), ())), preferred_element_type=f32)


def rms_scale(rows):
    return lax.rsqrt(jnp.mean(rows * rows, -1, keepdims=True) + epsilon)


def rms_norm(rows, gain):
    return rows * rms_scale(rows) * gain


def rope_tables(positions, head_size):
    half = head_size // 2
    inverse = rope_base ** (-(jnp.arange(half, dtype=f32) * 2.0 / head_size))
    angles = positions.astype(f32)[:, None] * inverse[None, :]
    return (jnp.cos(angles), jnp.sin(angles))


def rotate(rows, heads, cosine, sine):
    shaped = rows.reshape(rows.shape[0], heads, HEAD_WIDTH)
    half = HEAD_WIDTH // 2
    first, second = shaped[..., :half], shaped[..., half:]
    cosine, sine = cosine[:, None, :], sine[:, None, :]
    turned = jnp.concatenate(
        [first * cosine - second * sine, second * cosine + first * sine], -1
    )
    return turned.reshape(rows.shape)


def bits(axis):
    size = lax.axis_size(axis)
    return [(axis, 1 << place) for place in reversed(range(size.bit_length() - 1))]


def swap(block, axis, bit):
    size = lax.axis_size(axis)
    return lax.ppermute(block, axis, [(index, index ^ bit) for index in range(size)])


def gather_blocks(block, stages, order, arrived=None):
    held = []
    for stage in stages:
        axis, bit = stage
        other = swap(block, axis, bit)
        if arrived is not None and stage == stages[-1]:
            other = arrived(other)
        upper = (lax.axis_index(axis) & bit) > 0
        place = sum(order.index(known) < order.index(stage) for known in held)
        block = jnp.stack(
            [jnp.where(upper, other, block), jnp.where(upper, block, other)], place
        )
        held.append(stage)
    return block


class Sum:
    def __init__(self, sent, kept, stages):
        self.sent, self.kept, self.stages = sent, kept, list(stages)

    def step(self):
        axis, bit = self.stages.pop(0)
        other = swap(self.sent, axis, bit)
        if not self.stages:
            self.total = self.kept.astype(f32) + other.astype(f32)
            return
        half = self.kept.shape[0] // 2
        self.sent = (self.kept[half:].astype(f32) + other[half:].astype(f32)).astype(bf16)
        self.kept = (self.kept[:half].astype(f32) + other[:half].astype(f32)).astype(bf16)


def together(sums, also=()):
    for item in sums:
        item.step()
    live = [item for item in sums if item.stages]
    sent, also = lax.optimization_barrier(([item.sent for item in live], also))
    for item, block in zip(live, sent):
        item.sent = block
    return also


def flips(stages, sizes):
    masks = []
    for block in range(1 << len(stages)):
        mask = 0
        for place, (axis, bit) in enumerate(stages):
            if (block >> (len(stages) - 1 - place)) & 1:
                mask |= bit * sizes[axis]
        masks.append(mask)
    return masks


def visible_keys(meta, step, stretch):
    span = BLOCKS * stretch
    keys = step * span + lax.broadcasted_iota(jnp.int32, (span, 1), 0)
    queries = meta[0] * stretch + lax.broadcasted_iota(jnp.int32, (1, stretch), 1)

    def label(positions):
        found = jnp.zeros(positions.shape, jnp.int32)
        for index in range(NPIC):
            start = meta[1 + index]
            inside = (positions >= start) & (positions < start + PIC)
            found = jnp.where(inside, index + 1, found)
        return found

    query_label = label(queries)
    return (keys <= queries) | ((label(keys) == query_label) & (query_label > 0))


def for_each_step(meta, stretch, steps, process, skip=None):
    span = BLOCKS * stretch
    low, high = meta[0] * stretch, (meta[0] + 1) * stretch

    def turn(step, carry):
        needed = step * span < high + PIC - 1
        edge = (step + 1) * span > low

        @pl.when(needed & edge)
        def _():
            process(step, True)

        @pl.when(needed & jnp.logical_not(edge))
        def _():
            process(step, False)

        if skip is not None:

            @pl.when(jnp.logical_not(needed))
            def _():
                skip(step)

        return carry

    lax.fori_loop(0, steps, turn, 0)


def head_columns(head, start=0):
    return slice(start + head * HEAD_WIDTH, start + (head + 1) * HEAD_WIDTH)


def attend_kernel(meta, query, key_value, out, log_total, peak, total, accum):
    stretch = query.shape[0]
    span = BLOCKS * stretch
    peak[...] = jnp.full(peak.shape, big_negative, f32)
    total[...] = jnp.zeros(total.shape, f32)
    accum[...] = jnp.zeros(accum.shape, f32)

    def process(step, edge):
        rows = pl.ds(pl.multiple_of(step * span, span), span)
        if edge:
            visible = visible_keys(meta, step, stretch)
        keys, values = [], []
        for group in range(KEY_VALUE_HEADS):
            keys.append(key_value[rows, head_columns(group)])
            turned = key_value[rows, head_columns(group, KEY_WIDTH)].T
            values.append(jnp.concatenate([turned, jnp.ones((16, span), bf16)], 0))

        def score(head):
            scores = matmul_nt(keys[head // GROUPS], query[:, head_columns(head)])
            if edge:
                scores = jnp.where(visible, scores, big_negative)
            old = peak[head : head + 1, :]
            return scores, old, jnp.maximum(old, jnp.max(scores, 0, keepdims=True))

        def weigh(head, scores, old, new):
            weights = jnp.exp2((scores - new) * EXP2_SCALE).astype(bf16)
            shrink = jnp.exp2((old - new) * EXP2_SCALE)
            sums = matmul(values[head // GROUPS], weights)
            row, columns = slice(head, head + 1), head_columns(head)
            peak[row, :] = new
            total[row, :] = total[row, :] * shrink + sums[HEAD_WIDTH : HEAD_WIDTH + 1]
            accum[columns, :] = accum[columns, :] * shrink + sums[:HEAD_WIDTH]

        waiting = []
        for head in range(QUERY_HEADS):
            waiting.append((head, *score(head)))
            if len(waiting) > 2:
                weigh(*waiting.pop(0))
        for item in waiting:
            weigh(*item)

    for_each_step(meta, stretch, key_value.shape[0] // span, process)
    for head in range(QUERY_HEADS):
        row, columns = slice(head, head + 1), head_columns(head)
        out[:, columns] = (accum[columns, :] / total[row, :]).T
        log_total[row, :] = peak[row, :] * EXP2_SCALE + jnp.log2(total[row, :])


def attend_back_kernel(
    order,
    group,
    meta,
    query,
    slope,
    log_total,
    mixed,
    key_value,
    slope_query,
    out,
    accum,
    delta,
):
    stretch = query.shape[0]
    span = BLOCKS * stretch
    accum[...] = jnp.zeros(accum.shape, f32)
    for index in range(GROUPS):
        columns = head_columns(group * GROUPS + index)
        product = slope[:, columns].astype(f32) * mixed[:, columns]
        delta[index : index + 1, :] = jnp.sum(product.T, 0, keepdims=True)

    def store(step, part, columns, block):
        flip = jnp.bitwise_xor(BLOCKS * step + part, meta[0])
        first, *others = order
        place = 0
        for index, bit in enumerate(others):
            place = place + ((flip // bit) & 1) * (1 << (len(others) - 1 - index))
        place = pl.ds(pl.multiple_of(place * stretch, stretch), stretch)
        out[(flip // first) & 1, place, columns] = block

    def process(step, edge):
        rows = pl.ds(pl.multiple_of(step * span, span), span)
        if edge:
            visible = visible_keys(meta, step, stretch)
        keys = key_value[rows, head_columns(group)]
        values = key_value[rows, head_columns(group, KEY_WIDTH)]
        keys_turned = keys.T

        def slopes_of(index):
            columns = head_columns(group * GROUPS + index)
            row = slice(group * GROUPS + index, group * GROUPS + index + 1)
            scores = matmul_nt(keys, query[:, columns])
            probs = jnp.exp2(scores * EXP2_SCALE - log_total[row, :])
            if edge:
                probs = jnp.where(visible, probs, 0.0)
            slope_probs = matmul_nt(values, slope[:, columns])
            slope_scores = (probs * (slope_probs - delta[index : index + 1, :])).astype(bf16)
            return index, probs.astype(bf16), slope_scores

        slope_k = jnp.zeros((span, HEAD_WIDTH), f32)
        slope_v = jnp.zeros((span, HEAD_WIDTH), f32)
        waiting = []
        for index in range(GROUPS + SKEW):
            if index < GROUPS:
                waiting.append(slopes_of(index))
            if index >= SKEW:
                own, probs, slope_scores = waiting.pop(0)
                columns, place = head_columns(group * GROUPS + own), head_columns(own)
                slope_v = slope_v + matmul(probs, slope[:, columns])
                slope_k = slope_k + matmul(slope_scores, query[:, columns])
                accum[place, :] = accum[place, :] + matmul(keys_turned, slope_scores)
        slope_k, slope_v = (slope_k * SCALE).astype(bf16), slope_v.astype(bf16)
        for which, block in enumerate((slope_k, slope_v)):
            for part in range(BLOCKS):
                own = block[part * stretch : (part + 1) * stretch]
                store(step, part, head_columns(which), own)

    def skip(step):
        for part in range(BLOCKS):
            store(step, part, slice(None), jnp.zeros((stretch, 2 * HEAD_WIDTH), bf16))

    for_each_step(meta, stretch, key_value.shape[0] // span, process, skip)
    for index in range(GROUPS):
        columns = head_columns(index)
        slope_query[:, columns] = (accum[columns, :] * SCALE).T


def expert_kernel(
    which,
    rows,
    slopes,
    chosen,
    gate_up,
    down,
    router,
    hidden_out,
    result_out,
    gates_out,
    slots_out,
    pre_out,
    slope_out,
):
    hidden_width = down.shape[0]
    incoming = rows[...]
    logits = jnp.where(chosen[...] > 0, matmul(incoming, router[...]), big_negative)
    shares = jnp.exp(logits - jnp.max(logits, -1, keepdims=True))
    shares = jnp.where(chosen[...] > 0, shares, 0.0)
    column = lax.broadcasted_iota(jnp.int32, shares.shape, 1)
    own = jnp.sum(jnp.where(column == which[0], shares, 0.0), -1, keepdims=True)
    gates = own / jnp.maximum(jnp.sum(shares, -1, keepdims=True), 1e-30)
    slots = (gates * slopes[...].astype(f32)).astype(bf16)
    slots_out[...] = slots
    pre = matmul(incoming, gate_up[...])
    gate, up = pre[:, :hidden_width], pre[:, hidden_width:]
    root, cubic = math.sqrt(2.0 / math.pi), 0.044715
    square = gate * gate
    bend = jnp.tanh(root * (gate + cubic * gate * square))
    gelu = 0.5 * gate * (1.0 + bend)
    rise = 0.5 * (1.0 + bend) + 0.5 * gate * (1.0 - bend * bend) * root * (
        1.0 + 3.0 * cubic * square
    )
    hidden = (gelu * up).astype(bf16)
    hidden_out[...] = hidden
    result = matmul(hidden, down[...]).astype(bf16)
    result_out[...] = result
    gates_out[...] = jnp.sum(slopes[...].astype(f32) * result.astype(f32), -1, keepdims=True)
    slope_hidden = matmul_nt(slots, down[...])
    slope_pre = jnp.concatenate([slope_hidden * up * rise, slope_hidden * gelu], 1).astype(bf16)
    pre_out[...] = slope_pre
    slope_out[...] = matmul_nt(slope_pre, gate_up[...]).astype(bf16)


def expert(which, rows, slopes, chosen, gate_up, down, router):
    count, width = rows.shape
    hidden_width = down.shape[0]
    block = count // 2

    def tile(columns):
        return pl.BlockSpec((block, columns), lambda step: (step, 0))

    def whole(array):
        return pl.BlockSpec(array.shape, lambda step: (0, 0))

    shapes = [(hidden_width, bf16), (width, bf16), (1, f32), (width, bf16)]
    shapes += [(2 * hidden_width, bf16), (width, bf16)]
    return pl.pallas_call(
        expert_kernel,
        grid=(2,),
        out_shape=[jax.ShapeDtypeStruct((count, columns), kind) for columns, kind in shapes],
        in_specs=[
            pl.BlockSpec(memory_space=pltpu.SMEM),
            tile(width),
            tile(width),
            tile(LANES),
            whole(gate_up),
            whole(down),
            whole(router),
        ],
        out_specs=[tile(columns) for columns, _ in shapes],
        compiler_params=pltpu.CompilerParams(vmem_limit_bytes=VMEM_BYTES),
        cost_estimate=pl.CostEstimate(
            flops=12 * count * width * hidden_width,
            bytes_accessed=20 * count * width,
            transcendentals=count * hidden_width,
        ),
        name="expert",
    )(which, rows, slopes, chosen, gate_up, down, router)


def attention_call(kernel, outs, scratch, products, name, meta, *operands):
    vmem = pl.BlockSpec(memory_space=pltpu.VMEM)
    pairs = QUERY_HEADS * operands[0].shape[0] * operands[-1].shape[0]
    return pl.pallas_call(
        kernel,
        out_shape=outs,
        in_specs=[pl.BlockSpec(memory_space=pltpu.SMEM)] + [vmem] * len(operands),
        out_specs=(vmem,) * len(outs),
        scratch_shapes=[pltpu.VMEM(*shape) for shape in scratch],
        compiler_params=pltpu.CompilerParams(vmem_limit_bytes=VMEM_BYTES),
        cost_estimate=pl.CostEstimate(
            flops=products * pairs, bytes_accessed=QUERY_WIDTH * 1024, transcendentals=0
        ),
        name=name,
    )(meta, *operands)


def attend(meta, query, key_value):
    stretch = query.shape[0]
    stats = (QUERY_HEADS, stretch)
    outs = (
        jax.ShapeDtypeStruct((stretch, QUERY_WIDTH), f32),
        jax.ShapeDtypeStruct(stats, f32),
    )
    scratch = [(stats, f32), (stats, f32), ((QUERY_WIDTH, stretch), f32)]
    return attention_call(attend_kernel, outs, scratch, 2, "attend", meta, query, key_value)


def attend_back(order, group, meta, query, slope, log_total, mixed, key_value):
    stretch, rows = query.shape[0], key_value.shape[0]
    group_width = GROUPS * HEAD_WIDTH
    outs = (
        jax.ShapeDtypeStruct((stretch, group_width), f32),
        jax.ShapeDtypeStruct((2, rows // 2, 2 * HEAD_WIDTH), bf16),
    )
    operands = (meta, query, slope, log_total, mixed, key_value)
    scratch = [((group_width, stretch), f32), ((GROUPS, stretch), f32)]
    kernel = functools.partial(attend_back_kernel, order, group)
    return attention_call(kernel, outs, scratch, 2, "attend_back", *operands)


def body(
    tokens,
    cotangent,
    routes,
    fill_order,
    pic_starts,
    attn_gain,
    moe_gain,
    w_query,
    key_projection,
    value_projection,
    w_out,
    w_router,
    expert_gate,
    expert_up,
    expert_down,
):
    sequences, stretch, width = tokens.shape
    count = sequences * stretch
    parts = lax.axis_size("ctx")
    experts = parts
    capacity = (5 * count * TOP + 4 * experts - 1) // (4 * experts)
    query_width, key_width = QUERY_WIDTH, KEY_WIDTH
    hidden_width = expert_gate.shape[2]
    seq_bits, ctx_bits = bits("seq"), bits("ctx")
    all_bits = seq_bits + ctx_bits
    inward = ctx_bits[-1:] + seq_bits[::-1] + ctx_bits[-2::-1]
    sizes = {"seq": parts, "ctx": 1}
    me = lax.axis_index("seq") * parts + lax.axis_index("ctx")

    def padded(columns):
        block = jnp.concatenate(columns, 1)
        return jnp.pad(block, ((0, 0), (0, LANES - block.shape[1])))

    own_rows = w_query.shape[0]

    def feature(stages):
        owner = jnp.bitwise_xor(jnp.array(flips(stages, sizes), jnp.int32), me)
        return (owner[:, None] * own_rows + jnp.arange(own_rows, dtype=jnp.int32)).reshape(-1)

    def same(left, right):
        return (left[:, None] == right[None, :]).astype(bf16)

    turns = ctx_bits[:-2] + seq_bits + ctx_bits[-2:]
    natural = jnp.arange(width, dtype=jnp.int32)
    gathered, summed = feature(turns[::-1]), feature(inward)
    turn, turn_in, across = same(natural, summed), same(natural, gathered), same(gathered, summed)

    def relative(rows):
        return matmul(rows, turn).astype(bf16)

    def halves(left, right):
        middle = left.shape[1] // 2
        sent = matmul_tn(left[:, middle:], right).astype(bf16)
        return sent, matmul_tn(left[:, :middle], right).astype(bf16)

    picks = routes.reshape(count, TOP)
    order = fill_order.reshape(count)
    routed = jnp.any(picks[:, :, None] == jnp.arange(experts, dtype=jnp.int32), 1)
    earlier = (order[None, :] < order[:, None]).astype(bf16)
    place = matmul(earlier, routed.astype(bf16)).astype(jnp.int32)
    place = jnp.where(routed, place, capacity)
    half = capacity // 2
    chosen_slot = [
        place.T[:, None, :]
        == (begin + jnp.arange(half, dtype=jnp.int32))[None, :, None]
        for begin in (0, half)
    ]
    slot_map = [chosen.astype(bf16).reshape(-1, count) for chosen in chosen_slot]

    def exchange_rows(rows):
        rows = rows.reshape(experts, half, width)
        rows = lax.all_to_all(rows, "ctx", split_axis=0, concat_axis=0, tiled=True)
        return rows.reshape(-1, width)

    out_slope = cotangent.reshape(count, width)
    slot_routes = jnp.concatenate(
        [matmul(part, routed.astype(bf16)).reshape(experts, half, experts) for part in slot_map], 1
    ).astype(bf16)
    slot_routes = lax.all_to_all(slot_routes, "ctx", split_axis=0, concat_axis=0, tiled=True)
    slot_routes = jnp.pad(slot_routes, ((0, 0), (0, 0), (0, LANES - experts)))
    slot_routes = [
        slot_routes[:, begin : begin + half].reshape(-1, LANES) for begin in (0, half)
    ]
    slope_rows = [matmul(part, out_slope).astype(bf16) for part in slot_map]
    slope_rows = jnp.concatenate([part.reshape(experts, half, width) for part in slope_rows], 1)

    block = jnp.concatenate(
        [
            w_query,
            key_projection,
            value_projection,
            padded([attn_gain[:, None]]),
            w_out,
            padded([w_router, moe_gain[:, None]]),
        ],
        1,
    )
    first_width = query_width + 2 * key_width + LANES
    expert_parts = [expert_gate[0], expert_up[0]]
    for index, stage in enumerate(turns):
        other = swap(block if index < 2 else mine, *stage)
        if index in (1, 3) and len(seq_bits) == 1:
            part = index // 2
            other, expert_parts[part] = lax.optimization_barrier(
                (other, (expert_parts[part], swap(expert_parts[part], *seq_bits[0])))
            )
        if index < 2:
            block = jnp.concatenate([block, other], 0)
        if index == 1:
            block, slope_rows = lax.optimization_barrier((block, slope_rows))
            slope_rows = lax.all_to_all(slope_rows, "ctx", split_axis=0, concat_axis=0, tiled=True)
            mine, second_set = block[:, :first_width], block[:, first_width:]
        if index > 2:
            arrived = swap(second_set, *turns[index - 1])
            if index == len(turns) - 1:
                late = second_set, arrived
                continue
            if index < len(turns) - 1:
                other, arrived = lax.optimization_barrier((other, arrived))
            second_set = jnp.concatenate([second_set, arrived], 0)
        if 2 <= index < len(turns) - 1:
            mine = jnp.concatenate([mine, other], 0)
    inputs = tokens.reshape(count, width)
    inputs_turned = matmul(inputs, turn_in)
    inputs = inputs.astype(f32)
    inputs_scaled = inputs_turned * rms_scale(inputs)
    mine, other, slope_rows, slot_routes, inputs_scaled = lax.optimization_barrier(
        (mine, other, slope_rows, slot_routes, inputs_scaled)
    )
    slope_rows = [
        slope_rows[:, begin : begin + half].reshape(-1, width) for begin in (0, half)
    ]
    qkv_width = query_width + 2 * key_width
    weight_low, weight_high = mine[:, :qkv_width], other[:, :qkv_width]
    gain_one = jnp.concatenate([mine[:, qkv_width], other[:, qkv_width]]).astype(f32)

    def whole_expert(part):
        if isinstance(part, tuple):
            own, other = part
            upper = lax.axis_index("seq") > 0
            pair = [jnp.where(upper, other, own), jnp.where(upper, own, other)]
            return jnp.concatenate(pair, 0)
        return gather_blocks(part, seq_bits[::-1], seq_bits).reshape(-1, part.shape[1])

    gate_up = jnp.concatenate([whole_expert(part) for part in expert_parts], 1)
    positions = lax.axis_index("ctx") * stretch + jnp.arange(stretch, dtype=jnp.int32)
    cosine, sine = rope_tables(positions, HEAD_WIDTH)
    normed = (inputs_scaled * gain_one).astype(bf16)

    def project(columns):
        low = matmul(normed[:, : width // 2], weight_low[:, columns])
        return low + matmul(normed[:, width // 2 :], weight_high[:, columns])

    projected = project(slice(query_width, None))
    key_rows = rotate(projected[:, :key_width], KEY_VALUE_HEADS, cosine, sine)
    key_values = lax.all_gather(
        jnp.concatenate([key_rows, projected[:, key_width:]], 1).astype(bf16),
        "ctx",
        axis=0,
        tiled=True,
    )
    projected = project(slice(0, query_width))
    query_rows = rotate(projected, QUERY_HEADS, cosine, sine).astype(bf16)
    second_set, arrived = late
    arrived, query_rows = lax.optimization_barrier((arrived, query_rows))
    second_set = jnp.concatenate([second_set, arrived], 0)
    second_set = jnp.concatenate([second_set, swap(second_set, *turns[-1])], 0)
    second_set = matmul(turn_in, second_set).astype(bf16)
    full_out = second_set[:, :width]
    full_router = second_set[:, width : width + experts]
    gain_two = second_set[:, width + experts].astype(f32)
    meta = jnp.concatenate([lax.axis_index("ctx").astype(jnp.int32)[None], pic_starts[0]])
    mixed_heads, log_total = attend(meta, query_rows, key_values)

    def with_attention(other):
        nonlocal mixed_heads
        mixed_heads, other = lax.optimization_barrier((mixed_heads, other))
        return other

    down = gather_blocks(
        lax.optimization_barrier((expert_down[0], gain_one))[0],
        seq_bits[::-1],
        seq_bits,
        with_attention,
    ).reshape(-1, width)
    attended = mixed_heads.astype(bf16)

    middle = inputs + matmul(attended, full_out)
    enter = rms_norm(middle, gain_two).astype(bf16)
    arrived = [exchange_rows(matmul(part, enter).astype(bf16)) for part in slot_map]

    def gates_of(rows, chosen):
        logits = jnp.where(chosen, matmul(rows, full_router), big_negative)
        shares = jnp.exp(logits - jnp.max(logits, -1, keepdims=True))
        shares = jnp.where(chosen, shares, 0.0)
        return shares / jnp.maximum(jnp.sum(shares, -1, keepdims=True), 1e-30)

    gates = gates_of(enter, routed)

    attended_turned, enter_turned = map(relative, (attended, enter))
    normed_turned = matmul(normed, across).astype(bf16)
    arrived[0], attended_turned, enter_turned, normed_turned = lax.optimization_barrier(
        (arrived[0], attended_turned, enter_turned, normed_turned)
    )
    which = lax.axis_index("ctx").astype(jnp.int32)[None]
    router = second_set[:, width:]
    hidden, result, slope_gates, slope_slots, slope_pre, slope_arrived = ([] for _ in range(6))
    for index in range(2):
        made = list(expert(
            which, arrived[index], slope_rows[index], slot_routes[index], gate_up, down, router)
        )
        if index == 0:
            arrived[1], made[-1] = lax.optimization_barrier((arrived[1], made[-1]))
        for kept, item in zip(
            (hidden, result, slope_gates, slope_slots, slope_pre, slope_arrived), made
        ):
            kept.append(item)
    returned_slopes = [exchange_rows(slope_arrived[0])]
    slope_gates = jnp.concatenate([item.reshape(experts, half) for item in slope_gates], 1)
    slope_gates, returned_slopes[0] = lax.optimization_barrier((slope_gates, returned_slopes[0]))
    returned_gates = lax.all_to_all(slope_gates, "ctx", split_axis=0, concat_axis=0, tiled=True)
    slope_arrived[1], returned_gates, slope_pre, slope_slots = lax.optimization_barrier(
        (slope_arrived[1], returned_gates, slope_pre, slope_slots)
    )
    returned_slopes.append(exchange_rows(slope_arrived[1]))
    grad_gate, grad_up = (
        sum(matmul_tn(arrived[i], slope_pre[i][:, columns]) for i in range(2)).astype(bf16)
        for columns in (slice(0, hidden_width), slice(hidden_width, None))
    )
    grad_down = sum(matmul_tn(hidden[i], slope_slots[i]) for i in range(2)).astype(bf16)
    def sector_halves(grads):
        return grads.reshape([2] * len(seq_bits) + [-1, grads.shape[1]])

    def sector_sum(blocks, arrived):
        for axis, bit in seq_bits:
            mine = ((lax.axis_index(axis) & bit) > 0).astype(jnp.int32)
            sent = lax.dynamic_index_in_dim(blocks, 1 - mine, 0, keepdims=False)
            kept = lax.dynamic_index_in_dim(blocks, mine, 0, keepdims=False)
            other = swap(sent.astype(bf16), axis, bit)
            if (axis, bit) == seq_bits[-1]:
                return kept, arrived(other)
            blocks = kept.astype(f32) + other.astype(f32)

    def ended(pair):
        return pair[0].astype(f32) + pair[1].astype(f32)

    def with_slopes(other):
        nonlocal grad_gate, grad_up
        returned_slopes[1], other, grad_gate, grad_up = lax.optimization_barrier(
            (returned_slopes[1], other, grad_gate, grad_up)
        )
        return other

    grad_down = sector_sum(sector_halves(grad_down), with_slopes)
    returned = jnp.concatenate([part.reshape(experts, half, width) for part in result], 1)
    returned = lax.all_to_all(returned, "ctx", split_axis=0, concat_axis=0, tiled=True)

    slope_gate = 0.0
    for index, chosen in enumerate(chosen_slot):
        part = returned_gates[:, index * half : (index + 1) * half]
        slope_gate = slope_gate + jnp.sum(jnp.where(chosen, part[:, :, None], 0.0), 1).T
    slope_logits = gates * (slope_gate - jnp.sum(gates * slope_gate, -1, keepdims=True))
    slope_logits = slope_logits.astype(bf16)
    grad_router = matmul_tn(enter_turned, slope_logits)
    slope_enter = matmul_nt(slope_logits, full_router)
    for part, rows in zip(slot_map, returned_slopes):
        slope_enter = slope_enter + matmul_tn(part, rows)

    pull_two = jax.vjp(rms_norm, middle, gain_two)[1]
    slope_middle, grad_gain_two = pull_two(slope_enter)
    slope_middle = out_slope.astype(f32) + slope_middle
    slope_branch = slope_middle.astype(bf16)
    slope_attended = matmul_nt(slope_branch, full_out).astype(bf16)

    kv_order = ctx_bits[::-1]

    def back(group, meta):
        order = [bit for _, bit in kv_order]
        return attend_back(
            order, group, meta, query_rows, slope_attended, log_total, mixed_heads, key_values
        )

    first_q, first_kv = back(0, meta)

    def after_first(other):
        nonlocal first_q, first_kv, meta, grad_up
        first_q, first_kv, meta, grad_up, other = lax.optimization_barrier(
            (first_q, first_kv, meta, grad_up, other)
        )
        return other

    grad_gate = sector_sum(sector_halves(grad_gate), after_first)
    first_sum = Sum(first_kv[1], first_kv[0], kv_order)
    first_sum.step()
    second_q, second_kv = back(1, meta)

    def after_second(other):
        nonlocal second_q, second_kv, grad_gate, slope_branch
        second_q, second_kv, first_sum.sent, grad_gate, slope_branch, other = (
            lax.optimization_barrier(
                (second_q, second_kv, first_sum.sent, grad_gate, slope_branch, other)
            )
        )
        return other

    grad_up = sector_sum(sector_halves(grad_up), after_second)
    second_sum = Sum(second_kv[1], second_kv[0], kv_order)
    first_sum.step()
    second_sum.step()
    second_sum.sent, first_q, second_q, slope_branch = lax.optimization_barrier(
        (second_sum.sent, first_q, second_q, slope_branch)
    )
    out_sum = Sum(*halves(attended_turned, slope_branch), inward)
    slope_query = jnp.concatenate([first_q, second_q], 1)
    slope_query = rotate(slope_query, QUERY_HEADS, cosine, -sine).astype(bf16)
    query_sum = Sum(*halves(normed_turned, slope_query), inward)
    out_sum.step()
    query_sum.step()
    first_sum.sent, second_sum.sent, query_sum.sent, returned = lax.optimization_barrier(
        (first_sum.sent, second_sum.sent, query_sum.sent, returned)
    )
    query_sum.step()
    while len(first_sum.stages) > 1:
        together([first_sum, second_sum])
    slope_normed = [
        matmul_nt(slope_query, part[:, :query_width]) for part in (weight_low, weight_high)
    ]
    first_sum.step()
    second_sum.step()
    first_sum.total, second_sum.sent, query_sum.sent, out_sum.sent, returned = (
        lax.optimization_barrier(
            (first_sum.total, second_sum.sent, query_sum.sent, out_sum.sent, returned)
        )
    )
    output = middle
    for chosen, rows in ((jnp.concatenate(chosen_slot, 1), returned.reshape(-1, width)),):
        mix = jnp.where(chosen, gates.T[:, None, :], 0.0).reshape(-1, count)
        mix_high = mix.astype(bf16)
        mix_low = (mix - mix_high.astype(f32)).astype(bf16)
        output = output + matmul_tn(mix_high, rows) + matmul_tn(mix_low, rows)
    output = output.astype(bf16).reshape(tokens.shape)
    out_sum.step()
    second_sum.step()
    totals = [item.total for item in (first_sum, second_sum)]
    totals[1], slope_normed, output = lax.optimization_barrier(
        (totals[1], slope_normed, output)
    )
    slope_key = jnp.concatenate([total[:, :HEAD_WIDTH] for total in totals], 1)
    slope_key = rotate(slope_key, KEY_VALUE_HEADS, cosine, -sine)
    slope_rest = [slope_key] + [total[:, HEAD_WIDTH:] for total in totals]
    slope_rest = jnp.concatenate(slope_rest, 1).astype(bf16)
    slope_normed = jnp.concatenate(
        [
            early + matmul_nt(slope_rest, part[:, query_width:])
            for early, part in zip(slope_normed, (weight_low, weight_high))
        ],
        1,
    )
    pull_one = jax.vjp(rms_norm, inputs_turned, gain_one)[1]
    slope_inputs = pull_one(slope_normed)[0]
    small = padded([grad_router.astype(bf16), relative(grad_gain_two.astype(bf16)[None]).T])
    rest_sum = Sum(
        *(
            jnp.concatenate([grads, part], 1)
            for grads, part in zip(
                halves(normed_turned, slope_rest), (small[width // 2 :], small[: width // 2])
            )
        ),
        inward,
    )
    together([item for item in (rest_sum, query_sum) if item.stages])
    slope_inputs = together(
        [item for item in (rest_sum, query_sum, out_sum) if item.stages], slope_inputs
    )
    while rest_sum.stages:
        together([item for item in (rest_sum, query_sum, out_sum) if item.stages])
    for item in (query_sum, out_sum):
        while item.stages:
            item.step()
    grads_rest = rest_sum.total
    slope_high = slope_inputs.astype(bf16)
    slope_low = (slope_inputs - slope_high.astype(f32)).astype(bf16)
    grad_input = slope_middle + matmul_nt(slope_high, turn_in) + matmul_nt(slope_low, turn_in)
    grad_input = grad_input.reshape(tokens.shape)
    grad_gain_one = jnp.sum(w_query.astype(f32) * query_sum.total, 1)
    own_kv = jnp.concatenate([key_projection, value_projection], 1).astype(f32)
    grad_gain_one = grad_gain_one + jnp.sum(own_kv * grads_rest[:, : 2 * key_width], 1)
    grad_gain_one = grad_gain_one / attn_gain.astype(f32)
    return (
        output,
        grad_input,
        grad_gain_one,
        grads_rest[:, 2 * key_width + experts],
        query_sum.total,
        grads_rest[:, :key_width],
        grads_rest[:, key_width : 2 * key_width],
        out_sum.total,
        grads_rest[:, 2 * key_width : 2 * key_width + experts],
        ended(grad_gate)[None],
        ended(grad_up)[None],
        ended(grad_down)[None],
    )


def solution(mesh):
    rows = P("seq", "ctx", None)
    shard = P(("seq", "ctx"), None)
    vector = P(("seq", "ctx"))
    expert = P("ctx", "seq", None)
    return jax.shard_map(
        body,
        mesh=mesh,
        in_specs=(rows, rows, rows, P("seq", "ctx"), P("seq", None), vector, vector)
        + (shard,) * 5
        + (expert,) * 3,
        out_specs=(rows, rows, vector, vector) + (shard,) * 5 + (expert,) * 3,
        check_vma=False,
    )
```

```python
import functools
import math

import jax
import jax.numpy as jnp
from jax import lax
from jax.experimental import pallas as pl
from jax.experimental.pallas import tpu as pltpu
from jax.sharding import PartitionSpec as P

QUERY_HEADS = 12
KEY_VALUE_HEADS = 2
HEAD_WIDTH = 128
TOP = 4
PIC = 256
NPIC = 4
LANES = 128
GROUPS = QUERY_HEADS // KEY_VALUE_HEADS
QUERY_WIDTH = QUERY_HEADS * HEAD_WIDTH
KEY_WIDTH = KEY_VALUE_HEADS * HEAD_WIDTH
SCALE = 1.0 / math.sqrt(HEAD_WIDTH)
EXP2_SCALE = SCALE * math.log2(math.e)
BLOCKS = 2
SKEW = 1
VMEM_BYTES = 48 << 20

epsilon = 1e-06
rope_base = 10000.0
big_negative = -1e30
bf16 = jnp.bfloat16
f32 = jnp.float32


def matmul(left, right):
    return jnp.dot(left, right, preferred_element_type=f32)


def matmul_nt(left, right):
    return lax.dot_general(left, right, (((1,), (1,)), ((), ())), preferred_element_type=f32)


def matmul_tn(left, right):
    return lax.dot_general(left, right, (((0,), (0,)), ((), ())), preferred_element_type=f32)


def rms_scale(rows):
    return lax.rsqrt(jnp.mean(rows * rows, -1, keepdims=True) + epsilon)


def rms_norm(rows, gain):
    return rows * rms_scale(rows) * gain


def rope_tables(positions, head_size):
    half = head_size // 2
    inverse = rope_base ** (-(jnp.arange(half, dtype=f32) * 2.0 / head_size))
    angles = positions.astype(f32)[:, None] * inverse[None, :]
    return (jnp.cos(angles), jnp.sin(angles))


def rotate(rows, heads, cosine, sine):
    shaped = rows.reshape(rows.shape[0], heads, HEAD_WIDTH)
    half = HEAD_WIDTH // 2
    first, second = shaped[..., :half], shaped[..., half:]
    cosine, sine = cosine[:, None, :], sine[:, None, :]
    turned = jnp.concatenate(
        [first * cosine - second * sine, second * cosine + first * sine], -1
    )
    return turned.reshape(rows.shape)


def bits(axis):
    size = lax.axis_size(axis)
    return [(axis, 1 << place) for place in reversed(range(size.bit_length() - 1))]


def swap(block, axis, bit):
    size = lax.axis_size(axis)
    return lax.ppermute(block, axis, [(index, index ^ bit) for index in range(size)])


def gather_blocks(block, stages, order, arrived=None):
    held = []
    for stage in stages:
        axis, bit = stage
        other = swap(block, axis, bit)
        if arrived is not None and stage == stages[-1]:
            other = arrived(other)
        upper = (lax.axis_index(axis) & bit) > 0
        place = sum(order.index(known) < order.index(stage) for known in held)
        block = jnp.stack(
            [jnp.where(upper, other, block), jnp.where(upper, block, other)], place
        )
        held.append(stage)
    return block


class Sum:
    def __init__(self, sent, kept, stages):
        self.sent, self.kept, self.stages = sent, kept, list(stages)

    def step(self):
        axis, bit = self.stages.pop(0)
        other = swap(self.sent, axis, bit)
        if not self.stages:
            self.total = self.kept.astype(f32) + other.astype(f32)
            return
        half = self.kept.shape[0] // 2
        self.sent = (self.kept[half:].astype(f32) + other[half:].astype(f32)).astype(bf16)
        self.kept = (self.kept[:half].astype(f32) + other[:half].astype(f32)).astype(bf16)


def together(sums, also=()):
    for item in sums:
        item.step()
    live = [item for item in sums if item.stages]
    sent, also = lax.optimization_barrier(([item.sent for item in live], also))
    for item, block in zip(live, sent):
        item.sent = block
    return also


def flips(stages, sizes):
    masks = []
    for block in range(1 << len(stages)):
        mask = 0
        for place, (axis, bit) in enumerate(stages):
            if (block >> (len(stages) - 1 - place)) & 1:
                mask |= bit * sizes[axis]
        masks.append(mask)
    return masks


def visible_keys(meta, step, stretch):
    span = BLOCKS * stretch
    keys = step * span + lax.broadcasted_iota(jnp.int32, (span, 1), 0)
    queries = meta[0] * stretch + lax.broadcasted_iota(jnp.int32, (1, stretch), 1)

    def label(positions):
        found = jnp.zeros(positions.shape, jnp.int32)
        for index in range(NPIC):
            start = meta[1 + index]
            inside = (positions >= start) & (positions < start + PIC)
            found = jnp.where(inside, index + 1, found)
        return found

    query_label = label(queries)
    return (keys <= queries) | ((label(keys) == query_label) & (query_label > 0))


def for_each_step(meta, stretch, steps, process, skip=None):
    span = BLOCKS * stretch
    low, high = meta[0] * stretch, (meta[0] + 1) * stretch

    def turn(step, carry):
        needed = step * span < high + PIC - 1
        edge = (step + 1) * span > low

        @pl.when(needed & edge)
        def _():
            process(step, True)

        @pl.when(needed & jnp.logical_not(edge))
        def _():
            process(step, False)

        if skip is not None:

            @pl.when(jnp.logical_not(needed))
            def _():
                skip(step)

        return carry

    lax.fori_loop(0, steps, turn, 0)


def head_columns(head, start=0):
    return slice(start + head * HEAD_WIDTH, start + (head + 1) * HEAD_WIDTH)


def attend_kernel(meta, query, key_value, out, log_total, peak, total, accum):
    stretch = query.shape[0]
    span = BLOCKS * stretch
    peak[...] = jnp.full(peak.shape, big_negative, f32)
    total[...] = jnp.zeros(total.shape, f32)
    accum[...] = jnp.zeros(accum.shape, f32)

    def process(step, edge):
        rows = pl.ds(pl.multiple_of(step * span, span), span)
        if edge:
            visible = visible_keys(meta, step, stretch)
        keys, values = [], []
        for group in range(KEY_VALUE_HEADS):
            keys.append(key_value[rows, head_columns(group)])
            turned = key_value[rows, head_columns(group, KEY_WIDTH)].T
            values.append(jnp.concatenate([turned, jnp.ones((16, span), bf16)], 0))

        def score(head):
            scores = matmul_nt(keys[head // GROUPS], query[:, head_columns(head)])
            if edge:
                scores = jnp.where(visible, scores, big_negative)
            old = peak[head : head + 1, :]
            return scores, old, jnp.maximum(old, jnp.max(scores, 0, keepdims=True))

        def weigh(head, scores, old, new):
            weights = jnp.exp2((scores - new) * EXP2_SCALE).astype(bf16)
            shrink = jnp.exp2((old - new) * EXP2_SCALE)
            sums = matmul(values[head // GROUPS], weights)
            row, columns = slice(head, head + 1), head_columns(head)
            peak[row, :] = new
            total[row, :] = total[row, :] * shrink + sums[HEAD_WIDTH : HEAD_WIDTH + 1]
            accum[columns, :] = accum[columns, :] * shrink + sums[:HEAD_WIDTH]

        waiting = []
        for head in range(QUERY_HEADS):
            waiting.append((head, *score(head)))
            if len(waiting) > 2:
                weigh(*waiting.pop(0))
        for item in waiting:
            weigh(*item)

    for_each_step(meta, stretch, key_value.shape[0] // span, process)
    for head in range(QUERY_HEADS):
        row, columns = slice(head, head + 1), head_columns(head)
        out[:, columns] = (accum[columns, :] / total[row, :]).T
        log_total[row, :] = peak[row, :] * EXP2_SCALE + jnp.log2(total[row, :])


def attend_back_kernel(
    order,
    group,
    meta,
    query,
    slope,
    log_total,
    mixed,
    key_value,
    slope_query,
    out,
    accum,
    delta,
):
    stretch = query.shape[0]
    span = BLOCKS * stretch
    accum[...] = jnp.zeros(accum.shape, f32)
    for index in range(GROUPS):
        columns = head_columns(group * GROUPS + index)
        product = slope[:, columns].astype(f32) * mixed[:, columns]
        delta[index : index + 1, :] = jnp.sum(product.T, 0, keepdims=True)

    def store(step, part, columns, block):
        flip = jnp.bitwise_xor(BLOCKS * step + part, meta[0])
        first, *others = order
        place = 0
        for index, bit in enumerate(others):
            place = place + ((flip // bit) & 1) * (1 << (len(others) - 1 - index))
        place = pl.ds(pl.multiple_of(place * stretch, stretch), stretch)
        out[(flip // first) & 1, place, columns] = block

    def process(step, edge):
        rows = pl.ds(pl.multiple_of(step * span, span), span)
        if edge:
            visible = visible_keys(meta, step, stretch)
        keys = key_value[rows, head_columns(group)]
        values = key_value[rows, head_columns(group, KEY_WIDTH)]
        keys_turned = keys.T

        def slopes_of(index):
            columns = head_columns(group * GROUPS + index)
            row = slice(group * GROUPS + index, group * GROUPS + index + 1)
            scores = matmul_nt(keys, query[:, columns])
            probs = jnp.exp2(scores * EXP2_SCALE - log_total[row, :])
            if edge:
                probs = jnp.where(visible, probs, 0.0)
            slope_probs = matmul_nt(values, slope[:, columns])
            slope_scores = (probs * (slope_probs - delta[index : index + 1, :])).astype(bf16)
            return index, probs.astype(bf16), slope_scores

        slope_k = jnp.zeros((span, HEAD_WIDTH), f32)
        slope_v = jnp.zeros((span, HEAD_WIDTH), f32)
        waiting = []
        for index in range(GROUPS + SKEW):
            if index < GROUPS:
                waiting.append(slopes_of(index))
            if index >= SKEW:
                own, probs, slope_scores = waiting.pop(0)
                columns, place = head_columns(group * GROUPS + own), head_columns(own)
                slope_v = slope_v + matmul(probs, slope[:, columns])
                slope_k = slope_k + matmul(slope_scores, query[:, columns])
                accum[place, :] = accum[place, :] + matmul(keys_turned, slope_scores)
        slope_k, slope_v = (slope_k * SCALE).astype(bf16), slope_v.astype(bf16)
        for which, block in enumerate((slope_k, slope_v)):
            for part in range(BLOCKS):
                own = block[part * stretch : (part + 1) * stretch]
                store(step, part, head_columns(which), own)

    def skip(step):
        for part in range(BLOCKS):
            store(step, part, slice(None), jnp.zeros((stretch, 2 * HEAD_WIDTH), bf16))

    for_each_step(meta, stretch, key_value.shape[0] // span, process, skip)
    for index in range(GROUPS):
        columns = head_columns(index)
        slope_query[:, columns] = (accum[columns, :] * SCALE).T


def expert_kernel(
    which,
    rows,
    slopes,
    chosen,
    gate_up,
    down,
    router,
    hidden_out,
    result_out,
    gates_out,
    slots_out,
    pre_out,
    slope_out,
):
    hidden_width = down.shape[0]
    incoming = rows[...]
    logits = jnp.where(chosen[...] > 0, matmul(incoming, router[...]), big_negative)
    shares = jnp.exp(logits - jnp.max(logits, -1, keepdims=True))
    shares = jnp.where(chosen[...] > 0, shares, 0.0)
    column = lax.broadcasted_iota(jnp.int32, shares.shape, 1)
    own = jnp.sum(jnp.where(column == which[0], shares, 0.0), -1, keepdims=True)
    gates = own / jnp.maximum(jnp.sum(shares, -1, keepdims=True), 1e-30)
    slots = (gates * slopes[...].astype(f32)).astype(bf16)
    slots_out[...] = slots
    pre = matmul(incoming, gate_up[...])
    gate, up = pre[:, :hidden_width], pre[:, hidden_width:]
    root, cubic = math.sqrt(2.0 / math.pi), 0.044715
    square = gate * gate
    bend = jnp.tanh(root * (gate + cubic * gate * square))
    gelu = 0.5 * gate * (1.0 + bend)
    rise = 0.5 * (1.0 + bend) + 0.5 * gate * (1.0 - bend * bend) * root * (
        1.0 + 3.0 * cubic * square
    )
    hidden = (gelu * up).astype(bf16)
    hidden_out[...] = hidden
    result = matmul(hidden, down[...]).astype(bf16)
    result_out[...] = result
    gates_out[...] = jnp.sum(slopes[...].astype(f32) * result.astype(f32), -1, keepdims=True)
    slope_hidden = matmul_nt(slots, down[...])
    slope_pre = jnp.concatenate([slope_hidden * up * rise, slope_hidden * gelu], 1).astype(bf16)
    pre_out[...] = slope_pre
    slope_out[...] = matmul_nt(slope_pre, gate_up[...]).astype(bf16)


def expert(which, rows, slopes, chosen, gate_up, down, router):
    count, width = rows.shape
    hidden_width = down.shape[0]
    block = count // 2

    def tile(columns):
        return pl.BlockSpec((block, columns), lambda step: (step, 0))

    def whole(array):
        return pl.BlockSpec(array.shape, lambda step: (0, 0))

    shapes = [(hidden_width, bf16), (width, bf16), (1, f32), (width, bf16)]
    shapes += [(2 * hidden_width, bf16), (width, bf16)]
    return pl.pallas_call(
        expert_kernel,
        grid=(2,),
        out_shape=[jax.ShapeDtypeStruct((count, columns), kind) for columns, kind in shapes],
        in_specs=[
            pl.BlockSpec(memory_space=pltpu.SMEM),
            tile(width),
            tile(width),
            tile(LANES),
            whole(gate_up),
            whole(down),
            whole(router),
        ],
        out_specs=[tile(columns) for columns, _ in shapes],
        compiler_params=pltpu.CompilerParams(vmem_limit_bytes=VMEM_BYTES),
        cost_estimate=pl.CostEstimate(
            flops=12 * count * width * hidden_width,
            bytes_accessed=20 * count * width,
            transcendentals=count * hidden_width,
        ),
        name="expert",
    )(which, rows, slopes, chosen, gate_up, down, router)


def attention_call(kernel, outs, scratch, products, name, meta, *operands):
    vmem = pl.BlockSpec(memory_space=pltpu.VMEM)
    pairs = QUERY_HEADS * operands[0].shape[0] * operands[-1].shape[0]
    return pl.pallas_call(
        kernel,
        out_shape=outs,
        in_specs=[pl.BlockSpec(memory_space=pltpu.SMEM)] + [vmem] * len(operands),
        out_specs=(vmem,) * len(outs),
        scratch_shapes=[pltpu.VMEM(*shape) for shape in scratch],
        compiler_params=pltpu.CompilerParams(vmem_limit_bytes=VMEM_BYTES),
        cost_estimate=pl.CostEstimate(
            flops=products * pairs, bytes_accessed=QUERY_WIDTH * 1024, transcendentals=0
        ),
        name=name,
    )(meta, *operands)


def attend(meta, query, key_value):
    stretch = query.shape[0]
    stats = (QUERY_HEADS, stretch)
    outs = (
        jax.ShapeDtypeStruct((stretch, QUERY_WIDTH), f32),
        jax.ShapeDtypeStruct(stats, f32),
    )
    scratch = [(stats, f32), (stats, f32), ((QUERY_WIDTH, stretch), f32)]
    return attention_call(attend_kernel, outs, scratch, 2, "attend", meta, query, key_value)


def attend_back(order, group, meta, query, slope, log_total, mixed, key_value):
    stretch, rows = query.shape[0], key_value.shape[0]
    group_width = GROUPS * HEAD_WIDTH
    outs = (
        jax.ShapeDtypeStruct((stretch, group_width), f32),
        jax.ShapeDtypeStruct((2, rows // 2, 2 * HEAD_WIDTH), bf16),
    )
    operands = (meta, query, slope, log_total, mixed, key_value)
    scratch = [((group_width, stretch), f32), ((GROUPS, stretch), f32)]
    kernel = functools.partial(attend_back_kernel, order, group)
    return attention_call(kernel, outs, scratch, 2, "attend_back", *operands)


def body(
    tokens,
    cotangent,
    routes,
    fill_order,
    pic_starts,
    attn_gain,
    moe_gain,
    w_query,
    key_projection,
    value_projection,
    w_out,
    w_router,
    expert_gate,
    expert_up,
    expert_down,
):
    sequences, stretch, width = tokens.shape
    count = sequences * stretch
    parts = lax.axis_size("ctx")
    experts = parts
    capacity = (5 * count * TOP + 4 * experts - 1) // (4 * experts)
    query_width, key_width = QUERY_WIDTH, KEY_WIDTH
    hidden_width = expert_gate.shape[2]
    seq_bits, ctx_bits = bits("seq"), bits("ctx")
    all_bits = seq_bits + ctx_bits
    inward = ctx_bits[-1:] + seq_bits[::-1] + ctx_bits[-2::-1]
    sizes = {"seq": parts, "ctx": 1}
    me = lax.axis_index("seq") * parts + lax.axis_index("ctx")

    def padded(columns):
        block = jnp.concatenate(columns, 1)
        return jnp.pad(block, ((0, 0), (0, LANES - block.shape[1])))

    own_rows = w_query.shape[0]

    def feature(stages):
        owner = jnp.bitwise_xor(jnp.array(flips(stages, sizes), jnp.int32), me)
        return (owner[:, None] * own_rows + jnp.arange(own_rows, dtype=jnp.int32)).reshape(-1)

    def same(left, right):
        return (left[:, None] == right[None, :]).astype(bf16)

    turns = ctx_bits[:-2] + seq_bits + ctx_bits[-2:]
    natural = jnp.arange(width, dtype=jnp.int32)
    gathered, summed = feature(turns[::-1]), feature(inward)
    turn, turn_in, across = same(natural, summed), same(natural, gathered), same(gathered, summed)

    def relative(rows):
        return matmul(rows, turn).astype(bf16)

    def halves(left, right):
        middle = left.shape[1] // 2
        sent = matmul_tn(left[:, middle:], right).astype(bf16)
        return sent, matmul_tn(left[:, :middle], right).astype(bf16)

    picks = routes.reshape(count, TOP)
    order = fill_order.reshape(count)
    routed = jnp.any(picks[:, :, None] == jnp.arange(experts, dtype=jnp.int32), 1)
    earlier = (order[None, :] < order[:, None]).astype(bf16)
    place = matmul(earlier, routed.astype(bf16)).astype(jnp.int32)
    place = jnp.where(routed, place, capacity)
    half = capacity // 2
    chosen_slot = [
        place.T[:, None, :]
        == (begin + jnp.arange(half, dtype=jnp.int32))[None, :, None]
        for begin in (0, half)
    ]
    slot_map = [chosen.astype(bf16).reshape(-1, count) for chosen in chosen_slot]

    def exchange_rows(rows):
        rows = rows.reshape(experts, half, width)
        rows = lax.all_to_all(rows, "ctx", split_axis=0, concat_axis=0, tiled=True)
        return rows.reshape(-1, width)

    out_slope = cotangent.reshape(count, width)
    slot_routes = jnp.concatenate(
        [matmul(part, routed.astype(bf16)).reshape(experts, half, experts) for part in slot_map], 1
    ).astype(bf16)
    slot_routes = lax.all_to_all(slot_routes, "ctx", split_axis=0, concat_axis=0, tiled=True)
    slot_routes = jnp.pad(slot_routes, ((0, 0), (0, 0), (0, LANES - experts)))
    slot_routes = [
        slot_routes[:, begin : begin + half].reshape(-1, LANES) for begin in (0, half)
    ]
    slope_rows = [matmul(part, out_slope).astype(bf16) for part in slot_map]
    slope_rows = jnp.concatenate([part.reshape(experts, half, width) for part in slope_rows], 1)

    block = jnp.concatenate(
        [
            w_query,
            key_projection,
            value_projection,
            padded([attn_gain[:, None]]),
            w_out,
            padded([w_router, moe_gain[:, None]]),
        ],
        1,
    )
    first_width = query_width + 2 * key_width + LANES
    expert_parts = [expert_gate[0], expert_up[0]]
    for index, stage in enumerate(turns):
        other = swap(block if index < 2 else mine, *stage)
        if index in (1, 3) and len(seq_bits) == 1:
            part = index // 2
            other, expert_parts[part] = lax.optimization_barrier(
                (other, (expert_parts[part], swap(expert_parts[part], *seq_bits[0])))
            )
        if index < 2:
            block = jnp.concatenate([block, other], 0)
        if index == 1:
            block, slope_rows = lax.optimization_barrier((block, slope_rows))
            slope_rows = lax.all_to_all(slope_rows, "ctx", split_axis=0, concat_axis=0, tiled=True)
            mine, second_set = block[:, :first_width], block[:, first_width:]
        if index > 2:
            arrived = swap(second_set, *turns[index - 1])
            if index == len(turns) - 1:
                late = second_set, arrived
                continue
            if index < len(turns) - 1:
                other, arrived = lax.optimization_barrier((other, arrived))
            second_set = jnp.concatenate([second_set, arrived], 0)
        if 2 <= index < len(turns) - 1:
            mine = jnp.concatenate([mine, other], 0)
    inputs = tokens.reshape(count, width)
    inputs_turned = matmul(inputs, turn_in)
    inputs = inputs.astype(f32)
    inputs_scaled = inputs_turned * rms_scale(inputs)
    mine, other, slope_rows, slot_routes, inputs_scaled = lax.optimization_barrier(
        (mine, other, slope_rows, slot_routes, inputs_scaled)
    )
    slope_rows = [
        slope_rows[:, begin : begin + half].reshape(-1, width) for begin in (0, half)
    ]
    qkv_width = query_width + 2 * key_width
    weight_low, weight_high = mine[:, :qkv_width], other[:, :qkv_width]
    gain_one = jnp.concatenate([mine[:, qkv_width], other[:, qkv_width]]).astype(f32)

    def whole_expert(part):
        if isinstance(part, tuple):
            own, other = part
            upper = lax.axis_index("seq") > 0
            pair = [jnp.where(upper, other, own), jnp.where(upper, own, other)]
            return jnp.concatenate(pair, 0)
        return gather_blocks(part, seq_bits[::-1], seq_bits).reshape(-1, part.shape[1])

    gate_up = jnp.concatenate([whole_expert(part) for part in expert_parts], 1)
    positions = lax.axis_index("ctx") * stretch + jnp.arange(stretch, dtype=jnp.int32)
    cosine, sine = rope_tables(positions, HEAD_WIDTH)
    normed = (inputs_scaled * gain_one).astype(bf16)

    def project(columns):
        low = matmul(normed[:, : width // 2], weight_low[:, columns])
        return low + matmul(normed[:, width // 2 :], weight_high[:, columns])

    projected = project(slice(query_width, None))
    key_rows = rotate(projected[:, :key_width], KEY_VALUE_HEADS, cosine, sine)
    key_values = lax.all_gather(
        jnp.concatenate([key_rows, projected[:, key_width:]], 1).astype(bf16),
        "ctx",
        axis=0,
        tiled=True,
    )
    projected = project(slice(0, query_width))
    query_rows = rotate(projected, QUERY_HEADS, cosine, sine).astype(bf16)
    second_set, arrived = late
    arrived, query_rows = lax.optimization_barrier((arrived, query_rows))
    second_set = jnp.concatenate([second_set, arrived], 0)
    second_set = jnp.concatenate([second_set, swap(second_set, *turns[-1])], 0)
    second_set = matmul(turn_in, second_set).astype(bf16)
    full_out = second_set[:, :width]
    full_router = second_set[:, width : width + experts]
    gain_two = second_set[:, width + experts].astype(f32)
    meta = jnp.concatenate([lax.axis_index("ctx").astype(jnp.int32)[None], pic_starts[0]])
    mixed_heads, log_total = attend(meta, query_rows, key_values)

    def with_attention(other):
        nonlocal mixed_heads
        mixed_heads, other = lax.optimization_barrier((mixed_heads, other))
        return other

    down = gather_blocks(
        lax.optimization_barrier((expert_down[0], gain_one))[0],
        seq_bits[::-1],
        seq_bits,
        with_attention,
    ).reshape(-1, width)
    attended = mixed_heads.astype(bf16)

    middle = inputs + matmul(attended, full_out)
    enter = rms_norm(middle, gain_two).astype(bf16)
    arrived = [exchange_rows(matmul(part, enter).astype(bf16)) for part in slot_map]

    def gates_of(rows, chosen):
        logits = jnp.where(chosen, matmul(rows, full_router), big_negative)
        shares = jnp.exp(logits - jnp.max(logits, -1, keepdims=True))
        shares = jnp.where(chosen, shares, 0.0)
        return shares / jnp.maximum(jnp.sum(shares, -1, keepdims=True), 1e-30)

    gates = gates_of(enter, routed)

    attended_turned, enter_turned = map(relative, (attended, enter))
    normed_turned = matmul(normed, across).astype(bf16)
    arrived[0], attended_turned, enter_turned, normed_turned = lax.optimization_barrier(
        (arrived[0], attended_turned, enter_turned, normed_turned)
    )
    which = lax.axis_index("ctx").astype(jnp.int32)[None]
    router = second_set[:, width:]
    hidden, result, slope_gates, slope_slots, slope_pre, slope_arrived = ([] for _ in range(6))
    for index in range(2):
        made = list(expert(
            which, arrived[index], slope_rows[index], slot_routes[index], gate_up, down, router)
        )
        if index == 0:
            arrived[1], made[-1] = lax.optimization_barrier((arrived[1], made[-1]))
        for kept, item in zip(
            (hidden, result, slope_gates, slope_slots, slope_pre, slope_arrived), made
        ):
            kept.append(item)
    returned_slopes = [exchange_rows(slope_arrived[0])]
    slope_gates = jnp.concatenate([item.reshape(experts, half) for item in slope_gates], 1)
    slope_gates, returned_slopes[0] = lax.optimization_barrier((slope_gates, returned_slopes[0]))
    returned_gates = lax.all_to_all(slope_gates, "ctx", split_axis=0, concat_axis=0, tiled=True)
    slope_arrived[1], returned_gates, slope_pre, slope_slots = lax.optimization_barrier(
        (slope_arrived[1], returned_gates, slope_pre, slope_slots)
    )
    returned_slopes.append(exchange_rows(slope_arrived[1]))
    grad_gate, grad_up = (
        sum(matmul_tn(arrived[i], slope_pre[i][:, columns]) for i in range(2)).astype(bf16)
        for columns in (slice(0, hidden_width), slice(hidden_width, None))
    )
    grad_down = sum(matmul_tn(hidden[i], slope_slots[i]) for i in range(2)).astype(bf16)
    def sector_halves(grads):
        return grads.reshape([2] * len(seq_bits) + [-1, grads.shape[1]])

    def sector_sum(blocks, arrived):
        for axis, bit in seq_bits:
            mine = ((lax.axis_index(axis) & bit) > 0).astype(jnp.int32)
            sent = lax.dynamic_index_in_dim(blocks, 1 - mine, 0, keepdims=False)
            kept = lax.dynamic_index_in_dim(blocks, mine, 0, keepdims=False)
            other = swap(sent.astype(bf16), axis, bit)
            if (axis, bit) == seq_bits[-1]:
                return kept, arrived(other)
            blocks = kept.astype(f32) + other.astype(f32)

    def ended(pair):
        return pair[0].astype(f32) + pair[1].astype(f32)

    def with_slopes(other):
        nonlocal grad_gate, grad_up
        returned_slopes[1], other, grad_gate, grad_up = lax.optimization_barrier(
            (returned_slopes[1], other, grad_gate, grad_up)
        )
        return other

    grad_down = sector_sum(sector_halves(grad_down), with_slopes)
    returned = jnp.concatenate([part.reshape(experts, half, width) for part in result], 1)
    returned = lax.all_to_all(returned, "ctx", split_axis=0, concat_axis=0, tiled=True)

    slope_gate = 0.0
    for index, chosen in enumerate(chosen_slot):
        part = returned_gates[:, index * half : (index + 1) * half]
        slope_gate = slope_gate + jnp.sum(jnp.where(chosen, part[:, :, None], 0.0), 1).T
    slope_logits = gates * (slope_gate - jnp.sum(gates * slope_gate, -1, keepdims=True))
    slope_logits = slope_logits.astype(bf16)
    slope_enter = matmul_nt(slope_logits, full_router)
    for part, rows in zip(slot_map, returned_slopes):
        slope_enter = slope_enter + matmul_tn(part, rows)

    pull_two = jax.vjp(rms_norm, middle, gain_two)[1]
    slope_middle, grad_gain_two = pull_two(slope_enter)
    slope_middle = out_slope.astype(f32) + slope_middle
    slope_branch = slope_middle.astype(bf16)
    slope_attended = matmul_nt(slope_branch, full_out).astype(bf16)

    kv_order = ctx_bits[::-1]

    def back(group, meta):
        order = [bit for _, bit in kv_order]
        return attend_back(
            order, group, meta, query_rows, slope_attended, log_total, mixed_heads, key_values
        )

    first_q, first_kv = back(0, meta)

    def after_first(other):
        nonlocal first_q, first_kv, meta, grad_up
        first_q, first_kv, meta, grad_up, other = lax.optimization_barrier(
            (first_q, first_kv, meta, grad_up, other)
        )
        return other

    grad_gate = sector_sum(sector_halves(grad_gate), after_first)
    first_sum = Sum(first_kv[1], first_kv[0], kv_order)
    first_sum.step()
    second_q, second_kv = back(1, meta)

    def after_second(other):
        nonlocal second_q, second_kv, grad_gate, slope_branch
        second_q, second_kv, first_sum.sent, grad_gate, slope_branch, other = (
            lax.optimization_barrier(
                (second_q, second_kv, first_sum.sent, grad_gate, slope_branch, other)
            )
        )
        return other

    grad_up = sector_sum(sector_halves(grad_up), after_second)
    second_sum = Sum(second_kv[1], second_kv[0], kv_order)
    first_sum.step()
    second_sum.step()
    second_sum.sent, first_q, second_q = lax.optimization_barrier(
        (second_sum.sent, first_q, second_q)
    )
    slope_query = jnp.concatenate([first_q, second_q], 1)
    slope_query = rotate(slope_query, QUERY_HEADS, cosine, -sine).astype(bf16)
    query_sum = Sum(*halves(normed_turned, slope_query), inward)
    query_sum.step()
    first_sum.sent, second_sum.sent, query_sum.sent, slope_branch, returned = (
        lax.optimization_barrier(
            (first_sum.sent, second_sum.sent, query_sum.sent, slope_branch, returned)
        )
    )
    query_sum.step()
    out_sum = Sum(*halves(attended_turned, slope_branch), inward)
    out_sum.step()
    while len(first_sum.stages) > 1:
        together([first_sum, second_sum])
    first_sum.step()
    second_sum.step()
    (
        first_sum.total,
        second_sum.sent,
        query_sum.sent,
        out_sum.sent,
        slope_query,
        grad_gate,
        grad_up,
        grad_gain_two,
        enter_turned,
    ) = lax.optimization_barrier(
        (
            first_sum.total,
            second_sum.sent,
            query_sum.sent,
            out_sum.sent,
            slope_query,
            grad_gate,
            grad_up,
            grad_gain_two,
            enter_turned,
        )
    )
    grad_router = matmul_tn(enter_turned, slope_logits)
    out_sum.step()
    second_sum.step()
    totals = [first_sum.total, second_sum.total]
    totals[1], returned = lax.optimization_barrier((totals[1], returned))
    output = middle
    for chosen, rows in ((jnp.concatenate(chosen_slot, 1), returned.reshape(-1, width)),):
        mix = jnp.where(chosen, gates.T[:, None, :], 0.0).reshape(-1, count)
        mix_high = mix.astype(bf16)
        mix_low = (mix - mix_high.astype(f32)).astype(bf16)
        output = output + matmul_tn(mix_high, rows) + matmul_tn(mix_low, rows)
    output = output.astype(bf16).reshape(tokens.shape)
    slope_key = jnp.concatenate([total[:, :HEAD_WIDTH] for total in totals], 1)
    slope_key = rotate(slope_key, KEY_VALUE_HEADS, cosine, -sine)
    slope_rest = [slope_key] + [total[:, HEAD_WIDTH:] for total in totals]
    slope_rest = jnp.concatenate(slope_rest, 1).astype(bf16)
    slope_projected = jnp.concatenate([slope_query, slope_rest], 1)
    slope_normed = jnp.concatenate(
        [matmul_nt(slope_projected, part) for part in (weight_low, weight_high)], 1
    )
    pull_one = jax.vjp(rms_norm, inputs_turned, gain_one)[1]
    slope_inputs = pull_one(slope_normed)[0]
    small = padded([grad_router.astype(bf16), relative(grad_gain_two.astype(bf16)[None]).T])
    rest_sum = Sum(
        *(
            jnp.concatenate([grads, part], 1)
            for grads, part in zip(
                halves(normed_turned, slope_rest), (small[width // 2 :], small[: width // 2])
            )
        ),
        inward,
    )
    together([item for item in (rest_sum, query_sum) if item.stages])
    together([item for item in (rest_sum, query_sum, out_sum) if item.stages])
    while rest_sum.stages:
        together([item for item in (rest_sum, query_sum, out_sum) if item.stages])
    for item in (query_sum, out_sum):
        while item.stages:
            item.step()
    grads_rest = rest_sum.total
    slope_high = slope_inputs.astype(bf16)
    slope_low = (slope_inputs - slope_high.astype(f32)).astype(bf16)
    grad_input = slope_middle + matmul_nt(slope_high, turn_in) + matmul_nt(slope_low, turn_in)
    grad_input = grad_input.reshape(tokens.shape)
    grad_gain_one = jnp.sum(w_query.astype(f32) * query_sum.total, 1)
    own_kv = jnp.concatenate([key_projection, value_projection], 1).astype(f32)
    grad_gain_one = grad_gain_one + jnp.sum(own_kv * grads_rest[:, : 2 * key_width], 1)
    grad_gain_one = grad_gain_one / attn_gain.astype(f32)
    return (
        output,
        grad_input,
        grad_gain_one,
        grads_rest[:, 2 * key_width + experts],
        query_sum.total,
        grads_rest[:, :key_width],
        grads_rest[:, key_width : 2 * key_width],
        out_sum.total,
        grads_rest[:, 2 * key_width : 2 * key_width + experts],
        ended(grad_gate)[None],
        ended(grad_up)[None],
        ended(grad_down)[None],
    )


def solution(mesh):
    rows = P("seq", "ctx", None)
    shard = P(("seq", "ctx"), None)
    vector = P(("seq", "ctx"))
    expert = P("ctx", "seq", None)
    return jax.shard_map(
        body,
        mesh=mesh,
        in_specs=(rows, rows, rows, P("seq", "ctx"), P("seq", None), vector, vector)
        + (shard,) * 5
        + (expert,) * 3,
        out_specs=(rows, rows, vector, vector) + (shard,) * 5 + (expert,) * 3,
        check_vma=False,
    )
```

```python
import functools
import math

import jax
import jax.numpy as jnp
from jax import lax
from jax.experimental import pallas as pl
from jax.experimental.pallas import tpu as pltpu
from jax.sharding import PartitionSpec as P

QUERY_HEADS = 12
KEY_VALUE_HEADS = 2
HEAD_WIDTH = 128
TOP = 4
PIC = 256
NPIC = 4
LANES = 128
GROUPS = QUERY_HEADS // KEY_VALUE_HEADS
QUERY_WIDTH = QUERY_HEADS * HEAD_WIDTH
KEY_WIDTH = KEY_VALUE_HEADS * HEAD_WIDTH
SCALE = 1.0 / math.sqrt(HEAD_WIDTH)
EXP2_SCALE = SCALE * math.log2(math.e)
BLOCKS = 2
SKEW = 1
VMEM_BYTES = 48 << 20

epsilon = 1e-06
rope_base = 10000.0
big_negative = -1e30
bf16 = jnp.bfloat16
f32 = jnp.float32


def matmul(left, right):
    return jnp.dot(left, right, preferred_element_type=f32)


def matmul_nt(left, right):
    return lax.dot_general(left, right, (((1,), (1,)), ((), ())), preferred_element_type=f32)


def matmul_tn(left, right):
    return lax.dot_general(left, right, (((0,), (0,)), ((), ())), preferred_element_type=f32)


def rms_scale(rows):
    return lax.rsqrt(jnp.mean(rows * rows, -1, keepdims=True) + epsilon)


def rms_norm(rows, gain):
    return rows * rms_scale(rows) * gain


def rope_tables(positions, head_size):
    half = head_size // 2
    inverse = rope_base ** (-(jnp.arange(half, dtype=f32) * 2.0 / head_size))
    angles = positions.astype(f32)[:, None] * inverse[None, :]
    return (jnp.cos(angles), jnp.sin(angles))


def rotate(rows, heads, cosine, sine):
    shaped = rows.reshape(rows.shape[0], heads, HEAD_WIDTH)
    half = HEAD_WIDTH // 2
    first, second = shaped[..., :half], shaped[..., half:]
    cosine, sine = cosine[:, None, :], sine[:, None, :]
    turned = jnp.concatenate(
        [first * cosine - second * sine, second * cosine + first * sine], -1
    )
    return turned.reshape(rows.shape)


def bits(axis):
    size = lax.axis_size(axis)
    return [(axis, 1 << place) for place in reversed(range(size.bit_length() - 1))]


def swap(block, axis, bit):
    size = lax.axis_size(axis)
    return lax.ppermute(block, axis, [(index, index ^ bit) for index in range(size)])


def gather_blocks(block, stages, order, arrived=None):
    held = []
    for stage in stages:
        axis, bit = stage
        other = swap(block, axis, bit)
        if arrived is not None and stage == stages[-1]:
            other = arrived(other)
        upper = (lax.axis_index(axis) & bit) > 0
        place = sum(order.index(known) < order.index(stage) for known in held)
        block = jnp.stack(
            [jnp.where(upper, other, block), jnp.where(upper, block, other)], place
        )
        held.append(stage)
    return block


class Sum:
    def __init__(self, sent, kept, stages):
        self.sent, self.kept, self.stages = sent, kept, list(stages)

    def step(self):
        axis, bit = self.stages.pop(0)
        other = swap(self.sent, axis, bit)
        if not self.stages:
            self.total = self.kept.astype(f32) + other.astype(f32)
            return
        half = self.kept.shape[0] // 2
        self.sent = (self.kept[half:].astype(f32) + other[half:].astype(f32)).astype(bf16)
        self.kept = (self.kept[:half].astype(f32) + other[:half].astype(f32)).astype(bf16)


def together(sums, also=()):
    for item in sums:
        item.step()
    live = [item for item in sums if item.stages]
    sent, also = lax.optimization_barrier(([item.sent for item in live], also))
    for item, block in zip(live, sent):
        item.sent = block
    return also


def flips(stages, sizes):
    masks = []
    for block in range(1 << len(stages)):
        mask = 0
        for place, (axis, bit) in enumerate(stages):
            if (block >> (len(stages) - 1 - place)) & 1:
                mask |= bit * sizes[axis]
        masks.append(mask)
    return masks


def visible_keys(meta, step, stretch):
    span = BLOCKS * stretch
    keys = step * span + lax.broadcasted_iota(jnp.int32, (span, 1), 0)
    queries = meta[0] * stretch + lax.broadcasted_iota(jnp.int32, (1, stretch), 1)

    def label(positions):
        found = jnp.zeros(positions.shape, jnp.int32)
        for index in range(NPIC):
            start = meta[1 + index]
            inside = (positions >= start) & (positions < start + PIC)
            found = jnp.where(inside, index + 1, found)
        return found

    query_label = label(queries)
    return (keys <= queries) | ((label(keys) == query_label) & (query_label > 0))


def for_each_step(meta, stretch, steps, process, skip=None):
    span = BLOCKS * stretch
    low, high = meta[0] * stretch, (meta[0] + 1) * stretch

    def turn(step, carry):
        needed = step * span < high + PIC - 1
        edge = (step + 1) * span > low

        @pl.when(needed & edge)
        def _():
            process(step, True)

        @pl.when(needed & jnp.logical_not(edge))
        def _():
            process(step, False)

        if skip is not None:

            @pl.when(jnp.logical_not(needed))
            def _():
                skip(step)

        return carry

    lax.fori_loop(0, steps, turn, 0)


def head_columns(head, start=0):
    return slice(start + head * HEAD_WIDTH, start + (head + 1) * HEAD_WIDTH)


def attend_kernel(meta, query, key_value, out, log_total, peak, total, accum):
    stretch = query.shape[0]
    span = BLOCKS * stretch
    peak[...] = jnp.full(peak.shape, big_negative, f32)
    total[...] = jnp.zeros(total.shape, f32)
    accum[...] = jnp.zeros(accum.shape, f32)

    def process(step, edge):
        rows = pl.ds(pl.multiple_of(step * span, span), span)
        if edge:
            visible = visible_keys(meta, step, stretch)
        keys, values = [], []
        for group in range(KEY_VALUE_HEADS):
            keys.append(key_value[rows, head_columns(group)])
            turned = key_value[rows, head_columns(group, KEY_WIDTH)].T
            values.append(jnp.concatenate([turned, jnp.ones((16, span), bf16)], 0))

        def score(head):
            scores = matmul_nt(keys[head // GROUPS], query[:, head_columns(head)])
            if edge:
                scores = jnp.where(visible, scores, big_negative)
            old = peak[head : head + 1, :]
            return scores, old, jnp.maximum(old, jnp.max(scores, 0, keepdims=True))

        def weigh(head, scores, old, new):
            weights = jnp.exp2((scores - new) * EXP2_SCALE).astype(bf16)
            shrink = jnp.exp2((old - new) * EXP2_SCALE)
            sums = matmul(values[head // GROUPS], weights)
            row, columns = slice(head, head + 1), head_columns(head)
            peak[row, :] = new
            total[row, :] = total[row, :] * shrink + sums[HEAD_WIDTH : HEAD_WIDTH + 1]
            accum[columns, :] = accum[columns, :] * shrink + sums[:HEAD_WIDTH]

        waiting = []
        for head in range(QUERY_HEADS):
            waiting.append((head, *score(head)))
            if len(waiting) > 2:
                weigh(*waiting.pop(0))
        for item in waiting:
            weigh(*item)

    for_each_step(meta, stretch, key_value.shape[0] // span, process)
    for head in range(QUERY_HEADS):
        row, columns = slice(head, head + 1), head_columns(head)
        out[:, columns] = (accum[columns, :] / total[row, :]).T
        log_total[row, :] = peak[row, :] * EXP2_SCALE + jnp.log2(total[row, :])


def attend_back_kernel(
    order,
    group,
    meta,
    query,
    slope,
    log_total,
    mixed,
    key_value,
    slope_query,
    out,
    accum,
    delta,
):
    stretch = query.shape[0]
    span = BLOCKS * stretch
    accum[...] = jnp.zeros(accum.shape, f32)
    for index in range(GROUPS):
        columns = head_columns(group * GROUPS + index)
        product = slope[:, columns].astype(f32) * mixed[:, columns]
        delta[index : index + 1, :] = jnp.sum(product.T, 0, keepdims=True)

    def store(step, part, columns, block):
        flip = jnp.bitwise_xor(BLOCKS * step + part, meta[0])
        first, *others = order
        place = 0
        for index, bit in enumerate(others):
            place = place + ((flip // bit) & 1) * (1 << (len(others) - 1 - index))
        place = pl.ds(pl.multiple_of(place * stretch, stretch), stretch)
        out[(flip // first) & 1, place, columns] = block

    def process(step, edge):
        rows = pl.ds(pl.multiple_of(step * span, span), span)
        if edge:
            visible = visible_keys(meta, step, stretch)
        keys = key_value[rows, head_columns(group)]
        values = key_value[rows, head_columns(group, KEY_WIDTH)]
        keys_turned = keys.T

        def slopes_of(index):
            columns = head_columns(group * GROUPS + index)
            row = slice(group * GROUPS + index, group * GROUPS + index + 1)
            scores = matmul_nt(keys, query[:, columns])
            probs = jnp.exp2(scores * EXP2_SCALE - log_total[row, :])
            if edge:
                probs = jnp.where(visible, probs, 0.0)
            slope_probs = matmul_nt(values, slope[:, columns])
            slope_scores = (probs * (slope_probs - delta[index : index + 1, :])).astype(bf16)
            return index, probs.astype(bf16), slope_scores

        slope_k = jnp.zeros((span, HEAD_WIDTH), f32)
        slope_v = jnp.zeros((span, HEAD_WIDTH), f32)
        waiting = []
        for index in range(GROUPS + SKEW):
            if index < GROUPS:
                waiting.append(slopes_of(index))
            if index >= SKEW:
                own, probs, slope_scores = waiting.pop(0)
                columns, place = head_columns(group * GROUPS + own), head_columns(own)
                slope_v = slope_v + matmul(probs, slope[:, columns])
                slope_k = slope_k + matmul(slope_scores, query[:, columns])
                accum[place, :] = accum[place, :] + matmul(keys_turned, slope_scores)
        slope_k, slope_v = (slope_k * SCALE).astype(bf16), slope_v.astype(bf16)
        for which, block in enumerate((slope_k, slope_v)):
            for part in range(BLOCKS):
                own = block[part * stretch : (part + 1) * stretch]
                store(step, part, head_columns(which), own)

    def skip(step):
        for part in range(BLOCKS):
            store(step, part, slice(None), jnp.zeros((stretch, 2 * HEAD_WIDTH), bf16))

    for_each_step(meta, stretch, key_value.shape[0] // span, process, skip)
    for index in range(GROUPS):
        columns = head_columns(index)
        slope_query[:, columns] = (accum[columns, :] * SCALE).T


def expert_kernel(
    which,
    rows,
    slopes,
    chosen,
    gate_up,
    down,
    router,
    hidden_out,
    result_out,
    gates_out,
    slots_out,
    pre_out,
    slope_out,
):
    hidden_width = down.shape[0]
    incoming = rows[...]
    logits = jnp.where(chosen[...] > 0, matmul(incoming, router[...]), big_negative)
    shares = jnp.exp(logits - jnp.max(logits, -1, keepdims=True))
    shares = jnp.where(chosen[...] > 0, shares, 0.0)
    column = lax.broadcasted_iota(jnp.int32, shares.shape, 1)
    own = jnp.sum(jnp.where(column == which[0], shares, 0.0), -1, keepdims=True)
    gates = own / jnp.maximum(jnp.sum(shares, -1, keepdims=True), 1e-30)
    slots = (gates * slopes[...].astype(f32)).astype(bf16)
    slots_out[...] = slots
    pre = matmul(incoming, gate_up[...])
    gate, up = pre[:, :hidden_width], pre[:, hidden_width:]
    root, cubic = math.sqrt(2.0 / math.pi), 0.044715
    square = gate * gate
    bend = jnp.tanh(root * (gate + cubic * gate * square))
    gelu = 0.5 * gate * (1.0 + bend)
    rise = 0.5 * (1.0 + bend) + 0.5 * gate * (1.0 - bend * bend) * root * (
        1.0 + 3.0 * cubic * square
    )
    hidden = (gelu * up).astype(bf16)
    hidden_out[...] = hidden
    result = matmul(hidden, down[...]).astype(bf16)
    result_out[...] = result
    gates_out[...] = jnp.sum(slopes[...].astype(f32) * result.astype(f32), -1, keepdims=True)
    slope_hidden = matmul_nt(slots, down[...])
    slope_pre = jnp.concatenate([slope_hidden * up * rise, slope_hidden * gelu], 1).astype(bf16)
    pre_out[...] = slope_pre
    slope_out[...] = matmul_nt(slope_pre, gate_up[...]).astype(bf16)


def expert(which, rows, slopes, chosen, gate_up, down, router):
    count, width = rows.shape
    hidden_width = down.shape[0]
    block = count // 2

    def tile(columns):
        return pl.BlockSpec((block, columns), lambda step: (step, 0))

    def whole(array):
        return pl.BlockSpec(array.shape, lambda step: (0, 0))

    shapes = [(hidden_width, bf16), (width, bf16), (1, f32), (width, bf16)]
    shapes += [(2 * hidden_width, bf16), (width, bf16)]
    return pl.pallas_call(
        expert_kernel,
        grid=(2,),
        out_shape=[jax.ShapeDtypeStruct((count, columns), kind) for columns, kind in shapes],
        in_specs=[
            pl.BlockSpec(memory_space=pltpu.SMEM),
            tile(width),
            tile(width),
            tile(LANES),
            whole(gate_up),
            whole(down),
            whole(router),
        ],
        out_specs=[tile(columns) for columns, _ in shapes],
        compiler_params=pltpu.CompilerParams(vmem_limit_bytes=VMEM_BYTES),
        cost_estimate=pl.CostEstimate(
            flops=12 * count * width * hidden_width,
            bytes_accessed=20 * count * width,
            transcendentals=count * hidden_width,
        ),
        name="expert",
    )(which, rows, slopes, chosen, gate_up, down, router)


def attention_call(kernel, outs, scratch, products, name, meta, *operands):
    vmem = pl.BlockSpec(memory_space=pltpu.VMEM)
    pairs = QUERY_HEADS * operands[0].shape[0] * operands[-1].shape[0]
    return pl.pallas_call(
        kernel,
        out_shape=outs,
        in_specs=[pl.BlockSpec(memory_space=pltpu.SMEM)] + [vmem] * len(operands),
        out_specs=(vmem,) * len(outs),
        scratch_shapes=[pltpu.VMEM(*shape) for shape in scratch],
        compiler_params=pltpu.CompilerParams(vmem_limit_bytes=VMEM_BYTES),
        cost_estimate=pl.CostEstimate(
            flops=products * pairs, bytes_accessed=QUERY_WIDTH * 1024, transcendentals=0
        ),
        name=name,
    )(meta, *operands)


def attend(meta, query, key_value):
    stretch = query.shape[0]
    stats = (QUERY_HEADS, stretch)
    outs = (
        jax.ShapeDtypeStruct((stretch, QUERY_WIDTH), f32),
        jax.ShapeDtypeStruct(stats, f32),
    )
    scratch = [(stats, f32), (stats, f32), ((QUERY_WIDTH, stretch), f32)]
    return attention_call(attend_kernel, outs, scratch, 2, "attend", meta, query, key_value)


def attend_back(order, group, meta, query, slope, log_total, mixed, key_value):
    stretch, rows = query.shape[0], key_value.shape[0]
    group_width = GROUPS * HEAD_WIDTH
    outs = (
        jax.ShapeDtypeStruct((stretch, group_width), f32),
        jax.ShapeDtypeStruct((2, rows // 2, 2 * HEAD_WIDTH), bf16),
    )
    operands = (meta, query, slope, log_total, mixed, key_value)
    scratch = [((group_width, stretch), f32), ((GROUPS, stretch), f32)]
    kernel = functools.partial(attend_back_kernel, order, group)
    return attention_call(kernel, outs, scratch, 2, "attend_back", *operands)


def body(
    tokens,
    cotangent,
    routes,
    fill_order,
    pic_starts,
    attn_gain,
    moe_gain,
    w_query,
    key_projection,
    value_projection,
    w_out,
    w_router,
    expert_gate,
    expert_up,
    expert_down,
):
    sequences, stretch, width = tokens.shape
    count = sequences * stretch
    parts = lax.axis_size("ctx")
    experts = parts
    capacity = (5 * count * TOP + 4 * experts - 1) // (4 * experts)
    query_width, key_width = QUERY_WIDTH, KEY_WIDTH
    hidden_width = expert_gate.shape[2]
    seq_bits, ctx_bits = bits("seq"), bits("ctx")
    all_bits = seq_bits + ctx_bits
    inward = ctx_bits[-1:] + seq_bits[::-1] + ctx_bits[-2::-1]
    sizes = {"seq": parts, "ctx": 1}
    me = lax.axis_index("seq") * parts + lax.axis_index("ctx")

    def padded(columns):
        block = jnp.concatenate(columns, 1)
        return jnp.pad(block, ((0, 0), (0, LANES - block.shape[1])))

    own_rows = w_query.shape[0]

    def feature(stages):
        owner = jnp.bitwise_xor(jnp.array(flips(stages, sizes), jnp.int32), me)
        return (owner[:, None] * own_rows + jnp.arange(own_rows, dtype=jnp.int32)).reshape(-1)

    def same(left, right):
        return (left[:, None] == right[None, :]).astype(bf16)

    turns = ctx_bits[:-2] + seq_bits + ctx_bits[-2:]
    natural = jnp.arange(width, dtype=jnp.int32)
    gathered, summed = feature(turns[::-1]), feature(inward)
    turn, turn_in, across = same(natural, summed), same(natural, gathered), same(gathered, summed)

    def relative(rows):
        return matmul(rows, turn).astype(bf16)

    def halves(left, right):
        middle = left.shape[1] // 2
        sent = matmul_tn(left[:, middle:], right).astype(bf16)
        return sent, matmul_tn(left[:, :middle], right).astype(bf16)

    picks = routes.reshape(count, TOP)
    order = fill_order.reshape(count)
    routed = jnp.any(picks[:, :, None] == jnp.arange(experts, dtype=jnp.int32), 1)
    earlier = (order[None, :] < order[:, None]).astype(bf16)
    place = matmul(earlier, routed.astype(bf16)).astype(jnp.int32)
    place = jnp.where(routed, place, capacity)
    half = capacity // 2
    chosen_slot = [
        place.T[:, None, :]
        == (begin + jnp.arange(half, dtype=jnp.int32))[None, :, None]
        for begin in (0, half)
    ]
    slot_map = [chosen.astype(bf16).reshape(-1, count) for chosen in chosen_slot]

    def exchange_rows(rows):
        rows = rows.reshape(experts, half, width)
        rows = lax.all_to_all(rows, "ctx", split_axis=0, concat_axis=0, tiled=True)
        return rows.reshape(-1, width)

    out_slope = cotangent.reshape(count, width)
    slot_routes = jnp.concatenate(
        [matmul(part, routed.astype(bf16)).reshape(experts, half, experts) for part in slot_map], 1
    ).astype(bf16)
    slot_routes = lax.all_to_all(slot_routes, "ctx", split_axis=0, concat_axis=0, tiled=True)
    slot_routes = jnp.pad(slot_routes, ((0, 0), (0, 0), (0, LANES - experts)))
    slot_routes = [
        slot_routes[:, begin : begin + half].reshape(-1, LANES) for begin in (0, half)
    ]
    slope_rows = [matmul(part, out_slope).astype(bf16) for part in slot_map]
    slope_rows = jnp.concatenate([part.reshape(experts, half, width) for part in slope_rows], 1)

    block = jnp.concatenate(
        [
            w_query,
            key_projection,
            value_projection,
            padded([attn_gain[:, None]]),
            w_out,
            padded([w_router, moe_gain[:, None]]),
        ],
        1,
    )
    first_width = query_width + 2 * key_width + LANES
    expert_parts = [expert_gate[0], expert_up[0]]
    for index, stage in enumerate(turns):
        other = swap(block if index < 2 else mine, *stage)
        if index in (1, 3) and len(seq_bits) == 1:
            part = index // 2
            other, expert_parts[part] = lax.optimization_barrier(
                (other, (expert_parts[part], swap(expert_parts[part], *seq_bits[0])))
            )
        if index < 2:
            block = jnp.concatenate([block, other], 0)
        if index == 1:
            block, slope_rows = lax.optimization_barrier((block, slope_rows))
            slope_rows = lax.all_to_all(slope_rows, "ctx", split_axis=0, concat_axis=0, tiled=True)
            mine, second_set = block[:, :first_width], block[:, first_width:]
        if index > 2:
            arrived = swap(second_set, *turns[index - 1])
            if index == len(turns) - 1:
                late = second_set, arrived
                continue
            if index < len(turns) - 1:
                other, arrived = lax.optimization_barrier((other, arrived))
            second_set = jnp.concatenate([second_set, arrived], 0)
        if 2 <= index < len(turns) - 1:
            mine = jnp.concatenate([mine, other], 0)
    inputs = tokens.reshape(count, width)
    inputs_turned = matmul(inputs, turn_in)
    inputs = inputs.astype(f32)
    inputs_scaled = inputs_turned * rms_scale(inputs)
    mine, other, slope_rows, slot_routes, inputs_scaled = lax.optimization_barrier(
        (mine, other, slope_rows, slot_routes, inputs_scaled)
    )
    slope_rows = [
        slope_rows[:, begin : begin + half].reshape(-1, width) for begin in (0, half)
    ]
    qkv_width = query_width + 2 * key_width
    weight_low, weight_high = mine[:, :qkv_width], other[:, :qkv_width]
    gain_one = jnp.concatenate([mine[:, qkv_width], other[:, qkv_width]]).astype(f32)

    def whole_expert(part):
        if isinstance(part, tuple):
            own, other = part
            upper = lax.axis_index("seq") > 0
            pair = [jnp.where(upper, other, own), jnp.where(upper, own, other)]
            return jnp.concatenate(pair, 0)
        return gather_blocks(part, seq_bits[::-1], seq_bits).reshape(-1, part.shape[1])

    gate_up = jnp.concatenate([whole_expert(part) for part in expert_parts], 1)
    positions = lax.axis_index("ctx") * stretch + jnp.arange(stretch, dtype=jnp.int32)
    cosine, sine = rope_tables(positions, HEAD_WIDTH)
    normed = (inputs_scaled * gain_one).astype(bf16)

    def project(columns):
        low = matmul(normed[:, : width // 2], weight_low[:, columns])
        return low + matmul(normed[:, width // 2 :], weight_high[:, columns])

    projected = project(slice(query_width, None))
    key_rows = rotate(projected[:, :key_width], KEY_VALUE_HEADS, cosine, sine)
    key_values = lax.all_gather(
        jnp.concatenate([key_rows, projected[:, key_width:]], 1).astype(bf16),
        "ctx",
        axis=0,
        tiled=True,
    )
    projected = project(slice(0, query_width))
    query_rows = rotate(projected, QUERY_HEADS, cosine, sine).astype(bf16)
    second_set, arrived = late
    arrived, query_rows = lax.optimization_barrier((arrived, query_rows))
    second_set = jnp.concatenate([second_set, arrived], 0)
    second_set = jnp.concatenate([second_set, swap(second_set, *turns[-1])], 0)
    second_set = matmul(turn_in, second_set).astype(bf16)
    full_out = second_set[:, :width]
    full_router = second_set[:, width : width + experts]
    gain_two = second_set[:, width + experts].astype(f32)
    meta = jnp.concatenate([lax.axis_index("ctx").astype(jnp.int32)[None], pic_starts[0]])
    mixed_heads, log_total = attend(meta, query_rows, key_values)

    def with_attention(other):
        nonlocal mixed_heads
        mixed_heads, other = lax.optimization_barrier((mixed_heads, other))
        return other

    down = gather_blocks(
        lax.optimization_barrier((expert_down[0], gain_one))[0],
        seq_bits[::-1],
        seq_bits,
        with_attention,
    ).reshape(-1, width)
    attended = mixed_heads.astype(bf16)

    middle = inputs + matmul(attended, full_out)
    enter = rms_norm(middle, gain_two).astype(bf16)
    arrived = [exchange_rows(matmul(part, enter).astype(bf16)) for part in slot_map]

    def gates_of(rows, chosen):
        logits = jnp.where(chosen, matmul(rows, full_router), big_negative)
        shares = jnp.exp(logits - jnp.max(logits, -1, keepdims=True))
        shares = jnp.where(chosen, shares, 0.0)
        return shares / jnp.maximum(jnp.sum(shares, -1, keepdims=True), 1e-30)

    gates = gates_of(enter, routed)

    attended_turned, enter_turned = map(relative, (attended, enter))
    normed_turned = matmul(normed, across).astype(bf16)
    arrived[0], attended_turned, enter_turned, normed_turned = lax.optimization_barrier(
        (arrived[0], attended_turned, enter_turned, normed_turned)
    )
    which = lax.axis_index("ctx").astype(jnp.int32)[None]
    router = second_set[:, width:]
    hidden, result, slope_gates, slope_slots, slope_pre, slope_arrived = ([] for _ in range(6))
    for index in range(2):
        made = list(expert(
            which, arrived[index], slope_rows[index], slot_routes[index], gate_up, down, router)
        )
        if index == 0:
            arrived[1], made[-1] = lax.optimization_barrier((arrived[1], made[-1]))
        for kept, item in zip(
            (hidden, result, slope_gates, slope_slots, slope_pre, slope_arrived), made
        ):
            kept.append(item)
    returned_slopes = [exchange_rows(slope_arrived[0])]
    slope_gates = jnp.concatenate([item.reshape(experts, half) for item in slope_gates], 1)
    slope_gates, returned_slopes[0] = lax.optimization_barrier((slope_gates, returned_slopes[0]))
    returned_gates = lax.all_to_all(slope_gates, "ctx", split_axis=0, concat_axis=0, tiled=True)
    slope_arrived[1], returned_gates, slope_pre, slope_slots = lax.optimization_barrier(
        (slope_arrived[1], returned_gates, slope_pre, slope_slots)
    )
    returned_slopes.append(exchange_rows(slope_arrived[1]))
    grad_gate, grad_up = (
        sum(matmul_tn(arrived[i], slope_pre[i][:, columns]) for i in range(2)).astype(bf16)
        for columns in (slice(0, hidden_width), slice(hidden_width, None))
    )
    grad_down = sum(matmul_tn(hidden[i], slope_slots[i]) for i in range(2)).astype(bf16)
    def sector_halves(grads):
        return grads.reshape([2] * len(seq_bits) + [-1, grads.shape[1]])

    def sector_sum(blocks, arrived):
        for axis, bit in seq_bits:
            mine = ((lax.axis_index(axis) & bit) > 0).astype(jnp.int32)
            sent = lax.dynamic_index_in_dim(blocks, 1 - mine, 0, keepdims=False)
            kept = lax.dynamic_index_in_dim(blocks, mine, 0, keepdims=False)
            other = swap(sent.astype(bf16), axis, bit)
            if (axis, bit) == seq_bits[-1]:
                return kept, arrived(other)
            blocks = kept.astype(f32) + other.astype(f32)

    def ended(pair):
        return pair[0].astype(f32) + pair[1].astype(f32)

    def with_slopes(other):
        nonlocal grad_gate, grad_up
        returned_slopes[1], other, grad_gate, grad_up = lax.optimization_barrier(
            (returned_slopes[1], other, grad_gate, grad_up)
        )
        return other

    grad_down = sector_sum(sector_halves(grad_down), with_slopes)
    returned = jnp.concatenate([part.reshape(experts, half, width) for part in result], 1)
    returned = lax.all_to_all(returned, "ctx", split_axis=0, concat_axis=0, tiled=True)

    slope_gate = 0.0
    for index, chosen in enumerate(chosen_slot):
        part = returned_gates[:, index * half : (index + 1) * half]
        slope_gate = slope_gate + jnp.sum(jnp.where(chosen, part[:, :, None], 0.0), 1).T
    slope_logits = gates * (slope_gate - jnp.sum(gates * slope_gate, -1, keepdims=True))
    slope_logits = slope_logits.astype(bf16)
    slope_enter = matmul_nt(slope_logits, full_router)
    for part, rows in zip(slot_map, returned_slopes):
        slope_enter = slope_enter + matmul_tn(part, rows)

    pull_two = jax.vjp(rms_norm, middle, gain_two)[1]
    slope_middle, grad_gain_two = pull_two(slope_enter)
    slope_middle = out_slope.astype(f32) + slope_middle
    slope_branch = slope_middle.astype(bf16)
    slope_attended = matmul_nt(slope_branch, full_out).astype(bf16)

    kv_order = ctx_bits[::-1]

    def back(group, meta):
        order = [bit for _, bit in kv_order]
        return attend_back(
            order, group, meta, query_rows, slope_attended, log_total, mixed_heads, key_values
        )

    first_q, first_kv = back(0, meta)

    def after_first(other):
        nonlocal first_q, first_kv, meta, grad_up
        first_q, first_kv, meta, grad_up, other = lax.optimization_barrier(
            (first_q, first_kv, meta, grad_up, other)
        )
        return other

    grad_gate = sector_sum(sector_halves(grad_gate), after_first)
    first_sum = Sum(first_kv[1], first_kv[0], kv_order)
    first_sum.step()
    second_q, second_kv = back(1, meta)

    def after_second(other):
        nonlocal second_q, second_kv, grad_gate, slope_branch
        second_q, second_kv, first_sum.sent, grad_gate, slope_branch, other = (
            lax.optimization_barrier(
                (second_q, second_kv, first_sum.sent, grad_gate, slope_branch, other)
            )
        )
        return other

    grad_up = sector_sum(sector_halves(grad_up), after_second)
    second_sum = Sum(second_kv[1], second_kv[0], kv_order)
    first_sum.step()
    second_sum.step()
    second_sum.sent, first_q, second_q = lax.optimization_barrier(
        (second_sum.sent, first_q, second_q)
    )
    slope_query = jnp.concatenate([first_q, second_q], 1)
    slope_query = rotate(slope_query, QUERY_HEADS, cosine, -sine).astype(bf16)
    query_sum = Sum(*halves(normed_turned, slope_query), inward)
    query_sum.step()
    first_sum.sent, second_sum.sent, query_sum.sent, slope_branch, returned = (
        lax.optimization_barrier(
            (first_sum.sent, second_sum.sent, query_sum.sent, slope_branch, returned)
        )
    )
    query_sum.step()
    out_sum = Sum(*halves(attended_turned, slope_branch), inward)
    out_sum.step()
    while len(first_sum.stages) > 1:
        together([first_sum, second_sum])
    first_sum.step()
    second_sum.step()
    (
        first_sum.total,
        second_sum.sent,
        query_sum.sent,
        out_sum.sent,
        slope_query,
        grad_gate,
        grad_up,
        grad_gain_two,
        enter_turned,
    ) = lax.optimization_barrier(
        (
            first_sum.total,
            second_sum.sent,
            query_sum.sent,
            out_sum.sent,
            slope_query,
            grad_gate,
            grad_up,
            grad_gain_two,
            enter_turned,
        )
    )
    grad_router = matmul_tn(enter_turned, slope_logits)
    out_sum.step()
    second_sum.step()
    totals = [first_sum.total, second_sum.total]
    slope_key = jnp.concatenate([total[:, :HEAD_WIDTH] for total in totals], 1)
    slope_key = rotate(slope_key, KEY_VALUE_HEADS, cosine, -sine)
    slope_rest = [slope_key] + [total[:, HEAD_WIDTH:] for total in totals]
    slope_rest = jnp.concatenate(slope_rest, 1).astype(bf16)
    small = padded([grad_router.astype(bf16), relative(grad_gain_two.astype(bf16)[None]).T])
    rest_sum = Sum(
        *(
            jnp.concatenate([grads, part], 1)
            for grads, part in zip(
                halves(normed_turned, slope_rest), (small[width // 2 :], small[: width // 2])
            )
        ),
        inward,
    )
    slope_rest = together([item for item in (rest_sum, query_sum) if item.stages], slope_rest)
    slope_projected = jnp.concatenate([slope_query, slope_rest], 1)
    slope_normed = jnp.concatenate(
        [matmul_nt(slope_projected, part) for part in (weight_low, weight_high)], 1
    )
    pull_one = jax.vjp(rms_norm, inputs_turned, gain_one)[1]
    slope_inputs = pull_one(slope_normed)[0]
    returned = together(
        [item for item in (rest_sum, query_sum, out_sum) if item.stages], returned
    )
    output = middle
    for chosen, rows in ((jnp.concatenate(chosen_slot, 1), returned.reshape(-1, width)),):
        mix = jnp.where(chosen, gates.T[:, None, :], 0.0).reshape(-1, count)
        output = output + matmul_tn(mix.astype(bf16), rows)
    output = output.astype(bf16).reshape(tokens.shape)
    while rest_sum.stages:
        together([item for item in (rest_sum, query_sum, out_sum) if item.stages])
    for item in (query_sum, out_sum):
        while item.stages:
            item.step()
    grads_rest = rest_sum.total
    grad_input = slope_middle + matmul_nt(slope_inputs.astype(bf16), turn_in)
    grad_input = grad_input.reshape(tokens.shape)
    grad_gain_one = jnp.sum(w_query.astype(f32) * query_sum.total, 1)
    own_kv = jnp.concatenate([key_projection, value_projection], 1).astype(f32)
    grad_gain_one = grad_gain_one + jnp.sum(own_kv * grads_rest[:, : 2 * key_width], 1)
    grad_gain_one = grad_gain_one / attn_gain.astype(f32)
    return (
        output,
        grad_input,
        grad_gain_one,
        grads_rest[:, 2 * key_width + experts],
        query_sum.total,
        grads_rest[:, :key_width],
        grads_rest[:, key_width : 2 * key_width],
        out_sum.total,
        grads_rest[:, 2 * key_width : 2 * key_width + experts],
        ended(grad_gate)[None],
        ended(grad_up)[None],
        ended(grad_down)[None],
    )


def solution(mesh):
    rows = P("seq", "ctx", None)
    shard = P(("seq", "ctx"), None)
    vector = P(("seq", "ctx"))
    expert = P("ctx", "seq", None)
    return jax.shard_map(
        body,
        mesh=mesh,
        in_specs=(rows, rows, rows, P("seq", "ctx"), P("seq", None), vector, vector)
        + (shard,) * 5
        + (expert,) * 3,
        out_specs=(rows, rows, vector, vector) + (shard,) * 5 + (expert,) * 3,
        check_vma=False,
    )
```

```python
import functools
import math

import jax
import jax.numpy as jnp
from jax import lax
from jax.experimental import pallas as pl
from jax.experimental.pallas import tpu as pltpu
from jax.sharding import PartitionSpec as P

QUERY_HEADS = 12
KEY_VALUE_HEADS = 2
HEAD_WIDTH = 128
TOP = 4
PIC = 256
NPIC = 4
LANES = 128
GROUPS = QUERY_HEADS // KEY_VALUE_HEADS
QUERY_WIDTH = QUERY_HEADS * HEAD_WIDTH
KEY_WIDTH = KEY_VALUE_HEADS * HEAD_WIDTH
SCALE = 1.0 / math.sqrt(HEAD_WIDTH)
EXP2_SCALE = SCALE * math.log2(math.e)
BLOCKS = 2
SKEW = 1
VMEM_BYTES = 48 << 20

epsilon = 1e-06
rope_base = 10000.0
big_negative = -1e30
bf16 = jnp.bfloat16
f32 = jnp.float32


def matmul(left, right):
    return jnp.dot(left, right, preferred_element_type=f32)


def matmul_nt(left, right):
    return lax.dot_general(left, right, (((1,), (1,)), ((), ())), preferred_element_type=f32)


def matmul_tn(left, right):
    return lax.dot_general(left, right, (((0,), (0,)), ((), ())), preferred_element_type=f32)


def rms_scale(rows):
    return lax.rsqrt(jnp.mean(rows * rows, -1, keepdims=True) + epsilon)


def rms_norm(rows, gain):
    return rows * rms_scale(rows) * gain


def rope_tables(positions, head_size):
    half = head_size // 2
    inverse = rope_base ** (-(jnp.arange(half, dtype=f32) * 2.0 / head_size))
    angles = positions.astype(f32)[:, None] * inverse[None, :]
    return (jnp.cos(angles), jnp.sin(angles))


def rotate(rows, heads, cosine, sine):
    shaped = rows.reshape(rows.shape[0], heads, HEAD_WIDTH)
    half = HEAD_WIDTH // 2
    first, second = shaped[..., :half], shaped[..., half:]
    cosine, sine = cosine[:, None, :], sine[:, None, :]
    turned = jnp.concatenate(
        [first * cosine - second * sine, second * cosine + first * sine], -1
    )
    return turned.reshape(rows.shape)


def bits(axis):
    size = lax.axis_size(axis)
    return [(axis, 1 << place) for place in reversed(range(size.bit_length() - 1))]


def swap(block, axis, bit):
    size = lax.axis_size(axis)
    return lax.ppermute(block, axis, [(index, index ^ bit) for index in range(size)])


def gather_blocks(block, stages, order, arrived=None):
    held = []
    for stage in stages:
        axis, bit = stage
        other = swap(block, axis, bit)
        if arrived is not None and stage == stages[-1]:
            other = arrived(other)
        upper = (lax.axis_index(axis) & bit) > 0
        place = sum(order.index(known) < order.index(stage) for known in held)
        block = jnp.stack(
            [jnp.where(upper, other, block), jnp.where(upper, block, other)], place
        )
        held.append(stage)
    return block


class Sum:
    def __init__(self, sent, kept, stages):
        self.sent, self.kept, self.stages = sent, kept, list(stages)

    def step(self):
        axis, bit = self.stages.pop(0)
        other = swap(self.sent, axis, bit)
        if not self.stages:
            self.total = self.kept.astype(f32) + other.astype(f32)
            return
        half = self.kept.shape[0] // 2
        self.sent = (self.kept[half:].astype(f32) + other[half:].astype(f32)).astype(bf16)
        self.kept = (self.kept[:half].astype(f32) + other[:half].astype(f32)).astype(bf16)


def together(sums, also=()):
    for item in sums:
        item.step()
    live = [item for item in sums if item.stages]
    sent, also = lax.optimization_barrier(([item.sent for item in live], also))
    for item, block in zip(live, sent):
        item.sent = block
    return also


def flips(stages, sizes):
    masks = []
    for block in range(1 << len(stages)):
        mask = 0
        for place, (axis, bit) in enumerate(stages):
            if (block >> (len(stages) - 1 - place)) & 1:
                mask |= bit * sizes[axis]
        masks.append(mask)
    return masks


def visible_keys(meta, step, stretch):
    span = BLOCKS * stretch
    keys = step * span + lax.broadcasted_iota(jnp.int32, (span, 1), 0)
    queries = meta[0] * stretch + lax.broadcasted_iota(jnp.int32, (1, stretch), 1)

    def label(positions):
        found = jnp.zeros(positions.shape, jnp.int32)
        for index in range(NPIC):
            start = meta[1 + index]
            inside = (positions >= start) & (positions < start + PIC)
            found = jnp.where(inside, index + 1, found)
        return found

    query_label = label(queries)
    return (keys <= queries) | ((label(keys) == query_label) & (query_label > 0))


def for_each_step(meta, stretch, steps, process, skip=None):
    span = BLOCKS * stretch
    low, high = meta[0] * stretch, (meta[0] + 1) * stretch

    def turn(step, carry):
        needed = step * span < high + PIC - 1
        edge = (step + 1) * span > low

        @pl.when(needed & edge)
        def _():
            process(step, True)

        @pl.when(needed & jnp.logical_not(edge))
        def _():
            process(step, False)

        if skip is not None:

            @pl.when(jnp.logical_not(needed))
            def _():
                skip(step)

        return carry

    lax.fori_loop(0, steps, turn, 0)


def head_columns(head, start=0):
    return slice(start + head * HEAD_WIDTH, start + (head + 1) * HEAD_WIDTH)


def attend_kernel(meta, query, key_value, out, log_total, peak, total, accum):
    stretch = query.shape[0]
    span = BLOCKS * stretch
    peak[...] = jnp.full(peak.shape, big_negative, f32)
    total[...] = jnp.zeros(total.shape, f32)
    accum[...] = jnp.zeros(accum.shape, f32)

    def process(step, edge):
        rows = pl.ds(pl.multiple_of(step * span, span), span)
        if edge:
            visible = visible_keys(meta, step, stretch)
        keys, values = [], []
        for group in range(KEY_VALUE_HEADS):
            keys.append(key_value[rows, head_columns(group)])
            turned = key_value[rows, head_columns(group, KEY_WIDTH)].T
            values.append(jnp.concatenate([turned, jnp.ones((16, span), bf16)], 0))

        def score(head):
            scores = matmul_nt(keys[head // GROUPS], query[:, head_columns(head)])
            if edge:
                scores = jnp.where(visible, scores, big_negative)
            old = peak[head : head + 1, :]
            return scores, old, jnp.maximum(old, jnp.max(scores, 0, keepdims=True))

        def weigh(head, scores, old, new):
            weights = jnp.exp2((scores - new) * EXP2_SCALE).astype(bf16)
            shrink = jnp.exp2((old - new) * EXP2_SCALE)
            sums = matmul(values[head // GROUPS], weights)
            row, columns = slice(head, head + 1), head_columns(head)
            peak[row, :] = new
            total[row, :] = total[row, :] * shrink + sums[HEAD_WIDTH : HEAD_WIDTH + 1]
            accum[columns, :] = accum[columns, :] * shrink + sums[:HEAD_WIDTH]

        waiting = []
        for head in range(QUERY_HEADS):
            waiting.append((head, *score(head)))
            if len(waiting) > 2:
                weigh(*waiting.pop(0))
        for item in waiting:
            weigh(*item)

    for_each_step(meta, stretch, key_value.shape[0] // span, process)
    for head in range(QUERY_HEADS):
        row, columns = slice(head, head + 1), head_columns(head)
        out[:, columns] = (accum[columns, :] / total[row, :]).T
        log_total[row, :] = peak[row, :] * EXP2_SCALE + jnp.log2(total[row, :])


def attend_back_kernel(
    order,
    group,
    meta,
    query,
    slope,
    log_total,
    mixed,
    key_value,
    slope_query,
    out,
    accum,
    delta,
):
    stretch = query.shape[0]
    span = BLOCKS * stretch
    accum[...] = jnp.zeros(accum.shape, f32)
    for index in range(GROUPS):
        columns = head_columns(group * GROUPS + index)
        product = slope[:, columns].astype(f32) * mixed[:, columns]
        delta[index : index + 1, :] = jnp.sum(product.T, 0, keepdims=True)

    def store(step, part, columns, block):
        flip = jnp.bitwise_xor(BLOCKS * step + part, meta[0])
        first, *others = order
        place = 0
        for index, bit in enumerate(others):
            place = place + ((flip // bit) & 1) * (1 << (len(others) - 1 - index))
        place = pl.ds(pl.multiple_of(place * stretch, stretch), stretch)
        out[(flip // first) & 1, place, columns] = block

    def process(step, edge):
        rows = pl.ds(pl.multiple_of(step * span, span), span)
        if edge:
            visible = visible_keys(meta, step, stretch)
        keys = key_value[rows, head_columns(group)]
        values = key_value[rows, head_columns(group, KEY_WIDTH)]
        keys_turned = keys.T

        def slopes_of(index):
            columns = head_columns(group * GROUPS + index)
            row = slice(group * GROUPS + index, group * GROUPS + index + 1)
            scores = matmul_nt(keys, query[:, columns])
            probs = jnp.exp2(scores * EXP2_SCALE - log_total[row, :])
            if edge:
                probs = jnp.where(visible, probs, 0.0)
            slope_probs = matmul_nt(values, slope[:, columns])
            slope_scores = (probs * (slope_probs - delta[index : index + 1, :])).astype(bf16)
            return index, probs.astype(bf16), slope_scores

        slope_k = jnp.zeros((span, HEAD_WIDTH), f32)
        slope_v = jnp.zeros((span, HEAD_WIDTH), f32)
        waiting = []
        for index in range(GROUPS + SKEW):
            if index < GROUPS:
                waiting.append(slopes_of(index))
            if index >= SKEW:
                own, probs, slope_scores = waiting.pop(0)
                columns, place = head_columns(group * GROUPS + own), head_columns(own)
                slope_v = slope_v + matmul(probs, slope[:, columns])
                slope_k = slope_k + matmul(slope_scores, query[:, columns])
                accum[place, :] = accum[place, :] + matmul(keys_turned, slope_scores)
        slope_k, slope_v = (slope_k * SCALE).astype(bf16), slope_v.astype(bf16)
        for which, block in enumerate((slope_k, slope_v)):
            for part in range(BLOCKS):
                own = block[part * stretch : (part + 1) * stretch]
                store(step, part, head_columns(which), own)

    def skip(step):
        for part in range(BLOCKS):
            store(step, part, slice(None), jnp.zeros((stretch, 2 * HEAD_WIDTH), bf16))

    for_each_step(meta, stretch, key_value.shape[0] // span, process, skip)
    for index in range(GROUPS):
        columns = head_columns(index)
        slope_query[:, columns] = (accum[columns, :] * SCALE).T


def expert_kernel(
    which,
    rows,
    slopes,
    chosen,
    gate_up,
    down,
    router,
    hidden_out,
    result_out,
    gates_out,
    slots_out,
    pre_out,
    slope_out,
):
    hidden_width = down.shape[0]
    incoming = rows[...]
    logits = jnp.where(chosen[...] > 0, matmul(incoming, router[...]), big_negative)
    shares = jnp.exp(logits - jnp.max(logits, -1, keepdims=True))
    shares = jnp.where(chosen[...] > 0, shares, 0.0)
    column = lax.broadcasted_iota(jnp.int32, shares.shape, 1)
    own = jnp.sum(jnp.where(column == which[0], shares, 0.0), -1, keepdims=True)
    gates = own / jnp.maximum(jnp.sum(shares, -1, keepdims=True), 1e-30)
    slots = (gates * slopes[...].astype(f32)).astype(bf16)
    slots_out[...] = slots
    pre = matmul(incoming, gate_up[...])
    gate, up = pre[:, :hidden_width], pre[:, hidden_width:]
    root, cubic = math.sqrt(2.0 / math.pi), 0.044715
    square = gate * gate
    bend = jnp.tanh(root * (gate + cubic * gate * square))
    gelu = 0.5 * gate * (1.0 + bend)
    rise = 0.5 * (1.0 + bend) + 0.5 * gate * (1.0 - bend * bend) * root * (
        1.0 + 3.0 * cubic * square
    )
    hidden = (gelu * up).astype(bf16)
    hidden_out[...] = hidden
    result = matmul(hidden, down[...]).astype(bf16)
    result_out[...] = result
    gates_out[...] = jnp.sum(slopes[...].astype(f32) * result.astype(f32), -1, keepdims=True)
    slope_hidden = matmul_nt(slots, down[...])
    slope_pre = jnp.concatenate([slope_hidden * up * rise, slope_hidden * gelu], 1).astype(bf16)
    pre_out[...] = slope_pre
    slope_out[...] = matmul_nt(slope_pre, gate_up[...]).astype(bf16)


def expert(which, rows, slopes, chosen, gate_up, down, router):
    count, width = rows.shape
    hidden_width = down.shape[0]
    block = count // 2

    def tile(columns):
        return pl.BlockSpec((block, columns), lambda step: (step, 0))

    def whole(array):
        return pl.BlockSpec(array.shape, lambda step: (0, 0))

    shapes = [(hidden_width, bf16), (width, bf16), (1, f32), (width, bf16)]
    shapes += [(2 * hidden_width, bf16), (width, bf16)]
    return pl.pallas_call(
        expert_kernel,
        grid=(2,),
        out_shape=[jax.ShapeDtypeStruct((count, columns), kind) for columns, kind in shapes],
        in_specs=[
            pl.BlockSpec(memory_space=pltpu.SMEM),
            tile(width),
            tile(width),
            tile(LANES),
            whole(gate_up),
            whole(down),
            whole(router),
        ],
        out_specs=[tile(columns) for columns, _ in shapes],
        compiler_params=pltpu.CompilerParams(vmem_limit_bytes=VMEM_BYTES),
        cost_estimate=pl.CostEstimate(
            flops=12 * count * width * hidden_width,
            bytes_accessed=20 * count * width,
            transcendentals=count * hidden_width,
        ),
        name="expert",
    )(which, rows, slopes, chosen, gate_up, down, router)


def attention_call(kernel, outs, scratch, products, name, meta, *operands):
    vmem = pl.BlockSpec(memory_space=pltpu.VMEM)
    pairs = QUERY_HEADS * operands[0].shape[0] * operands[-1].shape[0]
    return pl.pallas_call(
        kernel,
        out_shape=outs,
        in_specs=[pl.BlockSpec(memory_space=pltpu.SMEM)] + [vmem] * len(operands),
        out_specs=(vmem,) * len(outs),
        scratch_shapes=[pltpu.VMEM(*shape) for shape in scratch],
        compiler_params=pltpu.CompilerParams(vmem_limit_bytes=VMEM_BYTES),
        cost_estimate=pl.CostEstimate(
            flops=products * pairs, bytes_accessed=QUERY_WIDTH * 1024, transcendentals=0
        ),
        name=name,
    )(meta, *operands)


def attend(meta, query, key_value):
    stretch = query.shape[0]
    stats = (QUERY_HEADS, stretch)
    outs = (
        jax.ShapeDtypeStruct((stretch, QUERY_WIDTH), f32),
        jax.ShapeDtypeStruct(stats, f32),
    )
    scratch = [(stats, f32), (stats, f32), ((QUERY_WIDTH, stretch), f32)]
    return attention_call(attend_kernel, outs, scratch, 2, "attend", meta, query, key_value)


def attend_back(order, group, meta, query, slope, log_total, mixed, key_value):
    stretch, rows = query.shape[0], key_value.shape[0]
    group_width = GROUPS * HEAD_WIDTH
    outs = (
        jax.ShapeDtypeStruct((stretch, group_width), f32),
        jax.ShapeDtypeStruct((2, rows // 2, 2 * HEAD_WIDTH), bf16),
    )
    operands = (meta, query, slope, log_total, mixed, key_value)
    scratch = [((group_width, stretch), f32), ((GROUPS, stretch), f32)]
    kernel = functools.partial(attend_back_kernel, order, group)
    return attention_call(kernel, outs, scratch, 2, "attend_back", *operands)


def body(
    tokens,
    cotangent,
    routes,
    fill_order,
    pic_starts,
    attn_gain,
    moe_gain,
    w_query,
    key_projection,
    value_projection,
    w_out,
    w_router,
    expert_gate,
    expert_up,
    expert_down,
):
    sequences, stretch, width = tokens.shape
    count = sequences * stretch
    parts = lax.axis_size("ctx")
    experts = parts
    capacity = (5 * count * TOP + 4 * experts - 1) // (4 * experts)
    query_width, key_width = QUERY_WIDTH, KEY_WIDTH
    hidden_width = expert_gate.shape[2]
    seq_bits, ctx_bits = bits("seq"), bits("ctx")
    all_bits = seq_bits + ctx_bits
    inward = ctx_bits[-1:] + seq_bits[::-1] + ctx_bits[-2::-1]
    sizes = {"seq": parts, "ctx": 1}
    me = lax.axis_index("seq") * parts + lax.axis_index("ctx")

    def padded(columns):
        block = jnp.concatenate(columns, 1)
        return jnp.pad(block, ((0, 0), (0, LANES - block.shape[1])))

    own_rows = w_query.shape[0]

    def feature(stages):
        owner = jnp.bitwise_xor(jnp.array(flips(stages, sizes), jnp.int32), me)
        return (owner[:, None] * own_rows + jnp.arange(own_rows, dtype=jnp.int32)).reshape(-1)

    def same(left, right):
        return (left[:, None] == right[None, :]).astype(bf16)

    turns = ctx_bits[:-2] + seq_bits + ctx_bits[-2:]
    natural = jnp.arange(width, dtype=jnp.int32)
    gathered, summed = feature(turns[::-1]), feature(inward)
    turn, turn_in, across = same(natural, summed), same(natural, gathered), same(gathered, summed)

    def relative(rows):
        return matmul(rows, turn).astype(bf16)

    def halves(left, right):
        middle = left.shape[1] // 2
        sent = matmul_tn(left[:, middle:], right).astype(bf16)
        return sent, matmul_tn(left[:, :middle], right).astype(bf16)

    picks = routes.reshape(count, TOP)
    order = fill_order.reshape(count)
    routed = jnp.any(picks[:, :, None] == jnp.arange(experts, dtype=jnp.int32), 1)
    earlier = (order[None, :] < order[:, None]).astype(bf16)
    place = matmul(earlier, routed.astype(bf16)).astype(jnp.int32)
    place = jnp.where(routed, place, capacity)
    half = capacity // 2
    chosen_slot = [
        place.T[:, None, :]
        == (begin + jnp.arange(half, dtype=jnp.int32))[None, :, None]
        for begin in (0, half)
    ]
    slot_map = [chosen.astype(bf16).reshape(-1, count) for chosen in chosen_slot]

    def exchange_rows(rows):
        rows = rows.reshape(experts, half, width)
        rows = lax.all_to_all(rows, "ctx", split_axis=0, concat_axis=0, tiled=True)
        return rows.reshape(-1, width)

    out_slope = cotangent.reshape(count, width)
    slot_routes = jnp.concatenate(
        [matmul(part, routed.astype(bf16)).reshape(experts, half, experts) for part in slot_map], 1
    ).astype(bf16)
    slot_routes = lax.all_to_all(slot_routes, "ctx", split_axis=0, concat_axis=0, tiled=True)
    slot_routes = jnp.pad(slot_routes, ((0, 0), (0, 0), (0, LANES - experts)))
    slot_routes = [
        slot_routes[:, begin : begin + half].reshape(-1, LANES) for begin in (0, half)
    ]
    slope_rows = [matmul(part, out_slope).astype(bf16) for part in slot_map]
    slope_rows = jnp.concatenate([part.reshape(experts, half, width) for part in slope_rows], 1)

    block = jnp.concatenate(
        [
            w_query,
            key_projection,
            value_projection,
            padded([attn_gain[:, None]]),
            w_out,
            padded([w_router, moe_gain[:, None]]),
        ],
        1,
    )
    first_width = query_width + 2 * key_width + LANES
    expert_parts = [expert_gate[0], expert_up[0]]
    for index, stage in enumerate(turns):
        other = swap(block if index < 2 else mine, *stage)
        if index in (1, 3) and len(seq_bits) == 1:
            part = index // 2
            other, expert_parts[part] = lax.optimization_barrier(
                (other, (expert_parts[part], swap(expert_parts[part], *seq_bits[0])))
            )
        if index < 2:
            block = jnp.concatenate([block, other], 0)
        if index == 1:
            block, slope_rows = lax.optimization_barrier((block, slope_rows))
            slope_rows = lax.all_to_all(slope_rows, "ctx", split_axis=0, concat_axis=0, tiled=True)
            mine, second_set = block[:, :first_width], block[:, first_width:]
        if index > 2:
            arrived = swap(second_set, *turns[index - 1])
            if index == len(turns) - 1:
                late = second_set, arrived
                continue
            if index < len(turns) - 1:
                other, arrived = lax.optimization_barrier((other, arrived))
            second_set = jnp.concatenate([second_set, arrived], 0)
        if 2 <= index < len(turns) - 1:
            mine = jnp.concatenate([mine, other], 0)
    inputs = tokens.reshape(count, width)
    inputs_turned = matmul(inputs, turn_in)
    inputs = inputs.astype(f32)
    inputs_scaled = inputs_turned * rms_scale(inputs)
    mine, other, slope_rows, slot_routes, inputs_scaled = lax.optimization_barrier(
        (mine, other, slope_rows, slot_routes, inputs_scaled)
    )
    slope_rows = [
        slope_rows[:, begin : begin + half].reshape(-1, width) for begin in (0, half)
    ]
    qkv_width = query_width + 2 * key_width
    weight_low, weight_high = mine[:, :qkv_width], other[:, :qkv_width]
    gain_one = jnp.concatenate([mine[:, qkv_width], other[:, qkv_width]]).astype(f32)

    def whole_expert(part):
        if isinstance(part, tuple):
            own, other = part
            upper = lax.axis_index("seq") > 0
            pair = [jnp.where(upper, other, own), jnp.where(upper, own, other)]
            return jnp.concatenate(pair, 0)
        return gather_blocks(part, seq_bits[::-1], seq_bits).reshape(-1, part.shape[1])

    gate_up = jnp.concatenate([whole_expert(part) for part in expert_parts], 1)
    positions = lax.axis_index("ctx") * stretch + jnp.arange(stretch, dtype=jnp.int32)
    cosine, sine = rope_tables(positions, HEAD_WIDTH)
    normed = (inputs_scaled * gain_one).astype(bf16)

    def project(columns):
        low = matmul(normed[:, : width // 2], weight_low[:, columns])
        return low + matmul(normed[:, width // 2 :], weight_high[:, columns])

    projected = project(slice(query_width, None))
    key_rows = rotate(projected[:, :key_width], KEY_VALUE_HEADS, cosine, sine)
    key_values = lax.all_gather(
        jnp.concatenate([key_rows, projected[:, key_width:]], 1).astype(bf16),
        "ctx",
        axis=0,
        tiled=True,
    )
    projected = project(slice(0, query_width))
    query_rows = rotate(projected, QUERY_HEADS, cosine, sine).astype(bf16)
    second_set, arrived = late
    arrived, query_rows = lax.optimization_barrier((arrived, query_rows))
    second_set = jnp.concatenate([second_set, arrived], 0)
    second_set = jnp.concatenate([second_set, swap(second_set, *turns[-1])], 0)
    second_set = matmul(turn_in, second_set).astype(bf16)
    full_out = second_set[:, :width]
    full_router = second_set[:, width : width + experts]
    gain_two = second_set[:, width + experts].astype(f32)
    meta = jnp.concatenate([lax.axis_index("ctx").astype(jnp.int32)[None], pic_starts[0]])
    mixed_heads, log_total = attend(meta, query_rows, key_values)

    def with_attention(other):
        nonlocal mixed_heads
        mixed_heads, other = lax.optimization_barrier((mixed_heads, other))
        return other

    down = gather_blocks(
        lax.optimization_barrier((expert_down[0], gain_one))[0],
        seq_bits[::-1],
        seq_bits,
        with_attention,
    ).reshape(-1, width)
    attended = mixed_heads.astype(bf16)

    middle = inputs + matmul(attended, full_out)
    enter = rms_norm(middle, gain_two).astype(bf16)
    arrived = [exchange_rows(matmul(part, enter).astype(bf16)) for part in slot_map]

    def gates_of(rows, chosen):
        logits = jnp.where(chosen, matmul(rows, full_router), big_negative)
        shares = jnp.exp(logits - jnp.max(logits, -1, keepdims=True))
        shares = jnp.where(chosen, shares, 0.0)
        return shares / jnp.maximum(jnp.sum(shares, -1, keepdims=True), 1e-30)

    gates = gates_of(enter, routed)

    attended_turned, enter_turned = map(relative, (attended, enter))
    normed_turned = matmul(normed, across).astype(bf16)
    arrived[0], attended_turned, enter_turned, normed_turned = lax.optimization_barrier(
        (arrived[0], attended_turned, enter_turned, normed_turned)
    )
    which = lax.axis_index("ctx").astype(jnp.int32)[None]
    router = second_set[:, width:]
    hidden, result, slope_gates, slope_slots, slope_pre, slope_arrived = ([] for _ in range(6))
    for index in range(2):
        made = list(expert(
            which, arrived[index], slope_rows[index], slot_routes[index], gate_up, down, router)
        )
        if index == 0:
            arrived[1], made[-1] = lax.optimization_barrier((arrived[1], made[-1]))
        for kept, item in zip(
            (hidden, result, slope_gates, slope_slots, slope_pre, slope_arrived), made
        ):
            kept.append(item)
    returned_slopes = [exchange_rows(slope_arrived[0])]
    slope_gates = jnp.concatenate([item.reshape(experts, half) for item in slope_gates], 1)
    returned = jnp.concatenate([part.reshape(experts, half, width) for part in result], 1)
    slope_gates, returned_slopes[0], returned = lax.optimization_barrier(
        (slope_gates, returned_slopes[0], returned)
    )
    returned_gates = lax.all_to_all(slope_gates, "ctx", split_axis=0, concat_axis=0, tiled=True)
    slope_arrived[1], returned_gates, slope_pre, slope_slots = lax.optimization_barrier(
        (slope_arrived[1], returned_gates, slope_pre, slope_slots)
    )
    returned_slopes.append(exchange_rows(slope_arrived[1]))
    grad_gate, grad_up = (
        sum(matmul_tn(arrived[i], slope_pre[i][:, columns]) for i in range(2)).astype(bf16)
        for columns in (slice(0, hidden_width), slice(hidden_width, None))
    )
    grad_down = sum(matmul_tn(hidden[i], slope_slots[i]) for i in range(2)).astype(bf16)
    def sector_cut(blocks, stage):
        axis, bit = stage
        mine = ((lax.axis_index(axis) & bit) > 0).astype(jnp.int32)
        sent = lax.dynamic_index_in_dim(blocks, 1 - mine, 0, keepdims=False)
        return sent, lax.dynamic_index_in_dim(blocks, mine, 0, keepdims=False)

    def sector_halves(grads):
        blocks = grads.reshape([2] * len(seq_bits) + [-1, grads.shape[1]])
        return sector_cut(blocks, seq_bits[0])

    def sector_sum(pair, arrived):
        for index, (axis, bit) in enumerate(seq_bits):
            sent, kept = pair
            other = swap(sent.astype(bf16), axis, bit)
            if index == len(seq_bits) - 1:
                return kept, arrived(other)
            total = kept.astype(f32) + other.astype(f32)
            pair = sector_cut(total, seq_bits[index + 1])

    def ended(pair):
        return pair[0].astype(f32) + pair[1].astype(f32)

    def with_slopes(other):
        nonlocal grad_gate, grad_up
        returned_slopes[1], other, grad_gate, grad_up = lax.optimization_barrier(
            (returned_slopes[1], other, grad_gate, grad_up)
        )
        return other

    grad_gate, grad_up = sector_halves(grad_gate), sector_halves(grad_up)
    grad_down = sector_sum(sector_halves(grad_down), with_slopes)
    returned = lax.all_to_all(returned, "ctx", split_axis=0, concat_axis=0, tiled=True)

    slope_gate = 0.0
    for index, chosen in enumerate(chosen_slot):
        part = returned_gates[:, index * half : (index + 1) * half]
        slope_gate = slope_gate + jnp.sum(jnp.where(chosen, part[:, :, None], 0.0), 1).T
    slope_logits = gates * (slope_gate - jnp.sum(gates * slope_gate, -1, keepdims=True))
    slope_logits = slope_logits.astype(bf16)
    slope_enter = matmul_nt(slope_logits, full_router)
    for part, rows in zip(slot_map, returned_slopes):
        slope_enter = slope_enter + matmul_tn(part, rows)

    pull_two = jax.vjp(rms_norm, middle, gain_two)[1]
    slope_middle, grad_gain_two = pull_two(slope_enter)
    slope_middle = out_slope.astype(f32) + slope_middle
    slope_branch = slope_middle.astype(bf16)
    slope_attended = matmul_nt(slope_branch, full_out).astype(bf16)

    kv_order = ctx_bits[::-1]

    def back(group, meta):
        order = [bit for _, bit in kv_order]
        return attend_back(
            order, group, meta, query_rows, slope_attended, log_total, mixed_heads, key_values
        )

    first_q, first_kv = back(0, meta)

    def after_first(other):
        nonlocal first_q, first_kv, meta, grad_up
        first_q, first_kv, meta, grad_up, other = lax.optimization_barrier(
            (first_q, first_kv, meta, grad_up, other)
        )
        return other

    grad_gate = sector_sum(grad_gate, after_first)
    first_sum = Sum(first_kv[1], first_kv[0], kv_order)
    first_sum.step()
    second_q, second_kv = back(1, meta)

    def after_second(other):
        nonlocal second_q, second_kv, grad_gate, slope_branch
        second_q, second_kv, first_sum.sent, grad_gate, slope_branch, other = (
            lax.optimization_barrier(
                (second_q, second_kv, first_sum.sent, grad_gate, slope_branch, other)
            )
        )
        return other

    grad_up = sector_sum(grad_up, after_second)
    second_sum = Sum(second_kv[1], second_kv[0], kv_order)
    first_sum.step()
    second_sum.step()
    second_sum.sent, first_q, second_q = lax.optimization_barrier(
        (second_sum.sent, first_q, second_q)
    )
    slope_query = jnp.concatenate([first_q, second_q], 1)
    slope_query = rotate(slope_query, QUERY_HEADS, cosine, -sine).astype(bf16)
    query_sum = Sum(*halves(normed_turned, slope_query), inward)
    query_sum.step()
    first_sum.sent, second_sum.sent, query_sum.sent, slope_branch, returned = (
        lax.optimization_barrier(
            (first_sum.sent, second_sum.sent, query_sum.sent, slope_branch, returned)
        )
    )
    query_sum.step()
    out_sum = Sum(*halves(attended_turned, slope_branch), inward)
    out_sum.step()
    while len(first_sum.stages) > 1:
        together([first_sum, second_sum])
    first_sum.step()
    second_sum.step()
    (
        first_sum.total,
        second_sum.sent,
        query_sum.sent,
        out_sum.sent,
        slope_query,
        grad_gate,
        grad_up,
        grad_gain_two,
        enter_turned,
    ) = lax.optimization_barrier(
        (
            first_sum.total,
            second_sum.sent,
            query_sum.sent,
            out_sum.sent,
            slope_query,
            grad_gate,
            grad_up,
            grad_gain_two,
            enter_turned,
        )
    )
    grad_router = matmul_tn(enter_turned, slope_logits)
    out_sum.step()
    second_sum.step()
    totals = [first_sum.total, second_sum.total]
    slope_key = jnp.concatenate([total[:, :HEAD_WIDTH] for total in totals], 1)
    slope_key = rotate(slope_key, KEY_VALUE_HEADS, cosine, -sine)
    slope_rest = [slope_key] + [total[:, HEAD_WIDTH:] for total in totals]
    slope_rest = jnp.concatenate(slope_rest, 1).astype(bf16)
    small = padded([grad_router.astype(bf16), relative(grad_gain_two.astype(bf16)[None]).T])
    rest_sum = Sum(
        *(
            jnp.concatenate([grads, part], 1)
            for grads, part in zip(
                halves(normed_turned, slope_rest), (small[width // 2 :], small[: width // 2])
            )
        ),
        inward,
    )
    slope_rest = together([item for item in (rest_sum, query_sum) if item.stages], slope_rest)
    slope_projected = jnp.concatenate([slope_query, slope_rest], 1)
    slope_normed = jnp.concatenate(
        [matmul_nt(slope_projected, part) for part in (weight_low, weight_high)], 1
    )
    pull_one = jax.vjp(rms_norm, inputs_turned, gain_one)[1]
    slope_inputs = pull_one(slope_normed)[0]
    returned = together(
        [item for item in (rest_sum, query_sum, out_sum) if item.stages], returned
    )
    output = middle
    for chosen, rows in ((jnp.concatenate(chosen_slot, 1), returned.reshape(-1, width)),):
        mix = jnp.where(chosen, gates.T[:, None, :], 0.0).reshape(-1, count)
        output = output + matmul_tn(mix.astype(bf16), rows)
    output = output.astype(bf16).reshape(tokens.shape)
    while rest_sum.stages:
        together([item for item in (rest_sum, query_sum, out_sum) if item.stages])
    for item in (query_sum, out_sum):
        while item.stages:
            item.step()
    grads_rest = rest_sum.total
    grad_input = slope_middle + matmul_nt(slope_inputs.astype(bf16), turn_in)
    grad_input = grad_input.reshape(tokens.shape)
    grad_gain_one = jnp.sum(w_query.astype(f32) * query_sum.total, 1)
    own_kv = jnp.concatenate([key_projection, value_projection], 1).astype(f32)
    grad_gain_one = grad_gain_one + jnp.sum(own_kv * grads_rest[:, : 2 * key_width], 1)
    grad_gain_one = grad_gain_one / attn_gain.astype(f32)
    return (
        output,
        grad_input,
        grad_gain_one,
        grads_rest[:, 2 * key_width + experts],
        query_sum.total,
        grads_rest[:, :key_width],
        grads_rest[:, key_width : 2 * key_width],
        out_sum.total,
        grads_rest[:, 2 * key_width : 2 * key_width + experts],
        ended(grad_gate)[None],
        ended(grad_up)[None],
        ended(grad_down)[None],
    )


def solution(mesh):
    rows = P("seq", "ctx", None)
    shard = P(("seq", "ctx"), None)
    vector = P(("seq", "ctx"))
    expert = P("ctx", "seq", None)
    return jax.shard_map(
        body,
        mesh=mesh,
        in_specs=(rows, rows, rows, P("seq", "ctx"), P("seq", None), vector, vector)
        + (shard,) * 5
        + (expert,) * 3,
        out_specs=(rows, rows, vector, vector) + (shard,) * 5 + (expert,) * 3,
        check_vma=False,
    )
```

```python
import functools
import math

import jax
import jax.numpy as jnp
from jax import lax
from jax.experimental import pallas as pl
from jax.experimental.pallas import tpu as pltpu
from jax.sharding import PartitionSpec as P

QUERY_HEADS = 12
KEY_VALUE_HEADS = 2
HEAD_WIDTH = 128
TOP = 4
PIC = 256
NPIC = 4
LANES = 128
GROUPS = QUERY_HEADS // KEY_VALUE_HEADS
QUERY_WIDTH = QUERY_HEADS * HEAD_WIDTH
KEY_WIDTH = KEY_VALUE_HEADS * HEAD_WIDTH
SCALE = 1.0 / math.sqrt(HEAD_WIDTH)
EXP2_SCALE = SCALE * math.log2(math.e)
BLOCKS = 2
SKEW = 1
VMEM_BYTES = 48 << 20

epsilon = 1e-06
rope_base = 10000.0
big_negative = -1e30
bf16 = jnp.bfloat16
f32 = jnp.float32


def matmul(left, right):
    return jnp.dot(left, right, preferred_element_type=f32)


def matmul_nt(left, right):
    return lax.dot_general(left, right, (((1,), (1,)), ((), ())), preferred_element_type=f32)


def matmul_tn(left, right):
    return lax.dot_general(left, right, (((0,), (0,)), ((), ())), preferred_element_type=f32)


def rms_scale(rows):
    return lax.rsqrt(jnp.mean(rows * rows, -1, keepdims=True) + epsilon)


def rms_norm(rows, gain):
    return rows * rms_scale(rows) * gain


def rope_tables(positions, head_size):
    half = head_size // 2
    inverse = rope_base ** (-(jnp.arange(half, dtype=f32) * 2.0 / head_size))
    angles = positions.astype(f32)[:, None] * inverse[None, :]
    return (jnp.cos(angles), jnp.sin(angles))


def rotate(rows, heads, cosine, sine):
    shaped = rows.reshape(rows.shape[0], heads, HEAD_WIDTH)
    half = HEAD_WIDTH // 2
    first, second = shaped[..., :half], shaped[..., half:]
    cosine, sine = cosine[:, None, :], sine[:, None, :]
    turned = jnp.concatenate(
        [first * cosine - second * sine, second * cosine + first * sine], -1
    )
    return turned.reshape(rows.shape)


def bits(axis):
    size = lax.axis_size(axis)
    return [(axis, 1 << place) for place in reversed(range(size.bit_length() - 1))]


def swap(block, axis, bit):
    size = lax.axis_size(axis)
    return lax.ppermute(block, axis, [(index, index ^ bit) for index in range(size)])


def gather_blocks(block, stages, order, arrived=None):
    held = []
    for stage in stages:
        axis, bit = stage
        other = swap(block, axis, bit)
        if arrived is not None and stage == stages[-1]:
            other = arrived(other)
        upper = (lax.axis_index(axis) & bit) > 0
        place = sum(order.index(known) < order.index(stage) for known in held)
        block = jnp.stack(
            [jnp.where(upper, other, block), jnp.where(upper, block, other)], place
        )
        held.append(stage)
    return block


class Sum:
    def __init__(self, sent, kept, stages):
        self.sent, self.kept, self.stages = sent, kept, list(stages)

    def step(self):
        axis, bit = self.stages.pop(0)
        other = swap(self.sent, axis, bit)
        if not self.stages:
            self.total = self.kept.astype(f32) + other.astype(f32)
            return
        half = self.kept.shape[0] // 2
        self.sent = (self.kept[half:].astype(f32) + other[half:].astype(f32)).astype(bf16)
        self.kept = (self.kept[:half].astype(f32) + other[:half].astype(f32)).astype(bf16)


def together(sums, also=()):
    for item in sums:
        item.step()
    live = [item for item in sums if item.stages]
    sent, also = lax.optimization_barrier(([item.sent for item in live], also))
    for item, block in zip(live, sent):
        item.sent = block
    return also


def flips(stages, sizes):
    masks = []
    for block in range(1 << len(stages)):
        mask = 0
        for place, (axis, bit) in enumerate(stages):
            if (block >> (len(stages) - 1 - place)) & 1:
                mask |= bit * sizes[axis]
        masks.append(mask)
    return masks


def visible_keys(meta, step, stretch):
    span = BLOCKS * stretch
    keys = step * span + lax.broadcasted_iota(jnp.int32, (span, 1), 0)
    queries = meta[0] * stretch + lax.broadcasted_iota(jnp.int32, (1, stretch), 1)

    def label(positions):
        found = jnp.zeros(positions.shape, jnp.int32)
        for index in range(NPIC):
            start = meta[1 + index]
            inside = (positions >= start) & (positions < start + PIC)
            found = jnp.where(inside, index + 1, found)
        return found

    query_label = label(queries)
    return (keys <= queries) | ((label(keys) == query_label) & (query_label > 0))


def for_each_step(meta, stretch, steps, process, skip=None):
    span = BLOCKS * stretch
    low, high = meta[0] * stretch, (meta[0] + 1) * stretch

    def turn(step, carry):
        needed = step * span < high + PIC - 1
        edge = (step + 1) * span > low

        @pl.when(needed & edge)
        def _():
            process(step, True)

        @pl.when(needed & jnp.logical_not(edge))
        def _():
            process(step, False)

        if skip is not None:

            @pl.when(jnp.logical_not(needed))
            def _():
                skip(step)

        return carry

    lax.fori_loop(0, steps, turn, 0)


def head_columns(head, start=0):
    return slice(start + head * HEAD_WIDTH, start + (head + 1) * HEAD_WIDTH)


def attend_kernel(meta, query, key_value, out, log_total, peak, total, accum):
    stretch = query.shape[0]
    span = BLOCKS * stretch
    peak[...] = jnp.full(peak.shape, big_negative, f32)
    total[...] = jnp.zeros(total.shape, f32)
    accum[...] = jnp.zeros(accum.shape, f32)

    def process(step, edge):
        rows = pl.ds(pl.multiple_of(step * span, span), span)
        if edge:
            visible = visible_keys(meta, step, stretch)
        keys, values = [], []
        for group in range(KEY_VALUE_HEADS):
            keys.append(key_value[rows, head_columns(group)])
            turned = key_value[rows, head_columns(group, KEY_WIDTH)].T
            values.append(jnp.concatenate([turned, jnp.ones((16, span), bf16)], 0))

        def score(head):
            scores = matmul_nt(keys[head // GROUPS], query[:, head_columns(head)])
            if edge:
                scores = jnp.where(visible, scores, big_negative)
            old = peak[head : head + 1, :]
            return scores, old, jnp.maximum(old, jnp.max(scores, 0, keepdims=True))

        def weigh(head, scores, old, new):
            weights = jnp.exp2((scores - new) * EXP2_SCALE).astype(bf16)
            shrink = jnp.exp2((old - new) * EXP2_SCALE)
            sums = matmul(values[head // GROUPS], weights)
            row, columns = slice(head, head + 1), head_columns(head)
            peak[row, :] = new
            total[row, :] = total[row, :] * shrink + sums[HEAD_WIDTH : HEAD_WIDTH + 1]
            accum[columns, :] = accum[columns, :] * shrink + sums[:HEAD_WIDTH]

        waiting = []
        for head in range(QUERY_HEADS):
            waiting.append((head, *score(head)))
            if len(waiting) > 2:
                weigh(*waiting.pop(0))
        for item in waiting:
            weigh(*item)

    for_each_step(meta, stretch, key_value.shape[0] // span, process)
    for head in range(QUERY_HEADS):
        row, columns = slice(head, head + 1), head_columns(head)
        out[:, columns] = (accum[columns, :] / total[row, :]).T
        log_total[row, :] = peak[row, :] * EXP2_SCALE + jnp.log2(total[row, :])


def attend_back_kernel(
    order,
    group,
    meta,
    query,
    slope,
    log_total,
    mixed,
    key_value,
    slope_query,
    out,
    accum,
    delta,
):
    stretch = query.shape[0]
    span = BLOCKS * stretch
    accum[...] = jnp.zeros(accum.shape, f32)
    for index in range(GROUPS):
        columns = head_columns(group * GROUPS + index)
        product = slope[:, columns].astype(f32) * mixed[:, columns]
        delta[index : index + 1, :] = jnp.sum(product.T, 0, keepdims=True)

    def store(step, part, columns, block):
        flip = jnp.bitwise_xor(BLOCKS * step + part, meta[0])
        first, *others = order
        place = 0
        for index, bit in enumerate(others):
            place = place + ((flip // bit) & 1) * (1 << (len(others) - 1 - index))
        place = pl.ds(pl.multiple_of(place * stretch, stretch), stretch)
        out[(flip // first) & 1, place, columns] = block

    def process(step, edge):
        rows = pl.ds(pl.multiple_of(step * span, span), span)
        if edge:
            visible = visible_keys(meta, step, stretch)
        keys = key_value[rows, head_columns(group)]
        values = key_value[rows, head_columns(group, KEY_WIDTH)]
        keys_turned = keys.T

        def slopes_of(index):
            columns = head_columns(group * GROUPS + index)
            row = slice(group * GROUPS + index, group * GROUPS + index + 1)
            scores = matmul_nt(keys, query[:, columns])
            probs = jnp.exp2(scores * EXP2_SCALE - log_total[row, :])
            if edge:
                probs = jnp.where(visible, probs, 0.0)
            slope_probs = matmul_nt(values, slope[:, columns])
            slope_scores = (probs * (slope_probs - delta[index : index + 1, :])).astype(bf16)
            return index, probs.astype(bf16), slope_scores

        slope_k = jnp.zeros((span, HEAD_WIDTH), f32)
        slope_v = jnp.zeros((span, HEAD_WIDTH), f32)
        waiting = []
        for index in range(GROUPS + SKEW):
            if index < GROUPS:
                waiting.append(slopes_of(index))
            if index >= SKEW:
                own, probs, slope_scores = waiting.pop(0)
                columns, place = head_columns(group * GROUPS + own), head_columns(own)
                slope_v = slope_v + matmul(probs, slope[:, columns])
                slope_k = slope_k + matmul(slope_scores, query[:, columns])
                accum[place, :] = accum[place, :] + matmul(keys_turned, slope_scores)
        slope_k, slope_v = (slope_k * SCALE).astype(bf16), slope_v.astype(bf16)
        for which, block in enumerate((slope_k, slope_v)):
            for part in range(BLOCKS):
                own = block[part * stretch : (part + 1) * stretch]
                store(step, part, head_columns(which), own)

    def skip(step):
        for part in range(BLOCKS):
            store(step, part, slice(None), jnp.zeros((stretch, 2 * HEAD_WIDTH), bf16))

    for_each_step(meta, stretch, key_value.shape[0] // span, process, skip)
    for index in range(GROUPS):
        columns = head_columns(index)
        slope_query[:, columns] = (accum[columns, :] * SCALE).T


def expert_kernel(
    which,
    rows,
    slopes,
    chosen,
    gate_up,
    down,
    router,
    hidden_out,
    result_out,
    gates_out,
    slots_out,
    pre_out,
    slope_out,
):
    hidden_width = down.shape[0]
    incoming = rows[...]
    logits = jnp.where(chosen[...] > 0, matmul(incoming, router[...]), big_negative)
    shares = jnp.exp(logits - jnp.max(logits, -1, keepdims=True))
    shares = jnp.where(chosen[...] > 0, shares, 0.0)
    column = lax.broadcasted_iota(jnp.int32, shares.shape, 1)
    own = jnp.sum(jnp.where(column == which[0], shares, 0.0), -1, keepdims=True)
    gates = own / jnp.maximum(jnp.sum(shares, -1, keepdims=True), 1e-30)
    slots = (gates * slopes[...].astype(f32)).astype(bf16)
    slots_out[...] = slots
    pre = matmul(incoming, gate_up[...])
    gate, up = pre[:, :hidden_width], pre[:, hidden_width:]
    root, cubic = math.sqrt(2.0 / math.pi), 0.044715
    square = gate * gate
    bend = jnp.tanh(root * (gate + cubic * gate * square))
    gelu = 0.5 * gate * (1.0 + bend)
    rise = 0.5 * (1.0 + bend) + 0.5 * gate * (1.0 - bend * bend) * root * (
        1.0 + 3.0 * cubic * square
    )
    hidden = (gelu * up).astype(bf16)
    hidden_out[...] = hidden
    result = matmul(hidden, down[...]).astype(bf16)
    result_out[...] = result
    gates_out[...] = jnp.sum(slopes[...].astype(f32) * result.astype(f32), -1, keepdims=True)
    slope_hidden = matmul_nt(slots, down[...])
    slope_pre = jnp.concatenate([slope_hidden * up * rise, slope_hidden * gelu], 1).astype(bf16)
    pre_out[...] = slope_pre
    slope_out[...] = matmul_nt(slope_pre, gate_up[...]).astype(bf16)


def expert(which, rows, slopes, chosen, gate_up, down, router):
    count, width = rows.shape
    hidden_width = down.shape[0]
    block = count // 2

    def tile(columns):
        return pl.BlockSpec((block, columns), lambda step: (step, 0))

    def whole(array):
        return pl.BlockSpec(array.shape, lambda step: (0, 0))

    shapes = [(hidden_width, bf16), (width, bf16), (1, f32), (width, bf16)]
    shapes += [(2 * hidden_width, bf16), (width, bf16)]
    return pl.pallas_call(
        expert_kernel,
        grid=(2,),
        out_shape=[jax.ShapeDtypeStruct((count, columns), kind) for columns, kind in shapes],
        in_specs=[
            pl.BlockSpec(memory_space=pltpu.SMEM),
            tile(width),
            tile(width),
            tile(LANES),
            whole(gate_up),
            whole(down),
            whole(router),
        ],
        out_specs=[tile(columns) for columns, _ in shapes],
        compiler_params=pltpu.CompilerParams(vmem_limit_bytes=VMEM_BYTES),
        cost_estimate=pl.CostEstimate(
            flops=12 * count * width * hidden_width,
            bytes_accessed=20 * count * width,
            transcendentals=count * hidden_width,
        ),
        name="expert",
    )(which, rows, slopes, chosen, gate_up, down, router)


def attention_call(kernel, outs, scratch, products, name, meta, *operands):
    vmem = pl.BlockSpec(memory_space=pltpu.VMEM)
    pairs = QUERY_HEADS * operands[0].shape[0] * operands[-1].shape[0]
    return pl.pallas_call(
        kernel,
        out_shape=outs,
        in_specs=[pl.BlockSpec(memory_space=pltpu.SMEM)] + [vmem] * len(operands),
        out_specs=(vmem,) * len(outs),
        scratch_shapes=[pltpu.VMEM(*shape) for shape in scratch],
        compiler_params=pltpu.CompilerParams(vmem_limit_bytes=VMEM_BYTES),
        cost_estimate=pl.CostEstimate(
            flops=products * pairs, bytes_accessed=QUERY_WIDTH * 1024, transcendentals=0
        ),
        name=name,
    )(meta, *operands)


def attend(meta, query, key_value):
    stretch = query.shape[0]
    stats = (QUERY_HEADS, stretch)
    outs = (
        jax.ShapeDtypeStruct((stretch, QUERY_WIDTH), f32),
        jax.ShapeDtypeStruct(stats, f32),
    )
    scratch = [(stats, f32), (stats, f32), ((QUERY_WIDTH, stretch), f32)]
    return attention_call(attend_kernel, outs, scratch, 2, "attend", meta, query, key_value)


def attend_back(order, group, meta, query, slope, log_total, mixed, key_value):
    stretch, rows = query.shape[0], key_value.shape[0]
    group_width = GROUPS * HEAD_WIDTH
    outs = (
        jax.ShapeDtypeStruct((stretch, group_width), f32),
        jax.ShapeDtypeStruct((2, rows // 2, 2 * HEAD_WIDTH), bf16),
    )
    operands = (meta, query, slope, log_total, mixed, key_value)
    scratch = [((group_width, stretch), f32), ((GROUPS, stretch), f32)]
    kernel = functools.partial(attend_back_kernel, order, group)
    return attention_call(kernel, outs, scratch, 2, "attend_back", *operands)


def body(
    tokens,
    cotangent,
    routes,
    fill_order,
    pic_starts,
    attn_gain,
    moe_gain,
    w_query,
    key_projection,
    value_projection,
    w_out,
    w_router,
    expert_gate,
    expert_up,
    expert_down,
):
    sequences, stretch, width = tokens.shape
    count = sequences * stretch
    parts = lax.axis_size("ctx")
    experts = parts
    capacity = (5 * count * TOP + 4 * experts - 1) // (4 * experts)
    query_width, key_width = QUERY_WIDTH, KEY_WIDTH
    hidden_width = expert_gate.shape[2]
    seq_bits, ctx_bits = bits("seq"), bits("ctx")
    all_bits = seq_bits + ctx_bits
    inward = ctx_bits[-1:] + seq_bits[::-1] + ctx_bits[-2::-1]
    sizes = {"seq": parts, "ctx": 1}
    me = lax.axis_index("seq") * parts + lax.axis_index("ctx")

    def padded(columns):
        block = jnp.concatenate(columns, 1)
        return jnp.pad(block, ((0, 0), (0, LANES - block.shape[1])))

    own_rows = w_query.shape[0]

    def feature(stages):
        owner = jnp.bitwise_xor(jnp.array(flips(stages, sizes), jnp.int32), me)
        return (owner[:, None] * own_rows + jnp.arange(own_rows, dtype=jnp.int32)).reshape(-1)

    def same(left, right):
        return (left[:, None] == right[None, :]).astype(bf16)

    turns = ctx_bits[:-2] + seq_bits + ctx_bits[-2:]
    natural = jnp.arange(width, dtype=jnp.int32)
    gathered, summed = feature(turns[::-1]), feature(inward)
    turn, turn_in, across = same(natural, summed), same(natural, gathered), same(gathered, summed)

    def relative(rows):
        return matmul(rows, turn).astype(bf16)

    def halves(left, right):
        middle = left.shape[1] // 2
        sent = matmul_tn(left[:, middle:], right).astype(bf16)
        return sent, matmul_tn(left[:, :middle], right).astype(bf16)

    picks = routes.reshape(count, TOP)
    order = fill_order.reshape(count)
    routed = jnp.any(picks[:, :, None] == jnp.arange(experts, dtype=jnp.int32), 1)
    earlier = (order[None, :] < order[:, None]).astype(bf16)
    place = matmul(earlier, routed.astype(bf16)).astype(jnp.int32)
    place = jnp.where(routed, place, capacity)
    half = capacity // 2
    chosen_slot = [
        place.T[:, None, :]
        == (begin + jnp.arange(half, dtype=jnp.int32))[None, :, None]
        for begin in (0, half)
    ]
    slot_map = [chosen.astype(bf16).reshape(-1, count) for chosen in chosen_slot]

    def exchange_rows(rows):
        rows = rows.reshape(experts, half, width)
        rows = lax.all_to_all(rows, "ctx", split_axis=0, concat_axis=0, tiled=True)
        return rows.reshape(-1, width)

    out_slope = cotangent.reshape(count, width)
    slot_routes = jnp.concatenate(
        [matmul(part, routed.astype(bf16)).reshape(experts, half, experts) for part in slot_map], 1
    ).astype(bf16)
    slot_routes = lax.all_to_all(slot_routes, "ctx", split_axis=0, concat_axis=0, tiled=True)
    slot_routes = jnp.pad(slot_routes, ((0, 0), (0, 0), (0, LANES - experts)))
    slot_routes = [
        slot_routes[:, begin : begin + half].reshape(-1, LANES) for begin in (0, half)
    ]
    slope_rows = [matmul(part, out_slope).astype(bf16) for part in slot_map]
    slope_rows = jnp.concatenate([part.reshape(experts, half, width) for part in slope_rows], 1)

    block = jnp.concatenate(
        [
            w_query,
            key_projection,
            value_projection,
            padded([attn_gain[:, None]]),
            w_out,
            padded([w_router, moe_gain[:, None]]),
        ],
        1,
    )
    first_width = query_width + 2 * key_width + LANES
    expert_parts = [expert_gate[0], expert_up[0]]
    for index, stage in enumerate(turns):
        other = swap(block if index < 2 else mine, *stage)
        if index in (1, 3) and len(seq_bits) == 1:
            part = index // 2
            other, expert_parts[part] = lax.optimization_barrier(
                (other, (expert_parts[part], swap(expert_parts[part], *seq_bits[0])))
            )
        if index < 2:
            block = jnp.concatenate([block, other], 0)
        if index == 1:
            block, slope_rows = lax.optimization_barrier((block, slope_rows))
            slope_rows = lax.all_to_all(slope_rows, "ctx", split_axis=0, concat_axis=0, tiled=True)
            mine, second_set = block[:, :first_width], block[:, first_width:]
        if index > 2:
            arrived = swap(second_set, *turns[index - 1])
            if index == len(turns) - 1:
                late = second_set, arrived
                continue
            if index < len(turns) - 1:
                other, arrived = lax.optimization_barrier((other, arrived))
            second_set = jnp.concatenate([second_set, arrived], 0)
        if 2 <= index < len(turns) - 1:
            mine = jnp.concatenate([mine, other], 0)
    inputs = tokens.reshape(count, width)
    inputs_turned = matmul(inputs, turn_in)
    inputs = inputs.astype(f32)
    inputs_scaled = inputs_turned * rms_scale(inputs)
    mine, other, slope_rows, slot_routes, inputs_scaled = lax.optimization_barrier(
        (mine, other, slope_rows, slot_routes, inputs_scaled)
    )
    slope_rows = [
        slope_rows[:, begin : begin + half].reshape(-1, width) for begin in (0, half)
    ]
    qkv_width = query_width + 2 * key_width
    weight_low, weight_high = mine[:, :qkv_width], other[:, :qkv_width]
    gain_one = jnp.concatenate([mine[:, qkv_width], other[:, qkv_width]]).astype(f32)

    def whole_expert(part):
        if isinstance(part, tuple):
            own, other = part
            upper = lax.axis_index("seq") > 0
            pair = [jnp.where(upper, other, own), jnp.where(upper, own, other)]
            return jnp.concatenate(pair, 0)
        return gather_blocks(part, seq_bits[::-1], seq_bits).reshape(-1, part.shape[1])

    gate_up = jnp.concatenate([whole_expert(part) for part in expert_parts], 1)
    positions = lax.axis_index("ctx") * stretch + jnp.arange(stretch, dtype=jnp.int32)
    cosine, sine = rope_tables(positions, HEAD_WIDTH)
    normed = (inputs_scaled * gain_one).astype(bf16)

    def project(columns):
        low = matmul(normed[:, : width // 2], weight_low[:, columns])
        return low + matmul(normed[:, width // 2 :], weight_high[:, columns])

    projected = project(slice(query_width, None))
    key_rows = rotate(projected[:, :key_width], KEY_VALUE_HEADS, cosine, sine)
    key_values = lax.all_gather(
        jnp.concatenate([key_rows, projected[:, key_width:]], 1).astype(bf16),
        "ctx",
        axis=0,
        tiled=True,
    )
    projected = project(slice(0, query_width))
    query_rows = rotate(projected, QUERY_HEADS, cosine, sine).astype(bf16)
    second_set, arrived = late
    arrived, query_rows = lax.optimization_barrier((arrived, query_rows))
    second_set = jnp.concatenate([second_set, arrived], 0)
    second_set = jnp.concatenate([second_set, swap(second_set, *turns[-1])], 0)
    second_set = matmul(turn_in, second_set).astype(bf16)
    full_out = second_set[:, :width]
    full_router = second_set[:, width : width + experts]
    gain_two = second_set[:, width + experts].astype(f32)
    meta = jnp.concatenate([lax.axis_index("ctx").astype(jnp.int32)[None], pic_starts[0]])
    mixed_heads, log_total = attend(meta, query_rows, key_values)

    def with_attention(other):
        nonlocal mixed_heads
        mixed_heads, other = lax.optimization_barrier((mixed_heads, other))
        return other

    down = gather_blocks(
        lax.optimization_barrier((expert_down[0], gain_one))[0],
        seq_bits[::-1],
        seq_bits,
        with_attention,
    ).reshape(-1, width)
    attended = mixed_heads.astype(bf16)

    middle = inputs + matmul(attended, full_out)
    enter = rms_norm(middle, gain_two).astype(bf16)
    arrived = [exchange_rows(matmul(part, enter).astype(bf16)) for part in slot_map]

    def gates_of(rows, chosen):
        logits = jnp.where(chosen, matmul(rows, full_router), big_negative)
        shares = jnp.exp(logits - jnp.max(logits, -1, keepdims=True))
        shares = jnp.where(chosen, shares, 0.0)
        return shares / jnp.maximum(jnp.sum(shares, -1, keepdims=True), 1e-30)

    gates = gates_of(enter, routed)

    attended_turned, enter_turned = map(relative, (attended, enter))
    normed_turned = matmul(normed, across).astype(bf16)
    arrived[0], attended_turned, enter_turned, normed_turned = lax.optimization_barrier(
        (arrived[0], attended_turned, enter_turned, normed_turned)
    )
    which = lax.axis_index("ctx").astype(jnp.int32)[None]
    router = second_set[:, width:]
    hidden, result, slope_gates, slope_slots, slope_pre, slope_arrived = ([] for _ in range(6))
    for index in range(2):
        made = list(expert(
            which, arrived[index], slope_rows[index], slot_routes[index], gate_up, down, router)
        )
        if index == 0:
            arrived[1], made[-1] = lax.optimization_barrier((arrived[1], made[-1]))
        for kept, item in zip(
            (hidden, result, slope_gates, slope_slots, slope_pre, slope_arrived), made
        ):
            kept.append(item)
    returned_slopes = [exchange_rows(slope_arrived[0])]
    slope_gates = jnp.concatenate([item.reshape(experts, half) for item in slope_gates], 1)
    returned = jnp.concatenate([part.reshape(experts, half, width) for part in result], 1)
    slope_gates, returned_slopes[0], returned = lax.optimization_barrier(
        (slope_gates, returned_slopes[0], returned)
    )
    returned_gates = lax.all_to_all(slope_gates, "ctx", split_axis=0, concat_axis=0, tiled=True)
    slope_arrived[1], returned_gates, slope_pre, slope_slots = lax.optimization_barrier(
        (slope_arrived[1], returned_gates, slope_pre, slope_slots)
    )
    returned_slopes.append(exchange_rows(slope_arrived[1]))
    grad_gate, grad_up = (
        sum(matmul_tn(arrived[i], slope_pre[i][:, columns]) for i in range(2)).astype(bf16)
        for columns in (slice(0, hidden_width), slice(hidden_width, None))
    )
    grad_down = sum(matmul_tn(hidden[i], slope_slots[i]) for i in range(2)).astype(bf16)
    def sector_cut(blocks, stage):
        axis, bit = stage
        mine = ((lax.axis_index(axis) & bit) > 0).astype(jnp.int32)
        sent = lax.dynamic_index_in_dim(blocks, 1 - mine, 0, keepdims=False)
        return sent, lax.dynamic_index_in_dim(blocks, mine, 0, keepdims=False)

    def sector_halves(grads):
        blocks = grads.reshape([2] * len(seq_bits) + [-1, grads.shape[1]])
        return sector_cut(blocks, seq_bits[0])

    def sector_sum(pair, arrived):
        for index, (axis, bit) in enumerate(seq_bits):
            sent, kept = pair
            other = swap(sent.astype(bf16), axis, bit)
            if index == len(seq_bits) - 1:
                return kept, arrived(other)
            total = kept.astype(f32) + other.astype(f32)
            pair = sector_cut(total, seq_bits[index + 1])

    def ended(pair):
        return pair[0].astype(f32) + pair[1].astype(f32)

    def with_slopes(other):
        nonlocal grad_gate, grad_up
        returned_slopes[1], other, grad_gate, grad_up = lax.optimization_barrier(
            (returned_slopes[1], other, grad_gate, grad_up)
        )
        return other

    grad_gate, grad_up = sector_halves(grad_gate), sector_halves(grad_up)
    grad_down = sector_sum(sector_halves(grad_down), with_slopes)
    returned = lax.all_to_all(returned, "ctx", split_axis=0, concat_axis=0, tiled=True)

    slope_gate = 0.0
    for index, chosen in enumerate(chosen_slot):
        part = returned_gates[:, index * half : (index + 1) * half]
        slope_gate = slope_gate + jnp.sum(jnp.where(chosen, part[:, :, None], 0.0), 1).T
    slope_logits = gates * (slope_gate - jnp.sum(gates * slope_gate, -1, keepdims=True))
    slope_logits = slope_logits.astype(bf16)
    slope_enter = matmul_nt(slope_logits, full_router)
    for part, rows in zip(slot_map, returned_slopes):
        slope_enter = slope_enter + matmul_tn(part, rows)

    pull_two = jax.vjp(rms_norm, middle, gain_two)[1]
    slope_middle, grad_gain_two = pull_two(slope_enter)
    slope_middle = out_slope.astype(f32) + slope_middle
    slope_branch = slope_middle.astype(bf16)
    slope_attended = matmul_nt(slope_branch, full_out).astype(bf16)

    kv_order = ctx_bits[::-1]

    def back(group, meta):
        order = [bit for _, bit in kv_order]
        return attend_back(
            order, group, meta, query_rows, slope_attended, log_total, mixed_heads, key_values
        )

    first_q, first_kv = back(0, meta)

    def after_first(other):
        nonlocal first_q, first_kv, meta, grad_up
        first_q, first_kv, meta, grad_up, other = lax.optimization_barrier(
            (first_q, first_kv, meta, grad_up, other)
        )
        return other

    grad_gate = sector_sum(grad_gate, after_first)
    first_sum = Sum(first_kv[1], first_kv[0], kv_order)
    first_sum.step()
    second_q, second_kv = back(1, meta)

    def after_second(other):
        nonlocal second_q, second_kv, grad_gate, slope_branch
        second_q, second_kv, first_sum.sent, grad_gate, slope_branch, other = (
            lax.optimization_barrier(
                (second_q, second_kv, first_sum.sent, grad_gate, slope_branch, other)
            )
        )
        return other

    grad_up = sector_sum(grad_up, after_second)
    second_sum = Sum(second_kv[1], second_kv[0], kv_order)
    first_sum.step()
    second_sum.step()
    second_sum.sent, first_q, second_q = lax.optimization_barrier(
        (second_sum.sent, first_q, second_q)
    )
    slope_query = jnp.concatenate([first_q, second_q], 1)
    slope_query = rotate(slope_query, QUERY_HEADS, cosine, -sine).astype(bf16)
    query_sum = Sum(*halves(normed_turned, slope_query), inward)
    query_sum.step()
    second_sum.sent, query_sum.sent = lax.optimization_barrier(
        (second_sum.sent, query_sum.sent)
    )
    query_sum.step()
    first_sum.sent, second_sum.sent, slope_branch, returned = lax.optimization_barrier(
        (first_sum.sent, second_sum.sent, slope_branch, returned)
    )
    out_sum = Sum(*halves(attended_turned, slope_branch), inward)
    out_sum.step()
    while len(first_sum.stages) > 1:
        query_sum.sent = together([first_sum, second_sum], query_sum.sent)
    first_sum.step()
    second_sum.step()
    (
        first_sum.total,
        second_sum.sent,
        query_sum.sent,
        out_sum.sent,
        slope_query,
        grad_gate,
        grad_up,
        grad_gain_two,
        enter_turned,
    ) = lax.optimization_barrier(
        (
            first_sum.total,
            second_sum.sent,
            query_sum.sent,
            out_sum.sent,
            slope_query,
            grad_gate,
            grad_up,
            grad_gain_two,
            enter_turned,
        )
    )
    grad_router = matmul_tn(enter_turned, slope_logits)
    out_sum.step()
    second_sum.step()
    totals = [first_sum.total, second_sum.total]
    slope_key = jnp.concatenate([total[:, :HEAD_WIDTH] for total in totals], 1)
    slope_key = rotate(slope_key, KEY_VALUE_HEADS, cosine, -sine)
    slope_rest = [slope_key] + [total[:, HEAD_WIDTH:] for total in totals]
    slope_rest = jnp.concatenate(slope_rest, 1).astype(bf16)
    small = padded([grad_router.astype(bf16), relative(grad_gain_two.astype(bf16)[None]).T])
    rest_sum = Sum(
        *(
            jnp.concatenate([grads, part], 1)
            for grads, part in zip(
                halves(normed_turned, slope_rest), (small[width // 2 :], small[: width // 2])
            )
        ),
        inward,
    )
    slope_rest = together([item for item in (rest_sum, query_sum) if item.stages], slope_rest)
    slope_projected = jnp.concatenate([slope_query, slope_rest], 1)
    slope_normed = jnp.concatenate(
        [matmul_nt(slope_projected, part) for part in (weight_low, weight_high)], 1
    )
    pull_one = jax.vjp(rms_norm, inputs_turned, gain_one)[1]
    slope_inputs = pull_one(slope_normed)[0]
    returned = together(
        [item for item in (rest_sum, query_sum, out_sum) if item.stages], returned
    )
    output = middle
    for chosen, rows in ((jnp.concatenate(chosen_slot, 1), returned.reshape(-1, width)),):
        mix = jnp.where(chosen, gates.T[:, None, :], 0.0).reshape(-1, count)
        output = output + matmul_tn(mix.astype(bf16), rows)
    output = output.astype(bf16).reshape(tokens.shape)
    while rest_sum.stages:
        together([item for item in (rest_sum, query_sum, out_sum) if item.stages])
    for item in (query_sum, out_sum):
        while item.stages:
            item.step()
    grads_rest = rest_sum.total
    grad_input = slope_middle + matmul_nt(slope_inputs.astype(bf16), turn_in)
    grad_input = grad_input.reshape(tokens.shape)
    grad_gain_one = jnp.sum(w_query.astype(f32) * query_sum.total, 1)
    own_kv = jnp.concatenate([key_projection, value_projection], 1).astype(f32)
    grad_gain_one = grad_gain_one + jnp.sum(own_kv * grads_rest[:, : 2 * key_width], 1)
    grad_gain_one = grad_gain_one / attn_gain.astype(f32)
    return (
        output,
        grad_input,
        grad_gain_one,
        grads_rest[:, 2 * key_width + experts],
        query_sum.total,
        grads_rest[:, :key_width],
        grads_rest[:, key_width : 2 * key_width],
        out_sum.total,
        grads_rest[:, 2 * key_width : 2 * key_width + experts],
        ended(grad_gate)[None],
        ended(grad_up)[None],
        ended(grad_down)[None],
    )


def solution(mesh):
    rows = P("seq", "ctx", None)
    shard = P(("seq", "ctx"), None)
    vector = P(("seq", "ctx"))
    expert = P("ctx", "seq", None)
    return jax.shard_map(
        body,
        mesh=mesh,
        in_specs=(rows, rows, rows, P("seq", "ctx"), P("seq", None), vector, vector)
        + (shard,) * 5
        + (expert,) * 3,
        out_specs=(rows, rows, vector, vector) + (shard,) * 5 + (expert,) * 3,
        check_vma=False,
    )
```

```python
import functools
import math

import jax
import jax.numpy as jnp
from jax import lax
from jax.experimental import pallas as pl
from jax.experimental.pallas import tpu as pltpu
from jax.sharding import PartitionSpec as P

QUERY_HEADS = 12
KEY_VALUE_HEADS = 2
HEAD_WIDTH = 128
TOP = 4
PIC = 256
NPIC = 4
LANES = 128
GROUPS = QUERY_HEADS // KEY_VALUE_HEADS
QUERY_WIDTH = QUERY_HEADS * HEAD_WIDTH
KEY_WIDTH = KEY_VALUE_HEADS * HEAD_WIDTH
SCALE = 1.0 / math.sqrt(HEAD_WIDTH)
EXP2_SCALE = SCALE * math.log2(math.e)
BLOCKS = 2
SKEW = 1
VMEM_BYTES = 48 << 20

epsilon = 1e-06
rope_base = 10000.0
big_negative = -1e30
bf16 = jnp.bfloat16
f32 = jnp.float32


def matmul(left, right):
    return jnp.dot(left, right, preferred_element_type=f32)


def matmul_nt(left, right):
    return lax.dot_general(left, right, (((1,), (1,)), ((), ())), preferred_element_type=f32)


def matmul_tn(left, right):
    return lax.dot_general(left, right, (((0,), (0,)), ((), ())), preferred_element_type=f32)


def rms_scale(rows):
    return lax.rsqrt(jnp.mean(rows * rows, -1, keepdims=True) + epsilon)


def rms_norm(rows, gain):
    return rows * rms_scale(rows) * gain


def rope_tables(positions, head_size):
    half = head_size // 2
    inverse = rope_base ** (-(jnp.arange(half, dtype=f32) * 2.0 / head_size))
    angles = positions.astype(f32)[:, None] * inverse[None, :]
    return (jnp.cos(angles), jnp.sin(angles))


def rotate(rows, heads, cosine, sine):
    shaped = rows.reshape(rows.shape[0], heads, HEAD_WIDTH)
    half = HEAD_WIDTH // 2
    first, second = shaped[..., :half], shaped[..., half:]
    cosine, sine = cosine[:, None, :], sine[:, None, :]
    turned = jnp.concatenate(
        [first * cosine - second * sine, second * cosine + first * sine], -1
    )
    return turned.reshape(rows.shape)


def bits(axis):
    size = lax.axis_size(axis)
    return [(axis, 1 << place) for place in reversed(range(size.bit_length() - 1))]


def swap(block, axis, bit):
    size = lax.axis_size(axis)
    return lax.ppermute(block, axis, [(index, index ^ bit) for index in range(size)])


def gather_blocks(block, stages, order, arrived=None):
    held = []
    for stage in stages:
        axis, bit = stage
        other = swap(block, axis, bit)
        if arrived is not None and stage == stages[-1]:
            other = arrived(other)
        upper = (lax.axis_index(axis) & bit) > 0
        place = sum(order.index(known) < order.index(stage) for known in held)
        block = jnp.stack(
            [jnp.where(upper, other, block), jnp.where(upper, block, other)], place
        )
        held.append(stage)
    return block


class Sum:
    def __init__(self, sent, kept, stages):
        self.sent, self.kept, self.stages = sent, kept, list(stages)

    def step(self):
        axis, bit = self.stages.pop(0)
        other = swap(self.sent, axis, bit)
        if not self.stages:
            self.total = self.kept.astype(f32) + other.astype(f32)
            return
        half = self.kept.shape[0] // 2
        self.sent = (self.kept[half:].astype(f32) + other[half:].astype(f32)).astype(bf16)
        self.kept = (self.kept[:half].astype(f32) + other[:half].astype(f32)).astype(bf16)


def together(sums, also=()):
    for item in sums:
        item.step()
    live = [item for item in sums if item.stages]
    sent, also = lax.optimization_barrier(([item.sent for item in live], also))
    for item, block in zip(live, sent):
        item.sent = block
    return also


def flips(stages, sizes):
    masks = []
    for block in range(1 << len(stages)):
        mask = 0
        for place, (axis, bit) in enumerate(stages):
            if (block >> (len(stages) - 1 - place)) & 1:
                mask |= bit * sizes[axis]
        masks.append(mask)
    return masks


def visible_keys(meta, step, stretch):
    span = BLOCKS * stretch
    keys = step * span + lax.broadcasted_iota(jnp.int32, (span, 1), 0)
    queries = meta[0] * stretch + lax.broadcasted_iota(jnp.int32, (1, stretch), 1)

    def label(positions):
        found = jnp.zeros(positions.shape, jnp.int32)
        for index in range(NPIC):
            start = meta[1 + index]
            inside = (positions >= start) & (positions < start + PIC)
            found = jnp.where(inside, index + 1, found)
        return found

    query_label = label(queries)
    return (keys <= queries) | ((label(keys) == query_label) & (query_label > 0))


def for_each_step(meta, stretch, steps, process, skip=None):
    span = BLOCKS * stretch
    low, high = meta[0] * stretch, (meta[0] + 1) * stretch

    def turn(step, carry):
        needed = step * span < high + PIC - 1
        edge = (step + 1) * span > low

        @pl.when(needed & edge)
        def _():
            process(step, True)

        @pl.when(needed & jnp.logical_not(edge))
        def _():
            process(step, False)

        if skip is not None:

            @pl.when(jnp.logical_not(needed))
            def _():
                skip(step)

        return carry

    lax.fori_loop(0, steps, turn, 0)


def head_columns(head, start=0):
    return slice(start + head * HEAD_WIDTH, start + (head + 1) * HEAD_WIDTH)


def attend_kernel(meta, query, key_value, out, log_total, peak, total, accum):
    stretch = query.shape[0]
    span = BLOCKS * stretch
    peak[...] = jnp.full(peak.shape, big_negative, f32)
    total[...] = jnp.zeros(total.shape, f32)
    accum[...] = jnp.zeros(accum.shape, f32)

    def process(step, edge):
        rows = pl.ds(pl.multiple_of(step * span, span), span)
        if edge:
            visible = visible_keys(meta, step, stretch)
        keys, values = [], []
        for group in range(KEY_VALUE_HEADS):
            keys.append(key_value[rows, head_columns(group)])
            turned = key_value[rows, head_columns(group, KEY_WIDTH)].T
            values.append(jnp.concatenate([turned, jnp.ones((16, span), bf16)], 0))

        def score(head):
            scores = matmul_nt(keys[head // GROUPS], query[:, head_columns(head)])
            if edge:
                scores = jnp.where(visible, scores, big_negative)
            old = peak[head : head + 1, :]
            return scores, old, jnp.maximum(old, jnp.max(scores, 0, keepdims=True))

        def weigh(head, scores, old, new):
            weights = jnp.exp2((scores - new) * EXP2_SCALE).astype(bf16)
            shrink = jnp.exp2((old - new) * EXP2_SCALE)
            sums = matmul(values[head // GROUPS], weights)
            row, columns = slice(head, head + 1), head_columns(head)
            peak[row, :] = new
            total[row, :] = total[row, :] * shrink + sums[HEAD_WIDTH : HEAD_WIDTH + 1]
            accum[columns, :] = accum[columns, :] * shrink + sums[:HEAD_WIDTH]

        waiting = []
        for head in range(QUERY_HEADS):
            waiting.append((head, *score(head)))
            if len(waiting) > 2:
                weigh(*waiting.pop(0))
        for item in waiting:
            weigh(*item)

    for_each_step(meta, stretch, key_value.shape[0] // span, process)
    for head in range(QUERY_HEADS):
        row, columns = slice(head, head + 1), head_columns(head)
        out[:, columns] = (accum[columns, :] / total[row, :]).T
        log_total[row, :] = peak[row, :] * EXP2_SCALE + jnp.log2(total[row, :])


def attend_back_kernel(
    order,
    group,
    meta,
    query,
    slope,
    log_total,
    mixed,
    key_value,
    slope_query,
    out,
    accum,
    delta,
):
    stretch = query.shape[0]
    span = BLOCKS * stretch
    accum[...] = jnp.zeros(accum.shape, f32)
    for index in range(GROUPS):
        columns = head_columns(group * GROUPS + index)
        product = slope[:, columns].astype(f32) * mixed[:, columns]
        delta[index : index + 1, :] = jnp.sum(product.T, 0, keepdims=True)

    def store(step, part, columns, block):
        flip = jnp.bitwise_xor(BLOCKS * step + part, meta[0])
        first, *others = order
        place = 0
        for index, bit in enumerate(others):
            place = place + ((flip // bit) & 1) * (1 << (len(others) - 1 - index))
        place = pl.ds(pl.multiple_of(place * stretch, stretch), stretch)
        out[(flip // first) & 1, place, columns] = block

    def process(step, edge):
        rows = pl.ds(pl.multiple_of(step * span, span), span)
        if edge:
            visible = visible_keys(meta, step, stretch)
        keys = key_value[rows, head_columns(group)]
        values = key_value[rows, head_columns(group, KEY_WIDTH)]
        keys_turned = keys.T

        def slopes_of(index):
            columns = head_columns(group * GROUPS + index)
            row = slice(group * GROUPS + index, group * GROUPS + index + 1)
            scores = matmul_nt(keys, query[:, columns])
            probs = jnp.exp2(scores * EXP2_SCALE - log_total[row, :])
            if edge:
                probs = jnp.where(visible, probs, 0.0)
            slope_probs = matmul_nt(values, slope[:, columns])
            slope_scores = (probs * (slope_probs - delta[index : index + 1, :])).astype(bf16)
            return index, probs.astype(bf16), slope_scores

        slope_k = jnp.zeros((span, HEAD_WIDTH), f32)
        slope_v = jnp.zeros((span, HEAD_WIDTH), f32)
        waiting = []
        for index in range(GROUPS + SKEW):
            if index < GROUPS:
                waiting.append(slopes_of(index))
            if index >= SKEW:
                own, probs, slope_scores = waiting.pop(0)
                columns, place = head_columns(group * GROUPS + own), head_columns(own)
                slope_v = slope_v + matmul(probs, slope[:, columns])
                slope_k = slope_k + matmul(slope_scores, query[:, columns])
                accum[place, :] = accum[place, :] + matmul(keys_turned, slope_scores)
        slope_k, slope_v = (slope_k * SCALE).astype(bf16), slope_v.astype(bf16)
        for which, block in enumerate((slope_k, slope_v)):
            for part in range(BLOCKS):
                own = block[part * stretch : (part + 1) * stretch]
                store(step, part, head_columns(which), own)

    def skip(step):
        for part in range(BLOCKS):
            store(step, part, slice(None), jnp.zeros((stretch, 2 * HEAD_WIDTH), bf16))

    for_each_step(meta, stretch, key_value.shape[0] // span, process, skip)
    for index in range(GROUPS):
        columns = head_columns(index)
        slope_query[:, columns] = (accum[columns, :] * SCALE).T


def expert_kernel(
    which,
    rows,
    slopes,
    chosen,
    gate_up,
    down,
    router,
    hidden_out,
    result_out,
    gates_out,
    slots_out,
    pre_out,
    slope_out,
):
    hidden_width = down.shape[0]
    incoming = rows[...]
    logits = jnp.where(chosen[...] > 0, matmul(incoming, router[...]), big_negative)
    shares = jnp.exp(logits - jnp.max(logits, -1, keepdims=True))
    shares = jnp.where(chosen[...] > 0, shares, 0.0)
    column = lax.broadcasted_iota(jnp.int32, shares.shape, 1)
    own = jnp.sum(jnp.where(column == which[0], shares, 0.0), -1, keepdims=True)
    gates = own / jnp.maximum(jnp.sum(shares, -1, keepdims=True), 1e-30)
    slots = (gates * slopes[...].astype(f32)).astype(bf16)
    slots_out[...] = slots
    pre = matmul(incoming, gate_up[...])
    gate, up = pre[:, :hidden_width], pre[:, hidden_width:]
    root, cubic = math.sqrt(2.0 / math.pi), 0.044715
    square = gate * gate
    bend = jnp.tanh(root * (gate + cubic * gate * square))
    gelu = 0.5 * gate * (1.0 + bend)
    rise = 0.5 * (1.0 + bend) + 0.5 * gate * (1.0 - bend * bend) * root * (
        1.0 + 3.0 * cubic * square
    )
    hidden = (gelu * up).astype(bf16)
    hidden_out[...] = hidden
    result = matmul(hidden, down[...]).astype(bf16)
    result_out[...] = result
    gates_out[...] = jnp.sum(slopes[...].astype(f32) * result.astype(f32), -1, keepdims=True)
    slope_hidden = matmul_nt(slots, down[...])
    slope_pre = jnp.concatenate([slope_hidden * up * rise, slope_hidden * gelu], 1).astype(bf16)
    pre_out[...] = slope_pre
    slope_out[...] = matmul_nt(slope_pre, gate_up[...]).astype(bf16)


def expert(which, rows, slopes, chosen, gate_up, down, router):
    count, width = rows.shape
    hidden_width = down.shape[0]
    block = count // 2

    def tile(columns):
        return pl.BlockSpec((block, columns), lambda step: (step, 0))

    def whole(array):
        return pl.BlockSpec(array.shape, lambda step: (0, 0))

    shapes = [(hidden_width, bf16), (width, bf16), (1, f32), (width, bf16)]
    shapes += [(2 * hidden_width, bf16), (width, bf16)]
    return pl.pallas_call(
        expert_kernel,
        grid=(2,),
        out_shape=[jax.ShapeDtypeStruct((count, columns), kind) for columns, kind in shapes],
        in_specs=[
            pl.BlockSpec(memory_space=pltpu.SMEM),
            tile(width),
            tile(width),
            tile(LANES),
            whole(gate_up),
            whole(down),
            whole(router),
        ],
        out_specs=[tile(columns) for columns, _ in shapes],
        compiler_params=pltpu.CompilerParams(vmem_limit_bytes=VMEM_BYTES),
        cost_estimate=pl.CostEstimate(
            flops=12 * count * width * hidden_width,
            bytes_accessed=20 * count * width,
            transcendentals=count * hidden_width,
        ),
        name="expert",
    )(which, rows, slopes, chosen, gate_up, down, router)


def attention_call(kernel, outs, scratch, products, name, meta, *operands):
    vmem = pl.BlockSpec(memory_space=pltpu.VMEM)
    pairs = QUERY_HEADS * operands[0].shape[0] * operands[-1].shape[0]
    return pl.pallas_call(
        kernel,
        out_shape=outs,
        in_specs=[pl.BlockSpec(memory_space=pltpu.SMEM)] + [vmem] * len(operands),
        out_specs=(vmem,) * len(outs),
        scratch_shapes=[pltpu.VMEM(*shape) for shape in scratch],
        compiler_params=pltpu.CompilerParams(vmem_limit_bytes=VMEM_BYTES),
        cost_estimate=pl.CostEstimate(
            flops=products * pairs, bytes_accessed=QUERY_WIDTH * 1024, transcendentals=0
        ),
        name=name,
    )(meta, *operands)


def attend(meta, query, key_value):
    stretch = query.shape[0]
    stats = (QUERY_HEADS, stretch)
    outs = (
        jax.ShapeDtypeStruct((stretch, QUERY_WIDTH), f32),
        jax.ShapeDtypeStruct(stats, f32),
    )
    scratch = [(stats, f32), (stats, f32), ((QUERY_WIDTH, stretch), f32)]
    return attention_call(attend_kernel, outs, scratch, 2, "attend", meta, query, key_value)


def attend_back(order, group, meta, query, slope, log_total, mixed, key_value):
    stretch, rows = query.shape[0], key_value.shape[0]
    group_width = GROUPS * HEAD_WIDTH
    outs = (
        jax.ShapeDtypeStruct((stretch, group_width), f32),
        jax.ShapeDtypeStruct((2, rows // 2, 2 * HEAD_WIDTH), bf16),
    )
    operands = (meta, query, slope, log_total, mixed, key_value)
    scratch = [((group_width, stretch), f32), ((GROUPS, stretch), f32)]
    kernel = functools.partial(attend_back_kernel, order, group)
    return attention_call(kernel, outs, scratch, 2, "attend_back", *operands)


def body(
    tokens,
    cotangent,
    routes,
    fill_order,
    pic_starts,
    attn_gain,
    moe_gain,
    w_query,
    key_projection,
    value_projection,
    w_out,
    w_router,
    expert_gate,
    expert_up,
    expert_down,
):
    sequences, stretch, width = tokens.shape
    count = sequences * stretch
    parts = lax.axis_size("ctx")
    experts = parts
    capacity = (5 * count * TOP + 4 * experts - 1) // (4 * experts)
    query_width, key_width = QUERY_WIDTH, KEY_WIDTH
    hidden_width = expert_gate.shape[2]
    seq_bits, ctx_bits = bits("seq"), bits("ctx")
    all_bits = seq_bits + ctx_bits
    inward = ctx_bits[-1:] + seq_bits[::-1] + ctx_bits[-2::-1]
    sizes = {"seq": parts, "ctx": 1}
    me = lax.axis_index("seq") * parts + lax.axis_index("ctx")

    def padded(columns):
        block = jnp.concatenate(columns, 1)
        return jnp.pad(block, ((0, 0), (0, LANES - block.shape[1])))

    own_rows = w_query.shape[0]

    def feature(stages):
        owner = jnp.bitwise_xor(jnp.array(flips(stages, sizes), jnp.int32), me)
        return (owner[:, None] * own_rows + jnp.arange(own_rows, dtype=jnp.int32)).reshape(-1)

    def same(left, right):
        return (left[:, None] == right[None, :]).astype(bf16)

    turns = ctx_bits[:-2] + seq_bits + ctx_bits[-2:]
    natural = jnp.arange(width, dtype=jnp.int32)
    gathered, summed = feature(turns[::-1]), feature(inward)
    turn, turn_in, across = same(natural, summed), same(natural, gathered), same(gathered, summed)

    def relative(rows):
        return matmul(rows, turn).astype(bf16)

    def halves(left, right):
        middle = left.shape[1] // 2
        sent = matmul_tn(left[:, middle:], right).astype(bf16)
        return sent, matmul_tn(left[:, :middle], right).astype(bf16)

    picks = routes.reshape(count, TOP)
    order = fill_order.reshape(count)
    routed = jnp.any(picks[:, :, None] == jnp.arange(experts, dtype=jnp.int32), 1)
    earlier = (order[None, :] < order[:, None]).astype(bf16)
    place = matmul(earlier, routed.astype(bf16)).astype(jnp.int32)
    place = jnp.where(routed, place, capacity)
    half = capacity // 2
    chosen_slot = [
        place.T[:, None, :]
        == (begin + jnp.arange(half, dtype=jnp.int32))[None, :, None]
        for begin in (0, half)
    ]
    slot_map = [chosen.astype(bf16).reshape(-1, count) for chosen in chosen_slot]

    def exchange_rows(rows):
        rows = rows.reshape(experts, half, width)
        rows = lax.all_to_all(rows, "ctx", split_axis=0, concat_axis=0, tiled=True)
        return rows.reshape(-1, width)

    out_slope = cotangent.reshape(count, width)
    slot_routes = jnp.concatenate(
        [matmul(part, routed.astype(bf16)).reshape(experts, half, experts) for part in slot_map], 1
    ).astype(bf16)
    slot_routes = lax.all_to_all(slot_routes, "ctx", split_axis=0, concat_axis=0, tiled=True)
    slot_routes = jnp.pad(slot_routes, ((0, 0), (0, 0), (0, LANES - experts)))
    slot_routes = [
        slot_routes[:, begin : begin + half].reshape(-1, LANES) for begin in (0, half)
    ]
    slope_rows = [matmul(part, out_slope).astype(bf16) for part in slot_map]
    slope_rows = jnp.concatenate([part.reshape(experts, half, width) for part in slope_rows], 1)

    block = jnp.concatenate(
        [
            w_query,
            key_projection,
            value_projection,
            padded([attn_gain[:, None]]),
            w_out,
            padded([w_router, moe_gain[:, None]]),
        ],
        1,
    )
    first_width = query_width + 2 * key_width + LANES
    expert_parts = [expert_gate[0], expert_up[0]]
    for index, stage in enumerate(turns):
        other = swap(block if index < 2 else mine, *stage)
        if index in (1, 3) and len(seq_bits) == 1:
            part = index // 2
            other, expert_parts[part] = lax.optimization_barrier(
                (other, (expert_parts[part], swap(expert_parts[part], *seq_bits[0])))
            )
        if index < 2:
            block = jnp.concatenate([block, other], 0)
        if index == 1:
            block, slope_rows = lax.optimization_barrier((block, slope_rows))
            slope_rows = lax.all_to_all(slope_rows, "ctx", split_axis=0, concat_axis=0, tiled=True)
            mine, second_set = block[:, :first_width], block[:, first_width:]
        if index > 2:
            arrived = swap(second_set, *turns[index - 1])
            if index == len(turns) - 1:
                late = second_set, arrived
                continue
            if index < len(turns) - 1:
                other, arrived = lax.optimization_barrier((other, arrived))
            second_set = jnp.concatenate([second_set, arrived], 0)
        if 2 <= index < len(turns) - 1:
            mine = jnp.concatenate([mine, other], 0)
    inputs = tokens.reshape(count, width)
    inputs_turned = matmul(inputs, turn_in)
    inputs = inputs.astype(f32)
    inputs_scaled = inputs_turned * rms_scale(inputs)
    mine, other, slope_rows, slot_routes, inputs_scaled = lax.optimization_barrier(
        (mine, other, slope_rows, slot_routes, inputs_scaled)
    )
    slope_rows = [
        slope_rows[:, begin : begin + half].reshape(-1, width) for begin in (0, half)
    ]
    qkv_width = query_width + 2 * key_width
    weight_low, weight_high = mine[:, :qkv_width], other[:, :qkv_width]
    gain_one = jnp.concatenate([mine[:, qkv_width], other[:, qkv_width]]).astype(f32)

    def whole_expert(part):
        if isinstance(part, tuple):
            own, other = part
            upper = lax.axis_index("seq") > 0
            pair = [jnp.where(upper, other, own), jnp.where(upper, own, other)]
            return jnp.concatenate(pair, 0)
        return gather_blocks(part, seq_bits[::-1], seq_bits).reshape(-1, part.shape[1])

    gate_up = jnp.concatenate([whole_expert(part) for part in expert_parts], 1)
    positions = lax.axis_index("ctx") * stretch + jnp.arange(stretch, dtype=jnp.int32)
    cosine, sine = rope_tables(positions, HEAD_WIDTH)
    normed = (inputs_scaled * gain_one).astype(bf16)

    def project(columns):
        low = matmul(normed[:, : width // 2], weight_low[:, columns])
        return low + matmul(normed[:, width // 2 :], weight_high[:, columns])

    projected = project(slice(query_width, None))
    key_rows = rotate(projected[:, :key_width], KEY_VALUE_HEADS, cosine, sine)
    key_values = lax.all_gather(
        jnp.concatenate([key_rows, projected[:, key_width:]], 1).astype(bf16),
        "ctx",
        axis=0,
        tiled=True,
    )
    projected = project(slice(0, query_width))
    query_rows = rotate(projected, QUERY_HEADS, cosine, sine).astype(bf16)
    second_set, arrived = late
    arrived, query_rows = lax.optimization_barrier((arrived, query_rows))
    second_set = jnp.concatenate([second_set, arrived], 0)
    second_set = jnp.concatenate([second_set, swap(second_set, *turns[-1])], 0)
    second_set = matmul(turn_in, second_set).astype(bf16)
    full_out = second_set[:, :width]
    full_router = second_set[:, width : width + experts]
    gain_two = second_set[:, width + experts].astype(f32)
    meta = jnp.concatenate([lax.axis_index("ctx").astype(jnp.int32)[None], pic_starts[0]])
    mixed_heads, log_total = attend(meta, query_rows, key_values)

    def with_attention(other):
        nonlocal mixed_heads
        mixed_heads, other = lax.optimization_barrier((mixed_heads, other))
        return other

    down = gather_blocks(
        lax.optimization_barrier((expert_down[0], gain_one))[0],
        seq_bits[::-1],
        seq_bits,
        with_attention,
    ).reshape(-1, width)
    attended = mixed_heads.astype(bf16)

    middle = inputs + matmul(attended, full_out)
    enter = rms_norm(middle, gain_two).astype(bf16)
    arrived = [exchange_rows(matmul(part, enter).astype(bf16)) for part in slot_map]

    def gates_of(rows, chosen):
        logits = jnp.where(chosen, matmul(rows, full_router), big_negative)
        shares = jnp.exp(logits - jnp.max(logits, -1, keepdims=True))
        shares = jnp.where(chosen, shares, 0.0)
        return shares / jnp.maximum(jnp.sum(shares, -1, keepdims=True), 1e-30)

    gates = gates_of(enter, routed)

    attended_turned, enter_turned = map(relative, (attended, enter))
    normed_turned = matmul(normed, across).astype(bf16)
    arrived[0], attended_turned, enter_turned, normed_turned = lax.optimization_barrier(
        (arrived[0], attended_turned, enter_turned, normed_turned)
    )
    which = lax.axis_index("ctx").astype(jnp.int32)[None]
    router = second_set[:, width:]
    hidden, result, slope_gates, slope_slots, slope_pre, slope_arrived = ([] for _ in range(6))
    for index in range(2):
        made = list(expert(
            which, arrived[index], slope_rows[index], slot_routes[index], gate_up, down, router)
        )
        if index == 0:
            arrived[1], made[-1] = lax.optimization_barrier((arrived[1], made[-1]))
        for kept, item in zip(
            (hidden, result, slope_gates, slope_slots, slope_pre, slope_arrived), made
        ):
            kept.append(item)
    returned_slopes = [exchange_rows(slope_arrived[0])]
    slope_gates = jnp.concatenate([item.reshape(experts, half) for item in slope_gates], 1)
    returned = jnp.concatenate([part.reshape(experts, half, width) for part in result], 1)
    slope_gates, returned_slopes[0], returned = lax.optimization_barrier(
        (slope_gates, returned_slopes[0], returned)
    )
    returned_gates = lax.all_to_all(slope_gates, "ctx", split_axis=0, concat_axis=0, tiled=True)
    slope_arrived[1], returned_gates, slope_pre, slope_slots = lax.optimization_barrier(
        (slope_arrived[1], returned_gates, slope_pre, slope_slots)
    )
    returned_slopes.append(exchange_rows(slope_arrived[1]))
    grad_gate, grad_up = (
        sum(matmul_tn(arrived[i], slope_pre[i][:, columns]) for i in range(2)).astype(bf16)
        for columns in (slice(0, hidden_width), slice(hidden_width, None))
    )
    grad_down = sum(matmul_tn(hidden[i], slope_slots[i]) for i in range(2)).astype(bf16)
    def sector_cut(blocks, stage):
        axis, bit = stage
        mine = ((lax.axis_index(axis) & bit) > 0).astype(jnp.int32)
        sent = lax.dynamic_index_in_dim(blocks, 1 - mine, 0, keepdims=False)
        return sent, lax.dynamic_index_in_dim(blocks, mine, 0, keepdims=False)

    def sector_halves(grads):
        blocks = grads.reshape([2] * len(seq_bits) + [-1, grads.shape[1]])
        return sector_cut(blocks, seq_bits[0])

    def sector_sum(pair, arrived):
        for index, (axis, bit) in enumerate(seq_bits):
            sent, kept = pair
            other = swap(sent.astype(bf16), axis, bit)
            if index == len(seq_bits) - 1:
                return kept, arrived(other)
            total = kept.astype(f32) + other.astype(f32)
            pair = sector_cut(total, seq_bits[index + 1])

    def ended(pair):
        return pair[0].astype(f32) + pair[1].astype(f32)

    def with_slopes(other):
        nonlocal grad_gate, grad_up
        returned_slopes[1], other, grad_gate, grad_up = lax.optimization_barrier(
            (returned_slopes[1], other, grad_gate, grad_up)
        )
        return other

    grad_gate, grad_up = sector_halves(grad_gate), sector_halves(grad_up)
    grad_down = sector_sum(sector_halves(grad_down), with_slopes)
    returned = lax.all_to_all(returned, "ctx", split_axis=0, concat_axis=0, tiled=True)

    slope_gate = 0.0
    for index, chosen in enumerate(chosen_slot):
        part = returned_gates[:, index * half : (index + 1) * half]
        slope_gate = slope_gate + jnp.sum(jnp.where(chosen, part[:, :, None], 0.0), 1).T
    slope_logits = gates * (slope_gate - jnp.sum(gates * slope_gate, -1, keepdims=True))
    slope_logits = slope_logits.astype(bf16)
    slope_enter = matmul_nt(slope_logits, full_router)
    for part, rows in zip(slot_map, returned_slopes):
        slope_enter = slope_enter + matmul_tn(part, rows)

    pull_two = jax.vjp(rms_norm, middle, gain_two)[1]
    slope_middle, grad_gain_two = pull_two(slope_enter)
    slope_middle = out_slope.astype(f32) + slope_middle
    slope_branch = slope_middle.astype(bf16)
    slope_attended = matmul_nt(slope_branch, full_out).astype(bf16)

    kv_order = ctx_bits[::-1]

    def back(group, meta):
        order = [bit for _, bit in kv_order]
        return attend_back(
            order, group, meta, query_rows, slope_attended, log_total, mixed_heads, key_values
        )

    first_q, first_kv = back(0, meta)

    def after_first(other):
        nonlocal first_q, first_kv, meta, grad_up
        first_q, first_kv, meta, grad_up, other = lax.optimization_barrier(
            (first_q, first_kv, meta, grad_up, other)
        )
        return other

    grad_gate = sector_sum(grad_gate, after_first)
    first_sum = Sum(first_kv[1], first_kv[0], kv_order)
    first_sum.step()
    second_q, second_kv = back(1, meta)

    second_q, second_kv, first_sum.sent, grad_gate, slope_branch = lax.optimization_barrier(
        (second_q, second_kv, first_sum.sent, grad_gate, slope_branch)
    )
    second_sum = Sum(second_kv[1], second_kv[0], kv_order)
    first_sum.step()
    second_sum.step()
    second_sum.sent, first_q, second_q = lax.optimization_barrier(
        (second_sum.sent, first_q, second_q)
    )
    slope_query = jnp.concatenate([first_q, second_q], 1)
    slope_query = rotate(slope_query, QUERY_HEADS, cosine, -sine).astype(bf16)
    query_sum = Sum(*halves(normed_turned, slope_query), inward)
    query_sum.step()

    def with_step(other):
        nonlocal slope_branch, returned
        blocks = first_sum.sent, second_sum.sent, query_sum.sent
        blocks, slope_branch, returned, other = lax.optimization_barrier(
            (blocks, slope_branch, returned, other)
        )
        first_sum.sent, second_sum.sent, query_sum.sent = blocks
        return other

    grad_up = sector_sum(grad_up, with_step)
    query_sum.step()
    out_sum = Sum(*halves(attended_turned, slope_branch), inward)
    out_sum.step()
    while len(first_sum.stages) > 1:
        together([first_sum, second_sum])
    first_sum.step()
    second_sum.step()
    (
        first_sum.total,
        second_sum.sent,
        query_sum.sent,
        out_sum.sent,
        slope_query,
        grad_gate,
        grad_up,
        grad_gain_two,
        enter_turned,
    ) = lax.optimization_barrier(
        (
            first_sum.total,
            second_sum.sent,
            query_sum.sent,
            out_sum.sent,
            slope_query,
            grad_gate,
            grad_up,
            grad_gain_two,
            enter_turned,
        )
    )
    grad_router = matmul_tn(enter_turned, slope_logits)
    out_sum.step()
    second_sum.step()
    totals = [first_sum.total, second_sum.total]
    slope_key = jnp.concatenate([total[:, :HEAD_WIDTH] for total in totals], 1)
    slope_key = rotate(slope_key, KEY_VALUE_HEADS, cosine, -sine)
    slope_rest = [slope_key] + [total[:, HEAD_WIDTH:] for total in totals]
    slope_rest = jnp.concatenate(slope_rest, 1).astype(bf16)
    small = padded([grad_router.astype(bf16), relative(grad_gain_two.astype(bf16)[None]).T])
    rest_sum = Sum(
        *(
            jnp.concatenate([grads, part], 1)
            for grads, part in zip(
                halves(normed_turned, slope_rest), (small[width // 2 :], small[: width // 2])
            )
        ),
        inward,
    )
    slope_rest = together([item for item in (rest_sum, query_sum) if item.stages], slope_rest)
    slope_projected = jnp.concatenate([slope_query, slope_rest], 1)
    slope_normed = jnp.concatenate(
        [matmul_nt(slope_projected, part) for part in (weight_low, weight_high)], 1
    )
    pull_one = jax.vjp(rms_norm, inputs_turned, gain_one)[1]
    slope_inputs = pull_one(slope_normed)[0]
    returned = together(
        [item for item in (rest_sum, query_sum, out_sum) if item.stages], returned
    )
    output = middle
    for chosen, rows in ((jnp.concatenate(chosen_slot, 1), returned.reshape(-1, width)),):
        mix = jnp.where(chosen, gates.T[:, None, :], 0.0).reshape(-1, count)
        output = output + matmul_tn(mix.astype(bf16), rows)
    output = output.astype(bf16).reshape(tokens.shape)
    while rest_sum.stages:
        together([item for item in (rest_sum, query_sum, out_sum) if item.stages])
    for item in (query_sum, out_sum):
        while item.stages:
            item.step()
    grads_rest = rest_sum.total
    grad_input = slope_middle + matmul_nt(slope_inputs.astype(bf16), turn_in)
    grad_input = grad_input.reshape(tokens.shape)
    grad_gain_one = jnp.sum(w_query.astype(f32) * query_sum.total, 1)
    own_kv = jnp.concatenate([key_projection, value_projection], 1).astype(f32)
    grad_gain_one = grad_gain_one + jnp.sum(own_kv * grads_rest[:, : 2 * key_width], 1)
    grad_gain_one = grad_gain_one / attn_gain.astype(f32)
    return (
        output,
        grad_input,
        grad_gain_one,
        grads_rest[:, 2 * key_width + experts],
        query_sum.total,
        grads_rest[:, :key_width],
        grads_rest[:, key_width : 2 * key_width],
        out_sum.total,
        grads_rest[:, 2 * key_width : 2 * key_width + experts],
        ended(grad_gate)[None],
        ended(grad_up)[None],
        ended(grad_down)[None],
    )


def solution(mesh):
    rows = P("seq", "ctx", None)
    shard = P(("seq", "ctx"), None)
    vector = P(("seq", "ctx"))
    expert = P("ctx", "seq", None)
    return jax.shard_map(
        body,
        mesh=mesh,
        in_specs=(rows, rows, rows, P("seq", "ctx"), P("seq", None), vector, vector)
        + (shard,) * 5
        + (expert,) * 3,
        out_specs=(rows, rows, vector, vector) + (shard,) * 5 + (expert,) * 3,
        check_vma=False,
    )
```
